32 devices in a mesh: dp: 4 (over y, core), fsdp: 8 (over z, x).
Axes of the slice: x: 2, y: 2, z: 4, core: 2. Of those that a mesh axis runs over, the one named last changes fastest.
Arguments:
- rows_in: bfloat16 [96, 320, 1024], P(('dp', 'fsdp')), may hold values from -6 to 6
- slot_row: int32 [192], P(('dp', 'fsdp')), may hold values from 0 to 11, as said below
- live_count: int32 [32], P(('dp', 'fsdp')), may hold values from 1 to 3, as said below
- slot_activation_gradient: bfloat16 [192, 320, 1024], P(('dp', 'fsdp')), may hold values from -6 to 6
- query_weight: bfloat16 [1024, 1024], P(('dp', 'fsdp')), may hold values from -0.1875 to 0.1875
- key_weight: bfloat16 [1024, 1024], P(('dp', 'fsdp')), may hold values from -0.1875 to 0.1875
- value_weight: bfloat16 [1024, 1024], P(('dp', 'fsdp')), may hold values from -0.1875 to 0.1875
- output_weight: bfloat16 [1024, 1024], P(('dp', 'fsdp')), may hold values from -1.5 to 1.5
- query_bias: bfloat16 [1024], P(('dp', 'fsdp')), may hold values from -3 to 3
- value_bias: bfloat16 [1024], P(('dp', 'fsdp')), may hold values from -3 to 3
- output_bias: bfloat16 [1024], P(('dp', 'fsdp')), may hold values from -3 to 3
- attn_gain: bfloat16 [1024], P(('dp', 'fsdp')), may hold values from 0.5 to 1.5
- attn_shift: bfloat16 [1024], P(('dp', 'fsdp')), may hold values from -3 to 3
- expand_weight: bfloat16 [1024, 4096], P(('dp', 'fsdp')), may hold values from -0.1875 to 0.1875
- up_bias: bfloat16 [4096], P(('dp', 'fsdp')), may hold values from -3 to 3
- down_weight: bfloat16 [4096, 1024], P(('dp', 'fsdp')), may hold values from -0.1875 to 0.1875
- down_bias: bfloat16 [1024], P(('dp', 'fsdp')), may hold values from -3 to 3
- ffn_gain: bfloat16 [1024], P(('dp', 'fsdp')), may hold values from 0.5 to 1.5
- ffn_shift: bfloat16 [1024], P(('dp', 'fsdp')), may hold values from -3 to 3
Outputs:
- slot_acts: bfloat16 [192, 320, 1024], P(('dp', 'fsdp'))
- input_grad: float32 [96, 320, 1024], P(('dp', 'fsdp'))
- query_weight_grad: float32 [1024, 1024], P(('dp', 'fsdp'))
- key_weight_grad: float32 [1024, 1024], P(('dp', 'fsdp'))
- value_weight_grad: float32 [1024, 1024], P(('dp', 'fsdp'))
- output_weight_grad: float32 [1024, 1024], P(('dp', 'fsdp'))
- query_bias_grad: float32 [1024], P(('dp', 'fsdp'))
- value_bias_grad: float32 [1024], P(('dp', 'fsdp'))
- output_bias_grad: float32 [1024], P(('dp', 'fsdp'))
- attn_gain_grad: float32 [1024], P(('dp', 'fsdp'))
- attn_shift_grad: float32 [1024], P(('dp', 'fsdp'))
- up_weight_grad: float32 [1024, 4096], P(('dp', 'fsdp'))
- up_bias_grad: float32 [4096], P(('dp', 'fsdp'))
- down_weight_grad: float32 [4096, 1024], P(('dp', 'fsdp'))
- down_bias_grad: float32 [1024], P(('dp', 'fsdp'))
- ffn_gain_grad: float32 [1024], P(('dp', 'fsdp'))
- ffn_shift_grad: float32 [1024], P(('dp', 'fsdp'))
The draws below stay inside these ranges and needn't reach their ends.
Inputs may be any that keep to these rules, and one draw needn't show every extreme that they name: v = slot_row[s] names row v % 3 of the device with dp index v // 3 and the slot's own fsdp index. Only live rows are named, and every live row is named by at least one slot. Row i of a device is live when i < live_count of that device. In every group of devices that share an fsdp index some device has 3.
All inputs are finite; a program needn't handle non-finite values.
Results may differ from the reference program's by a relative error of at most 0.02.
Values may be sent and summed in bfloat16 or wider, within the bound.
A program may use at most 256 MiB of HBM per device.

```python
import jax
import jax.numpy as jnp
from jax import lax

D = 1024
HEADS = 16
FF = 4096
SEQ = 320
U_CAP = 3
SLOTS_DEV = 6
UNIQUE = 96
SLOTS = 192
N_DP = 4
N_FSDP = 8


def dedup_tables(key):
    count_key, full_key, edge_key, place_key, extra_key = jax.random.split(key, 5)
    counts = jax.random.randint(count_key, (N_DP, N_FSDP), 1, U_CAP + 1)
    full_rank = jax.random.randint(full_key, (N_FSDP,), 0, N_DP)
    counts = counts.at[full_rank, jnp.arange(N_FSDP)].set(U_CAP)
    edge_group = jax.random.randint(edge_key, (), 0, N_FSDP)
    counts = counts.at[N_DP - 1, edge_group].set(U_CAP)
    group_slots = N_DP * SLOTS_DEV
    row_ids = jnp.arange(N_DP * U_CAP, dtype=jnp.int32)
    positions = jnp.arange(group_slots, dtype=jnp.int32)

    def one_group(group_counts, place_seed, extra_seed):
        live_rows = row_ids % U_CAP < group_counts[row_ids // U_CAP]
        listing = jnp.argsort(jnp.where(live_rows, 0, 1), stable=True).astype(jnp.int32)
        live_total = jnp.sum(live_rows.astype(jnp.int32))
        surplus_rank = jax.random.randint(extra_seed, (group_slots,), 0, live_total)
        ranks = jnp.where(positions < live_total, positions, surplus_rank)
        chosen = listing[ranks]
        placing = jax.random.permutation(place_seed, group_slots)
        return jnp.zeros((group_slots,), jnp.int32).at[placing].set(chosen)
    tables = jax.vmap(one_group)(counts.T, jax.random.split(place_key, N_FSDP), jax.random.split(extra_key, N_FSDP))
    slots = jnp.transpose(tables.reshape(N_FSDP, N_DP, SLOTS_DEV), (1, 0, 2)).reshape(-1)
    return (slots.astype(jnp.int32), counts.reshape(-1).astype(jnp.int32))


def draw_slot_row(key, part):
    slots, counts = dedup_tables(key)
    return slots


def draw_live_count(key, part):
    slots, counts = dedup_tables(key)
    return counts


def spiked(result, rng, source, target, blocks, factor):
    def block_of(position):
        return (jnp.arange(result.shape[position]) // (result.shape[position] // blocks)).reshape((-1,) + (1,) * (result.ndim - 1 - position))

    one_side = jax.random.permutation(rng, blocks)[block_of(target)]
    far = (block_of(target) + blocks // 2) % blocks
    return jnp.where((block_of(source) == one_side) | (block_of(source) == far), factor * result, result)


def level_of(own_key, extent, cuts, least, largest):
    def one(dim, shards_of):
        heights = jax.random.uniform(jax.random.fold_in(jax.random.fold_in(own_key, 6), dim), (shards_of,), jnp.float32, least / len(cuts), largest / len(cuts))
        return jnp.repeat(jnp.exp(heights), extent[dim] // shards_of).reshape((-1,) + (1,) * (len(extent) - dim - 1))

    level = one(*cuts[0])
    for cut in cuts[1:]:
        level = level * one(*cut)
    return level


def scatter_about(stream_key, extent, width, bound, cuts=(), kind=jnp.bfloat16):
    loudness = level_of(stream_key, extent, cuts, -0.22, 0.18) if cuts else 1.0
    result = jax.random.normal(stream_key, extent, jnp.float32) * width * loudness
    return jnp.minimum(jnp.maximum(result, -bound), bound).astype(kind)


def heavy_noise(own_key, extent, width, bound, cuts, heavy, kind=jnp.bfloat16):
    entries = width * jax.random.normal(own_key, extent, jnp.float32)
    if cuts:
        entries = entries * level_of(own_key, extent, cuts, -0.22, 0.18)
    return jnp.clip(spiked(entries, jax.random.fold_in(own_key, 3), *heavy), -bound, bound).astype(kind)


def setup_inputs(seed: int = 0) -> dict:
    key_list = jax.random.split(jax.random.key(seed), 20)
    return {
        "rows_in": heavy_noise(key_list[0], (UNIQUE, SEQ, D), 1.0, 6.0, ((0, 32),), (0, 2, 32, 2.75)),
        "slot_row": draw_slot_row(jax.random.fold_in(key_list[19], 71), 0),
        "live_count": draw_live_count(jax.random.fold_in(key_list[19], 71), 0),
        "slot_activation_gradient": scatter_about(key_list[3], (SLOTS, SEQ, D), 1.0, 6.0, ((0, 32),)),
        "query_weight": scatter_about(key_list[4], (D, D), D ** -0.5, 0.1875, ((0, 32),)),
        "key_weight": scatter_about(key_list[5], (D, D), D ** -0.5, 0.1875, ((0, 32),)),
        "value_weight": scatter_about(key_list[6], (D, D), D ** -0.5, 0.1875, ((0, 32),)),
        "output_weight": scatter_about(key_list[7], (D, D), (D // 64) ** -0.5, 1.5, ((0, 32),)),
        "query_bias": scatter_about(key_list[8], (D,), 0.5, 3.0, ((0, 32),)),
        "value_bias": scatter_about(key_list[9], (D,), 0.5, 3.0, ((0, 32),)),
        "output_bias": scatter_about(key_list[10], (D,), 0.5, 3.0, ((0, 32),)),
        "attn_gain": jnp.clip(1.0 + 0.1 * jax.random.normal(key_list[11], (D,), jnp.float32), 0.5, 1.5).astype(jnp.bfloat16),
        "attn_shift": scatter_about(key_list[12], (D,), 0.5, 3.0, ((0, 32),)),
        "expand_weight": scatter_about(key_list[13], (D, FF), D ** -0.5, 0.1875, ((0, 32),)),
        "up_bias": scatter_about(key_list[14], (FF,), 0.5, 3.0, ((0, 32),)),
        "down_weight": scatter_about(key_list[15], (FF, D), (FF // 4) ** -0.5, 0.1875, ((0, 32),)),
        "down_bias": scatter_about(key_list[16], (D,), 0.5, 3.0, ((0, 32),)),
        "ffn_gain": jnp.clip(1.0 + 0.1 * jax.random.normal(key_list[17], (D,), jnp.float32), 0.5, 1.5).astype(jnp.bfloat16),
        "ffn_shift": scatter_about(key_list[18], (D,), 0.5, 3.0, ((0, 32),)),
    }


EPSILON = 1e-05
HIGH = lax.Precision.HIGHEST

@jax.custom_vjp
def low(v):
    return lax.optimization_barrier(v.astype(jnp.bfloat16)).astype(jnp.float32)

@jax.custom_vjp
def low_back(v):
    return v

def low_keep(v):
    return (low(v), None)

def low_pass(kept, grad):
    return (grad,)

def back_keep(v):
    return (v, None)

def back_low(kept, grad):
    return (low(grad),)
low.defvjp(low_keep, low_pass)
low_back.defvjp(back_keep, back_low)

def norm_apply(hidden, gain, shift):
    center = hidden - lax.optimization_barrier(jnp.mean(hidden, axis=-1, keepdims=True))
    inverse = lax.rsqrt(lax.optimization_barrier(jnp.mean(center * center, axis=-1, keepdims=True)) + EPSILON)
    return center * inverse * gain + shift

def project_rows(acts, weight):
    return jnp.einsum('rsd,de->rse', acts, weight, precision=HIGH)

def layer(params, inputs):
    query_weight, key_weight, value_weight, output_weight, query_bias, value_bias, output_bias, attn_gain, attn_shift, expand_weight, up_bias, down_weight, down_bias, ffn_gain, ffn_shift = params
    row_count, token_count, feature_count = inputs.shape
    head_size = feature_count // HEADS
    split_shape = (row_count, token_count, HEADS, head_size)
    query = low(low_back(project_rows(inputs, query_weight) + query_bias)).reshape(split_shape)
    keys = low(low_back(project_rows(inputs, key_weight))).reshape(split_shape)
    values = low(low_back(project_rows(inputs, value_weight) + value_bias)).reshape(split_shape)
    scores = low_back(head_size ** (-0.5) * jnp.einsum('rqhd,rkhd->rhqk', query, keys, precision=HIGH))
    probs = low(jax.nn.softmax(scores, axis=-1))
    mixed = jnp.einsum('rhqk,rkhd->rqhd', probs, values, precision=HIGH)
    mixed = low(low_back(mixed.reshape(row_count, token_count, feature_count)))
    attn_out = low_back(project_rows(mixed, output_weight) + output_bias)
    normed1 = norm_apply(inputs + attn_out, attn_gain, attn_shift)
    pre_act = low_back(project_rows(low(normed1), expand_weight) + up_bias)
    act_low = low(jax.nn.gelu(pre_act, approximate=False))
    ffn_out = low_back(project_rows(act_low, down_weight) + down_bias)
    return norm_apply(normed1 + ffn_out, ffn_gain, ffn_shift)

def reference(rows_in, slot_row, live_count, slot_activation_gradient, query_weight, key_weight, value_weight, output_weight, query_bias, value_bias, output_bias, attn_gain, attn_shift, expand_weight, up_bias, down_weight, down_bias, ffn_gain, ffn_shift):
    device_total = N_DP * N_FSDP
    unique_total, token_count, feature_count = rows_in.shape
    slots_each = slot_activation_gradient.shape[0] // device_total
    rows_each = unique_total // device_total
    device_ids = jnp.arange(device_total, dtype=jnp.int32)
    group_ids = device_ids % N_FSDP
    group_rows = slot_row.reshape(device_total, slots_each)
    targets = (group_rows // rows_each * N_FSDP + group_ids[:, None]) * rows_each + group_rows % rows_each
    flat_grads = slot_activation_gradient.astype(jnp.float32).reshape(device_total * slots_each, token_count * feature_count)
    matching = targets[:, :, None] == targets[:, None, :]
    first_match = jnp.argmax(matching, axis=-1).astype(jnp.int32)
    leader_ids = (device_ids[:, None] * slots_each + first_match).reshape(-1).astype(jnp.int32)
    partial_sums = low(jax.ops.segment_sum(flat_grads, leader_ids, num_segments=device_total * slots_each))
    upstream = jax.ops.segment_sum(partial_sums, targets.reshape(-1).astype(jnp.int32), num_segments=unique_total)
    params = tuple((weight.astype(jnp.float32) for weight in (query_weight, key_weight, value_weight, output_weight, query_bias, value_bias, output_bias, attn_gain, attn_shift, expand_weight, up_bias, down_weight, down_bias, ffn_gain, ffn_shift)))
    block_rows = 4 * rows_each
    block_count = unique_total // block_rows
    inputs = rows_in.astype(jnp.float32).reshape(block_count, block_rows, token_count, feature_count)
    cotangent = upstream.reshape(block_count, block_rows, token_count, feature_count)

    def block_step(running, pair):
        inputs_block, cot_block = pair
        output, pullback = jax.vjp(layer, params, inputs_block)
        param_grads, input_grads = pullback(cot_block)
        return (jax.tree.map(jnp.add, running, param_grads), (output, input_grads))
    zeros = jax.tree.map(jnp.zeros_like, params)
    sums, (output_rows, input_grads) = lax.scan(block_step, zeros, (inputs, cotangent))
    outputs_low = output_rows.reshape(unique_total, token_count, feature_count).astype(jnp.bfloat16)
    slot_acts = outputs_low[targets.reshape(-1)]
    row_ids = jnp.arange(unique_total, dtype=jnp.int32)
    live_rows = row_ids % rows_each < live_count[row_ids // rows_each]
    input_grad = jnp.where(live_rows[:, None, None], input_grads.reshape(unique_total, token_count, feature_count), 0.0)
    return (slot_acts, input_grad, sums[0], sums[1], sums[2], sums[3], sums[4], sums[5], sums[6], sums[7], sums[8], sums[9], sums[10], sums[11], sums[12], sums[13], sums[14])
```

```python
from functools import partial

import jax
import jax.numpy as jnp
from jax import lax
from jax.sharding import PartitionSpec as P

HEADS = 16


EPSILON = 1e-05


def norm_forward(hidden, gain, shift):
    center = hidden - jnp.mean(hidden, axis=-1, keepdims=True)
    inverse = lax.rsqrt(jnp.mean(center * center, axis=-1, keepdims=True) + EPSILON)
    normed = center * inverse
    return (normed * gain + shift, normed, inverse)


def norm_backward(incoming, gain, normed, inverse):
    scaled = incoming * gain
    inner = (
        scaled
        - jnp.mean(scaled, axis=-1, keepdims=True)
        - normed * jnp.mean(scaled * normed, axis=-1, keepdims=True)
    )
    return (
        inner * inverse,
        jnp.sum(incoming * normed, axis=(0, 1)),
        jnp.sum(incoming, axis=(0, 1)),
    )


def apply_weight(acts, weight):
    return jnp.einsum("rsd,de->rse", acts, weight, preferred_element_type=jnp.float32)


def apply_back(grads, weight):
    return jnp.einsum("rse,de->rsd", grads, weight, preferred_element_type=jnp.float32)


def weight_term(acts, grads):
    return jnp.einsum("rsd,rse->de", acts, grads, preferred_element_type=jnp.float32)


def bias_term(grads):
    return jnp.sum(grads, axis=(0, 1), dtype=jnp.float32)


def on_device(
    rows_in,
    slot_row,
    live_count,
    slot_activation_gradient,
    query_weight,
    key_weight,
    value_weight,
    output_weight,
    query_bias,
    value_bias,
    output_bias,
    attn_gain,
    attn_shift,
    expand_weight,
    up_bias,
    down_weight,
    down_bias,
    ffn_gain,
    ffn_shift,
):
    row_count, token_count, feature_count = rows_in.shape
    head_size = feature_count // HEADS
    score_scale = head_size ** (-0.5)
    split_shape = (row_count, token_count, HEADS, head_size)
    wanted = lax.broadcasted_iota(
        jnp.int32, (row_count * lax.axis_size("dp"), slot_row.shape[0]), 0
    )
    one_hot_matrix = (wanted == slot_row[None, :]).astype(jnp.bfloat16)
    upstream = lax.psum_scatter(
        jnp.einsum(
            "az,zfy->afy",
            one_hot_matrix,
            slot_activation_gradient,
            preferred_element_type=jnp.float32,
        ).astype(jnp.bfloat16),
        "dp",
        scatter_dimension=0,
        tiled=True,
    ).astype(jnp.float32)
    smalls = (query_bias, value_bias, output_bias, attn_gain, attn_shift, down_bias, ffn_gain, ffn_shift)
    small_rows = query_bias.shape[0]
    packed = jnp.concatenate([v.reshape(-1, small_rows) for v in (*smalls, up_bias)], axis=0)
    packed_full = lax.all_gather(packed, ("dp", "fsdp"), axis=0)
    (
        qbias_full,
        vbias_full,
        obias_full,
        gain1_full,
        shift1_full,
        downbias_full,
        gain2_full,
        shift2_full,
    ) = (packed_full[:, i].reshape(-1) for i in range(8))
    upbias_full = packed_full[:, 8:].reshape(-1)
    query_full, key_full, value_full, output_full, up_full, down_full = (
        lax.all_gather(weight, ("dp", "fsdp"), axis=0, tiled=True)
        for weight in (query_weight, key_weight, value_weight, output_weight, expand_weight, down_weight)
    )
    inputs = rows_in.astype(jnp.float32)
    query = (apply_weight(rows_in, query_full) + qbias_full.astype(jnp.float32)).astype(
        jnp.bfloat16
    )
    keys = apply_weight(rows_in, key_full).astype(jnp.bfloat16)
    values = (apply_weight(rows_in, value_full) + vbias_full.astype(jnp.float32)).astype(
        jnp.bfloat16
    )
    query_heads = query.reshape(split_shape)
    key_heads = keys.reshape(split_shape)
    value_heads = values.reshape(split_shape)
    scores = (
        jnp.einsum("rqhd,rkhd->rhqk", query_heads, key_heads, preferred_element_type=jnp.float32)
        * score_scale
    )
    row_top = jnp.max(scores, axis=-1, keepdims=True)
    expo = jnp.exp(scores - row_top)
    row_sum = jnp.sum(expo, axis=-1, keepdims=True)
    logsum = row_top + jnp.log(row_sum)
    probs_low = (expo / row_sum).astype(jnp.bfloat16)
    mixed = jnp.einsum(
        "rhqk,rkhd->rqhd", probs_low, value_heads, preferred_element_type=jnp.float32
    )
    mixed = mixed.reshape(row_count, token_count, feature_count).astype(jnp.bfloat16)
    gain1 = gain1_full.astype(jnp.float32)
    resid1 = inputs + apply_weight(mixed, output_full) + obias_full.astype(jnp.float32)
    normed1_out, normed1, inverse1 = norm_forward(resid1, gain1, shift1_full.astype(jnp.float32))
    normed1_low = normed1_out.astype(jnp.bfloat16)
    pre_act = apply_weight(normed1_low, up_full) + upbias_full.astype(jnp.float32)
    act_low = jax.nn.gelu(pre_act, approximate=False).astype(jnp.bfloat16)
    gain2 = gain2_full.astype(jnp.float32)
    resid2 = normed1_out + apply_weight(act_low, down_full) + downbias_full.astype(jnp.float32)
    final, second_normed, inverse2 = norm_forward(resid2, gain2, shift2_full.astype(jnp.float32))
    final_low = final.astype(jnp.bfloat16)
    shard_rows = lax.all_gather(final_low, "dp", axis=0, tiled=True)
    span_rows = shard_rows.shape[0]
    inside = (slot_row >= 0) & (slot_row < span_rows)
    picked = jnp.take(shard_rows, jnp.clip(slot_row, 0, span_rows - 1), axis=0)
    slot_acts = jnp.where(
        inside[:, None, None], picked, jnp.zeros(slot_activation_gradient.shape, jnp.bfloat16)
    )
    gain1 = gain1_full.astype(jnp.float32)
    gain2 = gain2_full.astype(jnp.float32)
    grad2, gain2_grad, shift2_grad = norm_backward(upstream, gain2, second_normed, inverse2)
    ffn_low = grad2.astype(jnp.bfloat16)
    down_grad = weight_term(act_low, ffn_low)
    down_bias_grad = bias_term(ffn_low)
    act_grad = apply_back(ffn_low, down_full)
    gelu_value, gelu_back = jax.vjp(partial(jax.nn.gelu, approximate=False), pre_act)
    pre_grad = gelu_back(act_grad)[0].astype(jnp.bfloat16)
    up_grad = weight_term(normed1_low, pre_grad)
    up_bias_grad = bias_term(pre_grad)
    normed1_grad = grad2 + apply_back(pre_grad, up_full)
    grad1, gain1_grad, shift1_grad = norm_backward(normed1_grad, gain1, normed1, inverse1)
    attn_low = grad1.astype(jnp.bfloat16)
    output_grad = weight_term(mixed, attn_low)
    output_bias_grad = bias_term(attn_low)
    mixed_grad = apply_back(attn_low, output_full).astype(jnp.bfloat16).reshape(split_shape)
    scores_again = (
        jnp.einsum("rqhd,rkhd->rhqk", query_heads, key_heads, preferred_element_type=jnp.float32)
        * score_scale
    )
    probs = jnp.exp(scores_again - logsum)
    probs_again = probs.astype(jnp.bfloat16)
    value_grad = jnp.einsum(
        "rhqk,rqhd->rkhd", probs_again, mixed_grad, preferred_element_type=jnp.float32
    )
    value_grad = value_grad.astype(jnp.bfloat16).reshape(row_count, token_count, feature_count)
    prob_grad = jnp.einsum(
        "rqhd,rkhd->rhqk", mixed_grad, value_heads, preferred_element_type=jnp.float32
    )
    score_grad = (probs * (prob_grad - jnp.sum(probs * prob_grad, axis=-1, keepdims=True))).astype(
        jnp.bfloat16
    )
    query_grad = (
        jnp.einsum("rhqk,rkhd->rqhd", score_grad, key_heads, preferred_element_type=jnp.float32)
        * score_scale
    )
    query_grad = query_grad.astype(jnp.bfloat16).reshape(row_count, token_count, feature_count)
    key_grad = (
        jnp.einsum("rhqk,rqhd->rkhd", score_grad, query_heads, preferred_element_type=jnp.float32)
        * score_scale
    )
    key_grad = key_grad.astype(jnp.bfloat16).reshape(row_count, token_count, feature_count)
    query_wgrad = weight_term(rows_in, query_grad)
    key_wgrad = weight_term(rows_in, key_grad)
    value_wgrad = weight_term(rows_in, value_grad)
    query_bias_grad = bias_term(query_grad)
    value_bias_grad = bias_term(value_grad)
    input_full = (
        grad1
        + apply_back(query_grad, query_full)
        + apply_back(key_grad, key_full)
        + apply_back(value_grad, value_full)
    )
    live_rows = lax.broadcasted_iota(jnp.int32, (row_count,), 0) < live_count[0]
    input_grad = jnp.where(live_rows[:, None, None], input_full, 0.0)
    devices = packed_full.shape[0]
    small_terms = jnp.concatenate(
        [
            v.reshape(devices, -1, small_rows)
            for v in (
                query_bias_grad,
                value_bias_grad,
                output_bias_grad,
                gain1_grad,
                shift1_grad,
                down_bias_grad,
                gain2_grad,
                shift2_grad,
                up_bias_grad,
            )
        ],
        axis=1,
    )
    small_sum = lax.psum_scatter(small_terms, ("dp", "fsdp"), scatter_dimension=0, tiled=True)[0]
    down_sum, up_sum, output_sum, value_sum, query_sum, key_sum = (
        lax.psum_scatter(
            term.astype(jnp.bfloat16), ("dp", "fsdp"), scatter_dimension=0, tiled=True
        ).astype(jnp.float32)
        for term in (down_grad, up_grad, output_grad, value_wgrad, query_wgrad, key_wgrad)
    )
    return (
        slot_acts,
        input_grad,
        query_sum,
        key_sum,
        value_sum,
        output_sum,
        small_sum[0],
        small_sum[1],
        small_sum[2],
        small_sum[3],
        small_sum[4],
        up_sum,
        small_sum[8:].reshape(-1),
        down_sum,
        small_sum[5],
        small_sum[6],
        small_sum[7],
    )


def solution(mesh):
    placed = (
        P(("dp", "fsdp"), None, None),
        P(("dp", "fsdp")),
        P(("dp", "fsdp")),
        P(("dp", "fsdp"), None, None),
        P(("dp", "fsdp"), None),
        P(("dp", "fsdp"), None),
        P(("dp", "fsdp"), None),
        P(("dp", "fsdp"), None),
        P(("dp", "fsdp")),
        P(("dp", "fsdp")),
        P(("dp", "fsdp")),
        P(("dp", "fsdp")),
        P(("dp", "fsdp")),
        P(("dp", "fsdp"), None),
        P(("dp", "fsdp")),
        P(("dp", "fsdp"), None),
        P(("dp", "fsdp")),
        P(("dp", "fsdp")),
        P(("dp", "fsdp")),
    )
    return jax.shard_map(
        on_device,
        mesh=mesh,
        in_specs=placed,
        out_specs=(
            P(("dp", "fsdp"), None, None),
            P(("dp", "fsdp"), None, None),
            P(("dp", "fsdp"), None),
            P(("dp", "fsdp"), None),
            P(("dp", "fsdp"), None),
            P(("dp", "fsdp"), None),
            P(("dp", "fsdp")),
            P(("dp", "fsdp")),
            P(("dp", "fsdp")),
            P(("dp", "fsdp")),
            P(("dp", "fsdp")),
            P(("dp", "fsdp"), None),
            P(("dp", "fsdp")),
            P(("dp", "fsdp"), None),
            P(("dp", "fsdp")),
            P(("dp", "fsdp")),
            P(("dp", "fsdp")),
        ),
        check_vma=False,
    )
```

```python
from functools import partial

import jax
import jax.numpy as jnp
from jax import lax
from jax.experimental import pallas as pl
from jax.experimental.pallas import tpu as pltpu
from jax.sharding import PartitionSpec as P

HEADS = 16


EPSILON = 1e-05


MESH = pl.DeviceIdType.MESH
LANES = 128


def place(nz, nx):
    dp, fs = lax.axis_index("dp"), lax.axis_index("fsdp")
    y, core = dp // 2, lax.rem(dp, 2)
    z, x = fs // nx, lax.rem(fs, nx)
    return y, core, z, x


def device(y, core, z, x, nx):
    return (y * 2 + core, z * nx + x)


class Partners:
    def __init__(self, nz, nx):
        self.nz, self.nx = nz, nx
        self.y, self.core, self.z, self.x = place(nz, nx)
        y, core, z, x = self.y, self.core, self.z, self.x
        self.sibling = device(y, 1 - core, z, x, nx)
        self.across_x = device(y, core, z, 1 - x, nx)
        self.across_y = device(1 - y, core, z, x, nx)
        self.along_z = [device(y, core, lax.rem(z + k, nz), x, nx) for k in range(1, nz)]
        self.all = [self.sibling, self.across_x, self.across_y, *self.along_z]

    def meet(self):
        barrier = pltpu.get_barrier_semaphore()
        for other in self.all:
            pl.semaphore_signal(barrier, inc=1, device_id=other, device_id_type=MESH)
        pl.semaphore_wait(barrier, len(self.all))


def remote(src, dst, send, recv, to):
    return pltpu.make_async_remote_copy(
        src_ref=src, dst_ref=dst, send_sem=send, recv_sem=recv, device_id=to, device_id_type=MESH
    )


def added(*blocks):
    total = blocks[0].astype(jnp.float32)
    for block in blocks[1:]:
        total = total + block.astype(jnp.float32)
    return total


class Scatter:
    def __init__(self, at, wide, rc, r3a, r3b, r2, rz, send, recv):
        self.at, self.wide = at, wide
        self.rc, self.r3a, self.r3b, self.r2, self.rz = rc, r3a, r3b, r2, rz
        self.send, self.recv = send, recv

    def to_sibling(self, m, theirs):
        return remote(theirs, self.rc.at[m], self.send.at[m, 0], self.recv.at[m, 0], self.at.sibling)

    def first_a(self, m):
        at, wide = self.at, self.wide
        src = self.rc.at[m, :, :, 1 - at.x, :, pl.ds(0, wide)]
        return remote(src, self.r3a.at[m], self.send.at[m, 1], self.recv.at[m, 1], at.across_x)

    def first_b(self, m):
        at, wide = self.at, self.wide
        src = self.rc.at[m, 1 - at.y, :, :, :, pl.ds(wide, self.rc.shape[-1] - wide)]
        return remote(src, self.r3b.at[m], self.send.at[m, 2], self.recv.at[m, 2], at.across_y)

    def second_a(self, m):
        at, wide = self.at, self.wide
        src, dst = self.r3a.at[m, 1 - at.y], self.r2.at[m, :, :, pl.ds(0, wide)]
        return remote(src, dst, self.send.at[m, 3], self.recv.at[m, 3], at.across_y)

    def second_b(self, m):
        at, wide = self.at, self.wide
        src = self.r3b.at[m, :, 1 - at.x]
        dst = self.r2.at[m, :, :, pl.ds(wide, self.r2.shape[-1] - wide)]
        return remote(src, dst, self.send.at[m, 4], self.recv.at[m, 4], at.across_x)

    def last(self, m, k):
        at = self.at
        src = self.r2.at[m, lax.rem(at.z + k, at.nz)]
        return remote(src, self.rz.at[m, k - 1], self.send.at[m, 4 + k], self.recv.at[m, 4 + k], at.along_z[k - 1])

    def start(self, m, theirs):
        self.to_sibling(m, theirs).start()

    def step1(self, m, own):
        at, rc = self.at, self.rc
        self.to_sibling(m, rc.at[m]).wait_recv()
        nz = at.nz

        def add(i, carry):
            y, z = i // nz, lax.rem(i, nz)
            rc[m, y, z] = added(rc[m, y, z], own(y, z)).astype(rc.dtype)
            return carry

        lax.fori_loop(0, rc.shape[1] * nz, add, 0)
        self.first_a(m).start()
        self.first_b(m).start()

    def step2(self, m):
        at, rc, wide, r3a, r3b = self.at, self.rc, self.wide, self.r3a, self.r3b
        columns = rc.shape[-1]
        self.first_a(m).wait_recv()
        self.first_b(m).wait_recv()

        def add(z, carry):
            for y in range(rc.shape[1]):
                r3a[m, y, z] = added(r3a[m, y, z], rc[m, y, z, at.x, :, pl.ds(0, wide)]).astype(rc.dtype)
            r3b[m, z] = added(r3b[m, z], rc[m, at.y, z, :, :, pl.ds(wide, columns - wide)]).astype(rc.dtype)
            return carry

        lax.fori_loop(0, at.nz, add, 0)
        self.second_a(m).start()
        self.second_b(m).start()

    def step3(self, m):
        at, r3a, r3b, r2, wide = self.at, self.r3a, self.r3b, self.r2, self.wide
        columns = r2.shape[-1]
        self.second_a(m).wait_recv()
        self.second_b(m).wait_recv()

        def add(z, carry):
            left, right = pl.ds(0, wide), pl.ds(wide, columns - wide)
            r2[m, z, :, left] = added(r2[m, z, :, left], r3a[m, at.y, z]).astype(r2.dtype)
            r2[m, z, :, right] = added(r2[m, z, :, right], r3b[m, z, at.x]).astype(r2.dtype)
            return carry

        lax.fori_loop(0, at.nz, add, 0)
        for k in range(1, at.nz):
            self.last(m, k).start()

    def step4(self, m, out):
        at = self.at
        for k in range(1, at.nz):
            self.last(m, k).wait_recv()
        out[m] = added(self.r2[m, at.z], *[self.rz[m, k] for k in range(at.nz - 1)])

    def drain(self, m):
        self.to_sibling(m, self.rc.at[m]).wait_send()
        self.first_a(m).wait_send()
        self.first_b(m).wait_send()
        self.second_a(m).wait_send()
        self.second_b(m).wait_send()
        for k in range(1, self.at.nz):
            self.last(m, k).wait_send()


class SmallSum:
    def __init__(self, at, total, landing, send, recv):
        self.at, self.total, self.landing, self.send, self.recv = at, total, landing, send, recv

    def hop(self, i, to):
        return remote(self.total.at[i], self.landing.at[i], self.send.at[i], self.recv.at[i], to)

    def along(self, k):
        i = 2 + k
        return remote(self.total.at[3], self.landing.at[i], self.send.at[i], self.recv.at[i], self.at.along_z[k - 1])

    def start(self):
        self.hop(0, self.at.sibling).start()

    def step(self, i):
        at = self.at
        to = (at.sibling, at.across_x, at.across_y)
        self.hop(i, to[i]).wait_recv()
        self.total[i + 1] = self.total[i] + self.landing[i]
        if i < 2:
            self.hop(i + 1, to[i + 1]).start()
        else:
            for k in range(1, at.nz):
                self.along(k).start()

    def finish(self, out):
        at = self.at
        for k in range(1, at.nz):
            self.along(k).wait_recv()
        total = self.total[3]
        for k in range(1, at.nz):
            total = total + self.landing[2 + k]
        out[...] = total
        to = (at.sibling, at.across_x, at.across_y)
        for i in range(3):
            self.hop(i, to[i]).wait_send()
        for k in range(1, at.nz):
            self.along(k).wait_send()


def scatter_kernel(nz, nx, wide, count, terms, small, out, small_out, own, rc, r3a, r3b, r2, rz, send, recv, total, landing, ssend, srecv, osem):
    at = Partners(nz, nx)
    at.meet()
    scatter = Scatter(at, wide, rc, r3a, r3b, r2, rz, send, recv)
    sums = SmallSum(at, total, landing, ssend, srecv)
    total[0] = small[...]
    sums.start()

    def fetch(m):
        slot = lax.rem(m, 2)
        return pltpu.make_async_copy(terms.at[m, :, at.core], own.at[slot], osem.at[slot])

    def tick(i, carry):
        @pl.when(i < count)
        def _():
            fetch(i).start()
            scatter.start(i, terms.at[i, :, 1 - at.core])

        @pl.when((i >= 1) & (i < count + 1))
        def _():
            m = i - 1
            fetch(m).wait()
            slot = lax.rem(m, 2)
            scatter.step1(m, lambda y, z: own[slot, y, z])

        @pl.when((i >= 2) & (i < count + 2))
        def _():
            scatter.step2(i - 2)

        @pl.when((i >= 3) & (i < count + 3))
        def _():
            scatter.step3(i - 3)

        @pl.when(i >= 4)
        def _():
            scatter.step4(i - 4, out)

        return carry

    lax.fori_loop(0, 4, tick, 0)
    for i in range(3):
        sums.step(i)
    lax.fori_loop(4, count + 4, tick, 0)
    sums.finish(small_out)

    def drain(m, carry):
        scatter.drain(m)
        return carry

    lax.fori_loop(0, count, drain, 0)


def scatter_scratch(count, nz, nx, rows, columns, wide):
    bf16 = jnp.bfloat16
    return [
        pltpu.VMEM((count, 2, nz, nx, rows, columns), bf16),
        pltpu.VMEM((count, 2, nz, rows, wide), bf16),
        pltpu.VMEM((count, nz, nx, rows, columns - wide), bf16),
        pltpu.VMEM((count, nz, rows, columns), bf16),
        pltpu.VMEM((count, nz - 1, rows, columns), bf16),
        pltpu.SemaphoreType.DMA((count, 4 + nz)),
        pltpu.SemaphoreType.DMA((count, 4 + nz)),
    ]


def small_scratch(nz, shape):
    return [
        pltpu.VMEM((4, *shape), jnp.float32),
        pltpu.VMEM((2 + nz, *shape), jnp.float32),
        pltpu.SemaphoreType.DMA((2 + nz,)),
        pltpu.SemaphoreType.DMA((2 + nz,)),
    ]


def scatter_terms(terms, small, nz, nx):
    count, _, _, _, _, rows, columns = terms.shape
    wide = columns * 3 // 4
    vmem = pl.BlockSpec(memory_space=pltpu.VMEM)
    return pl.pallas_call(
        partial(scatter_kernel, nz, nx, wide, count),
        out_shape=[
            jax.ShapeDtypeStruct((count, rows, columns), jnp.float32),
            jax.ShapeDtypeStruct(small.shape, jnp.float32),
        ],
        in_specs=[pl.BlockSpec(memory_space=pl.ANY), vmem],
        out_specs=[vmem, vmem],
        scratch_shapes=[
            pltpu.VMEM((2, 2, nz, nx, rows, columns), jnp.bfloat16),
            *scatter_scratch(count, nz, nx, rows, columns, wide),
            *small_scratch(nz, small.shape),
            pltpu.SemaphoreType.DMA((2,)),
        ],
        compiler_params=pltpu.CompilerParams(
            collective_id=2, has_side_effects=True, vmem_limit_bytes=56 * 2**20
        ),
    )(terms, small)


def norm_forward(hidden, gain, shift):
    center = hidden - jnp.mean(hidden, axis=-1, keepdims=True)
    inverse = lax.rsqrt(jnp.mean(center * center, axis=-1, keepdims=True) + EPSILON)
    normed = center * inverse
    return (normed * gain + shift, normed, inverse)


def norm_backward(incoming, gain, normed, inverse):
    scaled = incoming * gain
    inner = (
        scaled
        - jnp.mean(scaled, axis=-1, keepdims=True)
        - normed * jnp.mean(scaled * normed, axis=-1, keepdims=True)
    )
    return (
        inner * inverse,
        jnp.sum(incoming * normed, axis=(0, 1)),
        jnp.sum(incoming, axis=(0, 1)),
    )


def apply_weight(acts, weight):
    return jnp.einsum("rsd,de->rse", acts, weight, preferred_element_type=jnp.float32)


def apply_back(grads, weight):
    return jnp.einsum("rse,de->rsd", grads, weight, preferred_element_type=jnp.float32)


def weight_term(acts, grads):
    return jnp.einsum("rsd,rse->de", acts, grads, preferred_element_type=jnp.float32)


def bias_term(grads):
    return jnp.sum(grads, axis=(0, 1), dtype=jnp.float32)


def on_device(
    rows_in,
    slot_row,
    live_count,
    slot_activation_gradient,
    query_weight,
    key_weight,
    value_weight,
    output_weight,
    query_bias,
    value_bias,
    output_bias,
    attn_gain,
    attn_shift,
    expand_weight,
    up_bias,
    down_weight,
    down_bias,
    ffn_gain,
    ffn_shift,
):
    row_count, token_count, feature_count = rows_in.shape
    head_size = feature_count // HEADS
    score_scale = head_size ** (-0.5)
    split_shape = (row_count, token_count, HEADS, head_size)
    wanted = lax.broadcasted_iota(
        jnp.int32, (row_count * lax.axis_size("dp"), slot_row.shape[0]), 0
    )
    one_hot_matrix = (wanted == slot_row[None, :]).astype(jnp.bfloat16)
    upstream = lax.psum_scatter(
        jnp.einsum(
            "az,zfy->afy",
            one_hot_matrix,
            slot_activation_gradient,
            preferred_element_type=jnp.float32,
        ).astype(jnp.bfloat16),
        "dp",
        scatter_dimension=0,
        tiled=True,
    ).astype(jnp.float32)
    smalls = (query_bias, value_bias, output_bias, attn_gain, attn_shift, down_bias, ffn_gain, ffn_shift)
    small_rows = query_bias.shape[0]
    packed = jnp.concatenate([v.reshape(-1, small_rows) for v in (*smalls, up_bias)], axis=0)
    packed_full = lax.all_gather(packed, ("dp", "fsdp"), axis=0)
    (
        qbias_full,
        vbias_full,
        obias_full,
        gain1_full,
        shift1_full,
        downbias_full,
        gain2_full,
        shift2_full,
    ) = (packed_full[:, i].reshape(-1) for i in range(8))
    upbias_full = packed_full[:, 8:].reshape(-1)
    query_full, key_full, value_full, output_full, up_full, down_full = (
        lax.all_gather(weight, ("dp", "fsdp"), axis=0, tiled=True)
        for weight in (query_weight, key_weight, value_weight, output_weight, expand_weight, down_weight)
    )
    inputs = rows_in.astype(jnp.float32)
    query = (apply_weight(rows_in, query_full) + qbias_full.astype(jnp.float32)).astype(
        jnp.bfloat16
    )
    keys = apply_weight(rows_in, key_full).astype(jnp.bfloat16)
    values = (apply_weight(rows_in, value_full) + vbias_full.astype(jnp.float32)).astype(
        jnp.bfloat16
    )
    query_heads = query.reshape(split_shape)
    key_heads = keys.reshape(split_shape)
    value_heads = values.reshape(split_shape)
    scores = (
        jnp.einsum("rqhd,rkhd->rhqk", query_heads, key_heads, preferred_element_type=jnp.float32)
        * score_scale
    )
    row_top = jnp.max(scores, axis=-1, keepdims=True)
    expo = jnp.exp(scores - row_top)
    row_sum = jnp.sum(expo, axis=-1, keepdims=True)
    logsum = row_top + jnp.log(row_sum)
    probs_low = (expo / row_sum).astype(jnp.bfloat16)
    mixed = jnp.einsum(
        "rhqk,rkhd->rqhd", probs_low, value_heads, preferred_element_type=jnp.float32
    )
    mixed = mixed.reshape(row_count, token_count, feature_count).astype(jnp.bfloat16)
    gain1 = gain1_full.astype(jnp.float32)
    resid1 = inputs + apply_weight(mixed, output_full) + obias_full.astype(jnp.float32)
    normed1_out, normed1, inverse1 = norm_forward(resid1, gain1, shift1_full.astype(jnp.float32))
    normed1_low = normed1_out.astype(jnp.bfloat16)
    pre_act = apply_weight(normed1_low, up_full) + upbias_full.astype(jnp.float32)
    act_low = jax.nn.gelu(pre_act, approximate=False).astype(jnp.bfloat16)
    gain2 = gain2_full.astype(jnp.float32)
    resid2 = normed1_out + apply_weight(act_low, down_full) + downbias_full.astype(jnp.float32)
    final, second_normed, inverse2 = norm_forward(resid2, gain2, shift2_full.astype(jnp.float32))
    final_low = final.astype(jnp.bfloat16)
    shard_rows = lax.all_gather(final_low, "dp", axis=0, tiled=True)
    span_rows = shard_rows.shape[0]
    inside = (slot_row >= 0) & (slot_row < span_rows)
    picked = jnp.take(shard_rows, jnp.clip(slot_row, 0, span_rows - 1), axis=0)
    slot_acts = jnp.where(
        inside[:, None, None], picked, jnp.zeros(slot_activation_gradient.shape, jnp.bfloat16)
    )
    gain1 = gain1_full.astype(jnp.float32)
    gain2 = gain2_full.astype(jnp.float32)
    grad2, gain2_grad, shift2_grad = norm_backward(upstream, gain2, second_normed, inverse2)
    ffn_low = grad2.astype(jnp.bfloat16)
    down_grad = weight_term(act_low, ffn_low)
    down_bias_grad = bias_term(ffn_low)
    act_grad = apply_back(ffn_low, down_full)
    gelu_value, gelu_back = jax.vjp(partial(jax.nn.gelu, approximate=False), pre_act)
    pre_grad = gelu_back(act_grad)[0].astype(jnp.bfloat16)
    up_grad = weight_term(normed1_low, pre_grad)
    up_bias_grad = bias_term(pre_grad)
    normed1_grad = grad2 + apply_back(pre_grad, up_full)
    grad1, gain1_grad, shift1_grad = norm_backward(normed1_grad, gain1, normed1, inverse1)
    attn_low = grad1.astype(jnp.bfloat16)
    output_grad = weight_term(mixed, attn_low)
    output_bias_grad = bias_term(attn_low)
    mixed_grad = apply_back(attn_low, output_full).astype(jnp.bfloat16).reshape(split_shape)
    scores_again = (
        jnp.einsum("rqhd,rkhd->rhqk", query_heads, key_heads, preferred_element_type=jnp.float32)
        * score_scale
    )
    probs = jnp.exp(scores_again - logsum)
    probs_again = probs.astype(jnp.bfloat16)
    value_grad = jnp.einsum(
        "rhqk,rqhd->rkhd", probs_again, mixed_grad, preferred_element_type=jnp.float32
    )
    value_grad = value_grad.astype(jnp.bfloat16).reshape(row_count, token_count, feature_count)
    prob_grad = jnp.einsum(
        "rqhd,rkhd->rhqk", mixed_grad, value_heads, preferred_element_type=jnp.float32
    )
    score_grad = (probs * (prob_grad - jnp.sum(probs * prob_grad, axis=-1, keepdims=True))).astype(
        jnp.bfloat16
    )
    query_grad = (
        jnp.einsum("rhqk,rkhd->rqhd", score_grad, key_heads, preferred_element_type=jnp.float32)
        * score_scale
    )
    query_grad = query_grad.astype(jnp.bfloat16).reshape(row_count, token_count, feature_count)
    key_grad = (
        jnp.einsum("rhqk,rqhd->rkhd", score_grad, query_heads, preferred_element_type=jnp.float32)
        * score_scale
    )
    key_grad = key_grad.astype(jnp.bfloat16).reshape(row_count, token_count, feature_count)
    query_wgrad = weight_term(rows_in, query_grad)
    key_wgrad = weight_term(rows_in, key_grad)
    value_wgrad = weight_term(rows_in, value_grad)
    query_bias_grad = bias_term(query_grad)
    value_bias_grad = bias_term(value_grad)
    input_full = (
        grad1
        + apply_back(query_grad, query_full)
        + apply_back(key_grad, key_full)
        + apply_back(value_grad, value_full)
    )
    live_rows = lax.broadcasted_iota(jnp.int32, (row_count,), 0) < live_count[0]
    input_grad = jnp.where(live_rows[:, None, None], input_full, 0.0)
    devices = packed_full.shape[0]
    if small_rows % 16 == 0 and lax.axis_size("dp") == 4:
        nx = 2
        nz = lax.axis_size("fsdp") // nx
        terms = [
            query_wgrad,
            key_wgrad,
            value_wgrad,
            output_grad,
            *(up_grad[:, j * feature_count : (j + 1) * feature_count] for j in range(4)),
            *(down_grad.reshape(devices, 4, -1, feature_count)[:, j] for j in range(4)),
        ]
        terms = jnp.stack(
            [t.astype(jnp.bfloat16).reshape(2, 2, nz, nx, small_rows, feature_count) for t in terms]
        )
        small = jnp.stack(
            [
                query_bias_grad,
                value_bias_grad,
                output_bias_grad,
                gain1_grad,
                shift1_grad,
                down_bias_grad,
                gain2_grad,
                shift2_grad,
                *up_bias_grad.reshape(devices, 4, small_rows).transpose(1, 0, 2).reshape(4, -1),
                *([jnp.zeros_like(gain1_grad)] * 4),
            ]
        )
        wsum, small_sum = scatter_terms(terms, small, nz, nx)
        me = lax.axis_index(("dp", "fsdp"))
        small_sum = lax.dynamic_slice(small_sum, (0, me * small_rows), (16, small_rows))
        query_sum, key_sum, value_sum, output_sum = (wsum[i] for i in range(4))
        up_sum = wsum[4:8].transpose(1, 0, 2).reshape(small_rows, -1)
        down_sum = wsum[8:12].reshape(-1, feature_count)
        small_sum = small_sum[:12]
    else:
        small_terms = jnp.concatenate(
            [
                v.reshape(devices, -1, small_rows)
                for v in (
                    query_bias_grad,
                    value_bias_grad,
                    output_bias_grad,
                    gain1_grad,
                    shift1_grad,
                    down_bias_grad,
                    gain2_grad,
                    shift2_grad,
                    up_bias_grad,
                )
            ],
            axis=1,
        )
        small_sum = lax.psum_scatter(small_terms, ("dp", "fsdp"), scatter_dimension=0, tiled=True)[0]
        down_sum, up_sum, output_sum, value_sum, query_sum, key_sum = (
            lax.psum_scatter(
                term.astype(jnp.bfloat16), ("dp", "fsdp"), scatter_dimension=0, tiled=True
            ).astype(jnp.float32)
            for term in (down_grad, up_grad, output_grad, value_wgrad, query_wgrad, key_wgrad)
        )
    return (
        slot_acts,
        input_grad,
        query_sum,
        key_sum,
        value_sum,
        output_sum,
        small_sum[0],
        small_sum[1],
        small_sum[2],
        small_sum[3],
        small_sum[4],
        up_sum,
        small_sum[8:].reshape(-1),
        down_sum,
        small_sum[5],
        small_sum[6],
        small_sum[7],
    )


def solution(mesh):
    placed = (
        P(("dp", "fsdp"), None, None),
        P(("dp", "fsdp")),
        P(("dp", "fsdp")),
        P(("dp", "fsdp"), None, None),
        P(("dp", "fsdp"), None),
        P(("dp", "fsdp"), None),
        P(("dp", "fsdp"), None),
        P(("dp", "fsdp"), None),
        P(("dp", "fsdp")),
        P(("dp", "fsdp")),
        P(("dp", "fsdp")),
        P(("dp", "fsdp")),
        P(("dp", "fsdp")),
        P(("dp", "fsdp"), None),
        P(("dp", "fsdp")),
        P(("dp", "fsdp"), None),
        P(("dp", "fsdp")),
        P(("dp", "fsdp")),
        P(("dp", "fsdp")),
    )
    return jax.shard_map(
        on_device,
        mesh=mesh,
        in_specs=placed,
        out_specs=(
            P(("dp", "fsdp"), None, None),
            P(("dp", "fsdp"), None, None),
            P(("dp", "fsdp"), None),
            P(("dp", "fsdp"), None),
            P(("dp", "fsdp"), None),
            P(("dp", "fsdp"), None),
            P(("dp", "fsdp")),
            P(("dp", "fsdp")),
            P(("dp", "fsdp")),
            P(("dp", "fsdp")),
            P(("dp", "fsdp")),
            P(("dp", "fsdp"), None),
            P(("dp", "fsdp")),
            P(("dp", "fsdp"), None),
            P(("dp", "fsdp")),
            P(("dp", "fsdp")),
            P(("dp", "fsdp")),
        ),
        check_vma=False,
    )
```

```python
import math
from functools import partial

import jax
import jax.numpy as jnp
from jax import lax
from jax.experimental import pallas as pl
from jax.experimental.pallas import tpu as pltpu
from jax.sharding import PartitionSpec as P

HEADS = 16


EPSILON = 1e-05


MESH = pl.DeviceIdType.MESH
LANES = 128


def place(nz, nx):
    dp, fs = lax.axis_index("dp"), lax.axis_index("fsdp")
    y, core = dp // 2, lax.rem(dp, 2)
    z, x = fs // nx, lax.rem(fs, nx)
    return y, core, z, x


def device(y, core, z, x, nx):
    return (y * 2 + core, z * nx + x)


class Partners:
    def __init__(self, nz, nx):
        self.nz, self.nx = nz, nx
        self.y, self.core, self.z, self.x = place(nz, nx)
        y, core, z, x = self.y, self.core, self.z, self.x
        self.sibling = device(y, 1 - core, z, x, nx)
        self.across_x = device(y, core, z, 1 - x, nx)
        self.across_y = device(1 - y, core, z, x, nx)
        self.along_z = [device(y, core, lax.rem(z + k, nz), x, nx) for k in range(1, nz)]
        self.all = [self.sibling, self.across_x, self.across_y, *self.along_z]

    def meet(self):
        barrier = pltpu.get_barrier_semaphore()
        for other in self.all:
            pl.semaphore_signal(barrier, inc=1, device_id=other, device_id_type=MESH)
        pl.semaphore_wait(barrier, len(self.all))


def remote(src, dst, send, recv, to):
    return pltpu.make_async_remote_copy(
        src_ref=src, dst_ref=dst, send_sem=send, recv_sem=recv, device_id=to, device_id_type=MESH
    )


def added(*blocks):
    total = blocks[0].astype(jnp.float32)
    for block in blocks[1:]:
        total = total + block.astype(jnp.float32)
    return total


class Scatter:
    def __init__(self, at, wide, rc, r3a, r3b, r2, rz, send, recv):
        self.at, self.wide = at, wide
        self.rc, self.r3a, self.r3b, self.r2, self.rz = rc, r3a, r3b, r2, rz
        self.send, self.recv = send, recv

    def to_sibling(self, m, theirs):
        return remote(theirs, self.rc.at[m], self.send.at[m, 0], self.recv.at[m, 0], self.at.sibling)

    def first_a(self, m):
        at, wide = self.at, self.wide
        src = self.rc.at[m, :, :, 1 - at.x, :, pl.ds(0, wide)]
        return remote(src, self.r3a.at[m], self.send.at[m, 1], self.recv.at[m, 1], at.across_x)

    def first_b(self, m):
        at, wide = self.at, self.wide
        src = self.rc.at[m, 1 - at.y, :, :, :, pl.ds(wide, self.rc.shape[-1] - wide)]
        return remote(src, self.r3b.at[m], self.send.at[m, 2], self.recv.at[m, 2], at.across_y)

    def second_a(self, m):
        at, wide = self.at, self.wide
        src, dst = self.r3a.at[m, 1 - at.y], self.r2.at[m, :, :, pl.ds(0, wide)]
        return remote(src, dst, self.send.at[m, 3], self.recv.at[m, 3], at.across_y)

    def second_b(self, m):
        at, wide = self.at, self.wide
        src = self.r3b.at[m, :, 1 - at.x]
        dst = self.r2.at[m, :, :, pl.ds(wide, self.r2.shape[-1] - wide)]
        return remote(src, dst, self.send.at[m, 4], self.recv.at[m, 4], at.across_x)

    def last(self, m, k):
        at = self.at
        src = self.r2.at[m, lax.rem(at.z + k, at.nz)]
        return remote(src, self.rz.at[m, k - 1], self.send.at[m, 4 + k], self.recv.at[m, 4 + k], at.along_z[k - 1])

    def start(self, m, theirs):
        self.to_sibling(m, theirs).start()

    def step1(self, m, own):
        at, rc = self.at, self.rc
        self.to_sibling(m, rc.at[m]).wait_recv()
        nz = at.nz

        def add(i, carry):
            y, z = i // nz, lax.rem(i, nz)
            rc[m, y, z] = added(rc[m, y, z], own(y, z)).astype(rc.dtype)
            return carry

        lax.fori_loop(0, rc.shape[1] * nz, add, 0)
        self.to_sibling(m, rc.at[m]).wait_send()
        self.first_a(m).start()
        self.first_b(m).start()

    def step2(self, m):
        at, rc, wide, r3a, r3b = self.at, self.rc, self.wide, self.r3a, self.r3b
        columns = rc.shape[-1]
        self.first_a(m).wait_recv()
        self.first_b(m).wait_recv()

        def add(z, carry):
            for y in range(rc.shape[1]):
                r3a[m, y, z] = added(r3a[m, y, z], rc[m, y, z, at.x, :, pl.ds(0, wide)]).astype(rc.dtype)
            r3b[m, z] = added(r3b[m, z], rc[m, at.y, z, :, :, pl.ds(wide, columns - wide)]).astype(rc.dtype)
            return carry

        lax.fori_loop(0, at.nz, add, 0)
        self.second_a(m).start()
        self.second_b(m).start()

    def step3(self, m):
        at, r3a, r3b, r2, wide = self.at, self.r3a, self.r3b, self.r2, self.wide
        columns = r2.shape[-1]
        self.second_a(m).wait_recv()
        self.second_b(m).wait_recv()

        def add(z, carry):
            left, right = pl.ds(0, wide), pl.ds(wide, columns - wide)
            r2[m, z, :, left] = added(r2[m, z, :, left], r3a[m, at.y, z]).astype(r2.dtype)
            r2[m, z, :, right] = added(r2[m, z, :, right], r3b[m, z, at.x]).astype(r2.dtype)
            return carry

        lax.fori_loop(0, at.nz, add, 0)
        for k in range(1, at.nz):
            self.last(m, k).start()

    def step4(self, m, out):
        at = self.at
        for k in range(1, at.nz):
            self.last(m, k).wait_recv()
        out[m] = added(self.r2[m, at.z], *[self.rz[m, k] for k in range(at.nz - 1)])

    def drain(self, m):
        self.first_a(m).wait_send()
        self.first_b(m).wait_send()
        self.second_a(m).wait_send()
        self.second_b(m).wait_send()
        for k in range(1, self.at.nz):
            self.last(m, k).wait_send()


class SmallSum:
    def __init__(self, at, total, landing, send, recv):
        self.at, self.total, self.landing, self.send, self.recv = at, total, landing, send, recv

    def hop(self, i, to):
        return remote(self.total.at[i], self.landing.at[i], self.send.at[i], self.recv.at[i], to)

    def along(self, k):
        i = 2 + k
        return remote(self.total.at[3], self.landing.at[i], self.send.at[i], self.recv.at[i], self.at.along_z[k - 1])

    def start(self):
        self.hop(0, self.at.sibling).start()

    def step(self, i):
        at = self.at
        to = (at.sibling, at.across_x, at.across_y)
        self.hop(i, to[i]).wait_recv()
        self.total[i + 1] = self.total[i] + self.landing[i]
        if i < 2:
            self.hop(i + 1, to[i + 1]).start()
        else:
            for k in range(1, at.nz):
                self.along(k).start()

    def finish(self, out):
        at = self.at
        for k in range(1, at.nz):
            self.along(k).wait_recv()
        total = self.total[3]
        for k in range(1, at.nz):
            total = total + self.landing[2 + k]
        out[...] = total
        to = (at.sibling, at.across_x, at.across_y)
        for i in range(3):
            self.hop(i, to[i]).wait_send()
        for k in range(1, at.nz):
            self.along(k).wait_send()


def scatter_scratch(count, nz, nx, rows, columns, wide):
    bf16 = jnp.bfloat16
    return [
        pltpu.VMEM((count, 2, nz, nx, rows, columns), bf16),
        pltpu.VMEM((count, 2, nz, rows, wide), bf16),
        pltpu.VMEM((count, nz, nx, rows, columns - wide), bf16),
        pltpu.VMEM((count, nz, rows, columns), bf16),
        pltpu.VMEM((count, nz - 1, rows, columns), bf16),
        pltpu.SemaphoreType.DMA((count, 4 + nz)),
        pltpu.SemaphoreType.DMA((count, 4 + nz)),
    ]


def small_scratch(nz, shape):
    return [
        pltpu.VMEM((4, *shape), jnp.float32),
        pltpu.VMEM((2 + nz, *shape), jnp.float32),
        pltpu.SemaphoreType.DMA((2 + nz,)),
        pltpu.SemaphoreType.DMA((2 + nz,)),
    ]


def exact_gelu(pre):
    half = 0.5 + 0.5 * lax.erf(pre * (0.5**0.5))
    bell = jnp.exp(-0.5 * pre * pre) * ((0.5 / math.pi) ** 0.5)
    return pre * half, half + pre * bell


def rms_center(hidden):
    center = hidden - jnp.mean(hidden, axis=-1, keepdims=True)
    inverse = lax.rsqrt(jnp.mean(center * center, axis=-1, keepdims=True) + EPSILON)
    return center * inverse, inverse


def half_masks(width):
    left = (lax.broadcasted_iota(jnp.int32, (1, width), 1) < width // 2).astype(jnp.float32)
    return left.astype(jnp.bfloat16), (1.0 - left).astype(jnp.bfloat16)


def across(left, right):
    return lax.dot_general(left, right, (((1,), (1,)), ((), ())), preferred_element_type=jnp.float32)


def down(left, right):
    return lax.dot_general(left, right, (((0,), (0,)), ((), ())), preferred_element_type=jnp.float32)


def dot(left, right):
    return jnp.dot(left, right, preferred_element_type=jnp.float32)


def span(i, size):
    return pl.ds(pl.multiple_of(i * size, size), size)


class Gather:
    def __init__(self, at, wide, count, shards, g, send, recv):
        self.at, self.wide, self.count, self.shards, self.g, self.send, self.recv = at, wide, count, shards, g, send, recv
        self.right = g.shape[-1] - wide

    def along(self, m, k):
        at = self.at
        dst = self.g.at[m, at.y, at.core, at.z, at.x]
        return remote(self.shards.at[m], dst, self.send.at[m, k - 1], self.recv.at[m, k - 1], at.along_z[k - 1])

    def same(self, part, m, i, to):
        return remote(part, part, self.send.at[m, i], self.recv.at[m, i], to)

    def first_a(self, m):
        at, nz = self.at, self.at.nz
        part = self.g.at[m, at.y, at.core, :, at.x, :, pl.ds(0, self.wide)]
        return self.same(part, m, nz - 1, at.across_y)

    def first_b(self, m):
        at, nz = self.at, self.at.nz
        part = self.g.at[m, at.y, at.core, :, at.x, :, pl.ds(self.wide, self.right)]
        return self.same(part, m, nz, at.across_x)

    def second_a(self, m):
        at, nz = self.at, self.at.nz
        part = self.g.at[m, :, at.core, :, at.x, :, pl.ds(0, self.wide)]
        return self.same(part, m, nz + 1, at.across_x)

    def second_b(self, m):
        at, nz = self.at, self.at.nz
        part = self.g.at[m, at.y, at.core, :, :, :, pl.ds(self.wide, self.right)]
        return self.same(part, m, nz + 2, at.across_y)

    def to_sibling(self, m):
        at, nz = self.at, self.at.nz
        return self.same(self.g.at[m, :, at.core], m, nz + 3, at.sibling)

    def step0(self, m):
        at = self.at
        for k in range(1, at.nz):
            self.along(m, k).start()
        self.g[m, at.y, at.core, at.z, at.x] = self.shards[m]

    def step1(self, m):
        for k in range(1, self.at.nz):
            self.along(m, k).wait_recv()
        self.first_a(m).start()
        self.first_b(m).start()

    def step2(self, m):
        self.first_a(m).wait_recv()
        self.first_b(m).wait_recv()
        self.second_a(m).start()
        self.second_b(m).start()

    def step3(self, m):
        self.second_a(m).wait_recv()
        self.second_b(m).wait_recv()
        self.to_sibling(m).start()

    def arrive(self, m):
        self.to_sibling(m).wait_recv()

    def tick(self, i):
        for step, ahead in ((self.step3, 3), (self.step2, 2), (self.step1, 1), (self.step0, -2)):
            m = i - ahead
            if isinstance(i, int):
                if 0 <= m < self.count:
                    step(m)
            else:
                pl.when((m >= 0) & (m < self.count))(partial(step, m))

    def drain(self, m):
        for k in range(1, self.at.nz):
            self.along(m, k).wait_send()
        for copy in (self.first_a, self.first_b, self.second_a, self.second_b, self.to_sibling):
            copy(m).wait_send()


def forward_kernel(
    nz, nx, wide, tokens, head_pair,
    x, shards, small, pick, slots,
    g_out, saved, act_out, slope_out, unit_out, final_out, own_out, across_out, small_full, inverse1, inverse2,
    g, pool, hidden, landed, total, landing,
    send, recv, ssend, srecv, usend, urecv, isem, gsem, vsem, asem, dsem, fsem,
):
    f32, bf16 = jnp.float32, jnp.bfloat16
    count = g.shape[0]
    all_rows, width = x.shape
    rows = all_rows // tokens
    at = Partners(nz, nx)
    at.meet()
    gather = Gather(at, wide, count, shards, g, send, recv)
    sums = SmallSum(at, total, landing, ssend, srecv)
    groups = slots.shape[0] // rows
    members = pick.shape[0] // rows

    def fetch(i):
        return pltpu.make_async_copy(slots.at[i], pool.at[i // rows, pl.ds((i % rows) * tokens, tokens)], isem.at[i])

    total[0] = small[...]
    sums.start()
    gather.step0(0)
    gather.step0(1)
    for i in range(slots.shape[0]):
        fetch(i).start()
    gather.tick(0)
    for i in range(slots.shape[0]):
        fetch(i).wait()
    gather.tick(1)

    high, part = 16, width // 2

    def sum_slots(i, carry):
        cols = span(lax.rem(i, 2), part)
        base = i // 2 * high
        held = [
            pool[s // rows, pl.ds(pl.multiple_of(base + (s % rows) * tokens, high), high), cols].astype(f32)
            for s in range(slots.shape[0])
        ]
        for t in range(pick.shape[0]):
            picked = pick[t, 0] * held[0]
            for s in range(1, slots.shape[0]):
                picked = picked + pick[t, s] * held[s]
            spot = pl.ds(pl.multiple_of(base + (t % rows) * tokens, high), high)
            pool[groups + t // rows, spot, cols] = picked.astype(bf16)
        return carry

    lax.fori_loop(0, tokens // high * 2, sum_slots, 0)

    def up_sibling(y):
        src = pool.at[groups + y * 2 + 1 - at.core]
        return remote(src, landed.at[y], usend.at[y], urecv.at[y], at.sibling)

    def up_across():
        return remote(landed.at[1 - at.y], across_out, usend.at[2], urecv.at[2], at.across_y)

    up_own = pltpu.make_async_copy(landed.at[at.y], own_out, isem.at[slots.shape[0]])

    for y in range(2):
        up_sibling(y).start()
    sums.step(0)
    gather.tick(2)
    for y in range(2):
        up_sibling(y).wait_recv()

    def chip_sum(i, carry):
        y, spot = i // (all_rows // 32), span(lax.rem(i, all_rows // 32), 32)
        landed[y, spot] = added(landed[y, spot], pool[groups + y * 2 + at.core, spot]).astype(bf16)
        return carry

    lax.fori_loop(0, 2 * all_rows // 32, chip_sum, 0)
    up_across().start()
    up_own.start()
    sums.step(1)
    gather.tick(3)
    for y in range(2):
        up_sibling(y).wait_send()
    sums.step(2)
    sums.finish(small_full)

    def keep(m):
        return pltpu.make_async_copy(g.at[m], g_out.at[m], gsem.at[m])

    def arrive(m):
        gather.arrive(m)
        keep(m).start()

    def tile(m, cols):
        return g[m, :, :, :, :, :, cols].reshape(width, cols.size)

    def bias(i, cols):
        return small_full[pl.ds(i, 1), cols]

    def tiles(size, body):
        def one(i, carry):
            body(span(i // rows, size), span(lax.rem(i, rows), tokens))
            return carry

        lax.fori_loop(0, width // size * rows, one, 0)

    def save(i):
        return pltpu.make_async_copy(pool.at[i], saved.at[i], vsem.at[i])

    def project(m):
        bias_row = (0, None, 1)[m]

        def body(cols, spot):
            y = dot(x[spot], tile(m, cols))
            if bias_row is not None:
                y = y + bias(bias_row, cols)
            pool[m, spot, cols] = y.astype(bf16)

        arrive(m)
        tiles(512, body)
        save(m).start()

    project(0)
    gather.tick(4)
    project(1)
    gather.tick(5)
    project(2)

    pairs = width // head_pair
    masks = half_masks(head_pair)
    scale = (head_pair // 2) ** (-0.5)

    def attend(i, carry):
        spot, cols = span(i // pairs, tokens), span(lax.rem(i, pairs), head_pair)
        query, keys, values = pool[0, spot, cols], pool[1, spot, cols], pool[2, spot, cols]
        query = query * jnp.asarray(scale, bf16)
        out = None
        for mask in masks:
            scores = across(query, keys * mask)
            weight = jnp.exp(scores - jnp.max(scores, axis=-1, keepdims=True))
            weight = weight * (1.0 / jnp.sum(weight, axis=-1, keepdims=True))
            term = dot(weight.astype(bf16), values * mask)
            out = term if out is None else out + term
        pool[3, spot, cols] = out.astype(bf16)
        turn = rows * pairs // 2
        pl.when(lax.rem(i, turn) == turn - 2)(lambda: gather.tick(6 + i // turn))
        return carry

    lax.fori_loop(0, rows * pairs, attend, 0)
    save(3).start()

    def mix(cols, spot):
        hidden[spot, cols] = dot(pool[3, spot], tile(3, cols)) + x[spot, cols].astype(f32) + bias(2, cols)

    arrive(3)
    tiles(512, mix)
    gather.tick(8)

    def unit(i):
        return pltpu.make_async_copy(pool.at[6], unit_out.at[i], fsem.at[i])

    def norm1(i, carry):
        spot = span(i, 32)
        normed, inverse = rms_center(hidden[spot])
        result = normed * small_full[3:4, :] + small_full[4:5, :]
        hidden[spot] = result
        pool[4, spot] = result.astype(bf16)
        pool[6, spot] = normed.astype(bf16)
        inverse1[spot] = inverse
        return carry

    lax.fori_loop(0, all_rows // 32, norm1, 0)
    save(4).start()
    unit(0).start()

    def save_act(j):
        return pltpu.make_async_copy(pool.at[5], act_out.at[j], asem)

    def save_slope(j):
        return pltpu.make_async_copy(pool.at[6], slope_out.at[j], dsem)

    unit(0).wait()

    def feed(j, carry):
        m = 4 + 2 * j
        pl.when(j >= 1)(lambda: gather.tick(m + 3))
        arrive(m)

        @pl.when(j >= 1)
        def _():
            save_act(j - 1).wait()
            save_slope(j - 1).wait()

        def up(cols, spot):
            value, slope = exact_gelu(dot(pool[4, spot], tile(m, cols)) + bias(8 + j, cols))
            pool[5, spot, cols] = value.astype(bf16)
            pool[6, spot, cols] = slope.astype(bf16)

        tiles(256, up)
        save_act(j).start()
        save_slope(j).start()
        pl.when(j >= 1)(lambda: gather.tick(m + 4))
        arrive(m + 1)

        def back(cols, spot):
            hidden[spot, cols] = hidden[spot, cols] + dot(pool[5, spot], tile(m + 1, cols))

        tiles(512, back)
        return carry

    blocks = (count - 4) // 2
    lax.fori_loop(0, blocks, feed, 0)
    save_act(blocks - 1).wait()
    save_slope(blocks - 1).wait()

    def norm2(i, carry):
        spot = span(i, 32)
        normed, inverse = rms_center(hidden[spot] + small_full[5:6, :])
        pool[5, spot] = (normed * small_full[6:7, :] + small_full[7:8, :]).astype(bf16)
        pool[6, spot] = normed.astype(bf16)
        inverse2[spot] = inverse
        return carry

    lax.fori_loop(0, all_rows // 32, norm2, 0)
    finish = pltpu.make_async_copy(pool.at[5], final_out, fsem.at[2])
    finish.start()
    unit(1).start()

    def drain(m, carry):
        gather.drain(m)
        keep(m).wait()
        return carry

    lax.fori_loop(0, count, drain, 0)
    for i in range(5):
        save(i).wait()
    up_own.wait()
    up_across().wait()
    finish.wait()
    unit(1).wait()


def forward(x, shards, small, pick, slots, nz, nx, tokens):
    f32, bf16 = jnp.float32, jnp.bfloat16
    count, shard_rows, width = shards.shape
    all_rows = x.shape[0]
    group_members = pick.shape[0] * tokens // all_rows
    assert group_members == 4 and slots.shape[0] * tokens == 2 * all_rows
    wide = width * 3 // 4
    vmem, anywhere = pl.BlockSpec(memory_space=pltpu.VMEM), pl.BlockSpec(memory_space=pl.ANY)
    acts = (all_rows, width)
    blocks = (count - 4) // 2
    dma = pltpu.SemaphoreType.DMA
    full = (count, 2, 2, nz, nx, shard_rows, width)
    out = jax.ShapeDtypeStruct
    return pl.pallas_call(
        partial(forward_kernel, nz, nx, wide, tokens, 2 * width // HEADS),
        out_shape=[
            out(full, bf16),
            out((5, *acts), bf16),
            out((blocks, *acts), bf16),
            out((blocks, *acts), bf16),
            out((2, *acts), bf16),
            out(acts, bf16),
            out(acts, bf16),
            out(acts, bf16),
            out(small.shape, f32),
            out((all_rows, 1), f32),
            out((all_rows, 1), f32),
        ],
        in_specs=[vmem, vmem, vmem, pl.BlockSpec(memory_space=pltpu.SMEM), anywhere],
        out_specs=[anywhere] * 8 + [vmem] * 3,
        scratch_shapes=[
            pltpu.VMEM(full, bf16),
            pltpu.VMEM((7, *acts), bf16),
            pltpu.VMEM(acts, f32),
            pltpu.VMEM((2, *acts), bf16),
            *small_scratch(nz, small.shape)[:2],
            dma((count, nz + 4)),
            dma((count, nz + 4)),
            dma((2 + nz,)),
            dma((2 + nz,)),
            dma((3,)),
            dma((3,)),
            dma((slots.shape[0] + 1,)),
            dma((count,)),
            dma((5,)),
            dma,
            dma,
            dma((3,)),
        ],
        compiler_params=pltpu.CompilerParams(
            collective_id=1, has_side_effects=True, vmem_limit_bytes=60 * 2**20
        ),
    )(x, shards, small, pick, slots)


def backward_kernel(
    nz, nx, wide, tokens, head_pair,
    x, own_up, across_up, final, unit, inverse1, inverse2, small_full, act, slope, saved, g,
    out, small_out, input_out, table,
    rc, r3a, r3b, r2, rz, send, recv, total, landing, ssend, srecv,
    term, weight, pool, hidden, wsem, psem, hsem, tsend, trecv, tsem,
):
    f32, bf16 = jnp.float32, jnp.bfloat16
    count = out.shape[0]
    all_rows, width = x.shape
    rows = all_rows // tokens
    at = Partners(nz, nx)
    at.meet()
    scatter = Scatter(at, wide, rc, r3a, r3b, r2, rz, send, recv)
    sums = SmallSum(at, total, landing, ssend, srecv)

    here = pltpu.make_async_copy(final, table.at[at.y, at.core], tsem)
    to_sibling = remote(final, table.at[at.y, at.core], tsend.at[0], trecv.at[0], at.sibling)
    to_across = remote(final, table.at[at.y, at.core], tsend.at[1], trecv.at[1], at.across_y)
    passed = table.at[1 - at.y, at.core]
    pass_on = remote(passed, passed, tsend.at[2], trecv.at[2], at.sibling)

    def load(src, entry, i):
        return pltpu.make_async_copy(src, pool.at[entry], psem.at[i])

    def fetch(m, slot, i):
        return pltpu.make_async_copy(g.at[m], weight.at[slot], wsem.at[i])

    blocks = act.shape[0]
    up_block, down_block = (lambda j: 4 + 2 * j), (lambda j: 5 + 2 * j)
    unit2, own_load, across_load = load(unit.at[1], 1, 0), load(own_up, 2, 1), load(across_up, 3, 2)
    act_entry = [5, 2, 3, 5]
    act_load = [load(act.at[j], act_entry[j], 3 + j) for j in range(blocks)]
    slope_entry = [4, 2, 3, 4]
    slope_load = [load(slope.at[j], slope_entry[j], 7 + j) for j in range(blocks)]
    low_load, unit1, mixed_load = load(saved.at[4], 6, 11), load(unit.at[0], 5, 12), load(saved.at[3], 4, 13)
    query_load, key_load, value_load = (load(saved.at[i], (2, 3, 6)[i], 14 + i) for i in range(3))
    x_load = load(x, 4, 17)
    down_fetch = [fetch(down_block(j), 0, 2 * j) for j in range(blocks)]
    up_fetch = [fetch(up_block(j), 1, 2 * j + 1) for j in range(blocks)]
    last = 2 * blocks
    output_fetch, query_fetch, key_fetch, value_fetch = (
        fetch(m, slot, last + i) for i, (m, slot) in enumerate(((3, 0), (0, 1), (1, 0), (2, 1)))
    )
    for copy in (unit2, own_load, across_load, act_load[0], down_fetch[0], up_fetch[0], slope_load[0], low_load):
        copy.start()
    to_across.start()
    to_sibling.start()
    here.start()
    total[0] = jnp.zeros_like(total[0])

    def folded(block):
        return jnp.sum(block.reshape(-1, 8, block.shape[-1]), axis=0)

    def norm_back(gain_row, shift_row, low_row, inverse, incoming, normed_entry, low_entry):
        def body(i, carry):
            spot = span(i, 32)
            grad, normed = incoming(spot), pool[normed_entry, spot].astype(f32)
            scaled = grad * small_full[gain_row : gain_row + 1, :]
            inner = (
                scaled
                - jnp.mean(scaled, axis=-1, keepdims=True)
                - normed * jnp.mean(scaled * normed, axis=-1, keepdims=True)
            )
            result = inner * inverse[spot]
            low = result.astype(bf16)
            hidden[spot] = result
            pool[low_entry, spot] = low
            return tuple(c + folded(b) for c, b in zip(carry, (grad * normed, grad, low.astype(f32))))

        zero = jnp.zeros((8, width), f32)
        found = lax.fori_loop(0, all_rows // 32, body, (zero, zero, zero))
        for row, value in zip((gain_row, shift_row, low_row), found):
            total[0, row : row + 1, :] = jnp.sum(value, axis=0, keepdims=True)

    def tiles(size, body):
        def one(i, carry):
            body(i // rows, span(i // rows, size), span(lax.rem(i, rows), tokens))
            return carry

        lax.fori_loop(0, width // size * rows, one, 0)

    def turned(slot, y):
        return weight[slot, y].reshape(width // 2, width)

    def own_half(slot):
        return lambda y, z: term[slot, y, at.core, z]

    def produce(m, left, right, after=True):
        slot = m % 2

        def half(core):
            def body(i, carry):
                y, cols = i // 2, span(lax.rem(i, 2), width // 2)
                picked = span(y * 2 + core, width // 4)
                value = down(pool[left, :, picked], pool[right, :, cols]).astype(bf16)
                term[slot, y, core, :, :, :, cols] = value.reshape(nz, nx, -1, width // 2)
                return carry

            lax.fori_loop(0, 4, body, 0)

        half(1 - at.core)
        scatter.start(m, term.at[slot, :, 1 - at.core])
        if m > 0 and after:
            scatter.step1(m - 1, own_half(1 - slot))
        half(at.core)

    def tick(i):
        for step, ahead in ((scatter.step4, 2), (scatter.step3, 1), (scatter.step2, 0)):
            m = i - ahead
            call = partial(step, m) if ahead < 2 else partial(step, m, out)
            if isinstance(i, int):
                if 0 <= m < count:
                    call()
            else:
                pl.when((m >= 0) & (m < count))(call)

    for copy in (unit2, own_load, across_load):
        copy.wait()
    norm_back(6, 7, 5, inverse2, lambda spot: added(pool[2, spot], pool[3, spot]), 1, 0)

    act_load[1].start()
    act_load[2].start()
    for j in range(blocks):
        act_load[j].wait()
        produce(j, act_entry[j], 0)
        if j == 0:
            act_load[3].start()
        elif j < 3:
            slope_load[j].start()
        else:
            unit1.start()
    tick(0)

    low_load.wait()
    for j in range(blocks):
        down_fetch[j].wait()
        slope_load[j].wait()

        def pre_back(n, cols, spot, j=j):
            value = across(pool[0, spot], turned(0, n)) * pool[slope_entry[j], spot, cols].astype(f32)
            value = value.astype(bf16)
            pool[1, spot, cols] = value
            row = pl.ds(8 + j, 1)
            total[0, row, cols] = total[0, row, cols] + jnp.sum(value.astype(f32), axis=0, keepdims=True)

        tiles(width // 2, pre_back)
        if j + 1 < blocks:
            down_fetch[j + 1].start()
        else:
            output_fetch.start()
        (lambda: slope_load[3].start(), query_load.start, key_load.start, mixed_load.start)[j]()
        produce(blocks + j, 6, 1)
        up_fetch[j].wait()

        def hidden_back(n, cols, spot):
            hidden[spot, cols] = hidden[spot, cols] + across(pool[1, spot], turned(1, n))

        tiles(width // 2, hidden_back)
        if j + 1 < blocks:
            up_fetch[j + 1].start()
        else:
            query_fetch.start()
        if j == blocks - 1:
            value_load.start()
        tick(1 + j)

    unit1.wait()
    norm_back(3, 4, 2, inverse1, lambda spot: hidden[spot], 5, 0)
    mixed_load.wait()
    produce(2 * blocks, 4, 0)
    x_load.start()
    output_fetch.wait()

    def mixed_back(n, cols, spot):
        pool[1, spot, cols] = across(pool[0, spot], turned(0, n)).astype(bf16)

    tiles(width // 2, mixed_back)
    key_fetch.start()
    for copy in (query_load, key_load, value_load):
        copy.wait()
    tick(5)
    scatter.step1(2 * blocks, own_half((2 * blocks) % 2))

    pairs = width // head_pair
    masks = half_masks(head_pair)
    scale = (head_pair // 2) ** (-0.5)

    def attend(i, carry):
        spot, cols = span(i // pairs, tokens), span(lax.rem(i, pairs), head_pair)
        query, keys, values, mixed_grad = (pool[e, spot, cols] for e in (2, 3, 6, 1))
        query_grad = key_grad = value_grad = None
        for mask in masks:
            own_keys = keys * (mask * jnp.asarray(scale, bf16))
            scores = across(own_keys, query)
            probs = jnp.exp(scores - jnp.max(scores, axis=0, keepdims=True))
            probs = probs * (1.0 / jnp.sum(probs, axis=0, keepdims=True))
            prob_grad = across(values * mask, mixed_grad)
            weighed = probs * prob_grad
            score_grad = (weighed - probs * jnp.sum(weighed, axis=0, keepdims=True)).astype(bf16)
            terms = (
                down(score_grad, own_keys),
                dot(score_grad, query * mask),
                dot(probs.astype(bf16), mixed_grad * mask),
            )
            if query_grad is None:
                query_grad, key_grad, value_grad = terms
            else:
                query_grad, key_grad, value_grad = query_grad + terms[0], key_grad + terms[1], value_grad + terms[2]
        query_grad, value_grad = query_grad.astype(bf16), value_grad.astype(bf16)
        pool[2, spot, cols] = query_grad
        pool[3, spot, cols] = (key_grad * scale).astype(bf16)
        pool[6, spot, cols] = value_grad
        for row, value in ((0, query_grad), (1, value_grad)):
            found = jnp.sum(value.astype(f32), axis=0, keepdims=True)
            total[0, row : row + 1, cols] = total[0, row : row + 1, cols] + found
        turn = rows * pairs // 3
        pl.when(lax.rem(i, turn) == turn - 1)(lambda: tick(6 + i // turn))
        return carry

    lax.fori_loop(0, rows * pairs, attend, 0)
    sums.start()

    x_load.wait()
    for i, entry in enumerate((6, 2, 3)):
        produce(2 * blocks + 1 + i, 4, entry, i > 0)
        sums.step(i)
    scatter.step1(count - 1, own_half((count - 1) % 2))
    tick(9)

    def input_back(slot, entry, fetched):
        def body(n, cols, spot):
            hidden[spot, cols] = hidden[spot, cols] + across(pool[entry, spot], turned(slot, n))

        fetched.wait()
        tiles(width // 2, body)

    input_back(1, 2, query_fetch)
    value_fetch.start()
    tick(10)
    input_back(0, 3, key_fetch)
    to_across.wait_recv()
    pass_on.start()
    tick(11)
    input_back(1, 6, value_fetch)
    done = pltpu.make_async_copy(hidden, input_out, hsem)
    done.start()
    tick(12)
    sums.finish(small_out)
    tick(13)
    done.wait()

    def drain(m, carry):
        scatter.drain(m)
        return carry

    lax.fori_loop(0, count, drain, 0)
    here.wait()
    to_sibling.wait()
    to_across.wait_send()
    pass_on.wait()


def backward(x, own_up, across_up, final, unit, inverse1, inverse2, small_full, act, slope, saved, g, nz, nx, tokens):
    f32, bf16 = jnp.float32, jnp.bfloat16
    count, _, _, _, _, shard_rows, width = g.shape
    acts = x.shape
    wide = width * 3 // 4
    vmem, anywhere = pl.BlockSpec(memory_space=pltpu.VMEM), pl.BlockSpec(memory_space=pl.ANY)
    dma = pltpu.SemaphoreType.DMA
    out = jax.ShapeDtypeStruct
    block = (2, 2, nz, nx, shard_rows, width)
    return pl.pallas_call(
        partial(backward_kernel, nz, nx, wide, tokens, 2 * width // HEADS),
        out_shape=[
            out((count, shard_rows, width), f32),
            out(small_full.shape, f32),
            out(acts, f32),
            out((2, 2, *acts), bf16),
        ],
        in_specs=[anywhere] * 5 + [vmem] * 3 + [anywhere] * 4,
        out_specs=[vmem, vmem, anywhere, anywhere],
        scratch_shapes=[
            *scatter_scratch(count, nz, nx, shard_rows, width, wide),
            *small_scratch(nz, small_full.shape),
            pltpu.VMEM((2, *block), bf16),
            pltpu.VMEM((2, *block), bf16),
            pltpu.VMEM((7, *acts), bf16),
            pltpu.VMEM(acts, f32),
            dma((count,)),
            dma((18,)),
            dma,
            dma((3,)),
            dma((3,)),
            dma,
        ],
        compiler_params=pltpu.CompilerParams(
            collective_id=2, has_side_effects=True, vmem_limit_bytes=60 * 2**20
        ),
    )(x, own_up, across_up, final, unit, inverse1, inverse2, small_full, act, slope, saved, g)


def pick_kernel(slot_row, row, out):
    out[...] = row[...]


def pick_rows(slot_row, table):
    members, tokens, width = table.shape
    block = (1, tokens, width)
    return pl.pallas_call(
        pick_kernel,
        out_shape=jax.ShapeDtypeStruct((slot_row.shape[0], tokens, width), table.dtype),
        grid_spec=pltpu.PrefetchScalarGridSpec(
            num_scalar_prefetch=1,
            grid=(slot_row.shape[0],),
            in_specs=[pl.BlockSpec(block, lambda s, slot_row: (jnp.clip(slot_row[s], 0, members - 1), 0, 0))],
            out_specs=pl.BlockSpec(block, lambda s, slot_row: (s, 0, 0)),
        ),
    )(slot_row, table)


def prepare(
    rows_in, slot_row, weights, small_parameters, up_bias, dp_size
):
    row_count, token_count, width = rows_in.shape
    query_weight, key_weight, value_weight, output_weight, expand_weight, down_weight = weights
    shard = query_weight.shape[0]
    blocks = down_weight.shape[0] // shard
    me = lax.axis_index(("dp", "fsdp"))
    ups = expand_weight.reshape(shard, -1, blocks, shard).transpose(2, 0, 1, 3).reshape(blocks, shard, width)
    downs = down_weight.reshape(blocks, shard, width)
    paired = jnp.stack([ups, downs], axis=1).reshape(2 * blocks, shard, width)
    shards = jnp.concatenate([jnp.stack([query_weight, key_weight, value_weight, output_weight]), paired])
    mine = jnp.concatenate([jnp.stack(small_parameters), up_bias.reshape(blocks, shard)]).astype(jnp.float32)
    small = lax.dynamic_update_slice(
        jnp.zeros((16, width), jnp.float32), mine, (jnp.int32(0), me * shard)
    )
    wanted = lax.broadcasted_iota(jnp.int32, (row_count * dp_size, slot_row.shape[0]), 0)
    pick = (wanted == slot_row[None, :]).astype(jnp.float32)
    return rows_in.reshape(-1, width), shards, small, pick


def on_device_kernels(
    rows_in,
    slot_row,
    live_count,
    slot_activation_gradient,
    query_weight,
    key_weight,
    value_weight,
    output_weight,
    query_bias,
    value_bias,
    output_bias,
    attn_gain,
    attn_shift,
    expand_weight,
    up_bias,
    down_weight,
    down_bias,
    ffn_gain,
    ffn_shift,
):
    row_count, token_count, width = rows_in.shape
    shard = query_weight.shape[0]
    nx = 2
    nz = lax.axis_size("fsdp") // nx
    x, shards, small, pick = prepare(
        rows_in,
        slot_row,
        (query_weight, key_weight, value_weight, output_weight, expand_weight, down_weight),
        (query_bias, value_bias, output_bias, attn_gain, attn_shift, down_bias, ffn_gain, ffn_shift),
        up_bias,
        lax.axis_size("dp"),
    )
    g, saved, act, slope, unit, final, own_up, across_up, small_full, inverse1, inverse2 = forward(
        x, shards, small, pick, slot_activation_gradient, nz, nx, token_count
    )
    sums, small_sums, input_full, table = backward(
        x, own_up, across_up, final, unit, inverse1, inverse2, small_full, act, slope, saved, g, nz, nx, token_count
    )
    slot_acts = pick_rows(slot_row, table.reshape(-1, token_count, width))
    live_rows = lax.broadcasted_iota(jnp.int32, (row_count,), 0) < live_count[0]
    input_grad = jnp.where(live_rows[:, None, None], input_full.reshape(rows_in.shape), 0.0)
    me = lax.axis_index(("dp", "fsdp"))
    mine = lax.dynamic_slice(small_sums, (jnp.int32(0), me * shard), (small_sums.shape[0], shard))
    blocks = (sums.shape[0] - 4) // 2
    down_sum = sums[:blocks].reshape(-1, width)
    ups = sums[blocks : 2 * blocks].reshape(blocks, shard, -1, shard)
    up_sum = ups.transpose(1, 2, 0, 3).reshape(shard, -1)
    output_sum, value_sum, query_sum, key_sum = (sums[2 * blocks + i] for i in range(4))
    return (
        slot_acts,
        input_grad,
        query_sum,
        key_sum,
        value_sum,
        output_sum,
        mine[0],
        mine[1],
        mine[2],
        mine[3],
        mine[4],
        up_sum,
        mine[8 : 8 + blocks].reshape(-1),
        down_sum,
        mine[5],
        mine[6],
        mine[7],
    )


def norm_forward(hidden, gain, shift):
    center = hidden - jnp.mean(hidden, axis=-1, keepdims=True)
    inverse = lax.rsqrt(jnp.mean(center * center, axis=-1, keepdims=True) + EPSILON)
    normed = center * inverse
    return (normed * gain + shift, normed, inverse)


def norm_backward(incoming, gain, normed, inverse):
    scaled = incoming * gain
    inner = (
        scaled
        - jnp.mean(scaled, axis=-1, keepdims=True)
        - normed * jnp.mean(scaled * normed, axis=-1, keepdims=True)
    )
    return (
        inner * inverse,
        jnp.sum(incoming * normed, axis=(0, 1)),
        jnp.sum(incoming, axis=(0, 1)),
    )


def apply_weight(acts, weight):
    return jnp.einsum("rsd,de->rse", acts, weight, preferred_element_type=jnp.float32)


def apply_back(grads, weight):
    return jnp.einsum("rse,de->rsd", grads, weight, preferred_element_type=jnp.float32)


def weight_term(acts, grads):
    return jnp.einsum("rsd,rse->de", acts, grads, preferred_element_type=jnp.float32)


def bias_term(grads):
    return jnp.sum(grads, axis=(0, 1), dtype=jnp.float32)


def on_device_plain(
    rows_in,
    slot_row,
    live_count,
    slot_activation_gradient,
    query_weight,
    key_weight,
    value_weight,
    output_weight,
    query_bias,
    value_bias,
    output_bias,
    attn_gain,
    attn_shift,
    expand_weight,
    up_bias,
    down_weight,
    down_bias,
    ffn_gain,
    ffn_shift,
):
    row_count, token_count, feature_count = rows_in.shape
    head_size = feature_count // HEADS
    score_scale = head_size ** (-0.5)
    split_shape = (row_count, token_count, HEADS, head_size)
    wanted = lax.broadcasted_iota(
        jnp.int32, (row_count * lax.axis_size("dp"), slot_row.shape[0]), 0
    )
    one_hot_matrix = (wanted == slot_row[None, :]).astype(jnp.bfloat16)
    upstream = lax.psum_scatter(
        jnp.einsum(
            "az,zfy->afy",
            one_hot_matrix,
            slot_activation_gradient,
            preferred_element_type=jnp.float32,
        ).astype(jnp.bfloat16),
        "dp",
        scatter_dimension=0,
        tiled=True,
    ).astype(jnp.float32)
    smalls = (query_bias, value_bias, output_bias, attn_gain, attn_shift, down_bias, ffn_gain, ffn_shift)
    small_rows = query_bias.shape[0]
    packed = jnp.concatenate([v.reshape(-1, small_rows) for v in (*smalls, up_bias)], axis=0)
    packed_full = lax.all_gather(packed, ("dp", "fsdp"), axis=0)
    (
        qbias_full,
        vbias_full,
        obias_full,
        gain1_full,
        shift1_full,
        downbias_full,
        gain2_full,
        shift2_full,
    ) = (packed_full[:, i].reshape(-1) for i in range(8))
    upbias_full = packed_full[:, 8:].reshape(-1)
    query_full, key_full, value_full, output_full, up_full, down_full = (
        lax.all_gather(weight, ("dp", "fsdp"), axis=0, tiled=True)
        for weight in (query_weight, key_weight, value_weight, output_weight, expand_weight, down_weight)
    )
    inputs = rows_in.astype(jnp.float32)
    query = (apply_weight(rows_in, query_full) + qbias_full.astype(jnp.float32)).astype(
        jnp.bfloat16
    )
    keys = apply_weight(rows_in, key_full).astype(jnp.bfloat16)
    values = (apply_weight(rows_in, value_full) + vbias_full.astype(jnp.float32)).astype(
        jnp.bfloat16
    )
    query_heads = query.reshape(split_shape)
    key_heads = keys.reshape(split_shape)
    value_heads = values.reshape(split_shape)
    scores = (
        jnp.einsum("rqhd,rkhd->rhqk", query_heads, key_heads, preferred_element_type=jnp.float32)
        * score_scale
    )
    row_top = jnp.max(scores, axis=-1, keepdims=True)
    expo = jnp.exp(scores - row_top)
    row_sum = jnp.sum(expo, axis=-1, keepdims=True)
    logsum = row_top + jnp.log(row_sum)
    probs_low = (expo / row_sum).astype(jnp.bfloat16)
    mixed = jnp.einsum(
        "rhqk,rkhd->rqhd", probs_low, value_heads, preferred_element_type=jnp.float32
    )
    mixed = mixed.reshape(row_count, token_count, feature_count).astype(jnp.bfloat16)
    gain1 = gain1_full.astype(jnp.float32)
    resid1 = inputs + apply_weight(mixed, output_full) + obias_full.astype(jnp.float32)
    normed1_out, normed1, inverse1 = norm_forward(resid1, gain1, shift1_full.astype(jnp.float32))
    normed1_low = normed1_out.astype(jnp.bfloat16)
    pre_act = apply_weight(normed1_low, up_full) + upbias_full.astype(jnp.float32)
    act_low = jax.nn.gelu(pre_act, approximate=False).astype(jnp.bfloat16)
    gain2 = gain2_full.astype(jnp.float32)
    resid2 = normed1_out + apply_weight(act_low, down_full) + downbias_full.astype(jnp.float32)
    final, second_normed, inverse2 = norm_forward(resid2, gain2, shift2_full.astype(jnp.float32))
    final_low = final.astype(jnp.bfloat16)
    shard_rows = lax.all_gather(final_low, "dp", axis=0, tiled=True)
    span_rows = shard_rows.shape[0]
    inside = (slot_row >= 0) & (slot_row < span_rows)
    picked = jnp.take(shard_rows, jnp.clip(slot_row, 0, span_rows - 1), axis=0)
    slot_acts = jnp.where(
        inside[:, None, None], picked, jnp.zeros(slot_activation_gradient.shape, jnp.bfloat16)
    )
    gain1 = gain1_full.astype(jnp.float32)
    gain2 = gain2_full.astype(jnp.float32)
    grad2, gain2_grad, shift2_grad = norm_backward(upstream, gain2, second_normed, inverse2)
    ffn_low = grad2.astype(jnp.bfloat16)
    down_grad = weight_term(act_low, ffn_low)
    down_bias_grad = bias_term(ffn_low)
    act_grad = apply_back(ffn_low, down_full)
    gelu_value, gelu_back = jax.vjp(partial(jax.nn.gelu, approximate=False), pre_act)
    pre_grad = gelu_back(act_grad)[0].astype(jnp.bfloat16)
    up_grad = weight_term(normed1_low, pre_grad)
    up_bias_grad = bias_term(pre_grad)
    normed1_grad = grad2 + apply_back(pre_grad, up_full)
    grad1, gain1_grad, shift1_grad = norm_backward(normed1_grad, gain1, normed1, inverse1)
    attn_low = grad1.astype(jnp.bfloat16)
    output_grad = weight_term(mixed, attn_low)
    output_bias_grad = bias_term(attn_low)
    mixed_grad = apply_back(attn_low, output_full).astype(jnp.bfloat16).reshape(split_shape)
    scores_again = (
        jnp.einsum("rqhd,rkhd->rhqk", query_heads, key_heads, preferred_element_type=jnp.float32)
        * score_scale
    )
    probs = jnp.exp(scores_again - logsum)
    probs_again = probs.astype(jnp.bfloat16)
    value_grad = jnp.einsum(
        "rhqk,rqhd->rkhd", probs_again, mixed_grad, preferred_element_type=jnp.float32
    )
    value_grad = value_grad.astype(jnp.bfloat16).reshape(row_count, token_count, feature_count)
    prob_grad = jnp.einsum(
        "rqhd,rkhd->rhqk", mixed_grad, value_heads, preferred_element_type=jnp.float32
    )
    score_grad = (probs * (prob_grad - jnp.sum(probs * prob_grad, axis=-1, keepdims=True))).astype(
        jnp.bfloat16
    )
    query_grad = (
        jnp.einsum("rhqk,rkhd->rqhd", score_grad, key_heads, preferred_element_type=jnp.float32)
        * score_scale
    )
    query_grad = query_grad.astype(jnp.bfloat16).reshape(row_count, token_count, feature_count)
    key_grad = (
        jnp.einsum("rhqk,rqhd->rkhd", score_grad, query_heads, preferred_element_type=jnp.float32)
        * score_scale
    )
    key_grad = key_grad.astype(jnp.bfloat16).reshape(row_count, token_count, feature_count)
    query_wgrad = weight_term(rows_in, query_grad)
    key_wgrad = weight_term(rows_in, key_grad)
    value_wgrad = weight_term(rows_in, value_grad)
    query_bias_grad = bias_term(query_grad)
    value_bias_grad = bias_term(value_grad)
    input_full = (
        grad1
        + apply_back(query_grad, query_full)
        + apply_back(key_grad, key_full)
        + apply_back(value_grad, value_full)
    )
    live_rows = lax.broadcasted_iota(jnp.int32, (row_count,), 0) < live_count[0]
    input_grad = jnp.where(live_rows[:, None, None], input_full, 0.0)
    devices = packed_full.shape[0]
    small_terms = jnp.concatenate(
        [
            v.reshape(devices, -1, small_rows)
            for v in (
                query_bias_grad,
                value_bias_grad,
                output_bias_grad,
                gain1_grad,
                shift1_grad,
                down_bias_grad,
                gain2_grad,
                shift2_grad,
                up_bias_grad,
            )
        ],
        axis=1,
    )
    small_sum = lax.psum_scatter(small_terms, ("dp", "fsdp"), scatter_dimension=0, tiled=True)[0]
    down_sum, up_sum, output_sum, value_sum, query_sum, key_sum = (
        lax.psum_scatter(
            term.astype(jnp.bfloat16), ("dp", "fsdp"), scatter_dimension=0, tiled=True
        ).astype(jnp.float32)
        for term in (down_grad, up_grad, output_grad, value_wgrad, query_wgrad, key_wgrad)
    )
    return (
        slot_acts,
        input_grad,
        query_sum,
        key_sum,
        value_sum,
        output_sum,
        small_sum[0],
        small_sum[1],
        small_sum[2],
        small_sum[3],
        small_sum[4],
        up_sum,
        small_sum[8:].reshape(-1),
        down_sum,
        small_sum[5],
        small_sum[6],
        small_sum[7],
    )


def solution(mesh):
    placed = (
        P(("dp", "fsdp"), None, None),
        P(("dp", "fsdp")),
        P(("dp", "fsdp")),
        P(("dp", "fsdp"), None, None),
        P(("dp", "fsdp"), None),
        P(("dp", "fsdp"), None),
        P(("dp", "fsdp"), None),
        P(("dp", "fsdp"), None),
        P(("dp", "fsdp")),
        P(("dp", "fsdp")),
        P(("dp", "fsdp")),
        P(("dp", "fsdp")),
        P(("dp", "fsdp")),
        P(("dp", "fsdp"), None),
        P(("dp", "fsdp")),
        P(("dp", "fsdp"), None),
        P(("dp", "fsdp")),
        P(("dp", "fsdp")),
        P(("dp", "fsdp")),
    )
    kernels = mesh.shape["dp"] == 4 and mesh.shape["fsdp"] == 8
    return jax.shard_map(
        on_device_kernels if kernels else on_device_plain,
        mesh=mesh,
        in_specs=placed,
        out_specs=(
            P(("dp", "fsdp"), None, None),
            P(("dp", "fsdp"), None, None),
            P(("dp", "fsdp"), None),
            P(("dp", "fsdp"), None),
            P(("dp", "fsdp"), None),
            P(("dp", "fsdp"), None),
            P(("dp", "fsdp")),
            P(("dp", "fsdp")),
            P(("dp", "fsdp")),
            P(("dp", "fsdp")),
            P(("dp", "fsdp")),
            P(("dp", "fsdp"), None),
            P(("dp", "fsdp")),
            P(("dp", "fsdp"), None),
            P(("dp", "fsdp")),
            P(("dp", "fsdp")),
            P(("dp", "fsdp")),
        ),
        check_vma=False,
    )
```

```python
import math
from functools import partial

import jax
import jax.numpy as jnp
from jax import lax
from jax.experimental import pallas as pl
from jax.experimental.pallas import tpu as pltpu
from jax.sharding import PartitionSpec as P

HEADS = 16


EPSILON = 1e-05


MESH = pl.DeviceIdType.MESH
LANES = 128


def place(nz, nx):
    dp, fs = lax.axis_index("dp"), lax.axis_index("fsdp")
    y, core = dp // 2, lax.rem(dp, 2)
    z, x = fs // nx, lax.rem(fs, nx)
    return y, core, z, x


def device(y, core, z, x, nx):
    return (y * 2 + core, z * nx + x)


class Partners:
    def __init__(self, nz, nx):
        self.nz, self.nx = nz, nx
        self.y, self.core, self.z, self.x = place(nz, nx)
        y, core, z, x = self.y, self.core, self.z, self.x
        self.sibling = device(y, 1 - core, z, x, nx)
        self.across_x = device(y, core, z, 1 - x, nx)
        self.across_y = device(1 - y, core, z, x, nx)
        self.along_z = [device(y, core, lax.rem(z + k, nz), x, nx) for k in range(1, nz)]
        self.all = [self.sibling, self.across_x, self.across_y, *self.along_z]

    def meet(self):
        barrier = pltpu.get_barrier_semaphore()
        for other in self.all:
            pl.semaphore_signal(barrier, inc=1, device_id=other, device_id_type=MESH)
        pl.semaphore_wait(barrier, len(self.all))


def remote(src, dst, send, recv, to):
    return pltpu.make_async_remote_copy(
        src_ref=src, dst_ref=dst, send_sem=send, recv_sem=recv, device_id=to, device_id_type=MESH
    )


def added(*blocks):
    total = blocks[0].astype(jnp.float32)
    for block in blocks[1:]:
        total = total + block.astype(jnp.float32)
    return total


class Scatter:
    def __init__(self, at, wide, rc, r3a, r3b, r2, rz, send, recv):
        self.at, self.wide = at, wide
        self.rc, self.r3a, self.r3b, self.r2, self.rz = rc, r3a, r3b, r2, rz
        self.send, self.recv = send, recv

    def to_sibling(self, m, theirs):
        return remote(theirs, self.rc.at[m], self.send.at[m, 0], self.recv.at[m, 0], self.at.sibling)

    def first_a(self, m):
        at, wide = self.at, self.wide
        src = self.rc.at[m, :, :, 1 - at.x, :, pl.ds(0, wide)]
        return remote(src, self.r3a.at[m], self.send.at[m, 1], self.recv.at[m, 1], at.across_x)

    def first_b(self, m):
        at, wide = self.at, self.wide
        src = self.rc.at[m, 1 - at.y, :, :, :, pl.ds(wide, self.rc.shape[-1] - wide)]
        return remote(src, self.r3b.at[m], self.send.at[m, 2], self.recv.at[m, 2], at.across_y)

    def second_a(self, m):
        at, wide = self.at, self.wide
        src, dst = self.r3a.at[m, 1 - at.y], self.r2.at[m, :, :, pl.ds(0, wide)]
        return remote(src, dst, self.send.at[m, 3], self.recv.at[m, 3], at.across_y)

    def second_b(self, m):
        at, wide = self.at, self.wide
        src = self.r3b.at[m, :, 1 - at.x]
        dst = self.r2.at[m, :, :, pl.ds(wide, self.r2.shape[-1] - wide)]
        return remote(src, dst, self.send.at[m, 4], self.recv.at[m, 4], at.across_x)

    def last(self, m, k):
        at = self.at
        src = self.r2.at[m, lax.rem(at.z + k, at.nz)]
        return remote(src, self.rz.at[m, k - 1], self.send.at[m, 4 + k], self.recv.at[m, 4 + k], at.along_z[k - 1])

    def start(self, m, theirs):
        self.to_sibling(m, theirs).start()

    def step1(self, m, own):
        at, rc = self.at, self.rc
        self.to_sibling(m, rc.at[m]).wait_recv()
        nz = at.nz

        def add(i, carry):
            y, z = i // nz, lax.rem(i, nz)
            rc[m, y, z] = added(rc[m, y, z], own(y, z)).astype(rc.dtype)
            return carry

        lax.fori_loop(0, rc.shape[1] * nz, add, 0)
        self.to_sibling(m, rc.at[m]).wait_send()
        self.first_a(m).start()
        self.first_b(m).start()

    def step2(self, m):
        at, rc, wide, r3a, r3b = self.at, self.rc, self.wide, self.r3a, self.r3b
        columns = rc.shape[-1]
        self.first_a(m).wait_recv()
        self.first_b(m).wait_recv()

        def add(z, carry):
            for y in range(rc.shape[1]):
                r3a[m, y, z] = added(r3a[m, y, z], rc[m, y, z, at.x, :, pl.ds(0, wide)]).astype(rc.dtype)
            r3b[m, z] = added(r3b[m, z], rc[m, at.y, z, :, :, pl.ds(wide, columns - wide)]).astype(rc.dtype)
            return carry

        lax.fori_loop(0, at.nz, add, 0)
        self.second_a(m).start()
        self.second_b(m).start()

    def step3(self, m):
        at, r3a, r3b, r2, wide = self.at, self.r3a, self.r3b, self.r2, self.wide
        columns = r2.shape[-1]
        self.second_a(m).wait_recv()
        self.second_b(m).wait_recv()

        def add(z, carry):
            left, right = pl.ds(0, wide), pl.ds(wide, columns - wide)
            r2[m, z, :, left] = added(r2[m, z, :, left], r3a[m, at.y, z]).astype(r2.dtype)
            r2[m, z, :, right] = added(r2[m, z, :, right], r3b[m, z, at.x]).astype(r2.dtype)
            return carry

        lax.fori_loop(0, at.nz, add, 0)
        for k in range(1, at.nz):
            self.last(m, k).start()

    def step4(self, m, out):
        at = self.at
        for k in range(1, at.nz):
            self.last(m, k).wait_recv()
        out[m] = added(self.r2[m, at.z], *[self.rz[m, k] for k in range(at.nz - 1)])

    def drain(self, m):
        self.first_a(m).wait_send()
        self.first_b(m).wait_send()
        self.second_a(m).wait_send()
        self.second_b(m).wait_send()
        for k in range(1, self.at.nz):
            self.last(m, k).wait_send()


class SmallSum:
    def __init__(self, at, total, landing, send, recv):
        self.at, self.total, self.landing, self.send, self.recv = at, total, landing, send, recv

    def hop(self, i, to):
        return remote(self.total.at[i], self.landing.at[i], self.send.at[i], self.recv.at[i], to)

    def along(self, k):
        i = 2 + k
        return remote(self.total.at[3], self.landing.at[i], self.send.at[i], self.recv.at[i], self.at.along_z[k - 1])

    def start(self):
        self.hop(0, self.at.sibling).start()

    def step(self, i):
        at = self.at
        to = (at.sibling, at.across_x, at.across_y)
        self.hop(i, to[i]).wait_recv()
        self.total[i + 1] = self.total[i] + self.landing[i]
        if i < 2:
            self.hop(i + 1, to[i + 1]).start()
        else:
            for k in range(1, at.nz):
                self.along(k).start()

    def finish(self, out):
        at = self.at
        for k in range(1, at.nz):
            self.along(k).wait_recv()
        total = self.total[3]
        for k in range(1, at.nz):
            total = total + self.landing[2 + k]
        out[...] = total
        to = (at.sibling, at.across_x, at.across_y)
        for i in range(3):
            self.hop(i, to[i]).wait_send()
        for k in range(1, at.nz):
            self.along(k).wait_send()


def scatter_scratch(count, nz, nx, rows, columns, wide):
    bf16 = jnp.bfloat16
    return [
        pltpu.VMEM((count, 2, nz, nx, rows, columns), bf16),
        pltpu.VMEM((count, 2, nz, rows, wide), bf16),
        pltpu.VMEM((count, nz, nx, rows, columns - wide), bf16),
        pltpu.VMEM((count, nz, rows, columns), bf16),
        pltpu.VMEM((count, nz - 1, rows, columns), bf16),
        pltpu.SemaphoreType.DMA((count, 4 + nz)),
        pltpu.SemaphoreType.DMA((count, 4 + nz)),
    ]


def small_scratch(nz, shape):
    return [
        pltpu.VMEM((4, *shape), jnp.float32),
        pltpu.VMEM((2 + nz, *shape), jnp.float32),
        pltpu.SemaphoreType.DMA((2 + nz,)),
        pltpu.SemaphoreType.DMA((2 + nz,)),
    ]


def exact_gelu(pre):
    half = 0.5 + 0.5 * lax.erf(pre * (0.5**0.5))
    bell = jnp.exp(-0.5 * pre * pre) * ((0.5 / math.pi) ** 0.5)
    return pre * half, half + pre * bell


def rms_center(hidden):
    center = hidden - jnp.mean(hidden, axis=-1, keepdims=True)
    inverse = lax.rsqrt(jnp.mean(center * center, axis=-1, keepdims=True) + EPSILON)
    return center * inverse, inverse


def half_masks(width):
    left = (lax.broadcasted_iota(jnp.int32, (1, width), 1) < width // 2).astype(jnp.float32)
    return left.astype(jnp.bfloat16), (1.0 - left).astype(jnp.bfloat16)


def across(left, right):
    return lax.dot_general(left, right, (((1,), (1,)), ((), ())), preferred_element_type=jnp.float32)


def down(left, right):
    return lax.dot_general(left, right, (((0,), (0,)), ((), ())), preferred_element_type=jnp.float32)


def dot(left, right):
    return jnp.dot(left, right, preferred_element_type=jnp.float32)


def span(i, size):
    return pl.ds(pl.multiple_of(i * size, size), size)


class Gather:
    def __init__(self, at, wide, count, shards, g, send, recv):
        self.at, self.wide, self.count, self.shards, self.g, self.send, self.recv = at, wide, count, shards, g, send, recv
        self.right = g.shape[-1] - wide

    def along(self, m, k):
        at = self.at
        dst = self.g.at[m, at.y, at.core, at.z, at.x]
        return remote(self.shards.at[m], dst, self.send.at[m, k - 1], self.recv.at[m, k - 1], at.along_z[k - 1])

    def same(self, part, m, i, to):
        return remote(part, part, self.send.at[m, i], self.recv.at[m, i], to)

    def first_a(self, m):
        at, nz = self.at, self.at.nz
        part = self.g.at[m, at.y, at.core, :, at.x, :, pl.ds(0, self.wide)]
        return self.same(part, m, nz - 1, at.across_y)

    def first_b(self, m):
        at, nz = self.at, self.at.nz
        part = self.g.at[m, at.y, at.core, :, at.x, :, pl.ds(self.wide, self.right)]
        return self.same(part, m, nz, at.across_x)

    def second_a(self, m):
        at, nz = self.at, self.at.nz
        part = self.g.at[m, :, at.core, :, at.x, :, pl.ds(0, self.wide)]
        return self.same(part, m, nz + 1, at.across_x)

    def second_b(self, m):
        at, nz = self.at, self.at.nz
        part = self.g.at[m, at.y, at.core, :, :, :, pl.ds(self.wide, self.right)]
        return self.same(part, m, nz + 2, at.across_y)

    def to_sibling(self, m):
        at, nz = self.at, self.at.nz
        return self.same(self.g.at[m, :, at.core], m, nz + 3, at.sibling)

    def step0(self, m):
        at = self.at
        for k in range(1, at.nz):
            self.along(m, k).start()
        self.g[m, at.y, at.core, at.z, at.x] = self.shards[m]

    def step1(self, m):
        for k in range(1, self.at.nz):
            self.along(m, k).wait_recv()
        self.first_a(m).start()
        self.first_b(m).start()

    def step2(self, m):
        self.first_a(m).wait_recv()
        self.first_b(m).wait_recv()
        self.second_a(m).start()
        self.second_b(m).start()

    def step3(self, m):
        self.second_a(m).wait_recv()
        self.second_b(m).wait_recv()
        self.to_sibling(m).start()

    def arrive(self, m):
        self.to_sibling(m).wait_recv()

    def turn(self, m):
        for step, ahead in ((self.step3, 0), (self.step2, 2), (self.step1, 4), (self.step0, 6)):
            if 0 <= m + ahead < self.count:
                step(m + ahead)

    def drain(self, m):
        for k in range(1, self.at.nz):
            self.along(m, k).wait_send()
        for copy in (self.first_a, self.first_b, self.second_a, self.second_b, self.to_sibling):
            copy(m).wait_send()


def forward_kernel(
    nz, nx, wide, tokens, head_pair,
    x, shards, small, pick, slots,
    g_out, saved, act_out, slope_out, unit_out, final_out, own_out, across_out, small_full, inverse1, inverse2,
    g, pool, hidden, landed, total, landing,
    send, recv, ssend, srecv, usend, urecv, across_send, across_recv, isem, gsem, vsem, asem, dsem, fsem,
):
    f32, bf16 = jnp.float32, jnp.bfloat16
    count = g.shape[0]
    all_rows, width = x.shape
    rows = all_rows // tokens
    at = Partners(nz, nx)
    at.meet()
    gather = Gather(at, wide, count, shards, g, send, recv)
    sums = SmallSum(at, total, landing, ssend, srecv)
    groups = slots.shape[0] // rows
    members = pick.shape[0] // rows

    def fetch(i):
        return pltpu.make_async_copy(slots.at[i], pool.at[i // rows, pl.ds((i % rows) * tokens, tokens)], isem.at[i])

    total[0] = small[...]
    sums.start()
    for m in range(4):
        gather.step0(m)
    for i in range(slots.shape[0]):
        fetch(i).start()
    for i in range(slots.shape[0]):
        fetch(i).wait()

    high, part = 16, width // 2

    def sum_slots(i, carry):
        cols = span(lax.rem(i, 2), part)
        base = i // 2 * high
        held = [
            pool[s // rows, pl.ds(pl.multiple_of(base + (s % rows) * tokens, high), high), cols].astype(f32)
            for s in range(slots.shape[0])
        ]
        for t in range(pick.shape[0]):
            picked = pick[t, 0] * held[0]
            for s in range(1, slots.shape[0]):
                picked = picked + pick[t, s] * held[s]
            spot = pl.ds(pl.multiple_of(base + (t % rows) * tokens, high), high)
            pool[groups + t // rows, spot, cols] = picked.astype(bf16)
        return carry

    gather.step1(0)
    sums.step(0)
    gather.step0(4)
    lax.fori_loop(0, tokens // high * 2, sum_slots, 0)
    gather.step1(1)
    gather.step2(0)
    sums.step(1)

    def up_sibling(y):
        src = pool.at[groups + y * 2 + 1 - at.core]
        return remote(src, landed.at[y], usend.at[y], urecv.at[y], at.sibling)

    pieces = across_send.shape[0]

    def up_across(i):
        piece = pl.ds(i * (all_rows // pieces), all_rows // pieces)
        return remote(
            landed.at[1 - at.y, piece], across_out.at[piece], across_send.at[i], across_recv.at[i], at.across_y
        )

    def turn(m):
        gather.turn(m)
        up_across(m).start()

    up_own = pltpu.make_async_copy(landed.at[at.y], own_out, isem.at[slots.shape[0]])

    for y in range(2):
        up_sibling(y).start()
    gather.step0(5)
    gather.step1(2)
    sums.step(2)
    gather.step2(1)
    gather.step1(3)
    for y in range(2):
        up_sibling(y).wait_recv()

    def chip_sum(i, carry):
        y, spot = i // (all_rows // 32), span(lax.rem(i, all_rows // 32), 32)
        landed[y, spot] = added(landed[y, spot], pool[groups + y * 2 + at.core, spot]).astype(bf16)
        return carry

    lax.fori_loop(0, 2 * all_rows // 32, chip_sum, 0)
    up_own.start()
    for y in range(2):
        up_sibling(y).wait_send()
    sums.finish(small_full)
    turn(0)

    def keep(m):
        return pltpu.make_async_copy(g.at[m], g_out.at[m], gsem.at[m])

    def arrive(m):
        gather.arrive(m)
        keep(m).start()

    def tile(m, cols):
        return g[m, :, :, :, :, :, cols].reshape(width, cols.size)

    def bias(i, cols):
        return small_full[pl.ds(i, 1), cols]

    def tiles(size, body):
        def one(i, carry):
            body(span(i // rows, size), span(lax.rem(i, rows), tokens))
            return carry

        lax.fori_loop(0, width // size * rows, one, 0)

    def save(i):
        return pltpu.make_async_copy(pool.at[i], saved.at[i], vsem.at[i])

    def project(m):
        bias_row = (0, None, 1)[m]

        def body(cols, spot):
            y = dot(x[spot], tile(m, cols))
            if bias_row is not None:
                y = y + bias(bias_row, cols)
            pool[m, spot, cols] = y.astype(bf16)

        arrive(m)
        tiles(512, body)
        save(m).start()

    project(0)
    turn(1)
    project(1)
    turn(2)
    project(2)

    pairs = width // head_pair
    masks = half_masks(head_pair)
    scale = (head_pair // 2) ** (-0.5)

    def attend(i, carry):
        spot, cols = span(i // pairs, tokens), span(lax.rem(i, pairs), head_pair)
        query, keys, values = pool[0, spot, cols], pool[1, spot, cols], pool[2, spot, cols]
        query = query * jnp.asarray(scale, bf16)
        out = None
        for mask in masks:
            scores = across(query, keys * mask)
            weight = jnp.exp(scores - jnp.max(scores, axis=-1, keepdims=True))
            weight = weight * (1.0 / jnp.sum(weight, axis=-1, keepdims=True))
            term = dot(weight.astype(bf16), values * mask)
            out = term if out is None else out + term
        pool[3, spot, cols] = out.astype(bf16)
        pl.when(i == rows * pairs // 4)(partial(turn, 3))
        pl.when(i == rows * pairs * 3 // 4)(partial(turn, 4))
        return carry

    lax.fori_loop(0, rows * pairs, attend, 0)
    save(3).start()

    def mix(cols, spot):
        hidden[spot, cols] = dot(pool[3, spot], tile(3, cols)) + x[spot, cols].astype(f32) + bias(2, cols)

    arrive(3)
    tiles(512, mix)
    turn(5)

    def unit(i):
        return pltpu.make_async_copy(pool.at[6], unit_out.at[i], fsem.at[i])

    def norm1(i, carry):
        spot = span(i, 64)
        normed, inverse = rms_center(hidden[spot])
        result = normed * small_full[3:4, :] + small_full[4:5, :]
        hidden[spot] = result
        pool[4, spot] = result.astype(bf16)
        pool[6, spot] = normed.astype(bf16)
        inverse1[spot] = inverse
        return carry

    lax.fori_loop(0, all_rows // 64, norm1, 0)
    save(4).start()
    unit(0).start()

    def save_act(j):
        return pltpu.make_async_copy(pool.at[5], act_out.at[j], asem)

    def save_slope(j):
        return pltpu.make_async_copy(pool.at[6], slope_out.at[j], dsem)

    unit(0).wait()

    def feed(j):
        m = 4 + 2 * j
        if m > 5:
            turn(m)
        arrive(m)
        if j >= 1:
            save_act(j - 1).wait()
            save_slope(j - 1).wait()

        def up(cols, spot):
            value, slope = exact_gelu(dot(pool[4, spot], tile(m, cols)) + bias(8 + j, cols))
            pool[5, spot, cols] = value.astype(bf16)
            pool[6, spot, cols] = slope.astype(bf16)

        tiles(256, up)
        save_act(j).start()
        save_slope(j).start()
        if m + 1 > 5:
            turn(m + 1)
        arrive(m + 1)

        def back(cols, spot):
            hidden[spot, cols] = hidden[spot, cols] + dot(pool[5, spot], tile(m + 1, cols))

        tiles(512, back)

    blocks = (count - 4) // 2
    for j in range(blocks):
        feed(j)
    save_act(blocks - 1).wait()
    save_slope(blocks - 1).wait()

    def norm2(i, carry):
        spot = span(i, 64)
        normed, inverse = rms_center(hidden[spot] + small_full[5:6, :])
        pool[5, spot] = (normed * small_full[6:7, :] + small_full[7:8, :]).astype(bf16)
        pool[6, spot] = normed.astype(bf16)
        inverse2[spot] = inverse
        return carry

    lax.fori_loop(0, all_rows // 64, norm2, 0)
    finish = pltpu.make_async_copy(pool.at[5], final_out, fsem.at[2])
    finish.start()
    unit(1).start()

    def drain(m, carry):
        gather.drain(m)
        keep(m).wait()
        return carry

    lax.fori_loop(0, count, drain, 0)
    for i in range(5):
        save(i).wait()
    up_own.wait()
    for i in range(pieces):
        up_across(i).wait()
    finish.wait()
    unit(1).wait()


def forward(x, shards, small, pick, slots, nz, nx, tokens):
    f32, bf16 = jnp.float32, jnp.bfloat16
    count, shard_rows, width = shards.shape
    all_rows = x.shape[0]
    group_members = pick.shape[0] * tokens // all_rows
    assert group_members == 4 and slots.shape[0] * tokens == 2 * all_rows
    wide = width * 3 // 4
    vmem, anywhere = pl.BlockSpec(memory_space=pltpu.VMEM), pl.BlockSpec(memory_space=pl.ANY)
    acts = (all_rows, width)
    blocks = (count - 4) // 2
    dma = pltpu.SemaphoreType.DMA
    full = (count, 2, 2, nz, nx, shard_rows, width)
    out = jax.ShapeDtypeStruct
    return pl.pallas_call(
        partial(forward_kernel, nz, nx, wide, tokens, 2 * width // HEADS),
        out_shape=[
            out(full, bf16),
            out((5, *acts), bf16),
            out((blocks, *acts), bf16),
            out((blocks, *acts), bf16),
            out((2, *acts), bf16),
            out(acts, bf16),
            out(acts, bf16),
            out(acts, bf16),
            out(small.shape, f32),
            out((all_rows, 1), f32),
            out((all_rows, 1), f32),
        ],
        in_specs=[vmem, vmem, vmem, pl.BlockSpec(memory_space=pltpu.SMEM), anywhere],
        out_specs=[anywhere] * 8 + [vmem] * 3,
        scratch_shapes=[
            pltpu.VMEM(full, bf16),
            pltpu.VMEM((7, *acts), bf16),
            pltpu.VMEM(acts, f32),
            pltpu.VMEM((2, *acts), bf16),
            *small_scratch(nz, small.shape)[:2],
            dma((count, nz + 4)),
            dma((count, nz + 4)),
            dma((2 + nz,)),
            dma((2 + nz,)),
            dma((2,)),
            dma((2,)),
            dma((count,)),
            dma((count,)),
            dma((slots.shape[0] + 1,)),
            dma((count,)),
            dma((5,)),
            dma,
            dma,
            dma((3,)),
        ],
        compiler_params=pltpu.CompilerParams(
            collective_id=1, has_side_effects=True, vmem_limit_bytes=60 * 2**20
        ),
    )(x, shards, small, pick, slots)


def backward_kernel(
    nz, nx, wide, tokens, head_pair,
    x, own_up, across_up, final, unit, inverse1, inverse2, small_full, act, slope, saved, g,
    out, small_out, input_out, table,
    rc, r3a, r3b, r2, rz, send, recv, total, landing, ssend, srecv,
    term, weight, pool, hidden, wsem, psem, hsem, tsend, trecv, across_send, across_recv, tsem,
):
    f32, bf16 = jnp.float32, jnp.bfloat16
    count = out.shape[0]
    all_rows, width = x.shape
    rows = all_rows // tokens
    at = Partners(nz, nx)
    at.meet()
    scatter = Scatter(at, wide, rc, r3a, r3b, r2, rz, send, recv)
    sums = SmallSum(at, total, landing, ssend, srecv)

    here = pltpu.make_async_copy(final, table.at[at.y, at.core], tsem)
    to_sibling = remote(final, table.at[at.y, at.core], tsend.at[0], trecv.at[0], at.sibling)
    pieces = across_send.shape[0]

    def to_across(i):
        piece = pl.ds(i * (all_rows // pieces), all_rows // pieces)
        dst = table.at[at.y, at.core, piece]
        return remote(final.at[piece], dst, across_send.at[i], across_recv.at[i], at.across_y)

    passed = table.at[1 - at.y, at.core]
    pass_on = remote(passed, passed, tsend.at[1], trecv.at[1], at.sibling)

    def load(src, entry, i):
        return pltpu.make_async_copy(src, pool.at[entry], psem.at[i])

    def fetch(m, slot, i):
        return pltpu.make_async_copy(g.at[m], weight.at[slot], wsem.at[i])

    blocks = act.shape[0]
    up_block, down_block = (lambda j: 4 + 2 * j), (lambda j: 5 + 2 * j)
    unit2, own_load, across_load = load(unit.at[1], 1, 0), load(own_up, 2, 1), load(across_up, 3, 2)
    act_entry = [5, 2, 3, 5]
    act_load = [load(act.at[j], act_entry[j], 3 + j) for j in range(blocks)]
    slope_entry = [4, 2, 3, 4]
    slope_load = [load(slope.at[j], slope_entry[j], 7 + j) for j in range(blocks)]
    low_load, unit1, mixed_load = load(saved.at[4], 6, 11), load(unit.at[0], 5, 12), load(saved.at[3], 4, 13)
    query_load, key_load, value_load = (load(saved.at[i], (2, 3, 6)[i], 14 + i) for i in range(3))
    x_load = load(x, 4, 17)
    down_fetch = [fetch(down_block(j), 0, 2 * j) for j in range(blocks)]
    up_fetch = [fetch(up_block(j), 1, 2 * j + 1) for j in range(blocks)]
    last = 2 * blocks
    output_fetch, query_fetch, key_fetch, value_fetch = (
        fetch(m, slot, last + i) for i, (m, slot) in enumerate(((3, 0), (0, 1), (1, 0), (2, 1)))
    )
    for copy in (unit2, own_load, across_load, act_load[0], down_fetch[0], up_fetch[0], slope_load[0], low_load):
        copy.start()
    to_across(0).start()
    to_sibling.start()
    here.start()
    total[0] = jnp.zeros_like(total[0])

    def folded(block):
        return jnp.sum(block.reshape(-1, 8, block.shape[-1]), axis=0)

    def norm_back(gain_row, shift_row, low_row, inverse, incoming, normed_entry, low_entry):
        def body(i, carry):
            spot = span(i, 64)
            grad, normed = incoming(spot), pool[normed_entry, spot].astype(f32)
            scaled = grad * small_full[gain_row : gain_row + 1, :]
            inner = (
                scaled
                - jnp.mean(scaled, axis=-1, keepdims=True)
                - normed * jnp.mean(scaled * normed, axis=-1, keepdims=True)
            )
            result = inner * inverse[spot]
            low = result.astype(bf16)
            hidden[spot] = result
            pool[low_entry, spot] = low
            return tuple(c + folded(b) for c, b in zip(carry, (grad * normed, grad, low.astype(f32))))

        zero = jnp.zeros((8, width), f32)
        found = lax.fori_loop(0, all_rows // 64, body, (zero, zero, zero))
        for row, value in zip((gain_row, shift_row, low_row), found):
            total[0, row : row + 1, :] = jnp.sum(value, axis=0, keepdims=True)

    def tiles(size, body):
        def one(i, carry):
            body(i // rows, span(i // rows, size), span(lax.rem(i, rows), tokens))
            return carry

        lax.fori_loop(0, width // size * rows, one, 0)

    def turned(slot, y):
        return weight[slot, y].reshape(width // 2, width)

    def own_half(slot):
        return lambda y, z: term[slot, y, at.core, z]

    def produce(m, left, right, after=True):
        slot = m % 2

        def half(core):
            def body(i, carry):
                y, cols = i // 2, span(lax.rem(i, 2), width // 2)
                picked = span(y * 2 + core, width // 4)
                value = down(pool[left, :, picked], pool[right, :, cols]).astype(bf16)
                term[slot, y, core, :, :, :, cols] = value.reshape(nz, nx, -1, width // 2)
                return carry

            lax.fori_loop(0, 4, body, 0)

        half(1 - at.core)
        scatter.start(m, term.at[slot, :, 1 - at.core])
        if m > 0 and after:
            scatter.step1(m - 1, own_half(1 - slot))
        half(at.core)

    def turn(m):
        for step, behind in ((scatter.step4, 4), (scatter.step3, 2), (scatter.step2, 0)):
            if 0 <= m - behind < count:
                step(*((m - behind, out) if behind == 4 else (m - behind,)))
        if 0 < m + 1 < pieces:
            to_across(m + 1).start()

    for copy in (unit2, own_load, across_load):
        copy.wait()
    norm_back(6, 7, 5, inverse2, lambda spot: added(pool[2, spot], pool[3, spot]), 1, 0)

    act_load[1].start()
    act_load[2].start()
    for j in range(blocks):
        act_load[j].wait()
        produce(j, act_entry[j], 0)
        if j == 0:
            act_load[3].start()
        elif j < 3:
            slope_load[j].start()
        else:
            unit1.start()
    turn(0)

    low_load.wait()
    for j in range(blocks):
        down_fetch[j].wait()
        slope_load[j].wait()

        def pre_back(n, cols, spot, j=j):
            value = across(pool[0, spot], turned(0, n)) * pool[slope_entry[j], spot, cols].astype(f32)
            value = value.astype(bf16)
            pool[1, spot, cols] = value
            row = pl.ds(8 + j, 1)
            total[0, row, cols] = total[0, row, cols] + jnp.sum(value.astype(f32), axis=0, keepdims=True)

        tiles(width // 2, pre_back)
        if j + 1 < blocks:
            down_fetch[j + 1].start()
        else:
            output_fetch.start()
        (lambda: slope_load[3].start(), query_load.start, key_load.start, mixed_load.start)[j]()
        produce(blocks + j, 6, 1)
        up_fetch[j].wait()

        def hidden_back(n, cols, spot):
            hidden[spot, cols] = hidden[spot, cols] + across(pool[1, spot], turned(1, n))

        tiles(width // 2, hidden_back)
        if j + 1 < blocks:
            up_fetch[j + 1].start()
        else:
            query_fetch.start()
        if j == blocks - 1:
            value_load.start()
        turn(1 + j)

    unit1.wait()
    norm_back(3, 4, 2, inverse1, lambda spot: hidden[spot], 5, 0)
    mixed_load.wait()
    produce(2 * blocks, 4, 0)
    x_load.start()
    output_fetch.wait()

    def mixed_back(n, cols, spot):
        pool[1, spot, cols] = across(pool[0, spot], turned(0, n)).astype(bf16)

    tiles(width // 2, mixed_back)
    key_fetch.start()
    for copy in (query_load, key_load, value_load):
        copy.wait()
    turn(5)
    scatter.step1(2 * blocks, own_half((2 * blocks) % 2))

    pairs = width // head_pair
    masks = half_masks(head_pair)
    scale = (head_pair // 2) ** (-0.5)

    def attend(i, carry):
        spot, cols = span(i // pairs, tokens), span(lax.rem(i, pairs), head_pair)
        query, keys, values, mixed_grad = (pool[e, spot, cols] for e in (2, 3, 6, 1))
        query_grad = key_grad = value_grad = None
        for mask in masks:
            own_keys = keys * (mask * jnp.asarray(scale, bf16))
            scores = across(own_keys, query)
            probs = jnp.exp(scores - jnp.max(scores, axis=0, keepdims=True))
            probs = probs * (1.0 / jnp.sum(probs, axis=0, keepdims=True))
            prob_grad = across(values * mask, mixed_grad)
            weighed = probs * prob_grad
            score_grad = (weighed - probs * jnp.sum(weighed, axis=0, keepdims=True)).astype(bf16)
            terms = (
                down(score_grad, own_keys),
                dot(score_grad, query * mask),
                dot(probs.astype(bf16), mixed_grad * mask),
            )
            if query_grad is None:
                query_grad, key_grad, value_grad = terms
            else:
                query_grad, key_grad, value_grad = query_grad + terms[0], key_grad + terms[1], value_grad + terms[2]
        query_grad, value_grad = query_grad.astype(bf16), value_grad.astype(bf16)
        pool[2, spot, cols] = query_grad
        pool[3, spot, cols] = (key_grad * scale).astype(bf16)
        pool[6, spot, cols] = value_grad
        for row, value in ((0, query_grad), (1, value_grad)):
            found = jnp.sum(value.astype(f32), axis=0, keepdims=True)
            total[0, row : row + 1, cols] = total[0, row : row + 1, cols] + found
        for third in range(3):
            pl.when(i == (2 * third + 1) * rows * pairs // 6)(partial(turn, 6 + third))
        return carry

    lax.fori_loop(0, rows * pairs, attend, 0)
    sums.start()

    x_load.wait()
    for i, entry in enumerate((6, 2, 3)):
        produce(2 * blocks + 1 + i, 4, entry, i > 0)
        sums.step(i)
    scatter.step1(count - 1, own_half((count - 1) % 2))
    turn(9)

    def input_back(slot, entry, fetched):
        def body(n, cols, spot):
            hidden[spot, cols] = hidden[spot, cols] + across(pool[entry, spot], turned(slot, n))

        fetched.wait()
        tiles(width // 2, body)

    input_back(1, 2, query_fetch)
    value_fetch.start()
    turn(10)
    input_back(0, 3, key_fetch)
    for i in range(pieces):
        to_across(i).wait_recv()
    pass_on.start()
    turn(11)
    input_back(1, 6, value_fetch)
    done = pltpu.make_async_copy(hidden, input_out, hsem)
    done.start()
    turn(12)
    turn(13)
    sums.finish(small_out)
    turn(14)
    turn(15)
    done.wait()

    def drain(m, carry):
        scatter.drain(m)
        return carry

    lax.fori_loop(0, count, drain, 0)
    here.wait()
    to_sibling.wait()
    for i in range(pieces):
        to_across(i).wait_send()
    pass_on.wait()


def backward(x, own_up, across_up, final, unit, inverse1, inverse2, small_full, act, slope, saved, g, nz, nx, tokens):
    f32, bf16 = jnp.float32, jnp.bfloat16
    count, _, _, _, _, shard_rows, width = g.shape
    acts = x.shape
    wide = width * 3 // 4
    vmem, anywhere = pl.BlockSpec(memory_space=pltpu.VMEM), pl.BlockSpec(memory_space=pl.ANY)
    dma = pltpu.SemaphoreType.DMA
    out = jax.ShapeDtypeStruct
    block = (2, 2, nz, nx, shard_rows, width)
    return pl.pallas_call(
        partial(backward_kernel, nz, nx, wide, tokens, 2 * width // HEADS),
        out_shape=[
            out((count, shard_rows, width), f32),
            out(small_full.shape, f32),
            out(acts, f32),
            out((2, 2, *acts), bf16),
        ],
        in_specs=[anywhere] * 5 + [vmem] * 3 + [anywhere] * 4,
        out_specs=[vmem, vmem, anywhere, anywhere],
        scratch_shapes=[
            *scatter_scratch(count, nz, nx, shard_rows, width, wide),
            *small_scratch(nz, small_full.shape),
            pltpu.VMEM((2, *block), bf16),
            pltpu.VMEM((2, *block), bf16),
            pltpu.VMEM((7, *acts), bf16),
            pltpu.VMEM(acts, f32),
            dma((count,)),
            dma((18,)),
            dma,
            dma((2,)),
            dma((2,)),
            dma((count,)),
            dma((count,)),
            dma,
        ],
        compiler_params=pltpu.CompilerParams(
            collective_id=2, has_side_effects=True, vmem_limit_bytes=60 * 2**20
        ),
    )(x, own_up, across_up, final, unit, inverse1, inverse2, small_full, act, slope, saved, g)


def pick_kernel(slot_row, row, out):
    out[...] = row[...]


def pick_rows(slot_row, table):
    members, tokens, width = table.shape
    block = (1, tokens, width)
    return pl.pallas_call(
        pick_kernel,
        out_shape=jax.ShapeDtypeStruct((slot_row.shape[0], tokens, width), table.dtype),
        grid_spec=pltpu.PrefetchScalarGridSpec(
            num_scalar_prefetch=1,
            grid=(slot_row.shape[0],),
            in_specs=[pl.BlockSpec(block, lambda s, slot_row: (jnp.clip(slot_row[s], 0, members - 1), 0, 0))],
            out_specs=pl.BlockSpec(block, lambda s, slot_row: (s, 0, 0)),
        ),
    )(slot_row, table)


def prepare(
    rows_in, slot_row, weights, small_parameters, up_bias, dp_size
):
    row_count, token_count, width = rows_in.shape
    query_weight, key_weight, value_weight, output_weight, expand_weight, down_weight = weights
    shard = query_weight.shape[0]
    blocks = down_weight.shape[0] // shard
    me = lax.axis_index(("dp", "fsdp"))
    ups = expand_weight.reshape(shard, -1, blocks, shard).transpose(2, 0, 1, 3).reshape(blocks, shard, width)
    downs = down_weight.reshape(blocks, shard, width)
    paired = jnp.stack([ups, downs], axis=1).reshape(2 * blocks, shard, width)
    shards = jnp.concatenate([jnp.stack([query_weight, key_weight, value_weight, output_weight]), paired])
    mine = jnp.concatenate([jnp.stack(small_parameters), up_bias.reshape(blocks, shard)]).astype(jnp.float32)
    small = lax.dynamic_update_slice(
        jnp.zeros((16, width), jnp.float32), mine, (jnp.int32(0), me * shard)
    )
    wanted = lax.broadcasted_iota(jnp.int32, (row_count * dp_size, slot_row.shape[0]), 0)
    pick = (wanted == slot_row[None, :]).astype(jnp.float32)
    return rows_in.reshape(-1, width), shards, small, pick


def on_device_kernels(
    rows_in,
    slot_row,
    live_count,
    slot_activation_gradient,
    query_weight,
    key_weight,
    value_weight,
    output_weight,
    query_bias,
    value_bias,
    output_bias,
    attn_gain,
    attn_shift,
    expand_weight,
    up_bias,
    down_weight,
    down_bias,
    ffn_gain,
    ffn_shift,
):
    row_count, token_count, width = rows_in.shape
    shard = query_weight.shape[0]
    nx = 2
    nz = lax.axis_size("fsdp") // nx
    x, shards, small, pick = prepare(
        rows_in,
        slot_row,
        (query_weight, key_weight, value_weight, output_weight, expand_weight, down_weight),
        (query_bias, value_bias, output_bias, attn_gain, attn_shift, down_bias, ffn_gain, ffn_shift),
        up_bias,
        lax.axis_size("dp"),
    )
    g, saved, act, slope, unit, final, own_up, across_up, small_full, inverse1, inverse2 = forward(
        x, shards, small, pick, slot_activation_gradient, nz, nx, token_count
    )
    sums, small_sums, input_full, table = backward(
        x, own_up, across_up, final, unit, inverse1, inverse2, small_full, act, slope, saved, g, nz, nx, token_count
    )
    slot_acts = pick_rows(slot_row, table.reshape(-1, token_count, width))
    live_rows = lax.broadcasted_iota(jnp.int32, (row_count,), 0) < live_count[0]
    input_grad = jnp.where(live_rows[:, None, None], input_full.reshape(rows_in.shape), 0.0)
    me = lax.axis_index(("dp", "fsdp"))
    mine = lax.dynamic_slice(small_sums, (jnp.int32(0), me * shard), (small_sums.shape[0], shard))
    blocks = (sums.shape[0] - 4) // 2
    down_sum = sums[:blocks].reshape(-1, width)
    ups = sums[blocks : 2 * blocks].reshape(blocks, shard, -1, shard)
    up_sum = ups.transpose(1, 2, 0, 3).reshape(shard, -1)
    output_sum, value_sum, query_sum, key_sum = (sums[2 * blocks + i] for i in range(4))
    return (
        slot_acts,
        input_grad,
        query_sum,
        key_sum,
        value_sum,
        output_sum,
        mine[0],
        mine[1],
        mine[2],
        mine[3],
        mine[4],
        up_sum,
        mine[8 : 8 + blocks].reshape(-1),
        down_sum,
        mine[5],
        mine[6],
        mine[7],
    )


def norm_forward(hidden, gain, shift):
    center = hidden - jnp.mean(hidden, axis=-1, keepdims=True)
    inverse = lax.rsqrt(jnp.mean(center * center, axis=-1, keepdims=True) + EPSILON)
    normed = center * inverse
    return (normed * gain + shift, normed, inverse)


def norm_backward(incoming, gain, normed, inverse):
    scaled = incoming * gain
    inner = (
        scaled
        - jnp.mean(scaled, axis=-1, keepdims=True)
        - normed * jnp.mean(scaled * normed, axis=-1, keepdims=True)
    )
    return (
        inner * inverse,
        jnp.sum(incoming * normed, axis=(0, 1)),
        jnp.sum(incoming, axis=(0, 1)),
    )


def apply_weight(acts, weight):
    return jnp.einsum("rsd,de->rse", acts, weight, preferred_element_type=jnp.float32)


def apply_back(grads, weight):
    return jnp.einsum("rse,de->rsd", grads, weight, preferred_element_type=jnp.float32)


def weight_term(acts, grads):
    return jnp.einsum("rsd,rse->de", acts, grads, preferred_element_type=jnp.float32)


def bias_term(grads):
    return jnp.sum(grads, axis=(0, 1), dtype=jnp.float32)


def on_device_plain(
    rows_in,
    slot_row,
    live_count,
    slot_activation_gradient,
    query_weight,
    key_weight,
    value_weight,
    output_weight,
    query_bias,
    value_bias,
    output_bias,
    attn_gain,
    attn_shift,
    expand_weight,
    up_bias,
    down_weight,
    down_bias,
    ffn_gain,
    ffn_shift,
):
    row_count, token_count, feature_count = rows_in.shape
    head_size = feature_count // HEADS
    score_scale = head_size ** (-0.5)
    split_shape = (row_count, token_count, HEADS, head_size)
    wanted = lax.broadcasted_iota(
        jnp.int32, (row_count * lax.axis_size("dp"), slot_row.shape[0]), 0
    )
    one_hot_matrix = (wanted == slot_row[None, :]).astype(jnp.bfloat16)
    upstream = lax.psum_scatter(
        jnp.einsum(
            "az,zfy->afy",
            one_hot_matrix,
            slot_activation_gradient,
            preferred_element_type=jnp.float32,
        ).astype(jnp.bfloat16),
        "dp",
        scatter_dimension=0,
        tiled=True,
    ).astype(jnp.float32)
    smalls = (query_bias, value_bias, output_bias, attn_gain, attn_shift, down_bias, ffn_gain, ffn_shift)
    small_rows = query_bias.shape[0]
    packed = jnp.concatenate([v.reshape(-1, small_rows) for v in (*smalls, up_bias)], axis=0)
    packed_full = lax.all_gather(packed, ("dp", "fsdp"), axis=0)
    (
        qbias_full,
        vbias_full,
        obias_full,
        gain1_full,
        shift1_full,
        downbias_full,
        gain2_full,
        shift2_full,
    ) = (packed_full[:, i].reshape(-1) for i in range(8))
    upbias_full = packed_full[:, 8:].reshape(-1)
    query_full, key_full, value_full, output_full, up_full, down_full = (
        lax.all_gather(weight, ("dp", "fsdp"), axis=0, tiled=True)
        for weight in (query_weight, key_weight, value_weight, output_weight, expand_weight, down_weight)
    )
    inputs = rows_in.astype(jnp.float32)
    query = (apply_weight(rows_in, query_full) + qbias_full.astype(jnp.float32)).astype(
        jnp.bfloat16
    )
    keys = apply_weight(rows_in, key_full).astype(jnp.bfloat16)
    values = (apply_weight(rows_in, value_full) + vbias_full.astype(jnp.float32)).astype(
        jnp.bfloat16
    )
    query_heads = query.reshape(split_shape)
    key_heads = keys.reshape(split_shape)
    value_heads = values.reshape(split_shape)
    scores = (
        jnp.einsum("rqhd,rkhd->rhqk", query_heads, key_heads, preferred_element_type=jnp.float32)
        * score_scale
    )
    row_top = jnp.max(scores, axis=-1, keepdims=True)
    expo = jnp.exp(scores - row_top)
    row_sum = jnp.sum(expo, axis=-1, keepdims=True)
    logsum = row_top + jnp.log(row_sum)
    probs_low = (expo / row_sum).astype(jnp.bfloat16)
    mixed = jnp.einsum(
        "rhqk,rkhd->rqhd", probs_low, value_heads, preferred_element_type=jnp.float32
    )
    mixed = mixed.reshape(row_count, token_count, feature_count).astype(jnp.bfloat16)
    gain1 = gain1_full.astype(jnp.float32)
    resid1 = inputs + apply_weight(mixed, output_full) + obias_full.astype(jnp.float32)
    normed1_out, normed1, inverse1 = norm_forward(resid1, gain1, shift1_full.astype(jnp.float32))
    normed1_low = normed1_out.astype(jnp.bfloat16)
    pre_act = apply_weight(normed1_low, up_full) + upbias_full.astype(jnp.float32)
    act_low = jax.nn.gelu(pre_act, approximate=False).astype(jnp.bfloat16)
    gain2 = gain2_full.astype(jnp.float32)
    resid2 = normed1_out + apply_weight(act_low, down_full) + downbias_full.astype(jnp.float32)
    final, second_normed, inverse2 = norm_forward(resid2, gain2, shift2_full.astype(jnp.float32))
    final_low = final.astype(jnp.bfloat16)
    shard_rows = lax.all_gather(final_low, "dp", axis=0, tiled=True)
    span_rows = shard_rows.shape[0]
    inside = (slot_row >= 0) & (slot_row < span_rows)
    picked = jnp.take(shard_rows, jnp.clip(slot_row, 0, span_rows - 1), axis=0)
    slot_acts = jnp.where(
        inside[:, None, None], picked, jnp.zeros(slot_activation_gradient.shape, jnp.bfloat16)
    )
    gain1 = gain1_full.astype(jnp.float32)
    gain2 = gain2_full.astype(jnp.float32)
    grad2, gain2_grad, shift2_grad = norm_backward(upstream, gain2, second_normed, inverse2)
    ffn_low = grad2.astype(jnp.bfloat16)
    down_grad = weight_term(act_low, ffn_low)
    down_bias_grad = bias_term(ffn_low)
    act_grad = apply_back(ffn_low, down_full)
    gelu_value, gelu_back = jax.vjp(partial(jax.nn.gelu, approximate=False), pre_act)
    pre_grad = gelu_back(act_grad)[0].astype(jnp.bfloat16)
    up_grad = weight_term(normed1_low, pre_grad)
    up_bias_grad = bias_term(pre_grad)
    normed1_grad = grad2 + apply_back(pre_grad, up_full)
    grad1, gain1_grad, shift1_grad = norm_backward(normed1_grad, gain1, normed1, inverse1)
    attn_low = grad1.astype(jnp.bfloat16)
    output_grad = weight_term(mixed, attn_low)
    output_bias_grad = bias_term(attn_low)
    mixed_grad = apply_back(attn_low, output_full).astype(jnp.bfloat16).reshape(split_shape)
    scores_again = (
        jnp.einsum("rqhd,rkhd->rhqk", query_heads, key_heads, preferred_element_type=jnp.float32)
        * score_scale
    )
    probs = jnp.exp(scores_again - logsum)
    probs_again = probs.astype(jnp.bfloat16)
    value_grad = jnp.einsum(
        "rhqk,rqhd->rkhd", probs_again, mixed_grad, preferred_element_type=jnp.float32
    )
    value_grad = value_grad.astype(jnp.bfloat16).reshape(row_count, token_count, feature_count)
    prob_grad = jnp.einsum(
        "rqhd,rkhd->rhqk", mixed_grad, value_heads, preferred_element_type=jnp.float32
    )
    score_grad = (probs * (prob_grad - jnp.sum(probs * prob_grad, axis=-1, keepdims=True))).astype(
        jnp.bfloat16
    )
    query_grad = (
        jnp.einsum("rhqk,rkhd->rqhd", score_grad, key_heads, preferred_element_type=jnp.float32)
        * score_scale
    )
    query_grad = query_grad.astype(jnp.bfloat16).reshape(row_count, token_count, feature_count)
    key_grad = (
        jnp.einsum("rhqk,rqhd->rkhd", score_grad, query_heads, preferred_element_type=jnp.float32)
        * score_scale
    )
    key_grad = key_grad.astype(jnp.bfloat16).reshape(row_count, token_count, feature_count)
    query_wgrad = weight_term(rows_in, query_grad)
    key_wgrad = weight_term(rows_in, key_grad)
    value_wgrad = weight_term(rows_in, value_grad)
    query_bias_grad = bias_term(query_grad)
    value_bias_grad = bias_term(value_grad)
    input_full = (
        grad1
        + apply_back(query_grad, query_full)
        + apply_back(key_grad, key_full)
        + apply_back(value_grad, value_full)
    )
    live_rows = lax.broadcasted_iota(jnp.int32, (row_count,), 0) < live_count[0]
    input_grad = jnp.where(live_rows[:, None, None], input_full, 0.0)
    devices = packed_full.shape[0]
    small_terms = jnp.concatenate(
        [
            v.reshape(devices, -1, small_rows)
            for v in (
                query_bias_grad,
                value_bias_grad,
                output_bias_grad,
                gain1_grad,
                shift1_grad,
                down_bias_grad,
                gain2_grad,
                shift2_grad,
                up_bias_grad,
            )
        ],
        axis=1,
    )
    small_sum = lax.psum_scatter(small_terms, ("dp", "fsdp"), scatter_dimension=0, tiled=True)[0]
    down_sum, up_sum, output_sum, value_sum, query_sum, key_sum = (
        lax.psum_scatter(
            term.astype(jnp.bfloat16), ("dp", "fsdp"), scatter_dimension=0, tiled=True
        ).astype(jnp.float32)
        for term in (down_grad, up_grad, output_grad, value_wgrad, query_wgrad, key_wgrad)
    )
    return (
        slot_acts,
        input_grad,
        query_sum,
        key_sum,
        value_sum,
        output_sum,
        small_sum[0],
        small_sum[1],
        small_sum[2],
        small_sum[3],
        small_sum[4],
        up_sum,
        small_sum[8:].reshape(-1),
        down_sum,
        small_sum[5],
        small_sum[6],
        small_sum[7],
    )


def solution(mesh):
    placed = (
        P(("dp", "fsdp"), None, None),
        P(("dp", "fsdp")),
        P(("dp", "fsdp")),
        P(("dp", "fsdp"), None, None),
        P(("dp", "fsdp"), None),
        P(("dp", "fsdp"), None),
        P(("dp", "fsdp"), None),
        P(("dp", "fsdp"), None),
        P(("dp", "fsdp")),
        P(("dp", "fsdp")),
        P(("dp", "fsdp")),
        P(("dp", "fsdp")),
        P(("dp", "fsdp")),
        P(("dp", "fsdp"), None),
        P(("dp", "fsdp")),
        P(("dp", "fsdp"), None),
        P(("dp", "fsdp")),
        P(("dp", "fsdp")),
        P(("dp", "fsdp")),
    )
    kernels = mesh.shape["dp"] == 4 and mesh.shape["fsdp"] == 8
    return jax.shard_map(
        on_device_kernels if kernels else on_device_plain,
        mesh=mesh,
        in_specs=placed,
        out_specs=(
            P(("dp", "fsdp"), None, None),
            P(("dp", "fsdp"), None, None),
            P(("dp", "fsdp"), None),
            P(("dp", "fsdp"), None),
            P(("dp", "fsdp"), None),
            P(("dp", "fsdp"), None),
            P(("dp", "fsdp")),
            P(("dp", "fsdp")),
            P(("dp", "fsdp")),
            P(("dp", "fsdp")),
            P(("dp", "fsdp")),
            P(("dp", "fsdp"), None),
            P(("dp", "fsdp")),
            P(("dp", "fsdp"), None),
            P(("dp", "fsdp")),
            P(("dp", "fsdp")),
            P(("dp", "fsdp")),
        ),
        check_vma=False,
    )
```

```python
import math
from functools import partial

import jax
import jax.numpy as jnp
from jax import lax
from jax.experimental import pallas as pl
from jax.experimental.pallas import tpu as pltpu
from jax.sharding import PartitionSpec as P

HEADS = 16


EPSILON = 1e-05


MESH = pl.DeviceIdType.MESH
LANES = 128


def place(nz, nx):
    dp, fs = lax.axis_index("dp"), lax.axis_index("fsdp")
    y, core = dp // 2, lax.rem(dp, 2)
    z, x = fs // nx, lax.rem(fs, nx)
    return y, core, z, x


def device(y, core, z, x, nx):
    return (y * 2 + core, z * nx + x)


class Partners:
    def __init__(self, nz, nx):
        self.nz, self.nx = nz, nx
        self.y, self.core, self.z, self.x = place(nz, nx)
        y, core, z, x = self.y, self.core, self.z, self.x
        self.sibling = device(y, 1 - core, z, x, nx)
        self.across_x = device(y, core, z, 1 - x, nx)
        self.across_y = device(1 - y, core, z, x, nx)
        self.along_z = [device(y, core, lax.rem(z + k, nz), x, nx) for k in range(1, nz)]
        self.all = [self.sibling, self.across_x, self.across_y, *self.along_z]

    def meet(self):
        barrier = pltpu.get_barrier_semaphore()
        for other in self.all:
            pl.semaphore_signal(barrier, inc=1, device_id=other, device_id_type=MESH)
        pl.semaphore_wait(barrier, len(self.all))


def remote(src, dst, send, recv, to):
    return pltpu.make_async_remote_copy(
        src_ref=src, dst_ref=dst, send_sem=send, recv_sem=recv, device_id=to, device_id_type=MESH
    )


def added(*blocks):
    total = blocks[0].astype(jnp.float32)
    for block in blocks[1:]:
        total = total + block.astype(jnp.float32)
    return total


class Scatter:
    def __init__(self, at, parts, rc, r3a, r3b, r2, rz, rcz, rcx, rcy, send, recv):
        self.at, self.parts = at, parts
        self.rc, self.r3a, self.r3b, self.r2, self.rz = rc, r3a, r3b, r2, rz
        self.rcz, self.rcx, self.rcy = rcz, rcx, rcy
        self.send, self.recv = send, recv

    def copy(self, m, i, src, dst, to):
        return remote(src, dst, self.send.at[m, i], self.recv.at[m, i], to)

    def to_sibling(self, m, theirs):
        return self.copy(m, 0, theirs, self.rc.at[m], self.at.sibling)

    def landings(self, m):
        a, b, c, _ = self.parts[m]
        a, b, c = (pl.ds(0, part.size) for part in (a, b, c))
        return (
            self.r3a.at[m, :, :, :, a],
            self.r3b.at[m, :, :, :, b],
            self.rcz.at[m, :, :, :, :, c],
            self.rcx.at[m, :, :, c],
            self.rcy.at[m, :, c],
        )

    def firsts(self, m):
        at, rc, nz = self.at, self.rc, self.at.nz
        a, b, c, _ = self.parts[m]
        r3a, r3b, rcz, _, _ = self.landings(m)
        return [
            self.copy(m, 1, rc.at[m, :, :, 1 - at.x, :, a], r3a, at.across_x),
            self.copy(m, 2, rc.at[m, 1 - at.y, :, :, :, b], r3b, at.across_y),
        ] + [
            self.copy(
                m, 2 + k, rc.at[m, :, lax.rem(at.z + k, nz), :, :, c], rcz.at[k - 1], at.along_z[k - 1]
            )
            for k in range(1, nz)
        ]

    def seconds(self, m):
        at, nz = self.at, self.at.nz
        a, b, _, _ = self.parts[m]
        r3a, r3b, rcz, rcx, _ = self.landings(m)
        return [
            self.copy(m, nz + 2, r3a.at[1 - at.y], self.r2.at[m, :, :, a], at.across_y),
            self.copy(m, nz + 3, r3b.at[:, 1 - at.x], self.r2.at[m, :, :, b], at.across_x),
            self.copy(m, nz + 4, rcz.at[0, :, 1 - at.x], rcx, at.across_x),
        ]

    def thirds(self, m):
        at, nz = self.at, self.at.nz
        ab = self.parts[m][3]
        rcx, rcy = self.landings(m)[3:]
        return [
            self.copy(
                m,
                nz + 4 + k,
                self.r2.at[m, lax.rem(at.z + k, nz), :, ab],
                self.rz.at[m, k - 1, :, ab],
                at.along_z[k - 1],
            )
            for k in range(1, nz)
        ] + [self.copy(m, 2 * nz + 4, rcx.at[1 - at.y], rcy, at.across_y)]

    def start(self, m, theirs):
        self.to_sibling(m, theirs).start()

    def step1(self, m, own):
        rc, nz = self.rc, self.at.nz
        self.to_sibling(m, rc.at[m]).wait_recv()

        def add(i, carry):
            y, z = i // nz, lax.rem(i, nz)
            rc[m, y, z] = added(rc[m, y, z], own(y, z)).astype(rc.dtype)
            return carry

        lax.fori_loop(0, rc.shape[1] * nz, add, 0)
        self.to_sibling(m, rc.at[m]).wait_send()
        for copy in self.firsts(m):
            copy.start()

    def step2(self, m):
        at, rc = self.at, self.rc
        a, b, c, _ = self.parts[m]
        r3a, r3b, rcz, _, _ = self.landings(m)
        for copy in self.firsts(m):
            copy.wait_recv()

        def add(z, carry):
            for y in range(rc.shape[1]):
                r3a[y, z] = added(r3a[y, z], rc[m, y, z, at.x, :, a]).astype(rc.dtype)
            r3b[z] = added(r3b[z], rc[m, at.y, z, :, :, b]).astype(rc.dtype)
            return carry

        lax.fori_loop(0, at.nz, add, 0)
        others = [rcz[k] for k in range(at.nz - 1)]
        rcz[0] = added(rc[m, :, at.z, :, :, c], *others).astype(rc.dtype)
        for copy in self.seconds(m):
            copy.start()

    def step3(self, m):
        at, r2 = self.at, self.r2
        a, b, _, _ = self.parts[m]
        r3a, r3b, rcz, rcx, _ = self.landings(m)
        for copy in self.seconds(m):
            copy.wait_recv()

        def add(z, carry):
            r2[m, z, :, a] = added(r2[m, z, :, a], r3a[at.y, z]).astype(r2.dtype)
            r2[m, z, :, b] = added(r2[m, z, :, b], r3b[z, at.x]).astype(r2.dtype)
            return carry

        lax.fori_loop(0, at.nz, add, 0)
        rcx[...] = added(rcx[...], rcz[0, :, at.x]).astype(r2.dtype)
        for copy in self.thirds(m):
            copy.start()

    def step4(self, m, out):
        at = self.at
        _, _, c, ab = self.parts[m]
        rcx, rcy = self.landings(m)[3:]
        for copy in self.thirds(m):
            copy.wait_recv()
        others = [self.rz[m, k, :, ab] for k in range(at.nz - 1)]
        out[m, :, ab] = added(self.r2[m, at.z, :, ab], *others)
        out[m, :, c] = added(rcx[at.y], rcy[...])

    def drain(self, m):
        for copy in self.firsts(m) + self.seconds(m) + self.thirds(m):
            copy.wait_send()


class SmallSum:
    def __init__(self, at, total, landing, send, recv):
        self.at, self.total, self.landing, self.send, self.recv = at, total, landing, send, recv

    def hop(self, i, to):
        return remote(self.total.at[i], self.landing.at[i], self.send.at[i], self.recv.at[i], to)

    def along(self, k):
        i = 2 + k
        return remote(self.total.at[3], self.landing.at[i], self.send.at[i], self.recv.at[i], self.at.along_z[k - 1])

    def start(self):
        self.hop(0, self.at.sibling).start()

    def step(self, i):
        at = self.at
        to = (at.sibling, at.across_x, at.across_y)
        self.hop(i, to[i]).wait_recv()
        self.total[i + 1] = self.total[i] + self.landing[i]
        if i < 2:
            self.hop(i + 1, to[i + 1]).start()
        else:
            for k in range(1, at.nz):
                self.along(k).start()

    def finish(self, out):
        at = self.at
        for k in range(1, at.nz):
            self.along(k).wait_recv()
        total = self.total[3]
        for k in range(1, at.nz):
            total = total + self.landing[2 + k]
        out[...] = total
        to = (at.sibling, at.across_x, at.across_y)
        for i in range(3):
            self.hop(i, to[i]).wait_send()
        for k in range(1, at.nz):
            self.along(k).wait_send()


def scatter_scratch(count, nz, nx, rows, columns, parts):
    bf16 = jnp.bfloat16
    a, b, c = (max(part[i].size for part in parts) for i in range(3))
    return [
        pltpu.VMEM((count, 2, nz, nx, rows, columns), bf16),
        pltpu.VMEM((count, 2, nz, rows, a), bf16),
        pltpu.VMEM((count, nz, nx, rows, b), bf16),
        pltpu.VMEM((count, nz, rows, columns), bf16),
        pltpu.VMEM((count, nz - 1, rows, columns), bf16),
        pltpu.VMEM((count, nz - 1, 2, nx, rows, c), bf16),
        pltpu.VMEM((count, 2, rows, c), bf16),
        pltpu.VMEM((count, rows, c), bf16),
        pltpu.SemaphoreType.DMA((count, 2 * nz + 5)),
        pltpu.SemaphoreType.DMA((count, 2 * nz + 5)),
    ]


def small_scratch(nz, shape):
    return [
        pltpu.VMEM((4, *shape), jnp.float32),
        pltpu.VMEM((2 + nz, *shape), jnp.float32),
        pltpu.SemaphoreType.DMA((2 + nz,)),
        pltpu.SemaphoreType.DMA((2 + nz,)),
    ]


def exact_gelu(pre):
    half = 0.5 + 0.5 * lax.erf(pre * (0.5**0.5))
    bell = jnp.exp(-0.5 * pre * pre) * ((0.5 / math.pi) ** 0.5)
    return pre * half, half + pre * bell


def rms_center(hidden):
    center = hidden - jnp.mean(hidden, axis=-1, keepdims=True)
    inverse = lax.rsqrt(jnp.mean(center * center, axis=-1, keepdims=True) + EPSILON)
    return center * inverse, inverse


def half_masks(width):
    left = (lax.broadcasted_iota(jnp.int32, (1, width), 1) < width // 2).astype(jnp.float32)
    return left.astype(jnp.bfloat16), (1.0 - left).astype(jnp.bfloat16)


def across(left, right):
    return lax.dot_general(left, right, (((1,), (1,)), ((), ())), preferred_element_type=jnp.float32)


def down(left, right):
    return lax.dot_general(left, right, (((0,), (0,)), ((), ())), preferred_element_type=jnp.float32)


def dot(left, right):
    return jnp.dot(left, right, preferred_element_type=jnp.float32)


def span(i, size):
    return pl.ds(pl.multiple_of(i * size, size), size)


class Gather:
    def __init__(self, at, parts, count, shards, g, send, recv):
        self.at, self.count, self.shards, self.g, self.send, self.recv = at, count, shards, g, send, recv
        self.parts = parts

    def copy(self, m, i, src, dst, to):
        return remote(src, dst, self.send.at[m, i], self.recv.at[m, i], to)

    def same(self, m, i, part, to):
        return self.copy(m, i, part, part, to)

    def stages(self, m):
        at, g, nz = self.at, self.g, self.at.nz
        a, b, c, ab = self.parts[m]
        y, core, z, x = at.y, at.core, at.z, at.x
        across_x, across_y, along_z = at.across_x, at.across_y, at.along_z
        first = [
            self.copy(m, k, self.shards.at[m, :, ab], g.at[m, y, core, z, x, :, ab], along_z[k])
            for k in range(nz - 1)
        ]
        first.append(self.copy(m, nz - 1, self.shards.at[m, :, c], g.at[m, y, core, z, x, :, c], across_y))
        second = [
            self.same(m, nz, g.at[m, y, core, :, x, :, a], across_y),
            self.same(m, nz + 1, g.at[m, y, core, :, x, :, b], across_x),
            self.same(m, nz + 2, g.at[m, :, core, z, x, :, c], across_x),
        ]
        third = [
            self.same(m, nz + 3, g.at[m, :, core, :, x, :, a], across_x),
            self.same(m, nz + 4, g.at[m, y, core, :, :, :, b], across_y),
        ]
        third += [self.same(m, nz + 5 + k, g.at[m, :, core, z, :, :, c], along_z[k]) for k in range(nz - 1)]
        return first, second, third, [self.same(m, 2 * nz + 4, g.at[m, :, core], at.sibling)]

    def step0(self, m):
        at = self.at
        for copy in self.stages(m)[0]:
            copy.start()
        self.g[m, at.y, at.core, at.z, at.x] = self.shards[m]

    def follow(self, stage, m):
        stages = self.stages(m)
        for copy in stages[stage - 1]:
            copy.wait_recv()
        for copy in stages[stage]:
            copy.start()

    def step1(self, m):
        self.follow(1, m)

    def step2(self, m):
        self.follow(2, m)

    def step3(self, m):
        self.follow(3, m)

    def arrive(self, m):
        self.stages(m)[3][0].wait_recv()

    def turn(self, m):
        for step, ahead in ((self.step3, 0), (self.step2, 2), (self.step1, 4), (self.step0, 6)):
            if 0 <= m + ahead < self.count:
                step(m + ahead)

    def drain(self, m):
        for stage in self.stages(m):
            for copy in stage:
                copy.wait_send()


def column_parts(width, shares):
    lanes = 128
    a, b = (share * lanes for share in shares)
    return pl.ds(0, a), pl.ds(a, b), pl.ds(a + b, width - a - b), pl.ds(0, a + b)


GATHER_SHARES = [(6, 1)] * 12
SCATTER_SHARES = [(6, 1)] * 12


def forward_kernel(
    nz, nx, parts, tokens, head_pair,
    x, attention_weights, expand, contract, small, pick, slots,
    g_out, probs_out, saved, act_out, slope_out, unit_out, final_out, own_out, across_out, small_full, inverse1, inverse2,
    g, shards, pool, hidden, landed, total, landing,
    send, recv, ssend, srecv, usend, urecv, across_send, across_recv, isem, gsem, vsem, asem, dsem, fsem, held_probs, ksem,
):
    f32, bf16 = jnp.float32, jnp.bfloat16
    count = g.shape[0]
    all_rows, width = x.shape
    rows = all_rows // tokens
    at = Partners(nz, nx)
    at.meet()
    gather = Gather(at, parts, count, shards, g, send, recv)
    sums = SmallSum(at, total, landing, ssend, srecv)
    groups = slots.shape[0] // rows
    members = pick.shape[0] // rows

    def fetch(i):
        return pltpu.make_async_copy(slots.at[i], pool.at[i // rows, pl.ds((i % rows) * tokens, tokens)], isem.at[i])

    shard = shards.shape[1]
    lane = lax.broadcasted_iota(jnp.int32, (1, width), 1)
    mine = lane // shard == lax.axis_index("dp") * (nz * nx) + lax.axis_index("fsdp")
    total[0] = jnp.where(mine, jnp.concatenate([small[...]] * (width // shard), axis=1), 0.0)
    sums.start()
    for m in range(4):
        shards[m] = attention_weights[m][...]
        gather.step0(m)
    for i in range(slots.shape[0]):
        fetch(i).start()
    for i in range(slots.shape[0]):
        fetch(i).wait()

    high, part = 16, width // 2

    def sum_slots(i, carry):
        cols = span(lax.rem(i, 2), part)
        base = i // 2 * high
        held = [
            pool[s // rows, pl.ds(pl.multiple_of(base + (s % rows) * tokens, high), high), cols].astype(f32)
            for s in range(slots.shape[0])
        ]
        for t in range(pick.shape[0]):
            picked = pick[t, 0] * held[0]
            for s in range(1, slots.shape[0]):
                picked = picked + pick[t, s] * held[s]
            spot = pl.ds(pl.multiple_of(base + (t % rows) * tokens, high), high)
            pool[groups + t // rows, spot, cols] = picked.astype(bf16)
        return carry

    def up_sibling(y):
        src = pool.at[groups + y * 2 + 1 - at.core]
        return remote(src, landed.at[y], usend.at[y], urecv.at[y], at.sibling)

    pieces = across_send.shape[0]

    def up_across(i):
        piece = pl.ds(i * (all_rows // pieces), all_rows // pieces)
        return remote(
            landed.at[1 - at.y, piece], across_out.at[piece], across_send.at[i], across_recv.at[i], at.across_y
        )

    def turn(m):
        gather.turn(m)
        if m < pieces:
            up_across(m).start()

    up_own = pltpu.make_async_copy(landed.at[at.y], own_out, isem.at[slots.shape[0]])

    steps = tokens // high * 2
    lax.fori_loop(0, steps // 4, sum_slots, 0)
    gather.step1(0)
    sums.step(0)
    blocks = (count - 4) // 2
    for j in range(blocks):
        shards[5 + 2 * j] = contract[j * shard : (j + 1) * shard, :]
    lanes = 128
    per = lanes // shard
    for q in range(width // lanes):
        natural = expand[:, q * lanes * blocks : (q + 1) * lanes * blocks].astype(f32)
        for j in range(blocks):
            found = [
                natural[:, t * blocks * shard + j * shard : t * blocks * shard + (j + 1) * shard] for t in range(per)
            ]
            shards[4 + 2 * j, :, q * lanes : (q + 1) * lanes] = jnp.concatenate(found, axis=1).astype(bf16)
    gather.step0(4)
    sums.step(1)
    lax.fori_loop(steps // 4, steps // 2, sum_slots, 0)
    gather.step1(1)
    gather.step2(0)
    lax.fori_loop(steps // 2, steps, sum_slots, 0)
    for y in range(2):
        up_sibling(y).start()
    sums.step(2)
    gather.step0(5)
    gather.step1(2)
    gather.step2(1)
    gather.step1(3)
    for y in range(2):
        up_sibling(y).wait_recv()

    def chip_sum(i, carry):
        y, spot = i // (all_rows // 32), span(lax.rem(i, all_rows // 32), 32)
        landed[y, spot] = added(landed[y, spot], pool[groups + y * 2 + at.core, spot]).astype(bf16)
        return carry

    lax.fori_loop(0, 2 * all_rows // 32, chip_sum, 0)
    up_own.start()
    for y in range(2):
        up_sibling(y).wait_send()
    sums.finish(small_full)
    turn(0)

    def keep(m):
        return pltpu.make_async_copy(g.at[m], g_out.at[m], gsem.at[m])

    def arrive(m):
        gather.arrive(m)
        keep(m).start()

    def tile(m, cols):
        return g[m, :, :, :, :, :, cols].reshape(width, cols.size)

    def bias(i, cols):
        return small_full[pl.ds(i, 1), cols]

    def tiles(size, body):
        def one(i, carry):
            body(span(i // rows, size), span(lax.rem(i, rows), tokens))
            return carry

        lax.fori_loop(0, width // size * rows, one, 0)

    def save(i):
        return pltpu.make_async_copy(pool.at[i], saved.at[i], vsem.at[i])

    def project(m):
        bias_row = (0, None, 1)[m]

        def body(cols, spot):
            y = dot(x[spot], tile(m, cols))
            if bias_row is not None:
                y = y + bias(bias_row, cols)
            pool[m, spot, cols] = y.astype(bf16)

        arrive(m)
        tiles(512, body)
        save(m).start()

    project(0)
    turn(1)
    project(1)
    turn(2)
    project(2)

    pairs = width // head_pair
    masks = half_masks(head_pair)
    scale = (head_pair // 2) ** (-0.5)

    def keep_probs(i):
        slot = lax.rem(i, 2)
        return pltpu.make_async_copy(held_probs.at[slot], probs_out.at[i], ksem.at[slot])

    def attend(i, carry):
        spot, cols = span(i // pairs, tokens), span(lax.rem(i, pairs), head_pair)
        query, keys, values = pool[0, spot, cols], pool[1, spot, cols], pool[2, spot, cols]
        query = query * jnp.asarray(scale, bf16)
        pl.when(i >= 2)(lambda: keep_probs(i - 2).wait())
        out = None
        for h, mask in enumerate(masks):
            scores = across(keys * mask, query)
            probs = jnp.exp(scores - jnp.max(scores, axis=0, keepdims=True))
            probs = (probs * (1.0 / jnp.sum(probs, axis=0, keepdims=True))).astype(bf16)
            held_probs[lax.rem(i, 2), h] = probs
            term = down(probs, values * mask)
            out = term if out is None else out + term
        keep_probs(i).start()
        pool[3, spot, cols] = out.astype(bf16)
        pl.when(i == rows * pairs // 4)(partial(turn, 3))
        pl.when(i == rows * pairs * 3 // 4)(partial(turn, 4))
        return carry

    lax.fori_loop(0, rows * pairs, attend, 0)
    save(3).start()
    for i in range(2):
        keep_probs(rows * pairs - 2 + i).wait()

    def mix(cols, spot):
        hidden[spot, cols] = dot(pool[3, spot], tile(3, cols)) + x[spot, cols].astype(f32) + bias(2, cols)

    arrive(3)
    tiles(512, mix)
    turn(5)

    def unit(i):
        return pltpu.make_async_copy(pool.at[6], unit_out.at[i], fsem.at[i])

    def norm1(i, carry):
        spot = span(i, 64)
        normed, inverse = rms_center(hidden[spot])
        result = normed * small_full[3:4, :] + small_full[4:5, :]
        hidden[spot] = result
        pool[4, spot] = result.astype(bf16)
        pool[6, spot] = normed.astype(bf16)
        inverse1[spot] = inverse
        return carry

    lax.fori_loop(0, all_rows // 64, norm1, 0)
    save(4).start()
    unit(0).start()

    def save_act(j):
        return pltpu.make_async_copy(pool.at[5], act_out.at[j], asem)

    def save_slope(j):
        return pltpu.make_async_copy(pool.at[6], slope_out.at[j], dsem)

    unit(0).wait()

    def feed(j):
        m = 4 + 2 * j
        if m > 5:
            turn(m)
        arrive(m)
        if j >= 1:
            save_act(j - 1).wait()
            save_slope(j - 1).wait()

        def up(cols, spot):
            value, slope = exact_gelu(dot(pool[4, spot], tile(m, cols)) + bias(8 + j, cols))
            pool[5, spot, cols] = value.astype(bf16)
            pool[6, spot, cols] = slope.astype(bf16)

        tiles(256, up)
        save_act(j).start()
        save_slope(j).start()
        if m + 1 > 5:
            turn(m + 1)
        arrive(m + 1)

        def back(cols, spot):
            hidden[spot, cols] = hidden[spot, cols] + dot(pool[5, spot], tile(m + 1, cols))

        tiles(512, back)

    for j in range(blocks):
        feed(j)
    save_act(blocks - 1).wait()
    save_slope(blocks - 1).wait()

    def norm2(i, carry):
        spot = span(i, 64)
        normed, inverse = rms_center(hidden[spot] + small_full[5:6, :])
        pool[5, spot] = (normed * small_full[6:7, :] + small_full[7:8, :]).astype(bf16)
        pool[6, spot] = normed.astype(bf16)
        inverse2[spot] = inverse
        return carry

    lax.fori_loop(0, all_rows // 64, norm2, 0)
    finish = pltpu.make_async_copy(pool.at[5], final_out, fsem.at[2])
    finish.start()
    unit(1).start()

    for m in range(count):
        gather.drain(m)
        keep(m).wait()
    for i in range(5):
        save(i).wait()
    up_own.wait()
    for i in range(pieces):
        up_across(i).wait()
    finish.wait()
    unit(1).wait()


def forward(x, attention_weights, expand, contract, small, pick, slots, nz, nx, tokens):
    f32, bf16 = jnp.float32, jnp.bfloat16
    shard_rows, width = attention_weights[0].shape
    count = 4 + 2 * contract.shape[0] // shard_rows
    small_shape = (small.shape[0], width)
    all_rows = x.shape[0]
    group_members = pick.shape[0] * tokens // all_rows
    assert group_members == 4 and slots.shape[0] * tokens == 2 * all_rows
    vmem, anywhere = pl.BlockSpec(memory_space=pltpu.VMEM), pl.BlockSpec(memory_space=pl.ANY)
    acts = (all_rows, width)
    rows = all_rows // tokens
    blocks = (count - 4) // 2
    dma = pltpu.SemaphoreType.DMA
    full = (count, 2, 2, nz, nx, shard_rows, width)
    out = jax.ShapeDtypeStruct
    return pl.pallas_call(
        partial(forward_kernel, nz, nx, [column_parts(width, s) for s in GATHER_SHARES], tokens, 2 * width // HEADS),
        out_shape=[
            out(full, bf16),
            out((rows * HEADS // 2, 2, tokens, tokens), bf16),
            out((5, *acts), bf16),
            out((blocks, *acts), bf16),
            out((blocks, *acts), bf16),
            out((2, *acts), bf16),
            out(acts, bf16),
            out(acts, bf16),
            out(acts, bf16),
            out(small_shape, f32),
            out((all_rows, 1), f32),
            out((all_rows, 1), f32),
        ],
        in_specs=[vmem, [vmem] * 4, vmem, vmem, vmem, pl.BlockSpec(memory_space=pltpu.SMEM), anywhere],
        out_specs=[anywhere] * 9 + [vmem] * 3,
        scratch_shapes=[
            pltpu.VMEM(full, bf16),
            pltpu.VMEM((count, shard_rows, width), bf16),
            pltpu.VMEM((7, *acts), bf16),
            pltpu.VMEM(acts, f32),
            pltpu.VMEM((2, *acts), bf16),
            *small_scratch(nz, small_shape)[:2],
            dma((count, 2 * nz + 5)),
            dma((count, 2 * nz + 5)),
            dma((2 + nz,)),
            dma((2 + nz,)),
            dma((2,)),
            dma((2,)),
            dma((count,)),
            dma((count,)),
            dma((slots.shape[0] + 1,)),
            dma((count,)),
            dma((5,)),
            dma,
            dma,
            dma((3,)),
            pltpu.VMEM((2, 2, tokens, tokens), bf16),
            dma((2,)),
        ],
        compiler_params=pltpu.CompilerParams(
            collective_id=1, has_side_effects=True, vmem_limit_bytes=60 * 2**20
        ),
    )(x, attention_weights, expand, contract, small, pick, slots)


def backward_kernel(
    nz, nx, parts, tokens, head_pair,
    x, own_up, across_up, final, unit, inverse1, inverse2, small_full, act, slope, saved, g, probs,
    out, small_out, input_out, table,
    rc, r3a, r3b, r2, rz, rcz, rcx, rcy, send, recv, total, landing, ssend, srecv,
    term, weight, pool, hidden, wsem, psem, hsem, tsend, trecv, across_send, across_recv, tsem, held_probs, ksem,
):
    f32, bf16 = jnp.float32, jnp.bfloat16
    count = out.shape[0]
    all_rows, width = x.shape
    rows = all_rows // tokens
    at = Partners(nz, nx)
    at.meet()
    scatter = Scatter(at, parts, rc, r3a, r3b, r2, rz, rcz, rcx, rcy, send, recv)
    sums = SmallSum(at, total, landing, ssend, srecv)

    here = pltpu.make_async_copy(final, table.at[at.y, at.core], tsem)
    to_sibling = remote(final, table.at[at.y, at.core], tsend.at[0], trecv.at[0], at.sibling)
    pieces = across_send.shape[0]

    def to_across(i):
        piece = pl.ds(i * (all_rows // pieces), all_rows // pieces)
        dst = table.at[at.y, at.core, piece]
        return remote(final.at[piece], dst, across_send.at[i], across_recv.at[i], at.across_y)

    passed = table.at[1 - at.y, at.core]
    pass_on = remote(passed, passed, tsend.at[1], trecv.at[1], at.sibling)

    def load(src, entry, i):
        return pltpu.make_async_copy(src, pool.at[entry], psem.at[i])

    def fetch(m, slot, i):
        return pltpu.make_async_copy(g.at[m], weight.at[slot], wsem.at[i])

    blocks = act.shape[0]
    up_block, down_block = (lambda j: 4 + 2 * j), (lambda j: 5 + 2 * j)
    unit2, own_load, across_load = load(unit.at[1], 1, 0), load(own_up, 2, 1), load(across_up, 3, 2)
    act_entry = [5, 2, 3, 5]
    act_load = [load(act.at[j], act_entry[j], 3 + j) for j in range(blocks)]
    slope_entry = [4, 2, 3, 4]
    slope_load = [load(slope.at[j], slope_entry[j], 7 + j) for j in range(blocks)]
    low_load, unit1, mixed_load = load(saved.at[4], 6, 11), load(unit.at[0], 5, 12), load(saved.at[3], 4, 13)
    query_load, key_load, value_load = (load(saved.at[i], (2, 3, 6)[i], 14 + i) for i in range(3))
    x_load = load(x, 4, 17)
    down_fetch = [fetch(down_block(j), 0, 2 * j) for j in range(blocks)]
    up_fetch = [fetch(up_block(j), 1, 2 * j + 1) for j in range(blocks)]
    last = 2 * blocks
    output_fetch, query_fetch, key_fetch, value_fetch = (
        fetch(m, slot, last + i) for i, (m, slot) in enumerate(((3, 0), (0, 1), (1, 0), (2, 1)))
    )
    for copy in (unit2, own_load, across_load, act_load[0], down_fetch[0], up_fetch[0], slope_load[0], low_load):
        copy.start()
    to_across(0).start()
    to_sibling.start()
    here.start()
    total[0] = jnp.zeros_like(total[0])

    def folded(block):
        return jnp.sum(block.reshape(-1, 8, block.shape[-1]), axis=0)

    def norm_back(gain_row, shift_row, low_row, inverse, incoming, normed_entry, low_entry):
        def body(i, carry):
            spot = span(i, 64)
            grad, normed = incoming(spot), pool[normed_entry, spot].astype(f32)
            scaled = grad * small_full[gain_row : gain_row + 1, :]
            inner = (
                scaled
                - jnp.mean(scaled, axis=-1, keepdims=True)
                - normed * jnp.mean(scaled * normed, axis=-1, keepdims=True)
            )
            result = inner * inverse[spot]
            low = result.astype(bf16)
            hidden[spot] = result
            pool[low_entry, spot] = low
            return tuple(c + folded(b) for c, b in zip(carry, (grad * normed, grad, low.astype(f32))))

        zero = jnp.zeros((8, width), f32)
        found = lax.fori_loop(0, all_rows // 64, body, (zero, zero, zero))
        for row, value in zip((gain_row, shift_row, low_row), found):
            total[0, row : row + 1, :] = jnp.sum(value, axis=0, keepdims=True)

    def tiles(size, body):
        def one(i, carry):
            body(i // rows, span(i // rows, size), span(lax.rem(i, rows), tokens))
            return carry

        lax.fori_loop(0, width // size * rows, one, 0)

    def turned(slot, y):
        return weight[slot, y].reshape(width // 2, width)

    def own_half(slot):
        return lambda y, z: term[slot, y, at.core, z]

    def produce(m, left, right, after=True):
        slot = m % 2

        def half(core):
            def body(i, carry):
                y, cols = i // 2, span(lax.rem(i, 2), width // 2)
                picked = span(y * 2 + core, width // 4)
                value = down(pool[left, :, picked], pool[right, :, cols]).astype(bf16)
                term[slot, y, core, :, :, :, cols] = value.reshape(nz, nx, -1, width // 2)
                return carry

            lax.fori_loop(0, 4, body, 0)

        half(1 - at.core)
        scatter.start(m, term.at[slot, :, 1 - at.core])
        if m > 0 and after:
            scatter.step1(m - 1, own_half(1 - slot))
        half(at.core)

    def turn(m):
        for step, behind in ((scatter.step4, 4), (scatter.step3, 2), (scatter.step2, 0)):
            if 0 <= m - behind < count:
                step(*((m - behind, out) if behind == 4 else (m - behind,)))
        if 0 < m + 1 < pieces:
            to_across(m + 1).start()

    for copy in (unit2, own_load, across_load):
        copy.wait()
    norm_back(6, 7, 5, inverse2, lambda spot: added(pool[2, spot], pool[3, spot]), 1, 0)

    act_load[1].start()
    act_load[2].start()
    for j in range(blocks):
        act_load[j].wait()
        produce(j, act_entry[j], 0)
        if j == 0:
            act_load[3].start()
        elif j < 3:
            slope_load[j].start()
        else:
            unit1.start()
    turn(0)

    low_load.wait()
    for j in range(blocks):
        down_fetch[j].wait()
        slope_load[j].wait()

        def pre_back(n, cols, spot, j=j):
            value = across(pool[0, spot], turned(0, n)) * pool[slope_entry[j], spot, cols].astype(f32)
            value = value.astype(bf16)
            pool[1, spot, cols] = value
            row = pl.ds(8 + j, 1)
            total[0, row, cols] = total[0, row, cols] + jnp.sum(value.astype(f32), axis=0, keepdims=True)

        tiles(width // 2, pre_back)
        if j + 1 < blocks:
            down_fetch[j + 1].start()
        else:
            output_fetch.start()
        (lambda: slope_load[3].start(), query_load.start, key_load.start, mixed_load.start)[j]()
        produce(blocks + j, 6, 1)
        up_fetch[j].wait()

        def hidden_back(n, cols, spot):
            hidden[spot, cols] = hidden[spot, cols] + across(pool[1, spot], turned(1, n))

        tiles(width // 2, hidden_back)
        if j + 1 < blocks:
            up_fetch[j + 1].start()
        else:
            query_fetch.start()
        if j == blocks - 1:
            value_load.start()
        turn(1 + j)

    unit1.wait()
    norm_back(3, 4, 2, inverse1, lambda spot: hidden[spot], 5, 0)
    mixed_load.wait()
    produce(2 * blocks, 4, 0)
    x_load.start()
    output_fetch.wait()

    def mixed_back(n, cols, spot):
        pool[1, spot, cols] = across(pool[0, spot], turned(0, n)).astype(bf16)

    tiles(width // 2, mixed_back)
    key_fetch.start()
    for copy in (query_load, key_load, value_load):
        copy.wait()
    turn(5)
    scatter.step1(2 * blocks, own_half((2 * blocks) % 2))

    pairs = width // head_pair
    masks = half_masks(head_pair)
    scale = (head_pair // 2) ** (-0.5)

    def fetch_probs(i):
        slot = lax.rem(i, 2)
        return pltpu.make_async_copy(probs.at[i], held_probs.at[slot], ksem.at[slot])

    fetch_probs(0).start()

    def attend(i, carry):
        pl.when(i + 1 < rows * pairs)(lambda: fetch_probs(i + 1).start())
        fetch_probs(i).wait()
        spot, cols = span(i // pairs, tokens), span(lax.rem(i, pairs), head_pair)
        query, keys, values, mixed_grad = (pool[e, spot, cols] for e in (2, 3, 6, 1))
        query_grad = key_grad = value_grad = None
        for h, mask in enumerate(masks):
            own_keys = keys * (mask * jnp.asarray(scale, bf16))
            low = held_probs[lax.rem(i, 2), h]
            prob = low.astype(f32)
            prob_grad = across(values * mask, mixed_grad)
            weighed = prob * prob_grad
            score_grad = (weighed - prob * jnp.sum(weighed, axis=0, keepdims=True)).astype(bf16)
            terms = (
                down(score_grad, own_keys),
                dot(score_grad, query * mask),
                dot(low, mixed_grad * mask),
            )
            if query_grad is None:
                query_grad, key_grad, value_grad = terms
            else:
                query_grad, key_grad, value_grad = query_grad + terms[0], key_grad + terms[1], value_grad + terms[2]
        query_grad, value_grad = query_grad.astype(bf16), value_grad.astype(bf16)
        pool[2, spot, cols] = query_grad
        pool[3, spot, cols] = (key_grad * scale).astype(bf16)
        pool[6, spot, cols] = value_grad
        for row, value in ((0, query_grad), (1, value_grad)):
            found = jnp.sum(value.astype(f32), axis=0, keepdims=True)
            total[0, row : row + 1, cols] = total[0, row : row + 1, cols] + found
        for third in range(3):
            pl.when(i == (2 * third + 1) * rows * pairs // 6)(partial(turn, 6 + third))
        return carry

    lax.fori_loop(0, rows * pairs, attend, 0)
    sums.start()

    x_load.wait()
    for i, entry in enumerate((6, 2, 3)):
        produce(2 * blocks + 1 + i, 4, entry, i > 0)
        sums.step(i)
    scatter.step1(count - 1, own_half((count - 1) % 2))
    turn(9)

    def input_back(slot, entry, fetched):
        def body(n, cols, spot):
            hidden[spot, cols] = hidden[spot, cols] + across(pool[entry, spot], turned(slot, n))

        fetched.wait()
        tiles(width // 2, body)

    input_back(1, 2, query_fetch)
    value_fetch.start()
    turn(10)
    input_back(0, 3, key_fetch)
    for i in range(pieces):
        to_across(i).wait_recv()
    pass_on.start()
    turn(11)
    input_back(1, 6, value_fetch)
    done = pltpu.make_async_copy(hidden, input_out, hsem)
    done.start()
    turn(12)
    turn(13)
    sums.finish(small_out)
    turn(14)
    turn(15)
    done.wait()

    for m in range(count):
        scatter.drain(m)
    here.wait()
    to_sibling.wait()
    for i in range(pieces):
        to_across(i).wait_send()
    pass_on.wait()


def backward(
    x, own_up, across_up, final, unit, inverse1, inverse2, small_full, act, slope, saved, g, probs, nz, nx, tokens
):
    f32, bf16 = jnp.float32, jnp.bfloat16
    count, _, _, _, _, shard_rows, width = g.shape
    acts = x.shape
    parts = [column_parts(width, s) for s in SCATTER_SHARES]
    vmem, anywhere = pl.BlockSpec(memory_space=pltpu.VMEM), pl.BlockSpec(memory_space=pl.ANY)
    dma = pltpu.SemaphoreType.DMA
    out = jax.ShapeDtypeStruct
    block = (2, 2, nz, nx, shard_rows, width)
    return pl.pallas_call(
        partial(backward_kernel, nz, nx, parts, tokens, 2 * width // HEADS),
        out_shape=[
            out((count, shard_rows, width), f32),
            out(small_full.shape, f32),
            out(acts, f32),
            out((2, 2, *acts), bf16),
        ],
        in_specs=[anywhere] * 5 + [vmem] * 3 + [anywhere] * 5,
        out_specs=[vmem, vmem, anywhere, anywhere],
        scratch_shapes=[
            *scatter_scratch(count, nz, nx, shard_rows, width, parts),
            *small_scratch(nz, small_full.shape),
            pltpu.VMEM((2, *block), bf16),
            pltpu.VMEM((2, *block), bf16),
            pltpu.VMEM((7, *acts), bf16),
            pltpu.VMEM(acts, f32),
            dma((count,)),
            dma((18,)),
            dma,
            dma((2,)),
            dma((2,)),
            dma((count,)),
            dma((count,)),
            dma,
            pltpu.VMEM((2, 2, tokens, tokens), bf16),
            dma((2,)),
        ],
        compiler_params=pltpu.CompilerParams(
            collective_id=2, has_side_effects=True, vmem_limit_bytes=60 * 2**20
        ),
    )(x, own_up, across_up, final, unit, inverse1, inverse2, small_full, act, slope, saved, g, probs)


def finish_kernel(
    slot_row, live_count, me, table, full, sums, small_sums,
    slot_acts, input_grad, query, keys, values, output, up, contract, *small,
):
    s = pl.program_id(0)
    slot_acts[...] = table[...]
    input_grad[...] = jnp.where(s // 2 < live_count[0], full[...], 0.0)

    @pl.when(s == 0)
    def _():
        blocks = (sums.shape[0] - 4) // 2
        shard, width = query.shape
        for j in range(blocks):
            contract[j * shard : (j + 1) * shard, :] = sums[j]
        lanes = 128
        per = lanes // shard
        for q in range(width // lanes):
            part = [sums[blocks + j, :, q * lanes : (q + 1) * lanes] for j in range(blocks)]
            for t in range(per):
                found = jnp.concatenate([p[:, t * shard : (t + 1) * shard] for p in part], axis=1)
                at = (q * per + t) * blocks * shard
                up[:, at : at + blocks * shard] = found
        for i, ref in enumerate((output, values, query, keys)):
            ref[...] = sums[2 * blocks + i]
        own = pltpu.roll(small_sums[...], width - me[0] * shard, 1)
        for i in range(8):
            small[i][...] = own[i, :shard]
        small[8][...] = jnp.concatenate([own[8 + j : 9 + j, :shard] for j in range(blocks)], axis=1)[0]


def finish(slot_row, live_count, table, full, sums, small_sums):
    f32 = jnp.float32
    members, tokens, width = table.shape
    slots, rows = slot_row.shape[0], full.shape[0]
    assert slots == 2 * rows
    count, shard, _ = sums.shape
    blocks = (count - 4) // 2
    me = lax.axis_index(("dp", "fsdp")).astype(jnp.int32).reshape(1)
    block, half = (1, tokens, width), (1, tokens // 2, width)

    def fixed(shape):
        return pl.BlockSpec(shape, lambda s, *_: (0,) * len(shape))

    fixed_outs = [(shard, width)] * 4 + [(shard, blocks * width), (blocks * shard, width)]
    fixed_outs += [(shard,)] * 8 + [(blocks * shard,)]
    row_half = pl.BlockSpec(half, lambda s, *_: (s // 2, lax.rem(s, 2), 0))
    out = jax.ShapeDtypeStruct
    return pl.pallas_call(
        finish_kernel,
        out_shape=[
            out((slots, tokens, width), table.dtype),
            out(full.shape, f32),
            *(out(shape, f32) for shape in fixed_outs),
        ],
        grid_spec=pltpu.PrefetchScalarGridSpec(
            num_scalar_prefetch=3,
            grid=(slots,),
            in_specs=[
                pl.BlockSpec(block, lambda s, slot_row, *_: (jnp.clip(slot_row[s], 0, members - 1), 0, 0)),
                row_half,
                fixed(sums.shape),
                fixed(small_sums.shape),
            ],
            out_specs=[
                pl.BlockSpec(block, lambda s, *_: (s, 0, 0)),
                row_half,
                *(fixed(shape) for shape in fixed_outs),
            ],
        ),
        compiler_params=pltpu.CompilerParams(vmem_limit_bytes=60 * 2**20),
    )(slot_row, live_count, me, table, full, sums, small_sums)


def prepare(slot_row, small_parameters, up_bias, row_count, dp_size):
    shard = small_parameters[0].shape[0]
    rows = [v.reshape(-1, shard) for v in (*small_parameters, up_bias)]
    rows = jnp.concatenate(rows, axis=0).astype(jnp.float32)
    small = jnp.pad(rows, ((0, 16 - rows.shape[0]), (0, 0)))
    wanted = lax.broadcasted_iota(jnp.int32, (row_count * dp_size, slot_row.shape[0]), 0)
    return small, (wanted == slot_row[None, :]).astype(jnp.float32)


def on_device_kernels(
    rows_in,
    slot_row,
    live_count,
    slot_activation_gradient,
    query_weight,
    key_weight,
    value_weight,
    output_weight,
    query_bias,
    value_bias,
    output_bias,
    attn_gain,
    attn_shift,
    expand_weight,
    up_bias,
    down_weight,
    down_bias,
    ffn_gain,
    ffn_shift,
):
    row_count, token_count, width = rows_in.shape
    nx = 2
    nz = lax.axis_size("fsdp") // nx
    small, pick = prepare(
        slot_row,
        (query_bias, value_bias, output_bias, attn_gain, attn_shift, down_bias, ffn_gain, ffn_shift),
        up_bias,
        row_count,
        lax.axis_size("dp"),
    )
    x = rows_in.reshape(-1, width)
    g, probs, saved, act, slope, unit, final, own_up, across_up, small_full, inverse1, inverse2 = forward(
        x,
        [query_weight, key_weight, value_weight, output_weight],
        expand_weight,
        down_weight,
        small,
        pick,
        slot_activation_gradient,
        nz,
        nx,
        token_count,
    )
    sums, small_sums, input_full, table = backward(
        x,
        own_up,
        across_up,
        final,
        unit,
        inverse1,
        inverse2,
        small_full,
        act,
        slope,
        saved,
        g,
        probs,
        nz,
        nx,
        token_count,
    )
    slot_acts, input_grad, query, keys, values, output, up, contract, *small_grads = finish(
        slot_row,
        live_count,
        table.reshape(-1, token_count, width),
        input_full.reshape(rows_in.shape),
        sums,
        small_sums,
    )
    return (
        slot_acts,
        input_grad,
        query,
        keys,
        values,
        output,
        *small_grads[:5],
        up,
        small_grads[8],
        contract,
        *small_grads[5:8],
    )


def norm_forward(hidden, gain, shift):
    center = hidden - jnp.mean(hidden, axis=-1, keepdims=True)
    inverse = lax.rsqrt(jnp.mean(center * center, axis=-1, keepdims=True) + EPSILON)
    normed = center * inverse
    return (normed * gain + shift, normed, inverse)


def norm_backward(incoming, gain, normed, inverse):
    scaled = incoming * gain
    inner = (
        scaled
        - jnp.mean(scaled, axis=-1, keepdims=True)
        - normed * jnp.mean(scaled * normed, axis=-1, keepdims=True)
    )
    return (
        inner * inverse,
        jnp.sum(incoming * normed, axis=(0, 1)),
        jnp.sum(incoming, axis=(0, 1)),
    )


def apply_weight(acts, weight):
    return jnp.einsum("rsd,de->rse", acts, weight, preferred_element_type=jnp.float32)


def apply_back(grads, weight):
    return jnp.einsum("rse,de->rsd", grads, weight, preferred_element_type=jnp.float32)


def weight_term(acts, grads):
    return jnp.einsum("rsd,rse->de", acts, grads, preferred_element_type=jnp.float32)


def bias_term(grads):
    return jnp.sum(grads, axis=(0, 1), dtype=jnp.float32)


def on_device_plain(
    rows_in,
    slot_row,
    live_count,
    slot_activation_gradient,
    query_weight,
    key_weight,
    value_weight,
    output_weight,
    query_bias,
    value_bias,
    output_bias,
    attn_gain,
    attn_shift,
    expand_weight,
    up_bias,
    down_weight,
    down_bias,
    ffn_gain,
    ffn_shift,
):
    row_count, token_count, feature_count = rows_in.shape
    head_size = feature_count // HEADS
    score_scale = head_size ** (-0.5)
    split_shape = (row_count, token_count, HEADS, head_size)
    wanted = lax.broadcasted_iota(
        jnp.int32, (row_count * lax.axis_size("dp"), slot_row.shape[0]), 0
    )
    one_hot_matrix = (wanted == slot_row[None, :]).astype(jnp.bfloat16)
    upstream = lax.psum_scatter(
        jnp.einsum(
            "az,zfy->afy",
            one_hot_matrix,
            slot_activation_gradient,
            preferred_element_type=jnp.float32,
        ).astype(jnp.bfloat16),
        "dp",
        scatter_dimension=0,
        tiled=True,
    ).astype(jnp.float32)
    smalls = (query_bias, value_bias, output_bias, attn_gain, attn_shift, down_bias, ffn_gain, ffn_shift)
    small_rows = query_bias.shape[0]
    packed = jnp.concatenate([v.reshape(-1, small_rows) for v in (*smalls, up_bias)], axis=0)
    packed_full = lax.all_gather(packed, ("dp", "fsdp"), axis=0)
    (
        qbias_full,
        vbias_full,
        obias_full,
        gain1_full,
        shift1_full,
        downbias_full,
        gain2_full,
        shift2_full,
    ) = (packed_full[:, i].reshape(-1) for i in range(8))
    upbias_full = packed_full[:, 8:].reshape(-1)
    query_full, key_full, value_full, output_full, up_full, down_full = (
        lax.all_gather(weight, ("dp", "fsdp"), axis=0, tiled=True)
        for weight in (query_weight, key_weight, value_weight, output_weight, expand_weight, down_weight)
    )
    inputs = rows_in.astype(jnp.float32)
    query = (apply_weight(rows_in, query_full) + qbias_full.astype(jnp.float32)).astype(
        jnp.bfloat16
    )
    keys = apply_weight(rows_in, key_full).astype(jnp.bfloat16)
    values = (apply_weight(rows_in, value_full) + vbias_full.astype(jnp.float32)).astype(
        jnp.bfloat16
    )
    query_heads = query.reshape(split_shape)
    key_heads = keys.reshape(split_shape)
    value_heads = values.reshape(split_shape)
    scores = (
        jnp.einsum("rqhd,rkhd->rhqk", query_heads, key_heads, preferred_element_type=jnp.float32)
        * score_scale
    )
    row_top = jnp.max(scores, axis=-1, keepdims=True)
    expo = jnp.exp(scores - row_top)
    row_sum = jnp.sum(expo, axis=-1, keepdims=True)
    logsum = row_top + jnp.log(row_sum)
    probs_low = (expo / row_sum).astype(jnp.bfloat16)
    mixed = jnp.einsum(
        "rhqk,rkhd->rqhd", probs_low, value_heads, preferred_element_type=jnp.float32
    )
    mixed = mixed.reshape(row_count, token_count, feature_count).astype(jnp.bfloat16)
    gain1 = gain1_full.astype(jnp.float32)
    resid1 = inputs + apply_weight(mixed, output_full) + obias_full.astype(jnp.float32)
    normed1_out, normed1, inverse1 = norm_forward(resid1, gain1, shift1_full.astype(jnp.float32))
    normed1_low = normed1_out.astype(jnp.bfloat16)
    pre_act = apply_weight(normed1_low, up_full) + upbias_full.astype(jnp.float32)
    act_low = jax.nn.gelu(pre_act, approximate=False).astype(jnp.bfloat16)
    gain2 = gain2_full.astype(jnp.float32)
    resid2 = normed1_out + apply_weight(act_low, down_full) + downbias_full.astype(jnp.float32)
    final, second_normed, inverse2 = norm_forward(resid2, gain2, shift2_full.astype(jnp.float32))
    final_low = final.astype(jnp.bfloat16)
    shard_rows = lax.all_gather(final_low, "dp", axis=0, tiled=True)
    span_rows = shard_rows.shape[0]
    inside = (slot_row >= 0) & (slot_row < span_rows)
    picked = jnp.take(shard_rows, jnp.clip(slot_row, 0, span_rows - 1), axis=0)
    slot_acts = jnp.where(
        inside[:, None, None], picked, jnp.zeros(slot_activation_gradient.shape, jnp.bfloat16)
    )
    gain1 = gain1_full.astype(jnp.float32)
    gain2 = gain2_full.astype(jnp.float32)
    grad2, gain2_grad, shift2_grad = norm_backward(upstream, gain2, second_normed, inverse2)
    ffn_low = grad2.astype(jnp.bfloat16)
    down_grad = weight_term(act_low, ffn_low)
    down_bias_grad = bias_term(ffn_low)
    act_grad = apply_back(ffn_low, down_full)
    gelu_value, gelu_back = jax.vjp(partial(jax.nn.gelu, approximate=False), pre_act)
    pre_grad = gelu_back(act_grad)[0].astype(jnp.bfloat16)
    up_grad = weight_term(normed1_low, pre_grad)
    up_bias_grad = bias_term(pre_grad)
    normed1_grad = grad2 + apply_back(pre_grad, up_full)
    grad1, gain1_grad, shift1_grad = norm_backward(normed1_grad, gain1, normed1, inverse1)
    attn_low = grad1.astype(jnp.bfloat16)
    output_grad = weight_term(mixed, attn_low)
    output_bias_grad = bias_term(attn_low)
    mixed_grad = apply_back(attn_low, output_full).astype(jnp.bfloat16).reshape(split_shape)
    scores_again = (
        jnp.einsum("rqhd,rkhd->rhqk", query_heads, key_heads, preferred_element_type=jnp.float32)
        * score_scale
    )
    probs = jnp.exp(scores_again - logsum)
    probs_again = probs.astype(jnp.bfloat16)
    value_grad = jnp.einsum(
        "rhqk,rqhd->rkhd", probs_again, mixed_grad, preferred_element_type=jnp.float32
    )
    value_grad = value_grad.astype(jnp.bfloat16).reshape(row_count, token_count, feature_count)
    prob_grad = jnp.einsum(
        "rqhd,rkhd->rhqk", mixed_grad, value_heads, preferred_element_type=jnp.float32
    )
    score_grad = (probs * (prob_grad - jnp.sum(probs * prob_grad, axis=-1, keepdims=True))).astype(
        jnp.bfloat16
    )
    query_grad = (
        jnp.einsum("rhqk,rkhd->rqhd", score_grad, key_heads, preferred_element_type=jnp.float32)
        * score_scale
    )
    query_grad = query_grad.astype(jnp.bfloat16).reshape(row_count, token_count, feature_count)
    key_grad = (
        jnp.einsum("rhqk,rqhd->rkhd", score_grad, query_heads, preferred_element_type=jnp.float32)
        * score_scale
    )
    key_grad = key_grad.astype(jnp.bfloat16).reshape(row_count, token_count, feature_count)
    query_wgrad = weight_term(rows_in, query_grad)
    key_wgrad = weight_term(rows_in, key_grad)
    value_wgrad = weight_term(rows_in, value_grad)
    query_bias_grad = bias_term(query_grad)
    value_bias_grad = bias_term(value_grad)
    input_full = (
        grad1
        + apply_back(query_grad, query_full)
        + apply_back(key_grad, key_full)
        + apply_back(value_grad, value_full)
    )
    live_rows = lax.broadcasted_iota(jnp.int32, (row_count,), 0) < live_count[0]
    input_grad = jnp.where(live_rows[:, None, None], input_full, 0.0)
    devices = packed_full.shape[0]
    small_terms = jnp.concatenate(
        [
            v.reshape(devices, -1, small_rows)
            for v in (
                query_bias_grad,
                value_bias_grad,
                output_bias_grad,
                gain1_grad,
                shift1_grad,
                down_bias_grad,
                gain2_grad,
                shift2_grad,
                up_bias_grad,
            )
        ],
        axis=1,
    )
    small_sum = lax.psum_scatter(small_terms, ("dp", "fsdp"), scatter_dimension=0, tiled=True)[0]
    down_sum, up_sum, output_sum, value_sum, query_sum, key_sum = (
        lax.psum_scatter(
            term.astype(jnp.bfloat16), ("dp", "fsdp"), scatter_dimension=0, tiled=True
        ).astype(jnp.float32)
        for term in (down_grad, up_grad, output_grad, value_wgrad, query_wgrad, key_wgrad)
    )
    return (
        slot_acts,
        input_grad,
        query_sum,
        key_sum,
        value_sum,
        output_sum,
        small_sum[0],
        small_sum[1],
        small_sum[2],
        small_sum[3],
        small_sum[4],
        up_sum,
        small_sum[8:].reshape(-1),
        down_sum,
        small_sum[5],
        small_sum[6],
        small_sum[7],
    )


def solution(mesh):
    placed = (
        P(("dp", "fsdp"), None, None),
        P(("dp", "fsdp")),
        P(("dp", "fsdp")),
        P(("dp", "fsdp"), None, None),
        P(("dp", "fsdp"), None),
        P(("dp", "fsdp"), None),
        P(("dp", "fsdp"), None),
        P(("dp", "fsdp"), None),
        P(("dp", "fsdp")),
        P(("dp", "fsdp")),
        P(("dp", "fsdp")),
        P(("dp", "fsdp")),
        P(("dp", "fsdp")),
        P(("dp", "fsdp"), None),
        P(("dp", "fsdp")),
        P(("dp", "fsdp"), None),
        P(("dp", "fsdp")),
        P(("dp", "fsdp")),
        P(("dp", "fsdp")),
    )
    kernels = mesh.shape["dp"] == 4 and mesh.shape["fsdp"] == 8
    return jax.shard_map(
        on_device_kernels if kernels else on_device_plain,
        mesh=mesh,
        in_specs=placed,
        out_specs=(
            P(("dp", "fsdp"), None, None),
            P(("dp", "fsdp"), None, None),
            P(("dp", "fsdp"), None),
            P(("dp", "fsdp"), None),
            P(("dp", "fsdp"), None),
            P(("dp", "fsdp"), None),
            P(("dp", "fsdp")),
            P(("dp", "fsdp")),
            P(("dp", "fsdp")),
            P(("dp", "fsdp")),
            P(("dp", "fsdp")),
            P(("dp", "fsdp"), None),
            P(("dp", "fsdp")),
            P(("dp", "fsdp"), None),
            P(("dp", "fsdp")),
            P(("dp", "fsdp")),
            P(("dp", "fsdp")),
        ),
        check_vma=False,
    )
```

```python
import math
from functools import partial

import jax
import jax.numpy as jnp
from jax import lax
from jax.experimental import pallas as pl
from jax.experimental.pallas import tpu as pltpu
from jax.sharding import PartitionSpec as P

HEADS = 16


EPSILON = 1e-05


MESH = pl.DeviceIdType.MESH
LANES = 128


def place(nz, nx):
    dp, fs = lax.axis_index("dp"), lax.axis_index("fsdp")
    y, core = dp // 2, lax.rem(dp, 2)
    z, x = fs // nx, lax.rem(fs, nx)
    return y, core, z, x


def device(y, core, z, x, nx):
    return (y * 2 + core, z * nx + x)


class Partners:
    def __init__(self, nz, nx):
        self.nz, self.nx = nz, nx
        self.y, self.core, self.z, self.x = place(nz, nx)
        y, core, z, x = self.y, self.core, self.z, self.x
        self.sibling = device(y, 1 - core, z, x, nx)
        self.across_x = device(y, core, z, 1 - x, nx)
        self.across_y = device(1 - y, core, z, x, nx)
        self.along_z = [device(y, core, lax.rem(z + k, nz), x, nx) for k in range(1, nz)]
        self.all = [self.sibling, self.across_x, self.across_y, *self.along_z]

    def meet(self):
        barrier = pltpu.get_barrier_semaphore()
        for other in self.all:
            pl.semaphore_signal(barrier, inc=1, device_id=other, device_id_type=MESH)
        pl.semaphore_wait(barrier, len(self.all))


def remote(src, dst, send, recv, to):
    return pltpu.make_async_remote_copy(
        src_ref=src, dst_ref=dst, send_sem=send, recv_sem=recv, device_id=to, device_id_type=MESH
    )


def added(*blocks):
    total = blocks[0].astype(jnp.float32)
    for block in blocks[1:]:
        total = total + block.astype(jnp.float32)
    return total


class Scatter:
    def __init__(self, at, parts, rc, r3a, r3b, r2, rz, rcz, rcx, rcy, send, recv):
        self.at, self.parts = at, parts
        self.rc, self.r3a, self.r3b, self.r2, self.rz = rc, r3a, r3b, r2, rz
        self.rcz, self.rcx, self.rcy = rcz, rcx, rcy
        self.send, self.recv = send, recv

    def copy(self, m, i, src, dst, to):
        return remote(src, dst, self.send.at[m, i], self.recv.at[m, i], to)

    def to_sibling(self, m, theirs):
        return self.copy(m, 0, theirs, self.rc.at[m], self.at.sibling)

    def landings(self, m):
        a, b, c, _ = self.parts[m]
        a, b, c = (pl.ds(0, part.size) for part in (a, b, c))
        return (
            self.r3a.at[m, :, :, :, a],
            self.r3b.at[m, :, :, :, b],
            self.rcz.at[m, :, :, :, :, c],
            self.rcx.at[m, :, :, c],
            self.rcy.at[m, :, c],
        )

    def firsts(self, m):
        at, rc, nz = self.at, self.rc, self.at.nz
        a, b, c, _ = self.parts[m]
        r3a, r3b, rcz, _, _ = self.landings(m)
        return [
            self.copy(m, 1, rc.at[m, :, :, 1 - at.x, :, a], r3a, at.across_x),
            self.copy(m, 2, rc.at[m, 1 - at.y, :, :, :, b], r3b, at.across_y),
        ] + [
            self.copy(
                m, 2 + k, rc.at[m, :, lax.rem(at.z + k, nz), :, :, c], rcz.at[k - 1], at.along_z[k - 1]
            )
            for k in range(1, nz)
        ]

    def seconds(self, m):
        at, nz = self.at, self.at.nz
        a, b, _, _ = self.parts[m]
        r3a, r3b, rcz, rcx, _ = self.landings(m)
        return [
            self.copy(m, nz + 2, r3a.at[1 - at.y], self.r2.at[m, :, :, a], at.across_y),
            self.copy(m, nz + 3, r3b.at[:, 1 - at.x], self.r2.at[m, :, :, b], at.across_x),
            self.copy(m, nz + 4, rcz.at[0, :, 1 - at.x], rcx, at.across_x),
        ]

    def thirds(self, m):
        at, nz = self.at, self.at.nz
        ab = self.parts[m][3]
        rcx, rcy = self.landings(m)[3:]
        return [
            self.copy(
                m,
                nz + 4 + k,
                self.r2.at[m, lax.rem(at.z + k, nz), :, ab],
                self.rz.at[m, k - 1, :, ab],
                at.along_z[k - 1],
            )
            for k in range(1, nz)
        ] + [self.copy(m, 2 * nz + 4, rcx.at[1 - at.y], rcy, at.across_y)]

    def start(self, m, theirs):
        self.to_sibling(m, theirs).start()

    def step1(self, m, own):
        rc = self.rc
        self.to_sibling(m, rc.at[m]).wait_recv()

        rc[m] = added(rc[m], own).astype(rc.dtype)
        self.to_sibling(m, rc.at[m]).wait_send()
        for copy in self.firsts(m):
            copy.start()

    def step2(self, m):
        at, rc = self.at, self.rc
        a, b, c, _ = self.parts[m]
        r3a, r3b, rcz, _, _ = self.landings(m)
        for copy in self.firsts(m):
            copy.wait_recv()

        r3a[...] = added(r3a[...], rc[m, :, :, at.x, :, a]).astype(rc.dtype)
        r3b[...] = added(r3b[...], rc[m, at.y, :, :, :, b]).astype(rc.dtype)
        others = [rcz[k] for k in range(at.nz - 1)]
        rcz[0] = added(rc[m, :, at.z, :, :, c], *others).astype(rc.dtype)
        for copy in self.seconds(m):
            copy.start()

    def step3(self, m):
        at, r2 = self.at, self.r2
        a, b, _, _ = self.parts[m]
        r3a, r3b, rcz, rcx, _ = self.landings(m)
        for copy in self.seconds(m):
            copy.wait_recv()

        r2[m, :, :, a] = added(r2[m, :, :, a], r3a[at.y]).astype(r2.dtype)
        r2[m, :, :, b] = added(r2[m, :, :, b], r3b[:, at.x]).astype(r2.dtype)
        rcx[...] = added(rcx[...], rcz[0, :, at.x]).astype(r2.dtype)
        for copy in self.thirds(m):
            copy.start()

    def step4(self, m, out):
        at = self.at
        _, _, c, ab = self.parts[m]
        rcx, rcy = self.landings(m)[3:]
        for copy in self.thirds(m):
            copy.wait_recv()
        others = [self.rz[m, k, :, ab] for k in range(at.nz - 1)]
        out[m, :, ab] = added(self.r2[m, at.z, :, ab], *others)
        out[m, :, c] = added(rcx[at.y], rcy[...])

    def drain(self, m):
        for copy in self.firsts(m) + self.seconds(m) + self.thirds(m):
            copy.wait_send()


class SmallSum:
    def __init__(self, at, total, landing, send, recv):
        self.at, self.total, self.landing, self.send, self.recv = at, total, landing, send, recv

    def hop(self, i, to):
        return remote(self.total.at[i], self.landing.at[i], self.send.at[i], self.recv.at[i], to)

    def along(self, k):
        i = 2 + k
        return remote(self.total.at[3], self.landing.at[i], self.send.at[i], self.recv.at[i], self.at.along_z[k - 1])

    def start(self):
        self.hop(0, self.at.sibling).start()

    def step(self, i):
        at = self.at
        to = (at.sibling, at.across_x, at.across_y)
        self.hop(i, to[i]).wait_recv()
        self.total[i + 1] = self.total[i] + self.landing[i]
        if i < 2:
            self.hop(i + 1, to[i + 1]).start()
        else:
            for k in range(1, at.nz):
                self.along(k).start()

    def finish(self, out):
        at = self.at
        for k in range(1, at.nz):
            self.along(k).wait_recv()
        total = self.total[3]
        for k in range(1, at.nz):
            total = total + self.landing[2 + k]
        out[...] = total
        to = (at.sibling, at.across_x, at.across_y)
        for i in range(3):
            self.hop(i, to[i]).wait_send()
        for k in range(1, at.nz):
            self.along(k).wait_send()


def scatter_scratch(count, nz, nx, rows, columns, parts):
    bf16 = jnp.bfloat16
    a, b, c = (max(part[i].size for part in parts) for i in range(3))
    return [
        pltpu.VMEM((count, 2, nz, nx, rows, columns), bf16),
        pltpu.VMEM((count, 2, nz, rows, a), bf16),
        pltpu.VMEM((count, nz, nx, rows, b), bf16),
        pltpu.VMEM((count, nz, rows, columns), bf16),
        pltpu.VMEM((count, nz - 1, rows, columns), bf16),
        pltpu.VMEM((count, nz - 1, 2, nx, rows, c), bf16),
        pltpu.VMEM((count, 2, rows, c), bf16),
        pltpu.VMEM((count, rows, c), bf16),
        pltpu.SemaphoreType.DMA((count, 2 * nz + 5)),
        pltpu.SemaphoreType.DMA((count, 2 * nz + 5)),
    ]


def small_scratch(nz, shape):
    return [
        pltpu.VMEM((4, *shape), jnp.float32),
        pltpu.VMEM((2 + nz, *shape), jnp.float32),
        pltpu.SemaphoreType.DMA((2 + nz,)),
        pltpu.SemaphoreType.DMA((2 + nz,)),
    ]


GATHER_SHARES = [
    (6, 1), (3, 3), (6, 1), (3, 4), (3, 3), (6, 1), (5, 1), (4, 2), (5, 1), (5, 1), (5, 1), (5, 1),
]
SCATTER_SHARES = [
    (4, 2), (5, 1), (4, 2), (6, 1), (5, 1), (4, 2), (4, 2), (6, 1), (5, 1), (5, 2), (4, 2), (3, 3),
]

FORWARD_ORDER = (
    100, 101, 102, 103, 0, 0, 104, 105, 106, 107, 0, 0, 0, 200, 0, 201, 0, 300, 500, 501, 202, 301, 203, 204,
    302, 502, 205, 400, 108, 206, 303, 0, 503, 401, 109, 304, 207, 402, 110, 305, 0, 0, 208, 0, 0, 403, 111,
    306, 0, 0, 0, 209, 0, 0, 0, 0, 404, 307, 0, 0, 504, 0, 210, 0, 405, 308, 0, 0, 211, 0, 406, 309, 505, 0,
    407, 310, 506, 0, 408, 311, 507, 0, 409, 508, 509, 410, 510, 0, 511, 0, 411, 0, 0,
)
BACKWARD_ORDER = (
    500, 0, 501, 0, 502, 0, 0, 0, 503, 100, 0, 0, 101, 0, 0, 504, 102, 0, 0, 200, 103, 0, 0, 0, 201, 104, 0,
    202, 0, 0, 300, 0, 105, 0, 505, 0, 203, 0, 400, 301, 0, 106, 0, 506, 0, 204, 0, 401, 302, 0, 107, 0, 205,
    303, 0, 507, 0, 402, 0, 206, 108, 304, 0, 0, 508, 0, 403, 0, 0, 509, 0, 207, 0, 0, 305, 0, 306, 0, 404, 0,
    510, 511, 0, 0, 0, 405, 208, 307, 0, 109, 406, 0, 0, 110, 0, 0, 111, 308, 407, 0, 209, 0, 210, 211, 309,
    408, 310, 311, 409, 410, 411,
)


def drive(order, items, run):
    todo = list(order)
    for item in items:
        while todo[0]:
            run(todo.pop(0))
        if callable(item):
            todo.pop(0)
            item()
            continue
        rounds, body = item
        between = []
        for _ in range(rounds):
            codes = []
            while todo[0]:
                codes.append(todo.pop(0))
            todo.pop(0)
            between.append(codes)

        def one(i, carry):
            for r, codes in enumerate(between):
                if codes:

                    @pl.when(i == r)
                    def _(codes=codes):
                        for code in codes:
                            run(code)

            body(i)
            return carry

        lax.fori_loop(0, rounds, one, 0)
    for code in todo:
        run(code)


def exact_gelu(pre):
    half = 0.5 + 0.5 * lax.erf(pre * (0.5**0.5))
    bell = jnp.exp(-0.5 * pre * pre) * ((0.5 / math.pi) ** 0.5)
    return pre * half, half + pre * bell


def rms_center(hidden):
    center = hidden - jnp.mean(hidden, axis=-1, keepdims=True)
    inverse = lax.rsqrt(jnp.mean(center * center, axis=-1, keepdims=True) + EPSILON)
    return center * inverse, inverse


def half_masks(width):
    left = (lax.broadcasted_iota(jnp.int32, (1, width), 1) < width // 2).astype(jnp.float32)
    return left.astype(jnp.bfloat16), (1.0 - left).astype(jnp.bfloat16)


def across(left, right):
    return lax.dot_general(left, right, (((1,), (1,)), ((), ())), preferred_element_type=jnp.float32)


def down(left, right):
    return lax.dot_general(left, right, (((0,), (0,)), ((), ())), preferred_element_type=jnp.float32)


def dot(left, right):
    return jnp.dot(left, right, preferred_element_type=jnp.float32)


def span(i, size):
    return pl.ds(pl.multiple_of(i * size, size), size)


class Gather:
    def __init__(self, at, parts, count, shards, g, send, recv):
        self.at, self.count, self.shards, self.g, self.send, self.recv = at, count, shards, g, send, recv
        self.parts = parts

    def copy(self, m, i, src, dst, to):
        return remote(src, dst, self.send.at[m, i], self.recv.at[m, i], to)

    def same(self, m, i, part, to):
        return self.copy(m, i, part, part, to)

    def stages(self, m):
        at, g, nz = self.at, self.g, self.at.nz
        a, b, c, ab = self.parts[m]
        y, core, z, x = at.y, at.core, at.z, at.x
        across_x, across_y, along_z = at.across_x, at.across_y, at.along_z
        first = [
            self.copy(m, k, self.shards.at[m, :, ab], g.at[m, y, core, z, x, :, ab], along_z[k])
            for k in range(nz - 1)
        ]
        first.append(self.copy(m, nz - 1, self.shards.at[m, :, c], g.at[m, y, core, z, x, :, c], across_y))
        second = [
            self.same(m, nz, g.at[m, y, core, :, x, :, a], across_y),
            self.same(m, nz + 1, g.at[m, y, core, :, x, :, b], across_x),
            self.same(m, nz + 2, g.at[m, :, core, z, x, :, c], across_x),
        ]
        third = [
            self.same(m, nz + 3, g.at[m, :, core, :, x, :, a], across_x),
            self.same(m, nz + 4, g.at[m, y, core, :, :, :, b], across_y),
        ]
        third += [self.same(m, nz + 5 + k, g.at[m, :, core, z, :, :, c], along_z[k]) for k in range(nz - 1)]
        return first, second, third, [self.same(m, 2 * nz + 4, g.at[m, :, core], at.sibling)]

    def step0(self, m):
        at = self.at
        for copy in self.stages(m)[0]:
            copy.start()
        self.g[m, at.y, at.core, at.z, at.x] = self.shards[m]

    def follow(self, stage, m):
        stages = self.stages(m)
        for copy in stages[stage - 1]:
            copy.wait_recv()
        for copy in stages[stage]:
            copy.start()

    def step1(self, m):
        self.follow(1, m)

    def step2(self, m):
        self.follow(2, m)

    def step3(self, m):
        self.follow(3, m)

    def arrive(self, m):
        self.stages(m)[3][0].wait_recv()

    def drain(self, m):
        for stage in self.stages(m):
            for copy in stage:
                copy.wait_send()


def column_parts(width, shares):
    lanes = 128
    a, b = (share * lanes for share in shares)
    return pl.ds(0, a), pl.ds(a, b), pl.ds(a + b, width - a - b), pl.ds(0, a + b)


UP_TILE = 256
NORM_ROWS = 192


def forward_kernel(
    nz, nx, parts, tokens, head_pair,
    x, attention_weights, expand, contract, small, pick, slots,
    g_out, probs_out, saved, act_out, slope_out, unit_out, final_out, own_out, across_out, small_full, inverse1, inverse2,
    g, shards, pool, hidden, landed, total, landing,
    send, recv, ssend, srecv, usend, urecv, across_send, across_recv, isem, gsem, vsem, asem, dsem, fsem, held_probs, ksem,
):
    f32, bf16 = jnp.float32, jnp.bfloat16
    count = g.shape[0]
    all_rows, width = x.shape
    rows = all_rows // tokens
    at = Partners(nz, nx)
    at.meet()
    gather = Gather(at, parts, count, shards, g, send, recv)
    sums = SmallSum(at, total, landing, ssend, srecv)
    groups = slots.shape[0] // rows

    def fetch(i):
        return pltpu.make_async_copy(slots.at[i], pool.at[i // rows, pl.ds((i % rows) * tokens, tokens)], isem.at[i])

    shard = shards.shape[1]
    lane = lax.broadcasted_iota(jnp.int32, (1, width), 1)
    mine = lane // shard == lax.axis_index("dp") * (nz * nx) + lax.axis_index("fsdp")
    total[0] = jnp.where(mine, jnp.concatenate([small[...]] * (width // shard), axis=1), 0.0)
    sums.start()
    for m in range(4):
        shards[m] = attention_weights[m][...]
    for i in range(slots.shape[0]):
        fetch(i).start()

    high, part = 32, width // 2

    def sum_slots(i, carry):
        cols = span(lax.rem(i, 2), part)
        base = i // 2 * high
        held = [
            pool[s // rows, pl.ds(pl.multiple_of(base + (s % rows) * tokens, high), high), cols].astype(f32)
            for s in range(slots.shape[0])
        ]
        for t in range(pick.shape[0]):
            picked = pick[t, 0] * held[0]
            for s in range(1, slots.shape[0]):
                picked = picked + pick[t, s] * held[s]
            spot = pl.ds(pl.multiple_of(base + (t % rows) * tokens, high), high)
            pool[groups + t // rows, spot, cols] = picked.astype(bf16)
        return carry

    def up_sibling(y):
        src = pool.at[groups + y * 2 + 1 - at.core]
        return remote(src, landed.at[y], usend.at[y], urecv.at[y], at.sibling)

    pieces = across_send.shape[0]

    def up_across(i):
        piece = pl.ds(i * (all_rows // pieces), all_rows // pieces)
        return remote(
            landed.at[1 - at.y, piece], across_out.at[piece], across_send.at[i], across_recv.at[i], at.across_y
        )

    up_own = pltpu.make_async_copy(landed.at[at.y], own_out, isem.at[slots.shape[0]])

    steps = tokens // high * 2

    def quarter(i):
        if i == 0:
            for s in range(slots.shape[0]):
                fetch(s).wait()
        lax.fori_loop(i * steps // 4, (i + 1) * steps // 4, sum_slots, 0)
        if i != 2:
            sums.step((0, 1, None, 2)[i])

    blocks = (count - 4) // 2

    def arrange():
        for j in range(blocks):
            shards[5 + 2 * j] = contract[j * shard : (j + 1) * shard, :]
        lanes = 128
        per = lanes // shard
        for q in range(width // lanes):
            natural = expand[:, q * lanes * blocks : (q + 1) * lanes * blocks].astype(f32)
            for j in range(blocks):
                starts = [t * blocks * shard + j * shard for t in range(per)]
                found = [natural[:, start : start + shard] for start in starts]
                shards[4 + 2 * j, :, q * lanes : (q + 1) * lanes] = jnp.concatenate(found, axis=1).astype(bf16)

    def exchange_cores():
        for y in range(2):
            up_sibling(y).start()

    def chip_sum(i, carry):
        y, spot = i // (all_rows // 192), span(lax.rem(i, all_rows // 192), 192)
        landed[y, spot] = added(landed[y, spot], pool[groups + y * 2 + at.core, spot]).astype(bf16)
        return carry

    def sum_chip():
        for y in range(2):
            up_sibling(y).wait_recv()
        lax.fori_loop(0, 2 * all_rows // 192, chip_sum, 0)
        up_own.start()
        for y in range(2):
            up_sibling(y).wait_send()

    def keep(m):
        return pltpu.make_async_copy(g.at[m], g_out.at[m], gsem.at[m])

    def arrive(m):
        gather.arrive(m)
        keep(m).start()

    def tile(m, cols):
        return g[m, :, :, :, :, :, cols].reshape(width, cols.size)

    def bias(i, cols):
        return small_full[pl.ds(i, 1), cols]

    every = pl.ds(0, all_rows)

    def tiles(size, body):
        def one(i, carry):
            body(span(i, size), every)
            return carry

        if size == width:
            body(pl.ds(0, width), every)
        else:
            lax.fori_loop(0, width // size, one, 0)

    def save(i):
        return pltpu.make_async_copy(pool.at[i], saved.at[i], vsem.at[i])

    def project(m):
        bias_row = (0, None, 1)[m]
        if m == 0:
            sums.finish(small_full)

        def body(cols, spot):
            y = dot(x[spot], tile(m, cols))
            if bias_row is not None:
                y = y + bias(bias_row, cols)
            pool[m, spot, cols] = y.astype(bf16)

        arrive(m)
        tiles(width, body)
        save(m).start()

    pairs = width // head_pair
    masks = half_masks(head_pair)
    scale = (head_pair // 2) ** (-0.5)

    def keep_probs(i):
        slot = lax.rem(i, 2)
        return pltpu.make_async_copy(held_probs.at[slot], probs_out.at[i], ksem.at[slot])

    def attend(i):
        spot, base = span(i // (pairs // 2), tokens), lax.rem(i, pairs // 2) * 2
        pl.when(i >= 2)(lambda: keep_probs(i - 2).wait())
        for p in range(2):
            cols = span(base + p, head_pair)
            query, keys, values = pool[0, spot, cols], pool[1, spot, cols], pool[2, spot, cols]
            query = query * jnp.asarray(scale, bf16)
            out = None
            for h, mask in enumerate(masks):
                scores = across(keys * mask, query)
                probs = jnp.exp(scores - jnp.max(scores, axis=0, keepdims=True))
                probs = (probs * (1.0 / jnp.sum(probs, axis=0, keepdims=True))).astype(bf16)
                held_probs[lax.rem(i, 2), 2 * p + h] = probs
                term = down(probs, values * mask)
                out = term if out is None else out + term
            pool[3, spot, cols] = out.astype(bf16)
        keep_probs(i).start()

    rounds = rows * pairs // 2

    def mix(cols, spot):
        hidden[spot, cols] = dot(pool[3, spot], tile(3, cols)) + x[spot, cols].astype(f32) + bias(2, cols)

    def join():
        save(3).start()
        for i in range(2):
            keep_probs(rounds - 2 + i).wait()
        arrive(3)
        tiles(width, mix)

    def unit(i):
        return pltpu.make_async_copy(pool.at[6], unit_out.at[i], fsem.at[i])

    def norm1(i, carry):
        spot = span(i, NORM_ROWS)
        normed, inverse = rms_center(hidden[spot])
        result = normed * small_full[3:4, :] + small_full[4:5, :]
        hidden[spot] = result
        pool[4, spot] = result.astype(bf16)
        pool[6, spot] = normed.astype(bf16)
        inverse1[spot] = inverse
        return carry

    def first_norm():
        lax.fori_loop(0, all_rows // NORM_ROWS, norm1, 0)
        save(4).start()
        unit(0).start()

    def save_act(j):
        return pltpu.make_async_copy(pool.at[5], act_out.at[j], asem)

    def save_slope(j):
        return pltpu.make_async_copy(pool.at[6], slope_out.at[j], dsem)

    def widen(j):
        m = 4 + 2 * j
        arrive(m)
        if j == 0:
            unit(0).wait()
        else:
            save_act(j - 1).wait()
            save_slope(j - 1).wait()

        def up(cols, spot):
            value, slope = exact_gelu(dot(pool[4, spot], tile(m, cols)) + bias(8 + j, cols))
            pool[5, spot, cols] = value.astype(bf16)
            pool[6, spot, cols] = slope.astype(bf16)

        tiles(UP_TILE, up)
        save_act(j).start()
        save_slope(j).start()

    def narrow(j):
        m = 5 + 2 * j
        arrive(m)

        def back(cols, spot):
            hidden[spot, cols] = hidden[spot, cols] + dot(pool[5, spot], tile(m, cols))

        tiles(width, back)

    def norm2(i, carry):
        spot = span(i, NORM_ROWS)
        normed, inverse = rms_center(hidden[spot] + small_full[5:6, :])
        pool[5, spot] = (normed * small_full[6:7, :] + small_full[7:8, :]).astype(bf16)
        pool[6, spot] = normed.astype(bf16)
        inverse2[spot] = inverse
        return carry

    finish = pltpu.make_async_copy(pool.at[5], final_out, fsem.at[2])

    def second_norm():
        save_act(blocks - 1).wait()
        save_slope(blocks - 1).wait()
        lax.fori_loop(0, all_rows // NORM_ROWS, norm2, 0)
        finish.start()
        unit(1).start()

    def run(code):
        kind, m = divmod(code, 100)
        if kind == 5:
            up_across(m).start()
        else:
            (gather.step0, gather.step1, gather.step2, gather.step3)[kind - 1](m)

    items = [partial(quarter, 0), arrange, *(partial(quarter, i) for i in (1, 2, 3)), exchange_cores, sum_chip]
    items += [partial(project, m) for m in range(3)] + [(rounds, attend), join, first_norm]
    for j in range(blocks):
        items += [partial(widen, j), partial(narrow, j)]
    drive(FORWARD_ORDER, [*items, second_norm], run)
    for m in range(count):
        gather.drain(m)
        keep(m).wait()
    for i in range(5):
        save(i).wait()
    up_own.wait()
    for i in range(pieces):
        up_across(i).wait()
    finish.wait()
    unit(1).wait()


def forward(x, attention_weights, expand, contract, small, pick, slots, nz, nx, tokens):
    f32, bf16 = jnp.float32, jnp.bfloat16
    shard_rows, width = attention_weights[0].shape
    count = 4 + 2 * contract.shape[0] // shard_rows
    small_shape = (small.shape[0], width)
    all_rows = x.shape[0]
    group_members = pick.shape[0] * tokens // all_rows
    assert group_members == 4 and slots.shape[0] * tokens == 2 * all_rows
    vmem, anywhere = pl.BlockSpec(memory_space=pltpu.VMEM), pl.BlockSpec(memory_space=pl.ANY)
    acts = (all_rows, width)
    rows = all_rows // tokens
    blocks = (count - 4) // 2
    dma = pltpu.SemaphoreType.DMA
    full = (count, 2, 2, nz, nx, shard_rows, width)
    out = jax.ShapeDtypeStruct
    return pl.pallas_call(
        partial(forward_kernel, nz, nx, [column_parts(width, s) for s in GATHER_SHARES], tokens, 2 * width // HEADS),
        out_shape=[
            out(full, bf16),
            out((rows * HEADS // 4, 4, tokens, tokens), bf16),
            out((5, *acts), bf16),
            out((blocks, *acts), bf16),
            out((blocks, *acts), bf16),
            out((2, *acts), bf16),
            out(acts, bf16),
            out(acts, bf16),
            out(acts, bf16),
            out(small_shape, f32),
            out((all_rows, 1), f32),
            out((all_rows, 1), f32),
        ],
        in_specs=[vmem, [vmem] * 4, vmem, vmem, vmem, pl.BlockSpec(memory_space=pltpu.SMEM), anywhere],
        out_specs=[anywhere] * 9 + [vmem] * 3,
        scratch_shapes=[
            pltpu.VMEM(full, bf16),
            pltpu.VMEM((count, shard_rows, width), bf16),
            pltpu.VMEM((7, *acts), bf16),
            pltpu.VMEM(acts, f32),
            pltpu.VMEM((2, *acts), bf16),
            *small_scratch(nz, small_shape)[:2],
            dma((count, 2 * nz + 5)),
            dma((count, 2 * nz + 5)),
            dma((2 + nz,)),
            dma((2 + nz,)),
            dma((2,)),
            dma((2,)),
            dma((count,)),
            dma((count,)),
            dma((slots.shape[0] + 1,)),
            dma((count,)),
            dma((5,)),
            dma,
            dma,
            dma((3,)),
            pltpu.VMEM((2, 4, tokens, tokens), bf16),
            dma((2,)),
        ],
        compiler_params=pltpu.CompilerParams(
            collective_id=1, has_side_effects=True, vmem_limit_bytes=60 * 2**20
        ),
    )(x, attention_weights, expand, contract, small, pick, slots)


def backward_kernel(
    nz, nx, parts, tokens, head_pair,
    x, own_up, across_up, final, unit, inverse1, inverse2, small_full, act, slope, saved, g, probs,
    out, small_out, input_out, table,
    rc, r3a, r3b, r2, rz, rcz, rcx, rcy, send, recv, total, landing, ssend, srecv,
    term, weight, pool, hidden, wsem, psem, hsem, tsend, trecv, across_send, across_recv, tsem, held_probs, ksem,
):
    f32, bf16 = jnp.float32, jnp.bfloat16
    count = out.shape[0]
    all_rows, width = x.shape
    rows = all_rows // tokens
    at = Partners(nz, nx)
    at.meet()
    scatter = Scatter(at, parts, rc, r3a, r3b, r2, rz, rcz, rcx, rcy, send, recv)
    sums = SmallSum(at, total, landing, ssend, srecv)

    here = pltpu.make_async_copy(final, table.at[at.y, at.core], tsem)
    to_sibling = remote(final, table.at[at.y, at.core], tsend.at[0], trecv.at[0], at.sibling)
    pieces = across_send.shape[0]

    def to_across(i):
        piece = pl.ds(i * (all_rows // pieces), all_rows // pieces)
        dst = table.at[at.y, at.core, piece]
        return remote(final.at[piece], dst, across_send.at[i], across_recv.at[i], at.across_y)

    passed = table.at[1 - at.y, at.core]
    pass_on = remote(passed, passed, tsend.at[1], trecv.at[1], at.sibling)

    def load(src, entry, i):
        return pltpu.make_async_copy(src, pool.at[entry], psem.at[i])

    def fetch(m, slot, i):
        return pltpu.make_async_copy(g.at[m], weight.at[slot], wsem.at[i])

    blocks = act.shape[0]
    up_block, down_block = (lambda j: 4 + 2 * j), (lambda j: 5 + 2 * j)
    unit2, own_load, across_load = load(unit.at[1], 1, 0), load(own_up, 2, 1), load(across_up, 3, 2)
    act_entry = [5, 2, 3, 5]
    act_load = [load(act.at[j], act_entry[j], 3 + j) for j in range(blocks)]
    slope_entry = [4, 2, 3, 4]
    slope_load = [load(slope.at[j], slope_entry[j], 7 + j) for j in range(blocks)]
    low_load, unit1, mixed_load = load(saved.at[4], 6, 11), load(unit.at[0], 5, 12), load(saved.at[3], 4, 13)
    query_load, key_load, value_load = (load(saved.at[i], (2, 3, 6)[i], 14 + i) for i in range(3))
    x_load = load(x, 4, 17)
    down_fetch = [fetch(down_block(j), 0, 2 * j) for j in range(blocks)]
    up_fetch = [fetch(up_block(j), 1, 2 * j + 1) for j in range(blocks)]
    last = 2 * blocks
    output_fetch, query_fetch, key_fetch, value_fetch = (
        fetch(m, slot, last + i) for i, (m, slot) in enumerate(((3, 0), (0, 1), (1, 0), (2, 1)))
    )
    for copy in (unit2, own_load, across_load, act_load[0], down_fetch[0], up_fetch[0], slope_load[0], low_load):
        copy.start()
    to_sibling.start()
    here.start()
    total[0] = jnp.zeros_like(total[0])

    def folded(block):
        return jnp.sum(block.reshape(-1, 8, block.shape[-1]), axis=0)

    def norm_back(gain_row, shift_row, low_row, inverse, incoming, normed_entry, low_entry):
        def body(i, carry):
            spot = span(i, NORM_ROWS)
            grad, normed = incoming(spot), pool[normed_entry, spot].astype(f32)
            scaled = grad * small_full[gain_row : gain_row + 1, :]
            inner = (
                scaled
                - jnp.mean(scaled, axis=-1, keepdims=True)
                - normed * jnp.mean(scaled * normed, axis=-1, keepdims=True)
            )
            result = inner * inverse[spot]
            low = result.astype(bf16)
            hidden[spot] = result
            pool[low_entry, spot] = low
            return tuple(c + folded(b) for c, b in zip(carry, (grad * normed, grad, low.astype(f32))))

        zero = jnp.zeros((8, width), f32)
        found = lax.fori_loop(0, all_rows // NORM_ROWS, body, (zero, zero, zero))
        for row, value in zip((gain_row, shift_row, low_row), found):
            total[0, row : row + 1, :] = jnp.sum(value, axis=0, keepdims=True)

    def turned(slot):
        return weight[slot].reshape(width, width)

    def own_half(slot):
        return term[slot, :, at.core]

    stepped = set()

    def half(m, left, right, core):
        assert m < 2 or m - 2 in stepped
        for y in range(2):
            picked = span(y * 2 + core, width // 4)
            value = down(pool[left, :, picked], pool[right]).astype(bf16)
            term[m % 2, y, core] = value.reshape(nz, nx, -1, width)

    def theirs(m, left, right):
        half(m, left, right, 1 - at.core)
        scatter.start(m, term.at[m % 2, :, 1 - at.core])

    def ours(m, left, right):
        half(m, left, right, at.core)

    def run(code):
        kind, m = divmod(code, 100)
        if kind == 5:
            to_across(m).start()
        elif kind == 1:
            scatter.step1(m, own_half(m % 2))
            stepped.add(m)
        elif kind == 4:
            scatter.step4(m, out)
        else:
            (scatter.step2, scatter.step3)[kind - 2](m)

    items = []

    def produce(m, left, right, before=(), after=()):
        def first():
            for call in before:
                call()
            theirs(m, left, right)

        def second():
            ours(m, left, right)
            for call in after:
                call()

        items.extend((first, second))

    def load_second():
        for copy in (unit2, own_load, across_load):
            copy.wait()

    def second_norm():
        norm_back(6, 7, 5, inverse2, lambda spot: added(pool[2, spot], pool[3, spot]), 1, 0)
        act_load[1].start()
        act_load[2].start()

    items += [load_second, second_norm]
    for j in range(blocks):
        after = (act_load[3].start, slope_load[1].start, slope_load[2].start, unit1.start)[j]
        produce(j, act_entry[j], 0, [act_load[j].wait], [after])

    def widen_back(j):
        down_fetch[j].wait()
        slope_load[j].wait()
        value = across(pool[0], turned(0)) * pool[slope_entry[j]].astype(f32)
        value = value.astype(bf16)
        pool[1] = value
        total[0, 8 + j : 9 + j, :] = jnp.sum(value.astype(f32), axis=0, keepdims=True)
        (down_fetch[j + 1] if j + 1 < blocks else output_fetch).start()
        (slope_load[3], query_load, key_load, mixed_load)[j].start()

    def narrow_back(j):
        up_fetch[j].wait()
        hidden[...] = hidden[...] + across(pool[1], turned(1))
        (up_fetch[j + 1] if j + 1 < blocks else query_fetch).start()
        if j == blocks - 1:
            value_load.start()

    for j in range(blocks):
        items.append(partial(widen_back, j))
        produce(blocks + j, 6, 1, [low_load.wait] if j == 0 else [])
        items.append(partial(narrow_back, j))

    def first_norm():
        unit1.wait()
        norm_back(3, 4, 2, inverse1, lambda spot: hidden[spot], 5, 0)

    def mixed_back():
        output_fetch.wait()
        pool[1] = across(pool[0], turned(0)).astype(bf16)
        key_fetch.start()
        for copy in (query_load, key_load, value_load):
            copy.wait()
        fetch_probs(0).start()

    items.append(first_norm)
    produce(2 * blocks, 4, 0, [mixed_load.wait], [x_load.start])
    items.append(mixed_back)

    pairs = width // head_pair
    masks = half_masks(head_pair)
    scale = (head_pair // 2) ** (-0.5)

    def fetch_probs(i):
        slot = lax.rem(i, 2)
        return pltpu.make_async_copy(probs.at[i], held_probs.at[slot], ksem.at[slot])

    rounds = rows * pairs // 2

    def attend(i):
        pl.when(i + 1 < rounds)(lambda: fetch_probs(i + 1).start())
        fetch_probs(i).wait()
        spot, base = span(i // (pairs // 2), tokens), lax.rem(i, pairs // 2) * 2
        for p in range(2):
            cols = span(base + p, head_pair)
            query, keys, values, mixed_grad = (pool[e, spot, cols] for e in (2, 3, 6, 1))
            query_grad = key_grad = value_grad = None
            for h, mask in enumerate(masks):
                own_keys = keys * (mask * jnp.asarray(scale, bf16))
                low = held_probs[lax.rem(i, 2), 2 * p + h]
                prob = low.astype(f32)
                prob_grad = across(values * mask, mixed_grad)
                weighed = prob * prob_grad
                score_grad = (weighed - prob * jnp.sum(weighed, axis=0, keepdims=True)).astype(bf16)
                terms = (
                    down(score_grad, own_keys),
                    dot(score_grad, query * mask),
                    dot(low, mixed_grad * mask),
                )
                if query_grad is None:
                    query_grad, key_grad, value_grad = terms
                else:
                    query_grad, key_grad, value_grad = query_grad + terms[0], key_grad + terms[1], value_grad + terms[2]
            query_grad, value_grad = query_grad.astype(bf16), value_grad.astype(bf16)
            pool[2, spot, cols] = query_grad
            pool[3, spot, cols] = (key_grad * scale).astype(bf16)
            pool[6, spot, cols] = value_grad
            for row, value in ((0, query_grad), (1, value_grad)):
                found = jnp.sum(value.astype(f32), axis=0, keepdims=True)
                total[0, row : row + 1, cols] = total[0, row : row + 1, cols] + found

    items.append((rounds, attend))
    for i, entry in enumerate((6, 2, 3)):
        before = [x_load.wait, sums.start] if i == 0 else []
        produce(2 * blocks + 1 + i, 4, entry, before, [partial(sums.step, i)])

    def input_back(slot, entry, fetched, after):
        fetched.wait()
        hidden[...] = hidden[...] + across(pool[entry], turned(slot))
        after()

    def pass_rows():
        for i in range(pieces):
            to_across(i).wait_recv()
        pass_on.start()

    done = pltpu.make_async_copy(hidden, input_out, hsem)
    items += [
        partial(input_back, 1, 2, query_fetch, value_fetch.start),
        partial(input_back, 0, 3, key_fetch, pass_rows),
        partial(input_back, 1, 6, value_fetch, done.start),
    ]
    drive(BACKWARD_ORDER, items, run)
    sums.finish(small_out)
    done.wait()

    for m in range(count):
        scatter.drain(m)
    here.wait()
    to_sibling.wait()
    for i in range(pieces):
        to_across(i).wait_send()
    pass_on.wait()


def backward(
    x, own_up, across_up, final, unit, inverse1, inverse2, small_full, act, slope, saved, g, probs, nz, nx, tokens
):
    f32, bf16 = jnp.float32, jnp.bfloat16
    count, _, _, _, _, shard_rows, width = g.shape
    acts = x.shape
    parts = [column_parts(width, s) for s in SCATTER_SHARES]
    vmem, anywhere = pl.BlockSpec(memory_space=pltpu.VMEM), pl.BlockSpec(memory_space=pl.ANY)
    dma = pltpu.SemaphoreType.DMA
    out = jax.ShapeDtypeStruct
    block = (2, 2, nz, nx, shard_rows, width)
    return pl.pallas_call(
        partial(backward_kernel, nz, nx, parts, tokens, 2 * width // HEADS),
        out_shape=[
            out((count, shard_rows, width), f32),
            out(small_full.shape, f32),
            out(acts, f32),
            out((2, 2, *acts), bf16),
        ],
        in_specs=[anywhere] * 5 + [vmem] * 3 + [anywhere] * 5,
        out_specs=[vmem, vmem, anywhere, anywhere],
        scratch_shapes=[
            *scatter_scratch(count, nz, nx, shard_rows, width, parts),
            *small_scratch(nz, small_full.shape),
            pltpu.VMEM((2, *block), bf16),
            pltpu.VMEM((2, *block), bf16),
            pltpu.VMEM((7, *acts), bf16),
            pltpu.VMEM(acts, f32),
            dma((count,)),
            dma((18,)),
            dma,
            dma((2,)),
            dma((2,)),
            dma((count,)),
            dma((count,)),
            dma,
            pltpu.VMEM((2, 4, tokens, tokens), bf16),
            dma((2,)),
        ],
        compiler_params=pltpu.CompilerParams(
            collective_id=2, has_side_effects=True, vmem_limit_bytes=63 * 2**20
        ),
    )(x, own_up, across_up, final, unit, inverse1, inverse2, small_full, act, slope, saved, g, probs)


def finish_kernel(
    slot_row, live_count, me, table, full, sums, small_sums,
    slot_acts, input_grad, query, keys, values, output, up, contract, *small,
):
    s = pl.program_id(0)
    slot_acts[...] = table[...]
    input_grad[...] = jnp.where(s // 2 < live_count[0], full[...], 0.0)

    @pl.when(s == 0)
    def _():
        blocks = (sums.shape[0] - 4) // 2
        shard, width = query.shape
        for j in range(blocks):
            contract[j * shard : (j + 1) * shard, :] = sums[j]
        lanes = 128
        per = lanes // shard
        for q in range(width // lanes):
            part = [sums[blocks + j, :, q * lanes : (q + 1) * lanes] for j in range(blocks)]
            for t in range(per):
                found = jnp.concatenate([p[:, t * shard : (t + 1) * shard] for p in part], axis=1)
                at = (q * per + t) * blocks * shard
                up[:, at : at + blocks * shard] = found
        for i, ref in enumerate((output, values, query, keys)):
            ref[...] = sums[2 * blocks + i]
        own = pltpu.roll(small_sums[...], width - me[0] * shard, 1)
        for i in range(8):
            small[i][...] = own[i, :shard]
        small[8][...] = jnp.concatenate([own[8 + j : 9 + j, :shard] for j in range(blocks)], axis=1)[0]


def finish(slot_row, live_count, table, full, sums, small_sums):
    f32 = jnp.float32
    members, tokens, width = table.shape
    slots, rows = slot_row.shape[0], full.shape[0]
    assert slots == 2 * rows
    count, shard, _ = sums.shape
    blocks = (count - 4) // 2
    me = lax.axis_index(("dp", "fsdp")).astype(jnp.int32).reshape(1)
    block, half = (1, tokens, width), (1, tokens // 2, width)

    def fixed(shape):
        return pl.BlockSpec(shape, lambda s, *_: (0,) * len(shape))

    fixed_outs = [(shard, width)] * 4 + [(shard, blocks * width), (blocks * shard, width)]
    fixed_outs += [(shard,)] * 8 + [(blocks * shard,)]
    row_half = pl.BlockSpec(half, lambda s, *_: (s // 2, lax.rem(s, 2), 0))
    out = jax.ShapeDtypeStruct
    return pl.pallas_call(
        finish_kernel,
        out_shape=[
            out((slots, tokens, width), table.dtype),
            out(full.shape, f32),
            *(out(shape, f32) for shape in fixed_outs),
        ],
        grid_spec=pltpu.PrefetchScalarGridSpec(
            num_scalar_prefetch=3,
            grid=(slots,),
            in_specs=[
                pl.BlockSpec(block, lambda s, slot_row, *_: (jnp.clip(slot_row[s], 0, members - 1), 0, 0)),
                row_half,
                fixed(sums.shape),
                fixed(small_sums.shape),
            ],
            out_specs=[
                pl.BlockSpec(block, lambda s, *_: (s, 0, 0)),
                row_half,
                *(fixed(shape) for shape in fixed_outs),
            ],
        ),
        compiler_params=pltpu.CompilerParams(vmem_limit_bytes=63 * 2**20),
    )(slot_row, live_count, me, table, full, sums, small_sums)


def prepare(slot_row, small_parameters, up_bias, row_count, dp_size):
    shard = small_parameters[0].shape[0]
    rows = [v.reshape(-1, shard) for v in (*small_parameters, up_bias)]
    rows = jnp.concatenate(rows, axis=0).astype(jnp.float32)
    small = jnp.pad(rows, ((0, 16 - rows.shape[0]), (0, 0)))
    wanted = lax.broadcasted_iota(jnp.int32, (row_count * dp_size, slot_row.shape[0]), 0)
    return small, (wanted == slot_row[None, :]).astype(jnp.float32)


def on_device_kernels(
    rows_in,
    slot_row,
    live_count,
    slot_activation_gradient,
    query_weight,
    key_weight,
    value_weight,
    output_weight,
    query_bias,
    value_bias,
    output_bias,
    attn_gain,
    attn_shift,
    expand_weight,
    up_bias,
    down_weight,
    down_bias,
    ffn_gain,
    ffn_shift,
):
    row_count, token_count, width = rows_in.shape
    nx = 2
    nz = lax.axis_size("fsdp") // nx
    small, pick = prepare(
        slot_row,
        (query_bias, value_bias, output_bias, attn_gain, attn_shift, down_bias, ffn_gain, ffn_shift),
        up_bias,
        row_count,
        lax.axis_size("dp"),
    )
    x = rows_in.reshape(-1, width)
    g, probs, saved, act, slope, unit, final, own_up, across_up, small_full, inverse1, inverse2 = forward(
        x,
        [query_weight, key_weight, value_weight, output_weight],
        expand_weight,
        down_weight,
        small,
        pick,
        slot_activation_gradient,
        nz,
        nx,
        token_count,
    )
    sums, small_sums, input_full, table = backward(
        x,
        own_up,
        across_up,
        final,
        unit,
        inverse1,
        inverse2,
        small_full,
        act,
        slope,
        saved,
        g,
        probs,
        nz,
        nx,
        token_count,
    )
    slot_acts, input_grad, query, keys, values, output, up, contract, *small_grads = finish(
        slot_row,
        live_count,
        table.reshape(-1, token_count, width),
        input_full.reshape(rows_in.shape),
        sums,
        small_sums,
    )
    return (
        slot_acts,
        input_grad,
        query,
        keys,
        values,
        output,
        *small_grads[:5],
        up,
        small_grads[8],
        contract,
        *small_grads[5:8],
    )


def norm_forward(hidden, gain, shift):
    center = hidden - jnp.mean(hidden, axis=-1, keepdims=True)
    inverse = lax.rsqrt(jnp.mean(center * center, axis=-1, keepdims=True) + EPSILON)
    normed = center * inverse
    return (normed * gain + shift, normed, inverse)


def norm_backward(incoming, gain, normed, inverse):
    scaled = incoming * gain
    inner = (
        scaled
        - jnp.mean(scaled, axis=-1, keepdims=True)
        - normed * jnp.mean(scaled * normed, axis=-1, keepdims=True)
    )
    return (
        inner * inverse,
        jnp.sum(incoming * normed, axis=(0, 1)),
        jnp.sum(incoming, axis=(0, 1)),
    )


def apply_weight(acts, weight):
    return jnp.einsum("rsd,de->rse", acts, weight, preferred_element_type=jnp.float32)


def apply_back(grads, weight):
    return jnp.einsum("rse,de->rsd", grads, weight, preferred_element_type=jnp.float32)


def weight_term(acts, grads):
    return jnp.einsum("rsd,rse->de", acts, grads, preferred_element_type=jnp.float32)


def bias_term(grads):
    return jnp.sum(grads, axis=(0, 1), dtype=jnp.float32)


def on_device_plain(
    rows_in,
    slot_row,
    live_count,
    slot_activation_gradient,
    query_weight,
    key_weight,
    value_weight,
    output_weight,
    query_bias,
    value_bias,
    output_bias,
    attn_gain,
    attn_shift,
    expand_weight,
    up_bias,
    down_weight,
    down_bias,
    ffn_gain,
    ffn_shift,
):
    row_count, token_count, feature_count = rows_in.shape
    head_size = feature_count // HEADS
    score_scale = head_size ** (-0.5)
    split_shape = (row_count, token_count, HEADS, head_size)
    wanted = lax.broadcasted_iota(
        jnp.int32, (row_count * lax.axis_size("dp"), slot_row.shape[0]), 0
    )
    one_hot_matrix = (wanted == slot_row[None, :]).astype(jnp.bfloat16)
    upstream = lax.psum_scatter(
        jnp.einsum(
            "az,zfy->afy",
            one_hot_matrix,
            slot_activation_gradient,
            preferred_element_type=jnp.float32,
        ).astype(jnp.bfloat16),
        "dp",
        scatter_dimension=0,
        tiled=True,
    ).astype(jnp.float32)
    smalls = (query_bias, value_bias, output_bias, attn_gain, attn_shift, down_bias, ffn_gain, ffn_shift)
    small_rows = query_bias.shape[0]
    packed = jnp.concatenate([v.reshape(-1, small_rows) for v in (*smalls, up_bias)], axis=0)
    packed_full = lax.all_gather(packed, ("dp", "fsdp"), axis=0)
    (
        qbias_full,
        vbias_full,
        obias_full,
        gain1_full,
        shift1_full,
        downbias_full,
        gain2_full,
        shift2_full,
    ) = (packed_full[:, i].reshape(-1) for i in range(8))
    upbias_full = packed_full[:, 8:].reshape(-1)
    query_full, key_full, value_full, output_full, up_full, down_full = (
        lax.all_gather(weight, ("dp", "fsdp"), axis=0, tiled=True)
        for weight in (query_weight, key_weight, value_weight, output_weight, expand_weight, down_weight)
    )
    inputs = rows_in.astype(jnp.float32)
    query = (apply_weight(rows_in, query_full) + qbias_full.astype(jnp.float32)).astype(
        jnp.bfloat16
    )
    keys = apply_weight(rows_in, key_full).astype(jnp.bfloat16)
    values = (apply_weight(rows_in, value_full) + vbias_full.astype(jnp.float32)).astype(
        jnp.bfloat16
    )
    query_heads = query.reshape(split_shape)
    key_heads = keys.reshape(split_shape)
    value_heads = values.reshape(split_shape)
    scores = (
        jnp.einsum("rqhd,rkhd->rhqk", query_heads, key_heads, preferred_element_type=jnp.float32)
        * score_scale
    )
    row_top = jnp.max(scores, axis=-1, keepdims=True)
    expo = jnp.exp(scores - row_top)
    row_sum = jnp.sum(expo, axis=-1, keepdims=True)
    logsum = row_top + jnp.log(row_sum)
    probs_low = (expo / row_sum).astype(jnp.bfloat16)
    mixed = jnp.einsum(
        "rhqk,rkhd->rqhd", probs_low, value_heads, preferred_element_type=jnp.float32
    )
    mixed = mixed.reshape(row_count, token_count, feature_count).astype(jnp.bfloat16)
    gain1 = gain1_full.astype(jnp.float32)
    resid1 = inputs + apply_weight(mixed, output_full) + obias_full.astype(jnp.float32)
    normed1_out, normed1, inverse1 = norm_forward(resid1, gain1, shift1_full.astype(jnp.float32))
    normed1_low = normed1_out.astype(jnp.bfloat16)
    pre_act = apply_weight(normed1_low, up_full) + upbias_full.astype(jnp.float32)
    act_low = jax.nn.gelu(pre_act, approximate=False).astype(jnp.bfloat16)
    gain2 = gain2_full.astype(jnp.float32)
    resid2 = normed1_out + apply_weight(act_low, down_full) + downbias_full.astype(jnp.float32)
    final, second_normed, inverse2 = norm_forward(resid2, gain2, shift2_full.astype(jnp.float32))
    final_low = final.astype(jnp.bfloat16)
    shard_rows = lax.all_gather(final_low, "dp", axis=0, tiled=True)
    span_rows = shard_rows.shape[0]
    inside = (slot_row >= 0) & (slot_row < span_rows)
    picked = jnp.take(shard_rows, jnp.clip(slot_row, 0, span_rows - 1), axis=0)
    slot_acts = jnp.where(
        inside[:, None, None], picked, jnp.zeros(slot_activation_gradient.shape, jnp.bfloat16)
    )
    gain1 = gain1_full.astype(jnp.float32)
    gain2 = gain2_full.astype(jnp.float32)
    grad2, gain2_grad, shift2_grad = norm_backward(upstream, gain2, second_normed, inverse2)
    ffn_low = grad2.astype(jnp.bfloat16)
    down_grad = weight_term(act_low, ffn_low)
    down_bias_grad = bias_term(ffn_low)
    act_grad = apply_back(ffn_low, down_full)
    gelu_value, gelu_back = jax.vjp(partial(jax.nn.gelu, approximate=False), pre_act)
    pre_grad = gelu_back(act_grad)[0].astype(jnp.bfloat16)
    up_grad = weight_term(normed1_low, pre_grad)
    up_bias_grad = bias_term(pre_grad)
    normed1_grad = grad2 + apply_back(pre_grad, up_full)
    grad1, gain1_grad, shift1_grad = norm_backward(normed1_grad, gain1, normed1, inverse1)
    attn_low = grad1.astype(jnp.bfloat16)
    output_grad = weight_term(mixed, attn_low)
    output_bias_grad = bias_term(attn_low)
    mixed_grad = apply_back(attn_low, output_full).astype(jnp.bfloat16).reshape(split_shape)
    scores_again = (
        jnp.einsum("rqhd,rkhd->rhqk", query_heads, key_heads, preferred_element_type=jnp.float32)
        * score_scale
    )
    probs = jnp.exp(scores_again - logsum)
    probs_again = probs.astype(jnp.bfloat16)
    value_grad = jnp.einsum(
        "rhqk,rqhd->rkhd", probs_again, mixed_grad, preferred_element_type=jnp.float32
    )
    value_grad = value_grad.astype(jnp.bfloat16).reshape(row_count, token_count, feature_count)
    prob_grad = jnp.einsum(
        "rqhd,rkhd->rhqk", mixed_grad, value_heads, preferred_element_type=jnp.float32
    )
    score_grad = (probs * (prob_grad - jnp.sum(probs * prob_grad, axis=-1, keepdims=True))).astype(
        jnp.bfloat16
    )
    query_grad = (
        jnp.einsum("rhqk,rkhd->rqhd", score_grad, key_heads, preferred_element_type=jnp.float32)
        * score_scale
    )
    query_grad = query_grad.astype(jnp.bfloat16).reshape(row_count, token_count, feature_count)
    key_grad = (
        jnp.einsum("rhqk,rqhd->rkhd", score_grad, query_heads, preferred_element_type=jnp.float32)
        * score_scale
    )
    key_grad = key_grad.astype(jnp.bfloat16).reshape(row_count, token_count, feature_count)
    query_wgrad = weight_term(rows_in, query_grad)
    key_wgrad = weight_term(rows_in, key_grad)
    value_wgrad = weight_term(rows_in, value_grad)
    query_bias_grad = bias_term(query_grad)
    value_bias_grad = bias_term(value_grad)
    input_full = (
        grad1
        + apply_back(query_grad, query_full)
        + apply_back(key_grad, key_full)
        + apply_back(value_grad, value_full)
    )
    live_rows = lax.broadcasted_iota(jnp.int32, (row_count,), 0) < live_count[0]
    input_grad = jnp.where(live_rows[:, None, None], input_full, 0.0)
    devices = packed_full.shape[0]
    small_terms = jnp.concatenate(
        [
            v.reshape(devices, -1, small_rows)
            for v in (
                query_bias_grad,
                value_bias_grad,
                output_bias_grad,
                gain1_grad,
                shift1_grad,
                down_bias_grad,
                gain2_grad,
                shift2_grad,
                up_bias_grad,
            )
        ],
        axis=1,
    )
    small_sum = lax.psum_scatter(small_terms, ("dp", "fsdp"), scatter_dimension=0, tiled=True)[0]
    down_sum, up_sum, output_sum, value_sum, query_sum, key_sum = (
        lax.psum_scatter(
            term.astype(jnp.bfloat16), ("dp", "fsdp"), scatter_dimension=0, tiled=True
        ).astype(jnp.float32)
        for term in (down_grad, up_grad, output_grad, value_wgrad, query_wgrad, key_wgrad)
    )
    return (
        slot_acts,
        input_grad,
        query_sum,
        key_sum,
        value_sum,
        output_sum,
        small_sum[0],
        small_sum[1],
        small_sum[2],
        small_sum[3],
        small_sum[4],
        up_sum,
        small_sum[8:].reshape(-1),
        down_sum,
        small_sum[5],
        small_sum[6],
        small_sum[7],
    )


def solution(mesh):
    placed = (
        P(("dp", "fsdp"), None, None),
        P(("dp", "fsdp")),
        P(("dp", "fsdp")),
        P(("dp", "fsdp"), None, None),
        P(("dp", "fsdp"), None),
        P(("dp", "fsdp"), None),
        P(("dp", "fsdp"), None),
        P(("dp", "fsdp"), None),
        P(("dp", "fsdp")),
        P(("dp", "fsdp")),
        P(("dp", "fsdp")),
        P(("dp", "fsdp")),
        P(("dp", "fsdp")),
        P(("dp", "fsdp"), None),
        P(("dp", "fsdp")),
        P(("dp", "fsdp"), None),
        P(("dp", "fsdp")),
        P(("dp", "fsdp")),
        P(("dp", "fsdp")),
    )
    kernels = mesh.shape["dp"] == 4 and mesh.shape["fsdp"] == 8
    return jax.shard_map(
        on_device_kernels if kernels else on_device_plain,
        mesh=mesh,
        in_specs=placed,
        out_specs=(
            P(("dp", "fsdp"), None, None),
            P(("dp", "fsdp"), None, None),
            P(("dp", "fsdp"), None),
            P(("dp", "fsdp"), None),
            P(("dp", "fsdp"), None),
            P(("dp", "fsdp"), None),
            P(("dp", "fsdp")),
            P(("dp", "fsdp")),
            P(("dp", "fsdp")),
            P(("dp", "fsdp")),
            P(("dp", "fsdp")),
            P(("dp", "fsdp"), None),
            P(("dp", "fsdp")),
            P(("dp", "fsdp"), None),
            P(("dp", "fsdp")),
            P(("dp", "fsdp")),
            P(("dp", "fsdp")),
        ),
        check_vma=False,
    )
```

```python
import math
from functools import partial

import jax
import jax.numpy as jnp
from jax import lax
from jax.experimental import pallas as pl
from jax.experimental.pallas import tpu as pltpu
from jax.sharding import PartitionSpec as P

HEADS = 16


EPSILON = 1e-05


MESH = pl.DeviceIdType.MESH
LANES = 128


def place(nz, nx):
    dp, fs = lax.axis_index("dp"), lax.axis_index("fsdp")
    y, core = dp // 2, lax.rem(dp, 2)
    z, x = fs // nx, lax.rem(fs, nx)
    return y, core, z, x


def device(y, core, z, x, nx):
    return (y * 2 + core, z * nx + x)


class Partners:
    def __init__(self, nz, nx):
        self.nz, self.nx = nz, nx
        self.y, self.core, self.z, self.x = place(nz, nx)
        y, core, z, x = self.y, self.core, self.z, self.x
        self.sibling = device(y, 1 - core, z, x, nx)
        self.across_x = device(y, core, z, 1 - x, nx)
        self.across_y = device(1 - y, core, z, x, nx)
        self.along_z = [device(y, core, lax.rem(z + k, nz), x, nx) for k in range(1, nz)]
        self.all = [self.sibling, self.across_x, self.across_y, *self.along_z]

    def meet(self):
        barrier = pltpu.get_barrier_semaphore()
        for other in self.all:
            pl.semaphore_signal(barrier, inc=1, device_id=other, device_id_type=MESH)
        pl.semaphore_wait(barrier, len(self.all))


def remote(src, dst, send, recv, to):
    return pltpu.make_async_remote_copy(
        src_ref=src, dst_ref=dst, send_sem=send, recv_sem=recv, device_id=to, device_id_type=MESH
    )


def added(*blocks):
    total = blocks[0].astype(jnp.float32)
    for block in blocks[1:]:
        total = total + block.astype(jnp.float32)
    return total


class Scatter:
    def __init__(self, at, parts, rc, r3a, r3b, r2, rz, rcz, rcx, rcy, send, recv):
        self.at, self.parts = at, parts
        self.rc, self.r3a, self.r3b, self.r2, self.rz = rc, r3a, r3b, r2, rz
        self.rcz, self.rcx, self.rcy = rcz, rcx, rcy
        self.send, self.recv = send, recv

    def copy(self, m, i, src, dst, to):
        return remote(src, dst, self.send.at[m, i], self.recv.at[m, i], to)

    def to_sibling(self, m, theirs):
        return self.copy(m, 0, theirs, self.rc.at[m], self.at.sibling)

    def landings(self, m):
        a, b, c, _ = self.parts[m]
        a, b, c = (pl.ds(0, part.size) for part in (a, b, c))
        return (
            self.r3a.at[m, :, :, :, a],
            self.r3b.at[m, :, :, :, b],
            self.rcz.at[m, :, :, :, :, c],
            self.rcx.at[m, :, :, c],
            self.rcy.at[m, :, c],
        )

    def firsts(self, m):
        at, rc, nz = self.at, self.rc, self.at.nz
        a, b, c, _ = self.parts[m]
        r3a, r3b, rcz, _, _ = self.landings(m)
        return [
            self.copy(m, 1, rc.at[m, :, :, 1 - at.x, :, a], r3a, at.across_x),
            self.copy(m, 2, rc.at[m, 1 - at.y, :, :, :, b], r3b, at.across_y),
        ] + [
            self.copy(
                m, 2 + k, rc.at[m, :, lax.rem(at.z + k, nz), :, :, c], rcz.at[k - 1], at.along_z[k - 1]
            )
            for k in range(1, nz)
        ]

    def seconds(self, m):
        at, nz = self.at, self.at.nz
        a, b, _, _ = self.parts[m]
        r3a, r3b, rcz, rcx, _ = self.landings(m)
        return [
            self.copy(m, nz + 2, r3a.at[1 - at.y], self.r2.at[m, :, :, a], at.across_y),
            self.copy(m, nz + 3, r3b.at[:, 1 - at.x], self.r2.at[m, :, :, b], at.across_x),
            self.copy(m, nz + 4, rcz.at[0, :, 1 - at.x], rcx, at.across_x),
        ]

    def thirds(self, m):
        at, nz = self.at, self.at.nz
        ab = self.parts[m][3]
        rcx, rcy = self.landings(m)[3:]
        return [
            self.copy(
                m,
                nz + 4 + k,
                self.r2.at[m, lax.rem(at.z + k, nz), :, ab],
                self.rz.at[m, k - 1, :, ab],
                at.along_z[k - 1],
            )
            for k in range(1, nz)
        ] + [self.copy(m, 2 * nz + 4, rcx.at[1 - at.y], rcy, at.across_y)]

    def start(self, m, theirs):
        self.to_sibling(m, theirs).start()

    def step1(self, m, own):
        rc = self.rc
        self.to_sibling(m, rc.at[m]).wait_recv()

        rc[m] = added(rc[m], own).astype(rc.dtype)
        self.to_sibling(m, rc.at[m]).wait_send()
        for copy in self.firsts(m):
            copy.start()

    def step2(self, m):
        at, rc = self.at, self.rc
        a, b, c, _ = self.parts[m]
        r3a, r3b, rcz, _, _ = self.landings(m)
        for copy in self.firsts(m):
            copy.wait_recv()

        r3a[...] = added(r3a[...], rc[m, :, :, at.x, :, a]).astype(rc.dtype)
        r3b[...] = added(r3b[...], rc[m, at.y, :, :, :, b]).astype(rc.dtype)
        others = [rcz[k] for k in range(at.nz - 1)]
        rcz[0] = added(rc[m, :, at.z, :, :, c], *others).astype(rc.dtype)
        for copy in self.seconds(m):
            copy.start()

    def step3(self, m):
        at, r2 = self.at, self.r2
        a, b, _, _ = self.parts[m]
        r3a, r3b, rcz, rcx, _ = self.landings(m)
        for copy in self.seconds(m):
            copy.wait_recv()

        r2[m, :, :, a] = added(r2[m, :, :, a], r3a[at.y]).astype(r2.dtype)
        r2[m, :, :, b] = added(r2[m, :, :, b], r3b[:, at.x]).astype(r2.dtype)
        rcx[...] = added(rcx[...], rcz[0, :, at.x]).astype(r2.dtype)
        for copy in self.thirds(m):
            copy.start()

    def step4(self, m, out):
        at = self.at
        _, _, c, ab = self.parts[m]
        rcx, rcy = self.landings(m)[3:]
        for copy in self.thirds(m):
            copy.wait_recv()
        others = [self.rz[m, k, :, ab] for k in range(at.nz - 1)]
        out[m, :, ab] = added(self.r2[m, at.z, :, ab], *others)
        out[m, :, c] = added(rcx[at.y], rcy[...])

    def drain(self, m):
        for copy in self.firsts(m) + self.seconds(m) + self.thirds(m):
            copy.wait_send()


class SmallSum:
    def __init__(self, at, total, landing, send, recv):
        self.at, self.total, self.landing, self.send, self.recv = at, total, landing, send, recv

    def hop(self, i, to):
        return remote(self.total.at[i], self.landing.at[i], self.send.at[i], self.recv.at[i], to)

    def along(self, k):
        i = 2 + k
        return remote(self.total.at[3], self.landing.at[i], self.send.at[i], self.recv.at[i], self.at.along_z[k - 1])

    def start(self):
        self.hop(0, self.at.sibling).start()

    def step(self, i):
        at = self.at
        to = (at.sibling, at.across_x, at.across_y)
        self.hop(i, to[i]).wait_recv()
        self.total[i + 1] = self.total[i] + self.landing[i]
        if i < 2:
            self.hop(i + 1, to[i + 1]).start()
        else:
            for k in range(1, at.nz):
                self.along(k).start()

    def finish(self, out):
        at = self.at
        for k in range(1, at.nz):
            self.along(k).wait_recv()
        total = self.total[3]
        for k in range(1, at.nz):
            total = total + self.landing[2 + k]
        out[...] = total
        to = (at.sibling, at.across_x, at.across_y)
        for i in range(3):
            self.hop(i, to[i]).wait_send()
        for k in range(1, at.nz):
            self.along(k).wait_send()


def scatter_scratch(count, nz, nx, rows, columns, parts):
    bf16 = jnp.bfloat16
    a, b, c = (max(part[i].size for part in parts) for i in range(3))
    return [
        pltpu.VMEM((count, 2, nz, nx, rows, columns), bf16),
        pltpu.VMEM((count, 2, nz, rows, a), bf16),
        pltpu.VMEM((count, nz, nx, rows, b), bf16),
        pltpu.VMEM((count, nz, rows, columns), bf16),
        pltpu.VMEM((count, nz - 1, rows, columns), bf16),
        pltpu.VMEM((count, nz - 1, 2, nx, rows, c), bf16),
        pltpu.VMEM((count, 2, rows, c), bf16),
        pltpu.VMEM((count, rows, c), bf16),
        pltpu.SemaphoreType.DMA((count, 2 * nz + 5)),
        pltpu.SemaphoreType.DMA((count, 2 * nz + 5)),
    ]


def small_scratch(nz, shape):
    return [
        pltpu.VMEM((4, *shape), jnp.float32),
        pltpu.VMEM((2 + nz, *shape), jnp.float32),
        pltpu.SemaphoreType.DMA((2 + nz,)),
        pltpu.SemaphoreType.DMA((2 + nz,)),
    ]


GATHER_SHARES = [
    (6, 1), (4, 2), (6, 1), (3, 4), (6, 1), (4, 3), (3, 4), (5, 1), (5, 1), (6, 1), (4, 2), (5, 1),
]
SCATTER_SHARES = [
    (5, 1), (4, 2), (6, 1), (4, 2), (4, 2), (4, 2), (5, 2), (6, 1), (6, 1), (5, 2), (4, 3), (3, 3),
]

FORWARD_ORDER = (
    100, 101, 102, 103, 0, 0, 104, 105, 0, 0, 0, 0, 200, 0, 201, 500, 300, 202, 301, 203, 302, 204, 205, 501,
    303, 400, 106, 0, 401, 107, 502, 304, 0, 402, 108, 305, 0, 403, 109, 503, 0, 206, 0, 0, 504, 0, 207, 0, 0,
    0, 404, 110, 0, 505, 0, 0, 208, 0, 306, 0, 405, 111, 0, 307, 0, 209, 0, 308, 210, 0, 406, 211, 0, 309, 407,
    506, 310, 0, 311, 408, 507, 0, 409, 508, 509, 410, 0, 510, 0, 411, 511, 0, 0,
)
BACKWARD_ORDER = (
    500, 0, 501, 0, 502, 0, 0, 503, 0, 100, 0, 0, 101, 0, 0, 504, 102, 0, 0, 103, 200, 0, 0, 0, 201, 104, 0, 0,
    505, 0, 0, 202, 105, 0, 203, 0, 300, 0, 301, 0, 106, 0, 204, 302, 0, 506, 0, 400, 0, 107, 205, 401, 303, 0,
    507, 0, 0, 508, 0, 206, 108, 402, 304, 0, 0, 0, 509, 0, 0, 403, 0, 207, 0, 305, 0, 306, 0, 510, 0, 404, 0,
    511, 0, 0, 0, 405, 208, 307, 0, 109, 0, 406, 0, 110, 0, 0, 111, 308, 407, 0, 209, 0, 210, 211, 309, 310,
    408, 311, 409, 410, 411,
)


def drive(order, items, run):
    todo = list(order)
    for item in items:
        while todo[0]:
            run(todo.pop(0))
        if callable(item):
            todo.pop(0)
            item()
            continue
        rounds, body = item
        between = []
        for _ in range(rounds):
            codes = []
            while todo[0]:
                codes.append(todo.pop(0))
            todo.pop(0)
            between.append(codes)

        def one(i, carry):
            for r, codes in enumerate(between):
                if codes:

                    @pl.when(i == r)
                    def _(codes=codes):
                        for code in codes:
                            run(code)

            body(i)
            return carry

        lax.fori_loop(0, rounds, one, 0)
    for code in todo:
        run(code)


def exact_gelu(pre):
    half = 0.5 + 0.5 * lax.erf(pre * (0.5**0.5))
    bell = jnp.exp(-0.5 * pre * pre) * ((0.5 / math.pi) ** 0.5)
    return pre * half, half + pre * bell


def rms_center(hidden):
    center = hidden - jnp.mean(hidden, axis=-1, keepdims=True)
    inverse = lax.rsqrt(jnp.mean(center * center, axis=-1, keepdims=True) + EPSILON)
    return center * inverse, inverse


def half_masks(width):
    left = (lax.broadcasted_iota(jnp.int32, (1, width), 1) < width // 2).astype(jnp.float32)
    return left.astype(jnp.bfloat16), (1.0 - left).astype(jnp.bfloat16)


def across(left, right):
    return lax.dot_general(left, right, (((1,), (1,)), ((), ())), preferred_element_type=jnp.float32)


def down(left, right):
    return lax.dot_general(left, right, (((0,), (0,)), ((), ())), preferred_element_type=jnp.float32)


def dot(left, right):
    return jnp.dot(left, right, preferred_element_type=jnp.float32)


def span(i, size):
    return pl.ds(pl.multiple_of(i * size, size), size)


class Gather:
    def __init__(self, at, parts, count, shards, g, send, recv):
        self.at, self.count, self.shards, self.g, self.send, self.recv = at, count, shards, g, send, recv
        self.parts = parts

    def copy(self, m, i, src, dst, to):
        return remote(src, dst, self.send.at[m, i], self.recv.at[m, i], to)

    def same(self, m, i, part, to):
        return self.copy(m, i, part, part, to)

    def stages(self, m):
        at, g, nz = self.at, self.g, self.at.nz
        a, b, c, ab = self.parts[m]
        y, core, z, x = at.y, at.core, at.z, at.x
        across_x, across_y, along_z = at.across_x, at.across_y, at.along_z
        first = [
            self.copy(m, k, self.shards.at[m, :, ab], g.at[m, y, core, z, x, :, ab], along_z[k])
            for k in range(nz - 1)
        ]
        first.append(self.copy(m, nz - 1, self.shards.at[m, :, c], g.at[m, y, core, z, x, :, c], across_y))
        second = [
            self.same(m, nz, g.at[m, y, core, :, x, :, a], across_y),
            self.same(m, nz + 1, g.at[m, y, core, :, x, :, b], across_x),
            self.same(m, nz + 2, g.at[m, :, core, z, x, :, c], across_x),
        ]
        third = [
            self.same(m, nz + 3, g.at[m, :, core, :, x, :, a], across_x),
            self.same(m, nz + 4, g.at[m, y, core, :, :, :, b], across_y),
        ]
        third += [self.same(m, nz + 5 + k, g.at[m, :, core, z, :, :, c], along_z[k]) for k in range(nz - 1)]
        return first, second, third, [self.same(m, 2 * nz + 4, g.at[m, :, core], at.sibling)]

    def step0(self, m):
        at = self.at
        for copy in self.stages(m)[0]:
            copy.start()
        self.g[m, at.y, at.core, at.z, at.x] = self.shards[m]

    def follow(self, stage, m):
        stages = self.stages(m)
        for copy in stages[stage - 1]:
            copy.wait_recv()
        for copy in stages[stage]:
            copy.start()

    def step1(self, m):
        self.follow(1, m)

    def step2(self, m):
        self.follow(2, m)

    def step3(self, m):
        self.follow(3, m)

    def arrive(self, m):
        self.stages(m)[3][0].wait_recv()

    def drain(self, m):
        for stage in self.stages(m):
            for copy in stage:
                copy.wait_send()


def column_parts(width, shares):
    lanes = 128
    a, b = (share * lanes for share in shares)
    return pl.ds(0, a), pl.ds(a, b), pl.ds(a + b, width - a - b), pl.ds(0, a + b)


UP_TILE = 256
NORM_ROWS = 192


def forward_kernel(
    nz, nx, parts, tokens, head_pair,
    x, attention_weights, expand, contract, small, slot_row, slots,
    g_out, probs_out, saved, act_out, slope_out, unit_out, final_out, own_out, across_out, small_full, inverse1, inverse2,
    g, shards, pool, hidden, landed, total, landing,
    send, recv, ssend, srecv, usend, urecv, across_send, across_recv, isem, gsem, vsem, asem, dsem, fsem, held_probs, ksem,
):
    f32, bf16 = jnp.float32, jnp.bfloat16
    count = g.shape[0]
    all_rows, width = x.shape
    rows = all_rows // tokens
    at = Partners(nz, nx)
    at.meet()
    gather = Gather(at, parts, count, shards, g, send, recv)
    sums = SmallSum(at, total, landing, ssend, srecv)
    groups = slots.shape[0] // rows

    def fetch(i):
        return pltpu.make_async_copy(slots.at[i], pool.at[i // rows, pl.ds((i % rows) * tokens, tokens)], isem.at[i])

    shard = shards.shape[1]
    lane = lax.broadcasted_iota(jnp.int32, (1, width), 1)
    mine = lane // shard == lax.axis_index("dp") * (nz * nx) + lax.axis_index("fsdp")
    own = [ref[...].astype(f32).reshape(1, -1) for ref in small]
    own = own[:-1] + [own[-1][:, i : i + shard] for i in range(0, own[-1].shape[1], shard)]
    own += [jnp.zeros((1, shard), f32)] * (total.shape[1] - len(own))
    own = jnp.concatenate(own, axis=0)
    total[0] = jnp.where(mine, jnp.concatenate([own] * (width // shard), axis=1), 0.0)
    sums.start()
    for m in range(4):
        shards[m] = attention_weights[m][...]
    for i in range(slots.shape[0]):
        fetch(i).start()

    high, part = 32, width // 2

    chosen = [
        [jnp.where(slot_row[s] == t, 1.0, 0.0) for s in range(slots.shape[0])] for t in range(2 * 2 * rows)
    ]

    def sum_slots(i, carry):
        cols = span(lax.rem(i, 2), part)
        base = i // 2 * high
        held = [
            pool[s // rows, pl.ds(pl.multiple_of(base + (s % rows) * tokens, high), high), cols].astype(f32)
            for s in range(slots.shape[0])
        ]
        for t in range(2 * 2 * rows):
            picked = chosen[t][0] * held[0]
            for s in range(1, slots.shape[0]):
                picked = picked + chosen[t][s] * held[s]
            spot = pl.ds(pl.multiple_of(base + (t % rows) * tokens, high), high)
            pool[groups + t // rows, spot, cols] = picked.astype(bf16)
        return carry

    def up_sibling(y):
        src = pool.at[groups + y * 2 + 1 - at.core]
        return remote(src, landed.at[y], usend.at[y], urecv.at[y], at.sibling)

    pieces = across_send.shape[0]

    def up_across(i):
        piece = pl.ds(i * (all_rows // pieces), all_rows // pieces)
        return remote(
            landed.at[1 - at.y, piece], across_out.at[piece], across_send.at[i], across_recv.at[i], at.across_y
        )

    up_own = pltpu.make_async_copy(landed.at[at.y], own_out, isem.at[slots.shape[0]])

    steps = tokens // high * 2

    def quarter(i):
        if i == 0:
            for s in range(slots.shape[0]):
                fetch(s).wait()
        lax.fori_loop(i * steps // 4, (i + 1) * steps // 4, sum_slots, 0)
        if i != 2:
            sums.step((0, 1, None, 2)[i])

    blocks = (count - 4) // 2

    def arrange():
        for j in range(blocks):
            shards[5 + 2 * j] = contract[j * shard : (j + 1) * shard, :]
        lanes = 128
        per = lanes // shard
        for q in range(width // lanes):
            natural = expand[:, q * lanes * blocks : (q + 1) * lanes * blocks].astype(f32)
            for j in range(blocks):
                starts = [t * blocks * shard + j * shard for t in range(per)]
                found = [natural[:, start : start + shard] for start in starts]
                shards[4 + 2 * j, :, q * lanes : (q + 1) * lanes] = jnp.concatenate(found, axis=1).astype(bf16)

    def exchange_cores():
        for y in range(2):
            up_sibling(y).start()

    def chip_sum(i, carry):
        y, spot = i // (all_rows // 192), span(lax.rem(i, all_rows // 192), 192)
        landed[y, spot] = added(landed[y, spot], pool[groups + y * 2 + at.core, spot]).astype(bf16)
        return carry

    def sum_chip():
        for y in range(2):
            up_sibling(y).wait_recv()
        lax.fori_loop(0, 2 * all_rows // 192, chip_sum, 0)
        up_own.start()
        for y in range(2):
            up_sibling(y).wait_send()

    def keep(m):
        return pltpu.make_async_copy(g.at[m], g_out.at[m], gsem.at[m])

    def arrive(m):
        gather.arrive(m)
        keep(m).start()

    def tile(m, cols):
        return g[m, :, :, :, :, :, cols].reshape(width, cols.size)

    def bias(i, cols):
        return small_full[pl.ds(i, 1), cols]

    every = pl.ds(0, all_rows)

    def tiles(size, body):
        def one(i, carry):
            body(span(i, size), every)
            return carry

        if size == width:
            body(pl.ds(0, width), every)
        else:
            lax.fori_loop(0, width // size, one, 0)

    def save(i):
        return pltpu.make_async_copy(pool.at[i], saved.at[i], vsem.at[i])

    def project(m):
        bias_row = (0, None, 1)[m]
        if m == 0:
            sums.finish(small_full)

        def body(cols, spot):
            y = dot(x[spot], tile(m, cols))
            if bias_row is not None:
                y = y + bias(bias_row, cols)
            pool[m, spot, cols] = y.astype(bf16)

        arrive(m)
        tiles(width, body)
        save(m).start()

    pairs = width // head_pair
    masks = half_masks(head_pair)
    scale = (head_pair // 2) ** (-0.5)

    def keep_probs(i):
        slot = lax.rem(i, 2)
        return pltpu.make_async_copy(held_probs.at[slot], probs_out.at[i], ksem.at[slot])

    def attend(i):
        spot, base = span(i // (pairs // 2), tokens), lax.rem(i, pairs // 2) * 2
        pl.when(i >= 2)(lambda: keep_probs(i - 2).wait())
        for p in range(2):
            cols = span(base + p, head_pair)
            query, keys, values = pool[0, spot, cols], pool[1, spot, cols], pool[2, spot, cols]
            query = query * jnp.asarray(scale, bf16)
            out = None
            for h, mask in enumerate(masks):
                scores = across(keys * mask, query)
                probs = jnp.exp(scores - jnp.max(scores, axis=0, keepdims=True))
                probs = (probs * (1.0 / jnp.sum(probs, axis=0, keepdims=True))).astype(bf16)
                held_probs[lax.rem(i, 2), 2 * p + h] = probs
                term = down(probs, values * mask)
                out = term if out is None else out + term
            pool[3, spot, cols] = out.astype(bf16)
        keep_probs(i).start()

    rounds = rows * pairs // 2

    def mix(cols, spot):
        hidden[spot, cols] = dot(pool[3, spot], tile(3, cols)) + x[spot, cols].astype(f32) + bias(2, cols)

    def join():
        save(3).start()
        for i in range(2):
            keep_probs(rounds - 2 + i).wait()
        arrive(3)
        tiles(width, mix)

    def unit(i):
        return pltpu.make_async_copy(pool.at[6], unit_out.at[i], fsem.at[i])

    def norm1(i, carry):
        spot = span(i, NORM_ROWS)
        normed, inverse = rms_center(hidden[spot])
        result = normed * small_full[3:4, :] + small_full[4:5, :]
        hidden[spot] = result
        pool[4, spot] = result.astype(bf16)
        pool[6, spot] = normed.astype(bf16)
        inverse1[spot] = inverse
        return carry

    def first_norm():
        lax.fori_loop(0, all_rows // NORM_ROWS, norm1, 0)
        save(4).start()
        unit(0).start()

    def save_act(j):
        return pltpu.make_async_copy(pool.at[5], act_out.at[j], asem)

    def save_slope(j):
        return pltpu.make_async_copy(pool.at[6], slope_out.at[j], dsem)

    def widen(j):
        m = 4 + 2 * j
        arrive(m)
        if j == 0:
            unit(0).wait()
        else:
            save_act(j - 1).wait()
            save_slope(j - 1).wait()

        def up(cols, spot):
            value, slope = exact_gelu(dot(pool[4, spot], tile(m, cols)) + bias(8 + j, cols))
            pool[5, spot, cols] = value.astype(bf16)
            pool[6, spot, cols] = slope.astype(bf16)

        tiles(UP_TILE, up)
        save_act(j).start()
        save_slope(j).start()

    def narrow(j):
        m = 5 + 2 * j
        arrive(m)

        def back(cols, spot):
            hidden[spot, cols] = hidden[spot, cols] + dot(pool[5, spot], tile(m, cols))

        tiles(width, back)

    def norm2(i, carry):
        spot = span(i, NORM_ROWS)
        normed, inverse = rms_center(hidden[spot] + small_full[5:6, :])
        pool[5, spot] = (normed * small_full[6:7, :] + small_full[7:8, :]).astype(bf16)
        pool[6, spot] = normed.astype(bf16)
        inverse2[spot] = inverse
        return carry

    finish = pltpu.make_async_copy(pool.at[5], final_out, fsem.at[2])

    def second_norm():
        save_act(blocks - 1).wait()
        save_slope(blocks - 1).wait()
        lax.fori_loop(0, all_rows // NORM_ROWS, norm2, 0)
        finish.start()
        unit(1).start()

    def run(code):
        kind, m = divmod(code, 100)
        if kind == 5:
            up_across(m).start()
        else:
            (gather.step0, gather.step1, gather.step2, gather.step3)[kind - 1](m)

    items = [partial(quarter, 0), arrange, *(partial(quarter, i) for i in (1, 2, 3)), exchange_cores, sum_chip]
    items += [partial(project, m) for m in range(3)] + [(rounds, attend), join, first_norm]
    for j in range(blocks):
        items += [partial(widen, j), partial(narrow, j)]
    drive(FORWARD_ORDER, [*items, second_norm], run)
    for m in range(count):
        gather.drain(m)
        keep(m).wait()
    for i in range(5):
        save(i).wait()
    up_own.wait()
    for i in range(pieces):
        up_across(i).wait()
    finish.wait()
    unit(1).wait()


def forward(x, attention_weights, expand, contract, small, slot_row, slots, nz, nx, tokens):
    f32, bf16 = jnp.float32, jnp.bfloat16
    shard_rows, width = attention_weights[0].shape
    count = 4 + 2 * contract.shape[0] // shard_rows
    small_shape = (16, width)
    all_rows = x.shape[0]
    assert slots.shape[0] * tokens == 2 * all_rows
    vmem, anywhere = pl.BlockSpec(memory_space=pltpu.VMEM), pl.BlockSpec(memory_space=pl.ANY)
    acts = (all_rows, width)
    rows = all_rows // tokens
    blocks = (count - 4) // 2
    dma = pltpu.SemaphoreType.DMA
    full = (count, 2, 2, nz, nx, shard_rows, width)
    out = jax.ShapeDtypeStruct
    return pl.pallas_call(
        partial(forward_kernel, nz, nx, [column_parts(width, s) for s in GATHER_SHARES], tokens, 2 * width // HEADS),
        out_shape=[
            out(full, bf16),
            out((rows * HEADS // 4, 4, tokens, tokens), bf16),
            out((5, *acts), bf16),
            out((blocks, *acts), bf16),
            out((blocks, *acts), bf16),
            out((2, *acts), bf16),
            out(acts, bf16),
            out(acts, bf16),
            out(acts, bf16),
            out(small_shape, f32),
            out((all_rows, 1), f32),
            out((all_rows, 1), f32),
        ],
        in_specs=[vmem, [vmem] * 4, vmem, vmem, [vmem] * len(small), pl.BlockSpec(memory_space=pltpu.SMEM), anywhere],
        out_specs=[anywhere] * 9 + [vmem] * 3,
        scratch_shapes=[
            pltpu.VMEM(full, bf16),
            pltpu.VMEM((count, shard_rows, width), bf16),
            pltpu.VMEM((7, *acts), bf16),
            pltpu.VMEM(acts, f32),
            pltpu.VMEM((2, *acts), bf16),
            *small_scratch(nz, small_shape)[:2],
            dma((count, 2 * nz + 5)),
            dma((count, 2 * nz + 5)),
            dma((2 + nz,)),
            dma((2 + nz,)),
            dma((2,)),
            dma((2,)),
            dma((count,)),
            dma((count,)),
            dma((slots.shape[0] + 1,)),
            dma((count,)),
            dma((5,)),
            dma,
            dma,
            dma((3,)),
            pltpu.VMEM((2, 4, tokens, tokens), bf16),
            dma((2,)),
        ],
        compiler_params=pltpu.CompilerParams(
            collective_id=1, has_side_effects=True, vmem_limit_bytes=60 * 2**20
        ),
    )(x, attention_weights, expand, contract, small, slot_row, slots)


def backward_kernel(
    nz, nx, parts, tokens, head_pair,
    x, own_up, across_up, final, unit, inverse1, inverse2, small_full, act, slope, saved, g, probs,
    out, small_out, input_out, table,
    rc, r3a, r3b, r2, rz, rcz, rcx, rcy, send, recv, total, landing, ssend, srecv,
    term, weight, pool, hidden, wsem, psem, hsem, tsend, trecv, across_send, across_recv, tsem, held_probs, ksem,
):
    f32, bf16 = jnp.float32, jnp.bfloat16
    count = out.shape[0]
    all_rows, width = x.shape
    rows = all_rows // tokens
    at = Partners(nz, nx)
    at.meet()
    scatter = Scatter(at, parts, rc, r3a, r3b, r2, rz, rcz, rcx, rcy, send, recv)
    sums = SmallSum(at, total, landing, ssend, srecv)

    here = pltpu.make_async_copy(final, table.at[at.y, at.core], tsem)
    to_sibling = remote(final, table.at[at.y, at.core], tsend.at[0], trecv.at[0], at.sibling)
    pieces = across_send.shape[0]

    def to_across(i):
        piece = pl.ds(i * (all_rows // pieces), all_rows // pieces)
        dst = table.at[at.y, at.core, piece]
        return remote(final.at[piece], dst, across_send.at[i], across_recv.at[i], at.across_y)

    passed = table.at[1 - at.y, at.core]
    pass_on = remote(passed, passed, tsend.at[1], trecv.at[1], at.sibling)

    def load(src, entry, i):
        return pltpu.make_async_copy(src, pool.at[entry], psem.at[i])

    def fetch(m, slot, i):
        return pltpu.make_async_copy(g.at[m], weight.at[slot], wsem.at[i])

    blocks = act.shape[0]
    up_block, down_block = (lambda j: 4 + 2 * j), (lambda j: 5 + 2 * j)
    unit2, own_load, across_load = load(unit.at[1], 1, 0), load(own_up, 2, 1), load(across_up, 3, 2)
    act_entry = [5, 2, 3, 5]
    act_load = [load(act.at[j], act_entry[j], 3 + j) for j in range(blocks)]
    slope_entry = [4, 2, 3, 4]
    slope_load = [load(slope.at[j], slope_entry[j], 7 + j) for j in range(blocks)]
    low_load, unit1, mixed_load = load(saved.at[4], 6, 11), load(unit.at[0], 5, 12), load(saved.at[3], 4, 13)
    query_load, key_load, value_load = (load(saved.at[i], (2, 3, 6)[i], 14 + i) for i in range(3))
    x_load = load(x, 4, 17)
    down_fetch = [fetch(down_block(j), 0, 2 * j) for j in range(blocks)]
    up_fetch = [fetch(up_block(j), 1, 2 * j + 1) for j in range(blocks)]
    last = 2 * blocks
    output_fetch, query_fetch, key_fetch, value_fetch = (
        fetch(m, slot, last + i) for i, (m, slot) in enumerate(((3, 0), (0, 1), (1, 0), (2, 1)))
    )
    for copy in (unit2, own_load, across_load, act_load[0], down_fetch[0], up_fetch[0], slope_load[0], low_load):
        copy.start()
    to_sibling.start()
    here.start()
    total[0] = jnp.zeros_like(total[0])

    def folded(block):
        return jnp.sum(block.reshape(-1, 8, block.shape[-1]), axis=0)

    def norm_back(gain_row, shift_row, low_row, inverse, incoming, normed_entry, low_entry):
        def body(i, carry):
            spot = span(i, NORM_ROWS)
            grad, normed = incoming(spot), pool[normed_entry, spot].astype(f32)
            scaled = grad * small_full[gain_row : gain_row + 1, :]
            inner = (
                scaled
                - jnp.mean(scaled, axis=-1, keepdims=True)
                - normed * jnp.mean(scaled * normed, axis=-1, keepdims=True)
            )
            result = inner * inverse[spot]
            low = result.astype(bf16)
            hidden[spot] = result
            pool[low_entry, spot] = low
            return tuple(c + folded(b) for c, b in zip(carry, (grad * normed, grad, low.astype(f32))))

        zero = jnp.zeros((8, width), f32)
        found = lax.fori_loop(0, all_rows // NORM_ROWS, body, (zero, zero, zero))
        for row, value in zip((gain_row, shift_row, low_row), found):
            total[0, row : row + 1, :] = jnp.sum(value, axis=0, keepdims=True)

    def turned(slot):
        return weight[slot].reshape(width, width)

    def own_half(slot):
        return term[slot, :, at.core]

    stepped = set()

    def half(m, left, right, core):
        assert m < 2 or m - 2 in stepped
        for y in range(2):
            picked = span(y * 2 + core, width // 4)
            value = down(pool[left, :, picked], pool[right]).astype(bf16)
            term[m % 2, y, core] = value.reshape(nz, nx, -1, width)

    def theirs(m, left, right):
        half(m, left, right, 1 - at.core)
        scatter.start(m, term.at[m % 2, :, 1 - at.core])

    def ours(m, left, right):
        half(m, left, right, at.core)

    def run(code):
        kind, m = divmod(code, 100)
        if kind == 5:
            to_across(m).start()
        elif kind == 1:
            scatter.step1(m, own_half(m % 2))
            stepped.add(m)
        elif kind == 4:
            scatter.step4(m, out)
        else:
            (scatter.step2, scatter.step3)[kind - 2](m)

    items = []

    def produce(m, left, right, before=(), after=()):
        def first():
            for call in before:
                call()
            theirs(m, left, right)

        def second():
            ours(m, left, right)
            for call in after:
                call()

        items.extend((first, second))

    def load_second():
        for copy in (unit2, own_load, across_load):
            copy.wait()

    def second_norm():
        norm_back(6, 7, 5, inverse2, lambda spot: added(pool[2, spot], pool[3, spot]), 1, 0)
        act_load[1].start()
        act_load[2].start()

    items += [load_second, second_norm]
    for j in range(blocks):
        after = (act_load[3].start, slope_load[1].start, slope_load[2].start, unit1.start)[j]
        produce(j, act_entry[j], 0, [act_load[j].wait], [after])

    def widen_back(j):
        down_fetch[j].wait()
        slope_load[j].wait()
        value = across(pool[0], turned(0)) * pool[slope_entry[j]].astype(f32)
        value = value.astype(bf16)
        pool[1] = value
        total[0, 8 + j : 9 + j, :] = jnp.sum(value.astype(f32), axis=0, keepdims=True)
        (down_fetch[j + 1] if j + 1 < blocks else output_fetch).start()
        (slope_load[3], query_load, key_load, mixed_load)[j].start()

    def narrow_back(j):
        up_fetch[j].wait()
        hidden[...] = hidden[...] + across(pool[1], turned(1))
        (up_fetch[j + 1] if j + 1 < blocks else query_fetch).start()
        if j == blocks - 1:
            value_load.start()

    for j in range(blocks):
        items.append(partial(widen_back, j))
        produce(blocks + j, 6, 1, [low_load.wait] if j == 0 else [])
        items.append(partial(narrow_back, j))

    def first_norm():
        unit1.wait()
        norm_back(3, 4, 2, inverse1, lambda spot: hidden[spot], 5, 0)

    def mixed_back():
        output_fetch.wait()
        pool[1] = across(pool[0], turned(0)).astype(bf16)
        key_fetch.start()
        for copy in (query_load, key_load, value_load):
            copy.wait()
        fetch_probs(0).start()

    items.append(first_norm)
    produce(2 * blocks, 4, 0, [mixed_load.wait], [x_load.start])
    items.append(mixed_back)

    pairs = width // head_pair
    masks = half_masks(head_pair)
    scale = (head_pair // 2) ** (-0.5)

    def fetch_probs(i):
        slot = lax.rem(i, 2)
        return pltpu.make_async_copy(probs.at[i], held_probs.at[slot], ksem.at[slot])

    rounds = rows * pairs // 2

    def attend(i):
        pl.when(i + 1 < rounds)(lambda: fetch_probs(i + 1).start())
        fetch_probs(i).wait()
        spot, base = span(i // (pairs // 2), tokens), lax.rem(i, pairs // 2) * 2
        for p in range(2):
            cols = span(base + p, head_pair)
            query, keys, values, mixed_grad = (pool[e, spot, cols] for e in (2, 3, 6, 1))
            query_grad = key_grad = value_grad = None
            for h, mask in enumerate(masks):
                own_keys = keys * (mask * jnp.asarray(scale, bf16))
                low = held_probs[lax.rem(i, 2), 2 * p + h]
                prob = low.astype(f32)
                prob_grad = across(values * mask, mixed_grad)
                weighed = prob * prob_grad
                score_grad = (weighed - prob * jnp.sum(weighed, axis=0, keepdims=True)).astype(bf16)
                terms = (
                    down(score_grad, own_keys),
                    dot(score_grad, query * mask),
                    dot(low, mixed_grad * mask),
                )
                if query_grad is None:
                    query_grad, key_grad, value_grad = terms
                else:
                    query_grad, key_grad, value_grad = query_grad + terms[0], key_grad + terms[1], value_grad + terms[2]
            query_grad, value_grad = query_grad.astype(bf16), value_grad.astype(bf16)
            pool[2, spot, cols] = query_grad
            pool[3, spot, cols] = (key_grad * scale).astype(bf16)
            pool[6, spot, cols] = value_grad
            for row, value in ((0, query_grad), (1, value_grad)):
                found = jnp.sum(value.astype(f32), axis=0, keepdims=True)
                total[0, row : row + 1, cols] = total[0, row : row + 1, cols] + found

    items.append((rounds, attend))
    for i, entry in enumerate((6, 2, 3)):
        before = [x_load.wait, sums.start] if i == 0 else []
        produce(2 * blocks + 1 + i, 4, entry, before, [partial(sums.step, i)])

    def input_back(slot, entry, fetched, after):
        fetched.wait()
        hidden[...] = hidden[...] + across(pool[entry], turned(slot))
        after()

    def pass_rows():
        for i in range(pieces):
            to_across(i).wait_recv()
        pass_on.start()

    done = pltpu.make_async_copy(hidden, input_out, hsem)
    items += [
        partial(input_back, 1, 2, query_fetch, value_fetch.start),
        partial(input_back, 0, 3, key_fetch, pass_rows),
        partial(input_back, 1, 6, value_fetch, done.start),
    ]
    drive(BACKWARD_ORDER, items, run)
    sums.finish(small_out)
    done.wait()

    for m in range(count):
        scatter.drain(m)
    here.wait()
    to_sibling.wait()
    for i in range(pieces):
        to_across(i).wait_send()
    pass_on.wait()


def backward(
    x, own_up, across_up, final, unit, inverse1, inverse2, small_full, act, slope, saved, g, probs, nz, nx, tokens
):
    f32, bf16 = jnp.float32, jnp.bfloat16
    count, _, _, _, _, shard_rows, width = g.shape
    acts = x.shape
    parts = [column_parts(width, s) for s in SCATTER_SHARES]
    vmem, anywhere = pl.BlockSpec(memory_space=pltpu.VMEM), pl.BlockSpec(memory_space=pl.ANY)
    dma = pltpu.SemaphoreType.DMA
    out = jax.ShapeDtypeStruct
    block = (2, 2, nz, nx, shard_rows, width)
    return pl.pallas_call(
        partial(backward_kernel, nz, nx, parts, tokens, 2 * width // HEADS),
        out_shape=[
            out((count, shard_rows, width), f32),
            out(small_full.shape, f32),
            out(acts, f32),
            out((2, 2, *acts), bf16),
        ],
        in_specs=[anywhere] * 5 + [vmem] * 3 + [anywhere] * 5,
        out_specs=[vmem, vmem, anywhere, anywhere],
        scratch_shapes=[
            *scatter_scratch(count, nz, nx, shard_rows, width, parts),
            *small_scratch(nz, small_full.shape),
            pltpu.VMEM((2, *block), bf16),
            pltpu.VMEM((2, *block), bf16),
            pltpu.VMEM((7, *acts), bf16),
            pltpu.VMEM(acts, f32),
            dma((count,)),
            dma((18,)),
            dma,
            dma((2,)),
            dma((2,)),
            dma((count,)),
            dma((count,)),
            dma,
            pltpu.VMEM((2, 4, tokens, tokens), bf16),
            dma((2,)),
        ],
        compiler_params=pltpu.CompilerParams(
            collective_id=2, has_side_effects=True, vmem_limit_bytes=63 * 2**20
        ),
    )(x, own_up, across_up, final, unit, inverse1, inverse2, small_full, act, slope, saved, g, probs)


def finish_kernel(
    slot_row, live_count, me, first, second, full, sums, small_sums,
    slot_acts, input_grad, query, keys, values, output, up, contract, *small,
):
    s = pl.program_id(0)
    slot_acts[0] = first[0]
    slot_acts[1] = second[0]
    input_grad[...] = jnp.where(s < live_count[0], full[...], 0.0)

    @pl.when(s == 0)
    def _():
        blocks = (sums.shape[0] - 4) // 2
        shard, width = query.shape
        for j in range(blocks):
            contract[j * shard : (j + 1) * shard, :] = sums[j]
        lanes = 128
        per = lanes // shard
        for q in range(width // lanes):
            part = [sums[blocks + j, :, q * lanes : (q + 1) * lanes] for j in range(blocks)]
            for t in range(per):
                found = jnp.concatenate([p[:, t * shard : (t + 1) * shard] for p in part], axis=1)
                at = (q * per + t) * blocks * shard
                up[:, at : at + blocks * shard] = found
        for i, ref in enumerate((output, values, query, keys)):
            ref[...] = sums[2 * blocks + i]
        own = pltpu.roll(small_sums[...], width - me[0] * shard, 1)
        for i in range(8):
            small[i][...] = own[i, :shard]
        small[8][...] = jnp.concatenate([own[8 + j : 9 + j, :shard] for j in range(blocks)], axis=1)[0]


def finish(slot_row, live_count, table, full, sums, small_sums):
    f32 = jnp.float32
    members, tokens, width = table.shape
    slots, rows = slot_row.shape[0], full.shape[0]
    assert slots == 2 * rows
    count, shard, _ = sums.shape
    blocks = (count - 4) // 2
    me = lax.axis_index(("dp", "fsdp")).astype(jnp.int32).reshape(1)
    block, pair = (1, tokens, width), (2, tokens, width)

    def fixed(shape):
        return pl.BlockSpec(shape, lambda s, *_: (0,) * len(shape))

    fixed_outs = [(shard, width)] * 4 + [(shard, blocks * width), (blocks * shard, width)]
    fixed_outs += [(shard,)] * 8 + [(blocks * shard,)]
    row = pl.BlockSpec(block, lambda s, *_: (s, 0, 0))

    def chosen(i):
        return pl.BlockSpec(block, lambda s, slot_row, *_: (jnp.clip(slot_row[2 * s + i], 0, members - 1), 0, 0))

    out = jax.ShapeDtypeStruct
    return pl.pallas_call(
        finish_kernel,
        out_shape=[
            out((slots, tokens, width), table.dtype),
            out(full.shape, f32),
            *(out(shape, f32) for shape in fixed_outs),
        ],
        grid_spec=pltpu.PrefetchScalarGridSpec(
            num_scalar_prefetch=3,
            grid=(rows,),
            in_specs=[
                chosen(0),
                chosen(1),
                row,
                fixed(sums.shape),
                fixed(small_sums.shape),
            ],
            out_specs=[
                pl.BlockSpec(pair, lambda s, *_: (s, 0, 0)),
                row,
                *(fixed(shape) for shape in fixed_outs),
            ],
        ),
        compiler_params=pltpu.CompilerParams(vmem_limit_bytes=63 * 2**20),
    )(slot_row, live_count, me, table, table, full, sums, small_sums)


def on_device_kernels(
    rows_in,
    slot_row,
    live_count,
    slot_activation_gradient,
    query_weight,
    key_weight,
    value_weight,
    output_weight,
    query_bias,
    value_bias,
    output_bias,
    attn_gain,
    attn_shift,
    expand_weight,
    up_bias,
    down_weight,
    down_bias,
    ffn_gain,
    ffn_shift,
):
    row_count, token_count, width = rows_in.shape
    nx = 2
    nz = lax.axis_size("fsdp") // nx
    small = [query_bias, value_bias, output_bias, attn_gain, attn_shift, down_bias, ffn_gain, ffn_shift, up_bias]
    x = rows_in.reshape(-1, width)
    g, probs, saved, act, slope, unit, final, own_up, across_up, small_full, inverse1, inverse2 = forward(
        x,
        [query_weight, key_weight, value_weight, output_weight],
        expand_weight,
        down_weight,
        small,
        slot_row,
        slot_activation_gradient,
        nz,
        nx,
        token_count,
    )
    sums, small_sums, input_full, table = backward(
        x,
        own_up,
        across_up,
        final,
        unit,
        inverse1,
        inverse2,
        small_full,
        act,
        slope,
        saved,
        g,
        probs,
        nz,
        nx,
        token_count,
    )
    slot_acts, input_grad, query, keys, values, output, up, contract, *small_grads = finish(
        slot_row,
        live_count,
        table.reshape(-1, token_count, width),
        input_full.reshape(rows_in.shape),
        sums,
        small_sums,
    )
    return (
        slot_acts,
        input_grad,
        query,
        keys,
        values,
        output,
        *small_grads[:5],
        up,
        small_grads[8],
        contract,
        *small_grads[5:8],
    )


def norm_forward(hidden, gain, shift):
    center = hidden - jnp.mean(hidden, axis=-1, keepdims=True)
    inverse = lax.rsqrt(jnp.mean(center * center, axis=-1, keepdims=True) + EPSILON)
    normed = center * inverse
    return (normed * gain + shift, normed, inverse)


def norm_backward(incoming, gain, normed, inverse):
    scaled = incoming * gain
    inner = (
        scaled
        - jnp.mean(scaled, axis=-1, keepdims=True)
        - normed * jnp.mean(scaled * normed, axis=-1, keepdims=True)
    )
    return (
        inner * inverse,
        jnp.sum(incoming * normed, axis=(0, 1)),
        jnp.sum(incoming, axis=(0, 1)),
    )


def apply_weight(acts, weight):
    return jnp.einsum("rsd,de->rse", acts, weight, preferred_element_type=jnp.float32)


def apply_back(grads, weight):
    return jnp.einsum("rse,de->rsd", grads, weight, preferred_element_type=jnp.float32)


def weight_term(acts, grads):
    return jnp.einsum("rsd,rse->de", acts, grads, preferred_element_type=jnp.float32)


def bias_term(grads):
    return jnp.sum(grads, axis=(0, 1), dtype=jnp.float32)


def on_device_plain(
    rows_in,
    slot_row,
    live_count,
    slot_activation_gradient,
    query_weight,
    key_weight,
    value_weight,
    output_weight,
    query_bias,
    value_bias,
    output_bias,
    attn_gain,
    attn_shift,
    expand_weight,
    up_bias,
    down_weight,
    down_bias,
    ffn_gain,
    ffn_shift,
):
    row_count, token_count, feature_count = rows_in.shape
    head_size = feature_count // HEADS
    score_scale = head_size ** (-0.5)
    split_shape = (row_count, token_count, HEADS, head_size)
    wanted = lax.broadcasted_iota(
        jnp.int32, (row_count * lax.axis_size("dp"), slot_row.shape[0]), 0
    )
    one_hot_matrix = (wanted == slot_row[None, :]).astype(jnp.bfloat16)
    upstream = lax.psum_scatter(
        jnp.einsum(
            "az,zfy->afy",
            one_hot_matrix,
            slot_activation_gradient,
            preferred_element_type=jnp.float32,
        ).astype(jnp.bfloat16),
        "dp",
        scatter_dimension=0,
        tiled=True,
    ).astype(jnp.float32)
    smalls = (query_bias, value_bias, output_bias, attn_gain, attn_shift, down_bias, ffn_gain, ffn_shift)
    small_rows = query_bias.shape[0]
    packed = jnp.concatenate([v.reshape(-1, small_rows) for v in (*smalls, up_bias)], axis=0)
    packed_full = lax.all_gather(packed, ("dp", "fsdp"), axis=0)
    (
        qbias_full,
        vbias_full,
        obias_full,
        gain1_full,
        shift1_full,
        downbias_full,
        gain2_full,
        shift2_full,
    ) = (packed_full[:, i].reshape(-1) for i in range(8))
    upbias_full = packed_full[:, 8:].reshape(-1)
    query_full, key_full, value_full, output_full, up_full, down_full = (
        lax.all_gather(weight, ("dp", "fsdp"), axis=0, tiled=True)
        for weight in (query_weight, key_weight, value_weight, output_weight, expand_weight, down_weight)
    )
    inputs = rows_in.astype(jnp.float32)
    query = (apply_weight(rows_in, query_full) + qbias_full.astype(jnp.float32)).astype(
        jnp.bfloat16
    )
    keys = apply_weight(rows_in, key_full).astype(jnp.bfloat16)
    values = (apply_weight(rows_in, value_full) + vbias_full.astype(jnp.float32)).astype(
        jnp.bfloat16
    )
    query_heads = query.reshape(split_shape)
    key_heads = keys.reshape(split_shape)
    value_heads = values.reshape(split_shape)
    scores = (
        jnp.einsum("rqhd,rkhd->rhqk", query_heads, key_heads, preferred_element_type=jnp.float32)
        * score_scale
    )
    row_top = jnp.max(scores, axis=-1, keepdims=True)
    expo = jnp.exp(scores - row_top)
    row_sum = jnp.sum(expo, axis=-1, keepdims=True)
    logsum = row_top + jnp.log(row_sum)
    probs_low = (expo / row_sum).astype(jnp.bfloat16)
    mixed = jnp.einsum(
        "rhqk,rkhd->rqhd", probs_low, value_heads, preferred_element_type=jnp.float32
    )
    mixed = mixed.reshape(row_count, token_count, feature_count).astype(jnp.bfloat16)
    gain1 = gain1_full.astype(jnp.float32)
    resid1 = inputs + apply_weight(mixed, output_full) + obias_full.astype(jnp.float32)
    normed1_out, normed1, inverse1 = norm_forward(resid1, gain1, shift1_full.astype(jnp.float32))
    normed1_low = normed1_out.astype(jnp.bfloat16)
    pre_act = apply_weight(normed1_low, up_full) + upbias_full.astype(jnp.float32)
    act_low = jax.nn.gelu(pre_act, approximate=False).astype(jnp.bfloat16)
    gain2 = gain2_full.astype(jnp.float32)
    resid2 = normed1_out + apply_weight(act_low, down_full) + downbias_full.astype(jnp.float32)
    final, second_normed, inverse2 = norm_forward(resid2, gain2, shift2_full.astype(jnp.float32))
    final_low = final.astype(jnp.bfloat16)
    shard_rows = lax.all_gather(final_low, "dp", axis=0, tiled=True)
    span_rows = shard_rows.shape[0]
    inside = (slot_row >= 0) & (slot_row < span_rows)
    picked = jnp.take(shard_rows, jnp.clip(slot_row, 0, span_rows - 1), axis=0)
    slot_acts = jnp.where(
        inside[:, None, None], picked, jnp.zeros(slot_activation_gradient.shape, jnp.bfloat16)
    )
    gain1 = gain1_full.astype(jnp.float32)
    gain2 = gain2_full.astype(jnp.float32)
    grad2, gain2_grad, shift2_grad = norm_backward(upstream, gain2, second_normed, inverse2)
    ffn_low = grad2.astype(jnp.bfloat16)
    down_grad = weight_term(act_low, ffn_low)
    down_bias_grad = bias_term(ffn_low)
    act_grad = apply_back(ffn_low, down_full)
    gelu_value, gelu_back = jax.vjp(partial(jax.nn.gelu, approximate=False), pre_act)
    pre_grad = gelu_back(act_grad)[0].astype(jnp.bfloat16)
    up_grad = weight_term(normed1_low, pre_grad)
    up_bias_grad = bias_term(pre_grad)
    normed1_grad = grad2 + apply_back(pre_grad, up_full)
    grad1, gain1_grad, shift1_grad = norm_backward(normed1_grad, gain1, normed1, inverse1)
    attn_low = grad1.astype(jnp.bfloat16)
    output_grad = weight_term(mixed, attn_low)
    output_bias_grad = bias_term(attn_low)
    mixed_grad = apply_back(attn_low, output_full).astype(jnp.bfloat16).reshape(split_shape)
    scores_again = (
        jnp.einsum("rqhd,rkhd->rhqk", query_heads, key_heads, preferred_element_type=jnp.float32)
        * score_scale
    )
    probs = jnp.exp(scores_again - logsum)
    probs_again = probs.astype(jnp.bfloat16)
    value_grad = jnp.einsum(
        "rhqk,rqhd->rkhd", probs_again, mixed_grad, preferred_element_type=jnp.float32
    )
    value_grad = value_grad.astype(jnp.bfloat16).reshape(row_count, token_count, feature_count)
    prob_grad = jnp.einsum(
        "rqhd,rkhd->rhqk", mixed_grad, value_heads, preferred_element_type=jnp.float32
    )
    score_grad = (probs * (prob_grad - jnp.sum(probs * prob_grad, axis=-1, keepdims=True))).astype(
        jnp.bfloat16
    )
    query_grad = (
        jnp.einsum("rhqk,rkhd->rqhd", score_grad, key_heads, preferred_element_type=jnp.float32)
        * score_scale
    )
    query_grad = query_grad.astype(jnp.bfloat16).reshape(row_count, token_count, feature_count)
    key_grad = (
        jnp.einsum("rhqk,rqhd->rkhd", score_grad, query_heads, preferred_element_type=jnp.float32)
        * score_scale
    )
    key_grad = key_grad.astype(jnp.bfloat16).reshape(row_count, token_count, feature_count)
    query_wgrad = weight_term(rows_in, query_grad)
    key_wgrad = weight_term(rows_in, key_grad)
    value_wgrad = weight_term(rows_in, value_grad)
    query_bias_grad = bias_term(query_grad)
    value_bias_grad = bias_term(value_grad)
    input_full = (
        grad1
        + apply_back(query_grad, query_full)
        + apply_back(key_grad, key_full)
        + apply_back(value_grad, value_full)
    )
    live_rows = lax.broadcasted_iota(jnp.int32, (row_count,), 0) < live_count[0]
    input_grad = jnp.where(live_rows[:, None, None], input_full, 0.0)
    devices = packed_full.shape[0]
    small_terms = jnp.concatenate(
        [
            v.reshape(devices, -1, small_rows)
            for v in (
                query_bias_grad,
                value_bias_grad,
                output_bias_grad,
                gain1_grad,
                shift1_grad,
                down_bias_grad,
                gain2_grad,
                shift2_grad,
                up_bias_grad,
            )
        ],
        axis=1,
    )
    small_sum = lax.psum_scatter(small_terms, ("dp", "fsdp"), scatter_dimension=0, tiled=True)[0]
    down_sum, up_sum, output_sum, value_sum, query_sum, key_sum = (
        lax.psum_scatter(
            term.astype(jnp.bfloat16), ("dp", "fsdp"), scatter_dimension=0, tiled=True
        ).astype(jnp.float32)
        for term in (down_grad, up_grad, output_grad, value_wgrad, query_wgrad, key_wgrad)
    )
    return (
        slot_acts,
        input_grad,
        query_sum,
        key_sum,
        value_sum,
        output_sum,
        small_sum[0],
        small_sum[1],
        small_sum[2],
        small_sum[3],
        small_sum[4],
        up_sum,
        small_sum[8:].reshape(-1),
        down_sum,
        small_sum[5],
        small_sum[6],
        small_sum[7],
    )


def solution(mesh):
    placed = (
        P(("dp", "fsdp"), None, None),
        P(("dp", "fsdp")),
        P(("dp", "fsdp")),
        P(("dp", "fsdp"), None, None),
        P(("dp", "fsdp"), None),
        P(("dp", "fsdp"), None),
        P(("dp", "fsdp"), None),
        P(("dp", "fsdp"), None),
        P(("dp", "fsdp")),
        P(("dp", "fsdp")),
        P(("dp", "fsdp")),
        P(("dp", "fsdp")),
        P(("dp", "fsdp")),
        P(("dp", "fsdp"), None),
        P(("dp", "fsdp")),
        P(("dp", "fsdp"), None),
        P(("dp", "fsdp")),
        P(("dp", "fsdp")),
        P(("dp", "fsdp")),
    )
    kernels = mesh.shape["dp"] == 4 and mesh.shape["fsdp"] == 8
    return jax.shard_map(
        on_device_kernels if kernels else on_device_plain,
        mesh=mesh,
        in_specs=placed,
        out_specs=(
            P(("dp", "fsdp"), None, None),
            P(("dp", "fsdp"), None, None),
            P(("dp", "fsdp"), None),
            P(("dp", "fsdp"), None),
            P(("dp", "fsdp"), None),
            P(("dp", "fsdp"), None),
            P(("dp", "fsdp")),
            P(("dp", "fsdp")),
            P(("dp", "fsdp")),
            P(("dp", "fsdp")),
            P(("dp", "fsdp")),
            P(("dp", "fsdp"), None),
            P(("dp", "fsdp")),
            P(("dp", "fsdp"), None),
            P(("dp", "fsdp")),
            P(("dp", "fsdp")),
            P(("dp", "fsdp")),
        ),
        check_vma=False,
    )
```

```python
import math
from functools import partial

import jax
import jax.numpy as jnp
from jax import lax
from jax.experimental import pallas as pl
from jax.experimental.pallas import tpu as pltpu
from jax.sharding import PartitionSpec as P

HEADS = 16


EPSILON = 1e-05


MESH = pl.DeviceIdType.MESH
LANES = 128


def place(nz, nx):
    dp, fs = lax.axis_index("dp"), lax.axis_index("fsdp")
    y, core = dp // 2, lax.rem(dp, 2)
    z, x = fs // nx, lax.rem(fs, nx)
    return y, core, z, x


def device(y, core, z, x, nx):
    return (y * 2 + core, z * nx + x)


class Partners:
    def __init__(self, nz, nx):
        self.nz, self.nx = nz, nx
        self.y, self.core, self.z, self.x = place(nz, nx)
        y, core, z, x = self.y, self.core, self.z, self.x
        self.sibling = device(y, 1 - core, z, x, nx)
        self.across_x = device(y, core, z, 1 - x, nx)
        self.across_y = device(1 - y, core, z, x, nx)
        self.along_z = [device(y, core, lax.rem(z + k, nz), x, nx) for k in range(1, nz)]
        self.all = [self.sibling, self.across_x, self.across_y, *self.along_z]

    def meet(self):
        barrier = pltpu.get_barrier_semaphore()
        for other in self.all:
            pl.semaphore_signal(barrier, inc=1, device_id=other, device_id_type=MESH)
        pl.semaphore_wait(barrier, len(self.all))


def remote(src, dst, send, recv, to):
    return pltpu.make_async_remote_copy(
        src_ref=src, dst_ref=dst, send_sem=send, recv_sem=recv, device_id=to, device_id_type=MESH
    )


def added(*blocks):
    total = blocks[0].astype(jnp.float32)
    for block in blocks[1:]:
        total = total + block.astype(jnp.float32)
    return total


class Scatter:
    def __init__(self, at, parts, rc, r3a, r3b, r2, rz, rcz, rcx, rcy, send, recv):
        self.at, self.parts = at, parts
        self.rc, self.r3a, self.r3b, self.r2, self.rz = rc, r3a, r3b, r2, rz
        self.rcz, self.rcx, self.rcy = rcz, rcx, rcy
        self.send, self.recv = send, recv

    def copy(self, m, i, src, dst, to):
        return remote(src, dst, self.send.at[m, i], self.recv.at[m, i], to)

    def to_sibling(self, m, theirs):
        return self.copy(m, 0, theirs, self.rc.at[m], self.at.sibling)

    def landings(self, m):
        a, b, c, _ = self.parts[m]
        a, b, c = (pl.ds(0, part.size) for part in (a, b, c))
        return (
            self.r3a.at[m, :, :, :, a],
            self.r3b.at[m, :, :, :, b],
            self.rcz.at[m, :, :, :, :, c],
            self.rcx.at[m, :, :, c],
            self.rcy.at[m, :, c],
        )

    def firsts(self, m):
        at, rc, nz = self.at, self.rc, self.at.nz
        a, b, c, _ = self.parts[m]
        r3a, r3b, rcz, _, _ = self.landings(m)
        return [
            self.copy(m, 1, rc.at[m, :, :, 1 - at.x, :, a], r3a, at.across_x),
            self.copy(m, 2, rc.at[m, 1 - at.y, :, :, :, b], r3b, at.across_y),
        ] + [
            self.copy(
                m, 2 + k, rc.at[m, :, lax.rem(at.z + k, nz), :, :, c], rcz.at[k - 1], at.along_z[k - 1]
            )
            for k in range(1, nz)
        ]

    def seconds(self, m):
        at, nz = self.at, self.at.nz
        a, b, _, _ = self.parts[m]
        r3a, r3b, rcz, rcx, _ = self.landings(m)
        return [
            self.copy(m, nz + 2, r3a.at[1 - at.y], self.r2.at[m, :, :, a], at.across_y),
            self.copy(m, nz + 3, r3b.at[:, 1 - at.x], self.r2.at[m, :, :, b], at.across_x),
            self.copy(m, nz + 4, rcz.at[0, :, 1 - at.x], rcx, at.across_x),
        ]

    def thirds(self, m):
        at, nz = self.at, self.at.nz
        ab = self.parts[m][3]
        rcx, rcy = self.landings(m)[3:]
        return [
            self.copy(
                m,
                nz + 4 + k,
                self.r2.at[m, lax.rem(at.z + k, nz), :, ab],
                self.rz.at[m, k - 1, :, ab],
                at.along_z[k - 1],
            )
            for k in range(1, nz)
        ] + [self.copy(m, 2 * nz + 4, rcx.at[1 - at.y], rcy, at.across_y)]

    def start(self, m, theirs):
        self.to_sibling(m, theirs).start()

    def step1(self, m, own):
        rc = self.rc
        self.to_sibling(m, rc.at[m]).wait_recv()

        rc[m] = added(rc[m], own).astype(rc.dtype)
        self.to_sibling(m, rc.at[m]).wait_send()
        for copy in self.firsts(m):
            copy.start()

    def step2(self, m):
        at, rc = self.at, self.rc
        a, b, c, _ = self.parts[m]
        r3a, r3b, rcz, _, _ = self.landings(m)
        for copy in self.firsts(m):
            copy.wait_recv()

        r3a[...] = added(r3a[...], rc[m, :, :, at.x, :, a]).astype(rc.dtype)
        r3b[...] = added(r3b[...], rc[m, at.y, :, :, :, b]).astype(rc.dtype)
        others = [rcz[k] for k in range(at.nz - 1)]
        rcz[0] = added(rc[m, :, at.z, :, :, c], *others).astype(rc.dtype)
        for copy in self.seconds(m):
            copy.start()

    def step3(self, m):
        at, r2 = self.at, self.r2
        a, b, _, _ = self.parts[m]
        r3a, r3b, rcz, rcx, _ = self.landings(m)
        for copy in self.seconds(m):
            copy.wait_recv()

        r2[m, :, :, a] = added(r2[m, :, :, a], r3a[at.y]).astype(r2.dtype)
        r2[m, :, :, b] = added(r2[m, :, :, b], r3b[:, at.x]).astype(r2.dtype)
        rcx[...] = added(rcx[...], rcz[0, :, at.x]).astype(r2.dtype)
        for copy in self.thirds(m):
            copy.start()

    def step4(self, m, out):
        at = self.at
        _, _, c, ab = self.parts[m]
        rcx, rcy = self.landings(m)[3:]
        for copy in self.thirds(m):
            copy.wait_recv()
        others = [self.rz[m, k, :, ab] for k in range(at.nz - 1)]
        out[m, :, ab] = added(self.r2[m, at.z, :, ab], *others)
        out[m, :, c] = added(rcx[at.y], rcy[...])

    def drain(self, m):
        for copy in self.firsts(m) + self.seconds(m) + self.thirds(m):
            copy.wait_send()


class SmallSum:
    def __init__(self, at, total, landing, send, recv):
        self.at, self.total, self.landing, self.send, self.recv = at, total, landing, send, recv

    def hop(self, i, to):
        return remote(self.total.at[i], self.landing.at[i], self.send.at[i], self.recv.at[i], to)

    def along(self, k):
        i = 2 + k
        return remote(self.total.at[3], self.landing.at[i], self.send.at[i], self.recv.at[i], self.at.along_z[k - 1])

    def start(self):
        self.hop(0, self.at.sibling).start()

    def step(self, i):
        at = self.at
        to = (at.sibling, at.across_x, at.across_y)
        self.hop(i, to[i]).wait_recv()
        self.total[i + 1] = self.total[i] + self.landing[i]
        if i < 2:
            self.hop(i + 1, to[i + 1]).start()
        else:
            for k in range(1, at.nz):
                self.along(k).start()

    def finish(self, out):
        at = self.at
        for k in range(1, at.nz):
            self.along(k).wait_recv()
        total = self.total[3]
        for k in range(1, at.nz):
            total = total + self.landing[2 + k]
        out[...] = total
        to = (at.sibling, at.across_x, at.across_y)
        for i in range(3):
            self.hop(i, to[i]).wait_send()
        for k in range(1, at.nz):
            self.along(k).wait_send()


def scatter_scratch(count, nz, nx, rows, columns, parts):
    bf16 = jnp.bfloat16
    a, b, c, ab = (max(part[i].size for part in parts) for i in range(4))
    return [
        pltpu.VMEM((count, 2, nz, nx, rows, columns), bf16),
        pltpu.VMEM((count, 2, nz, rows, a), bf16),
        pltpu.VMEM((count, nz, nx, rows, b), bf16),
        pltpu.VMEM((count, nz, rows, ab), bf16),
        pltpu.VMEM((count, nz - 1, rows, ab), bf16),
        pltpu.VMEM((count, nz - 1, 2, nx, rows, c), bf16),
        pltpu.VMEM((count, 2, rows, c), bf16),
        pltpu.VMEM((count, rows, c), bf16),
        pltpu.SemaphoreType.DMA((count, 2 * nz + 5)),
        pltpu.SemaphoreType.DMA((count, 2 * nz + 5)),
    ]


def small_scratch(nz, shape):
    return [
        pltpu.VMEM((4, *shape), jnp.float32),
        pltpu.VMEM((2 + nz, *shape), jnp.float32),
        pltpu.SemaphoreType.DMA((2 + nz,)),
        pltpu.SemaphoreType.DMA((2 + nz,)),
    ]


GATHER_SHARES = [
    (6, 1), (4, 2), (6, 1), (3, 4), (6, 1), (4, 3), (3, 4), (5, 1), (5, 1), (6, 1), (4, 2), (5, 1),
]
SCATTER_SHARES = [
    (5, 1), (4, 2), (6, 1), (4, 2), (4, 2), (4, 2), (5, 2), (6, 1), (6, 1), (5, 2), (4, 3), (3, 3),
]

FORWARD_ORDER = (
    100, 101, 102, 103, 0, 0, 104, 105, 0, 0, 0, 0, 200, 0, 201, 500, 300, 202, 301, 203, 302, 204, 205, 501,
    303, 400, 106, 0, 401, 107, 502, 304, 0, 402, 108, 305, 0, 403, 109, 503, 0, 206, 0, 0, 504, 0, 207, 0, 0,
    0, 404, 110, 0, 505, 0, 0, 208, 0, 306, 0, 405, 111, 0, 307, 0, 209, 0, 308, 210, 0, 406, 211, 0, 309, 407,
    506, 310, 0, 311, 408, 507, 0, 409, 508, 509, 410, 0, 510, 0, 411, 511, 0, 0,
)
BACKWARD_ORDER = (
    500, 0, 501, 0, 502, 0, 0, 503, 0, 100, 0, 0, 101, 0, 0, 504, 102, 0, 0, 103, 200, 0, 0, 0, 201, 104, 0, 0,
    505, 0, 0, 202, 105, 0, 203, 0, 300, 0, 301, 0, 106, 0, 204, 302, 0, 506, 0, 400, 0, 107, 205, 401, 303, 0,
    507, 0, 0, 508, 0, 206, 108, 402, 304, 0, 0, 0, 509, 0, 0, 403, 0, 207, 0, 305, 0, 306, 0, 510, 0, 404, 0,
    511, 0, 0, 0, 405, 208, 307, 0, 109, 0, 406, 0, 110, 0, 0, 111, 308, 407, 0, 209, 0, 210, 211, 309, 310,
    408, 311, 409, 410, 411,
)


def drive(order, items, run):
    todo = list(order)
    for item in items:
        while todo[0]:
            run(todo.pop(0))
        if callable(item):
            todo.pop(0)
            item()
            continue
        rounds, body = item
        between = []
        for _ in range(rounds):
            codes = []
            while todo[0]:
                codes.append(todo.pop(0))
            todo.pop(0)
            between.append(codes)

        def one(i, carry):
            for r, codes in enumerate(between):
                if codes:

                    @pl.when(i == r)
                    def _(codes=codes):
                        for code in codes:
                            run(code)

            body(i)
            return carry

        lax.fori_loop(0, rounds, one, 0)
    for code in todo:
        run(code)


def exact_gelu(pre):
    half = 0.5 + 0.5 * lax.erf(pre * (0.5**0.5))
    bell = jnp.exp(-0.5 * pre * pre) * ((0.5 / math.pi) ** 0.5)
    return pre * half, half + pre * bell


def rms_center(hidden):
    center = hidden - jnp.mean(hidden, axis=-1, keepdims=True)
    inverse = lax.rsqrt(jnp.mean(center * center, axis=-1, keepdims=True) + EPSILON)
    return center * inverse, inverse


def half_masks(width):
    left = (lax.broadcasted_iota(jnp.int32, (1, width), 1) < width // 2).astype(jnp.float32)
    return left.astype(jnp.bfloat16), (1.0 - left).astype(jnp.bfloat16)


def across(left, right):
    return lax.dot_general(left, right, (((1,), (1,)), ((), ())), preferred_element_type=jnp.float32)


def down(left, right):
    return lax.dot_general(left, right, (((0,), (0,)), ((), ())), preferred_element_type=jnp.float32)


def dot(left, right):
    return jnp.dot(left, right, preferred_element_type=jnp.float32)


def span(i, size):
    return pl.ds(pl.multiple_of(i * size, size), size)


class Gather:
    def __init__(self, at, parts, count, shards, g, send, recv):
        self.at, self.count, self.shards, self.g, self.send, self.recv = at, count, shards, g, send, recv
        self.parts = parts

    def copy(self, m, i, src, dst, to):
        return remote(src, dst, self.send.at[m, i], self.recv.at[m, i], to)

    def same(self, m, i, part, to):
        return self.copy(m, i, part, part, to)

    def stages(self, m):
        at, g, nz = self.at, self.g, self.at.nz
        a, b, c, ab = self.parts[m]
        y, core, z, x = at.y, at.core, at.z, at.x
        across_x, across_y, along_z = at.across_x, at.across_y, at.along_z
        first = [
            self.copy(m, k, self.shards.at[m, :, ab], g.at[m, y, core, z, x, :, ab], along_z[k])
            for k in range(nz - 1)
        ]
        first.append(self.copy(m, nz - 1, self.shards.at[m, :, c], g.at[m, y, core, z, x, :, c], across_y))
        second = [
            self.same(m, nz, g.at[m, y, core, :, x, :, a], across_y),
            self.same(m, nz + 1, g.at[m, y, core, :, x, :, b], across_x),
            self.same(m, nz + 2, g.at[m, :, core, z, x, :, c], across_x),
        ]
        third = [
            self.same(m, nz + 3, g.at[m, :, core, :, x, :, a], across_x),
            self.same(m, nz + 4, g.at[m, y, core, :, :, :, b], across_y),
        ]
        third += [self.same(m, nz + 5 + k, g.at[m, :, core, z, :, :, c], along_z[k]) for k in range(nz - 1)]
        return first, second, third, [self.same(m, 2 * nz + 4, g.at[m, :, core], at.sibling)]

    def step0(self, m):
        at = self.at
        for copy in self.stages(m)[0]:
            copy.start()
        self.g[m, at.y, at.core, at.z, at.x] = self.shards[m]

    def follow(self, stage, m):
        stages = self.stages(m)
        for copy in stages[stage - 1]:
            copy.wait_recv()
        for copy in stages[stage]:
            copy.start()

    def step1(self, m):
        self.follow(1, m)

    def step2(self, m):
        self.follow(2, m)

    def step3(self, m):
        self.follow(3, m)

    def arrive(self, m):
        part = self.g.at[m, :, self.at.core]
        self.same(m, 2 * self.at.nz + 4, part, self.at.sibling).wait_recv()

    def drain(self, m):
        for stage in self.stages(m):
            for copy in stage:
                copy.wait_send()


def column_parts(width, shares):
    lanes = 128
    a, b = (share * lanes for share in shares)
    return pl.ds(0, a), pl.ds(a, b), pl.ds(a + b, width - a - b), pl.ds(0, a + b)


UP_TILE = 256
NORM_ROWS = 192


def forward_kernel(
    nz, nx, parts, tokens, head_pair,
    x, attention_weights, expand, contract, small, slot_row, slots,
    g_out, probs_out, saved, act_out, slope_out, unit_out, final_out, own_out, across_out, small_full, inverse1, inverse2,
    g, shards, pool, hidden, landed, total, landing,
    send, recv, ssend, srecv, usend, urecv, across_send, across_recv, isem, gsem, vsem, asem, dsem, fsem, held_probs, ksem,
):
    f32, bf16 = jnp.float32, jnp.bfloat16
    count = g.shape[0]
    all_rows, width = x.shape
    rows = all_rows // tokens
    at = Partners(nz, nx)
    at.meet()
    gather = Gather(at, parts, count, shards, g, send, recv)
    sums = SmallSum(at, total, landing, ssend, srecv)
    groups = slots.shape[0] // rows

    def fetch(i):
        return pltpu.make_async_copy(slots.at[i], pool.at[i // rows, pl.ds((i % rows) * tokens, tokens)], isem.at[i])

    shard = shards.shape[1]
    lane = lax.broadcasted_iota(jnp.int32, (1, width), 1)
    mine = lane // shard == lax.axis_index("dp") * (nz * nx) + lax.axis_index("fsdp")
    own = [ref[...].astype(f32).reshape(1, -1) for ref in small]
    own = own[:-1] + [own[-1][:, i : i + shard] for i in range(0, own[-1].shape[1], shard)]
    own += [jnp.zeros((1, shard), f32)] * (total.shape[1] - len(own))
    own = jnp.concatenate(own, axis=0)
    total[0] = jnp.where(mine, jnp.concatenate([own] * (width // shard), axis=1), 0.0)
    sums.start()
    for m in range(4):
        shards[m] = attention_weights[m][...]
    for i in range(slots.shape[0]):
        fetch(i).start()

    high, part = 32, width // 2

    chosen = [
        [jnp.where(slot_row[s] == t, 1.0, 0.0) for s in range(slots.shape[0])] for t in range(2 * 2 * rows)
    ]

    def sum_slots(i, carry):
        cols = span(lax.rem(i, 2), part)
        base = i // 2 * high
        held = [
            pool[s // rows, pl.ds(pl.multiple_of(base + (s % rows) * tokens, high), high), cols].astype(f32)
            for s in range(slots.shape[0])
        ]
        for t in range(2 * 2 * rows):
            picked = chosen[t][0] * held[0]
            for s in range(1, slots.shape[0]):
                picked = picked + chosen[t][s] * held[s]
            spot = pl.ds(pl.multiple_of(base + (t % rows) * tokens, high), high)
            pool[groups + t // rows, spot, cols] = picked.astype(bf16)
        return carry

    def up_sibling(y):
        src = pool.at[groups + y * 2 + 1 - at.core]
        return remote(src, landed.at[y], usend.at[y], urecv.at[y], at.sibling)

    pieces = across_send.shape[0]

    def up_across(i):
        piece = pl.ds(i * (all_rows // pieces), all_rows // pieces)
        return remote(
            landed.at[1 - at.y, piece], across_out.at[piece], across_send.at[i], across_recv.at[i], at.across_y
        )

    up_own = pltpu.make_async_copy(landed.at[at.y], own_out, isem.at[slots.shape[0]])

    steps = tokens // high * 2

    def quarter(i):
        if i == 0:
            for s in range(slots.shape[0]):
                fetch(s).wait()
        lax.fori_loop(i * steps // 4, (i + 1) * steps // 4, sum_slots, 0)
        if i != 2:
            sums.step((0, 1, None, 2)[i])

    blocks = (count - 4) // 2

    def arrange():
        for j in range(blocks):
            shards[5 + 2 * j] = contract[j * shard : (j + 1) * shard, :]
        lanes = 128
        per = lanes // shard
        for q in range(width // lanes):
            natural = expand[:, q * lanes * blocks : (q + 1) * lanes * blocks].astype(f32)
            for j in range(blocks):
                starts = [t * blocks * shard + j * shard for t in range(per)]
                found = [natural[:, start : start + shard] for start in starts]
                shards[4 + 2 * j, :, q * lanes : (q + 1) * lanes] = jnp.concatenate(found, axis=1).astype(bf16)

    def exchange_cores():
        for y in range(2):
            up_sibling(y).start()

    def chip_sum(i, carry):
        y, spot = i // (all_rows // 192), span(lax.rem(i, all_rows // 192), 192)
        landed[y, spot] = added(landed[y, spot], pool[groups + y * 2 + at.core, spot]).astype(bf16)
        return carry

    def sum_chip():
        for y in range(2):
            up_sibling(y).wait_recv()
        lax.fori_loop(0, 2 * all_rows // 192, chip_sum, 0)
        up_own.start()
        for y in range(2):
            up_sibling(y).wait_send()

    def keep(m):
        return pltpu.make_async_copy(g.at[m], g_out.at[m], gsem.at[m])

    def arrive(m):
        gather.arrive(m)
        keep(m).start()

    def tile(m, cols):
        return g[m, :, :, :, :, :, cols].reshape(width, cols.size)

    def bias(i, cols):
        return small_full[pl.ds(i, 1), cols]

    every = pl.ds(0, all_rows)
    halves = [pl.ds(i * width // 2, width // 2) for i in range(2)]

    def tiles(size, body):
        def one(i, carry):
            body(span(i, size), every)
            return carry

        lax.fori_loop(0, width // size, one, 0)

    def save(i):
        return pltpu.make_async_copy(pool.at[i], saved.at[i], vsem.at[i])

    def project(m):
        row = lax.rem(m, 2) * 12 + m // 2
        arrive(m)
        pl.when(m == 0)(lambda: sums.finish(small_full))
        for cols in halves:
            pool[m, :, cols] = (dot(x[...], tile(m, cols)) + bias(row, cols)).astype(bf16)
        save(m).start()

    pairs = width // head_pair
    masks = half_masks(head_pair)
    scale = (head_pair // 2) ** (-0.5)

    def keep_probs(i):
        slot = lax.rem(i, 2)
        return pltpu.make_async_copy(held_probs.at[slot], probs_out.at[i], ksem.at[slot])

    def attend(i):
        spot, base = span(i // (pairs // 2), tokens), lax.rem(i, pairs // 2) * 2
        pl.when(i >= 2)(lambda: keep_probs(i - 2).wait())
        for p in range(2):
            cols = span(base + p, head_pair)
            query, keys, values = pool[0, spot, cols], pool[1, spot, cols], pool[2, spot, cols]
            query = query * jnp.asarray(scale, bf16)
            out = None
            for h, mask in enumerate(masks):
                scores = across(keys * mask, query)
                probs = jnp.exp(scores - jnp.max(scores, axis=0, keepdims=True))
                probs = (probs * (1.0 / jnp.sum(probs, axis=0, keepdims=True))).astype(bf16)
                held_probs[lax.rem(i, 2), 2 * p + h] = probs
                term = down(probs, values * mask)
                out = term if out is None else out + term
            pool[3, spot, cols] = out.astype(bf16)
        keep_probs(i).start()

    rounds = rows * pairs // 2

    def mix(cols, spot):
        hidden[spot, cols] = dot(pool[3, spot], tile(3, cols)) + x[spot, cols].astype(f32) + bias(2, cols)

    def join():
        save(3).start()
        for i in range(2):
            keep_probs(rounds - 2 + i).wait()
        arrive(3)
        for cols in halves:
            mix(cols, every)

    def unit(i):
        return pltpu.make_async_copy(pool.at[6], unit_out.at[i], fsem.at[i])

    def norm1(i, carry):
        spot = span(i, NORM_ROWS)
        normed, inverse = rms_center(hidden[spot])
        result = normed * small_full[3:4, :] + small_full[4:5, :]
        hidden[spot] = result
        pool[4, spot] = result.astype(bf16)
        pool[6, spot] = normed.astype(bf16)
        inverse1[spot] = inverse
        return carry

    def first_norm():
        lax.fori_loop(0, all_rows // NORM_ROWS, norm1, 0)
        save(4).start()
        unit(0).start()

    def save_act(j):
        return pltpu.make_async_copy(pool.at[5], act_out.at[j], asem)

    def save_slope(j):
        return pltpu.make_async_copy(pool.at[6], slope_out.at[j], dsem)

    def widen(j):
        pl.when(j == 0)(lambda: unit(0).wait())

        @pl.when(j > 0)
        def _():
            save_act(j - 1).wait()
            save_slope(j - 1).wait()

        def up(cols, spot):
            value, slope = exact_gelu(dot(pool[4, spot], tile(4 + 2 * j, cols)) + bias(8 + j, cols))
            pool[5, spot, cols] = value.astype(bf16)
            pool[6, spot, cols] = slope.astype(bf16)

        tiles(UP_TILE, up)
        save_act(j).start()
        save_slope(j).start()

    def narrow(j):
        for cols in halves:
            hidden[:, cols] = hidden[:, cols] + dot(pool[5], tile(5 + 2 * j, cols))

    def feed(i):
        arrive(4 + i)
        pl.when(lax.rem(i, 2) == 0)(lambda: widen(i // 2))
        pl.when(lax.rem(i, 2) == 1)(lambda: narrow(i // 2))

    def norm2(i, carry):
        spot = span(i, NORM_ROWS)
        normed, inverse = rms_center(hidden[spot] + small_full[5:6, :])
        pool[5, spot] = (normed * small_full[6:7, :] + small_full[7:8, :]).astype(bf16)
        pool[6, spot] = normed.astype(bf16)
        inverse2[spot] = inverse
        return carry

    finish = pltpu.make_async_copy(pool.at[5], final_out, fsem.at[2])

    def second_norm():
        save_act(blocks - 1).wait()
        save_slope(blocks - 1).wait()
        lax.fori_loop(0, all_rows // NORM_ROWS, norm2, 0)
        finish.start()
        unit(1).start()

    def run(code):
        kind, m = divmod(code, 100)
        if kind == 5:
            up_across(m).start()
        else:
            (gather.step0, gather.step1, gather.step2, gather.step3)[kind - 1](m)

    items = [partial(quarter, 0), arrange, *(partial(quarter, i) for i in (1, 2, 3)), exchange_cores, sum_chip]
    items += [(3, project), (rounds, attend), join, first_norm, (2 * blocks, feed), second_norm]
    drive(FORWARD_ORDER, items, run)
    for m in range(count):
        gather.drain(m)
        keep(m).wait()
    for i in range(5):
        save(i).wait()
    up_own.wait()
    for i in range(pieces):
        up_across(i).wait()
    finish.wait()
    unit(1).wait()


def forward(x, attention_weights, expand, contract, small, slot_row, slots, nz, nx, tokens):
    f32, bf16 = jnp.float32, jnp.bfloat16
    shard_rows, width = attention_weights[0].shape
    count = 4 + 2 * contract.shape[0] // shard_rows
    small_shape = (16, width)
    all_rows = x.shape[0]
    assert slots.shape[0] * tokens == 2 * all_rows
    vmem, anywhere = pl.BlockSpec(memory_space=pltpu.VMEM), pl.BlockSpec(memory_space=pl.ANY)
    acts = (all_rows, width)
    rows = all_rows // tokens
    blocks = (count - 4) // 2
    dma = pltpu.SemaphoreType.DMA
    full = (count, 2, 2, nz, nx, shard_rows, width)
    out = jax.ShapeDtypeStruct
    return pl.pallas_call(
        partial(forward_kernel, nz, nx, [column_parts(width, s) for s in GATHER_SHARES], tokens, 2 * width // HEADS),
        out_shape=[
            out(full, bf16),
            out((rows * HEADS // 4, 4, tokens, tokens), bf16),
            out((5, *acts), bf16),
            out((blocks, *acts), bf16),
            out((blocks, *acts), bf16),
            out((2, *acts), bf16),
            out(acts, bf16),
            out(acts, bf16),
            out(acts, bf16),
            out(small_shape, f32),
            out((all_rows, 1), f32),
            out((all_rows, 1), f32),
        ],
        in_specs=[vmem, [vmem] * 4, vmem, vmem, [vmem] * len(small), pl.BlockSpec(memory_space=pltpu.SMEM), anywhere],
        out_specs=[anywhere] * 9 + [vmem] * 3,
        scratch_shapes=[
            pltpu.VMEM(full, bf16),
            pltpu.VMEM((count, shard_rows, width), bf16),
            pltpu.VMEM((7, *acts), bf16),
            pltpu.VMEM(acts, f32),
            pltpu.VMEM((2, *acts), bf16),
            *small_scratch(nz, small_shape)[:2],
            dma((count, 2 * nz + 5)),
            dma((count, 2 * nz + 5)),
            dma((2 + nz,)),
            dma((2 + nz,)),
            dma((2,)),
            dma((2,)),
            dma((count,)),
            dma((count,)),
            dma((slots.shape[0] + 1,)),
            dma((count,)),
            dma((5,)),
            dma,
            dma,
            dma((3,)),
            pltpu.VMEM((2, 4, tokens, tokens), bf16),
            dma((2,)),
        ],
        compiler_params=pltpu.CompilerParams(
            collective_id=1, has_side_effects=True, vmem_limit_bytes=60 * 2**20
        ),
    )(x, attention_weights, expand, contract, small, slot_row, slots)


def quietly(call):
    call()


def backward_kernel(
    nz, nx, parts, tokens, head_pair,
    x, own_up, across_up, final, unit, inverse1, inverse2, small_full, act, slope, saved, g, probs,
    out, small_out, input_out, table,
    rc, r3a, r3b, r2, rz, rcz, rcx, rcy, send, recv, total, landing, ssend, srecv,
    term, weight, pool, hidden, wsem, psem, hsem, tsend, trecv, across_send, across_recv, tsem, held_probs, ksem,
):
    f32, bf16 = jnp.float32, jnp.bfloat16
    count = out.shape[0]
    all_rows, width = x.shape
    rows = all_rows // tokens
    at = Partners(nz, nx)
    at.meet()
    scatter = Scatter(at, parts, rc, r3a, r3b, r2, rz, rcz, rcx, rcy, send, recv)
    sums = SmallSum(at, total, landing, ssend, srecv)

    here = pltpu.make_async_copy(final, table.at[at.y, at.core], tsem)
    to_sibling = remote(final, table.at[at.y, at.core], tsend.at[0], trecv.at[0], at.sibling)
    pieces = across_send.shape[0]

    def to_across(i):
        piece = pl.ds(i * (all_rows // pieces), all_rows // pieces)
        dst = table.at[at.y, at.core, piece]
        return remote(final.at[piece], dst, across_send.at[i], across_recv.at[i], at.across_y)

    passed = table.at[1 - at.y, at.core]
    pass_on = remote(passed, passed, tsend.at[1], trecv.at[1], at.sibling)

    def load(src, entry, i):
        return pltpu.make_async_copy(src, pool.at[entry], psem.at[i])

    def fetch(m, slot, i):
        return pltpu.make_async_copy(g.at[m], weight.at[slot], wsem.at[i])

    blocks = act.shape[0]
    up_block, down_block = (lambda j: 4 + 2 * j), (lambda j: 5 + 2 * j)
    unit2, own_load, across_load = load(unit.at[1], 1, 0), load(own_up, 2, 1), load(across_up, 3, 2)
    act_entry = [5, 2, 3, 5]
    act_load = [load(act.at[j], act_entry[j], 3 + j) for j in range(blocks)]
    slope_entry = [4, 2, 3, 4]
    slope_load = [load(slope.at[j], slope_entry[j], 7 + j) for j in range(blocks)]
    low_load, unit1, mixed_load = load(saved.at[4], 6, 11), load(unit.at[0], 5, 12), load(saved.at[3], 4, 13)
    query_load, key_load, value_load = (load(saved.at[i], (2, 3, 6)[i], 14 + i) for i in range(3))
    x_load = load(x, 4, 17)
    down_fetch = [fetch(down_block(j), 0, 2 * j) for j in range(blocks)]
    up_fetch = [fetch(up_block(j), 1, 2 * j + 1) for j in range(blocks)]
    last = 2 * blocks
    output_fetch, query_fetch, key_fetch, value_fetch = (
        fetch(m, slot, last + i) for i, (m, slot) in enumerate(((3, 0), (0, 1), (1, 0), (2, 1)))
    )
    for copy in (unit2, own_load, across_load, act_load[0], down_fetch[0], up_fetch[0], slope_load[0], low_load):
        copy.start()
    to_sibling.start()
    here.start()
    total[0] = jnp.zeros_like(total[0])

    def folded(block):
        return jnp.sum(block.reshape(-1, 8, block.shape[-1]), axis=0)

    def norm_back(gain_row, shift_row, low_row, inverse, incoming, normed_entry, low_entry):
        def body(i, carry):
            spot = span(i, NORM_ROWS)
            grad, normed = incoming(spot), pool[normed_entry, spot].astype(f32)
            scaled = grad * small_full[gain_row : gain_row + 1, :]
            inner = (
                scaled
                - jnp.mean(scaled, axis=-1, keepdims=True)
                - normed * jnp.mean(scaled * normed, axis=-1, keepdims=True)
            )
            result = inner * inverse[spot]
            low = result.astype(bf16)
            hidden[spot] = result
            pool[low_entry, spot] = low
            return tuple(c + folded(b) for c, b in zip(carry, (grad * normed, grad, low.astype(f32))))

        zero = jnp.zeros((8, width), f32)
        found = lax.fori_loop(0, all_rows // NORM_ROWS, body, (zero, zero, zero))
        for row, value in zip((gain_row, shift_row, low_row), found):
            total[0, row : row + 1, :] = jnp.sum(value, axis=0, keepdims=True)

    def turned(slot):
        for y in range(2):
            yield pl.ds(y * width // 2, width // 2), weight[slot, y].reshape(width // 2, width)

    def own_half(slot):
        return term[slot, :, at.core]

    def half(i, m, left, right):
        core = lax.rem(at.core + 1 + i, 2)
        for y in range(2):
            picked = span(y * 2 + core, width // 4)
            value = down(pool[left, :, picked], pool[right]).astype(bf16)
            term[lax.rem(m, 2), y, core] = value.reshape(nz, nx, -1, width)
        pl.when(i == 0)(lambda: scatter.start(m, term.at[lax.rem(m, 2), :, 1 - at.core]))

    def run(code):
        kind, m = divmod(code, 100)
        if kind == 5:
            to_across(m).start()
        elif kind == 1:
            scatter.step1(m, own_half(m % 2))
        elif kind == 4:
            scatter.step4(m, out)
        else:
            (scatter.step2, scatter.step3)[kind - 2](m)

    def when(value, calls):
        for at_value, call in calls.items():
            pl.when(value == at_value)(partial(quietly, call))

    def load_second():
        for copy in (unit2, own_load, across_load):
            copy.wait()

    def second_norm():
        norm_back(6, 7, 5, inverse2, lambda spot: added(pool[2, spot], pool[3, spot]), 1, 0)
        act_load[1].start()
        act_load[2].start()

    def contract_term(i):
        j = i // 2
        middle = j * (3 - j) // 2
        when(i, {2 * n: act_load[n].wait for n in range(blocks)})
        half(lax.rem(i, 2), j, middle * (j + 1) + (1 - middle) * 5, 0)
        when(i, {1: act_load[3].start, 3: slope_load[1].start, 5: slope_load[2].start, 7: unit1.start})

    def widen_back(j):
        for n in range(blocks):
            when(j, {n: down_fetch[n].wait})
            when(j, {n: slope_load[n].wait})
        middle = j * (3 - j) // 2
        entry = middle * (j + 1) + (1 - middle) * 4
        for cols, part in turned(0):
            value = (across(pool[0], part) * pool[entry, :, cols].astype(f32)).astype(bf16)
            pool[1, :, cols] = value
            total[0, pl.ds(8 + j, 1), cols] = jnp.sum(value.astype(f32), axis=0, keepdims=True)
        fetches = [*down_fetch[1:], output_fetch]
        when(j, {n: fetches[n].start for n in range(blocks)})
        when(j, {0: slope_load[3].start, 1: query_load.start, 2: key_load.start, 3: mixed_load.start})

    def narrow_back(j):
        when(j, {n: up_fetch[n].wait for n in range(blocks)})
        for cols, part in turned(1):
            hidden[:, cols] = hidden[:, cols] + across(pool[1], part)
        fetches = [*up_fetch[1:], query_fetch]
        when(j, {n: fetches[n].start for n in range(blocks)})
        when(j, {blocks - 1: value_load.start})

    def feed_back(i):
        j, kind = i // 4, lax.rem(i, 4)
        when(i, {1: low_load.wait})
        pl.when(kind == 0)(lambda: widen_back(j))
        pl.when((kind == 1) | (kind == 2))(lambda: half(kind - 1, blocks + j, 6, 1))
        pl.when(kind == 3)(lambda: narrow_back(j))

    def first_norm():
        unit1.wait()
        norm_back(3, 4, 2, inverse1, lambda spot: hidden[spot], 5, 0)

    def mixed_back():
        output_fetch.wait()
        for cols, part in turned(0):
            pool[1, :, cols] = across(pool[0], part).astype(bf16)
        key_fetch.start()
        for copy in (query_load, key_load, value_load):
            copy.wait()
        fetch_probs(0).start()

    def output_term(i):
        when(i, {0: mixed_load.wait})
        half(i, jnp.int32(2 * blocks), 4, 0)
        when(i, {1: x_load.start})

    pairs = width // head_pair
    masks = half_masks(head_pair)
    scale = (head_pair // 2) ** (-0.5)

    def fetch_probs(i):
        slot = lax.rem(i, 2)
        return pltpu.make_async_copy(probs.at[i], held_probs.at[slot], ksem.at[slot])

    rounds = rows * pairs // 2

    def attend(i):
        pl.when(i + 1 < rounds)(lambda: fetch_probs(i + 1).start())
        fetch_probs(i).wait()
        spot, base = span(i // (pairs // 2), tokens), lax.rem(i, pairs // 2) * 2
        for p in range(2):
            cols = span(base + p, head_pair)
            query, keys, values, mixed_grad = (pool[e, spot, cols] for e in (2, 3, 6, 1))
            query_grad = key_grad = value_grad = None
            for h, mask in enumerate(masks):
                own_keys = keys * (mask * jnp.asarray(scale, bf16))
                low = held_probs[lax.rem(i, 2), 2 * p + h]
                prob = low.astype(f32)
                prob_grad = across(values * mask, mixed_grad)
                weighed = prob * prob_grad
                score_grad = (weighed - prob * jnp.sum(weighed, axis=0, keepdims=True)).astype(bf16)
                terms = (
                    down(score_grad, own_keys),
                    dot(score_grad, query * mask),
                    dot(low, mixed_grad * mask),
                )
                if query_grad is None:
                    query_grad, key_grad, value_grad = terms
                else:
                    query_grad, key_grad, value_grad = query_grad + terms[0], key_grad + terms[1], value_grad + terms[2]
            query_grad, value_grad = query_grad.astype(bf16), value_grad.astype(bf16)
            pool[2, spot, cols] = query_grad
            pool[3, spot, cols] = (key_grad * scale).astype(bf16)
            pool[6, spot, cols] = value_grad
            for row, value in ((0, query_grad), (1, value_grad)):
                found = jnp.sum(value.astype(f32), axis=0, keepdims=True)
                total[0, row : row + 1, cols] = total[0, row : row + 1, cols] + found

    def projection_term(i):
        n = i // 2
        later = (n + 1) // 2
        when(i, {0: x_load.wait})
        when(i, {0: sums.start})
        half(lax.rem(i, 2), 2 * blocks + 1 + n, 4, later * (n + 1) + (1 - later) * 6)
        when(i, {2 * n + 1: partial(sums.step, n) for n in range(3)})

    def pass_rows():
        for i in range(pieces):
            to_across(i).wait_recv()
        pass_on.start()

    done = pltpu.make_async_copy(hidden, input_out, hsem)

    def input_back(i):
        when(i, {0: query_fetch.wait, 1: key_fetch.wait, 2: value_fetch.wait})
        for cols, part in turned(lax.rem(i + 1, 2)):
            hidden[:, cols] = hidden[:, cols] + across(pool[2 + i + i // 2 * 2], part)
        when(i, {0: value_fetch.start, 1: pass_rows, 2: done.start})

    items = [load_second, second_norm, (2 * blocks, contract_term), (4 * blocks, feed_back), first_norm]
    items += [(2, output_term), mixed_back, (rounds, attend), (6, projection_term), (3, input_back)]
    drive(BACKWARD_ORDER, items, run)
    sums.finish(small_out)
    done.wait()

    for m in range(count):
        scatter.drain(m)
    here.wait()
    to_sibling.wait()
    for i in range(pieces):
        to_across(i).wait_send()
    pass_on.wait()


def backward(
    x, own_up, across_up, final, unit, inverse1, inverse2, small_full, act, slope, saved, g, probs, nz, nx, tokens
):
    f32, bf16 = jnp.float32, jnp.bfloat16
    count, _, _, _, _, shard_rows, width = g.shape
    acts = x.shape
    parts = [column_parts(width, s) for s in SCATTER_SHARES]
    vmem, anywhere = pl.BlockSpec(memory_space=pltpu.VMEM), pl.BlockSpec(memory_space=pl.ANY)
    dma = pltpu.SemaphoreType.DMA
    out = jax.ShapeDtypeStruct
    block = (2, 2, nz, nx, shard_rows, width)
    return pl.pallas_call(
        partial(backward_kernel, nz, nx, parts, tokens, 2 * width // HEADS),
        out_shape=[
            out((count, shard_rows, width), f32),
            out(small_full.shape, f32),
            out(acts, f32),
            out((2, 2, *acts), bf16),
        ],
        in_specs=[anywhere] * 5 + [vmem] * 3 + [anywhere] * 5,
        out_specs=[vmem, vmem, anywhere, anywhere],
        scratch_shapes=[
            *scatter_scratch(count, nz, nx, shard_rows, width, parts),
            *small_scratch(nz, small_full.shape),
            pltpu.VMEM((2, *block), bf16),
            pltpu.VMEM((2, *block), bf16),
            pltpu.VMEM((7, *acts), bf16),
            pltpu.VMEM(acts, f32),
            dma((count,)),
            dma((18,)),
            dma,
            dma((2,)),
            dma((2,)),
            dma((count,)),
            dma((count,)),
            dma,
            pltpu.VMEM((2, 4, tokens, tokens), bf16),
            dma((2,)),
        ],
        compiler_params=pltpu.CompilerParams(
            collective_id=2, has_side_effects=True, vmem_limit_bytes=63 * 2**20
        ),
    )(x, own_up, across_up, final, unit, inverse1, inverse2, small_full, act, slope, saved, g, probs)


def finish_kernel(
    slot_row, live_count, me, first, second, full, sums, small_sums,
    slot_acts, input_grad, query, keys, values, output, up, contract, *small,
):
    s = pl.program_id(0)
    slot_acts[0] = first[0]
    slot_acts[1] = second[0]
    input_grad[...] = jnp.where(s < live_count[0], full[...], 0.0)

    @pl.when(s == 0)
    def _():
        blocks = (sums.shape[0] - 4) // 2
        shard, width = query.shape
        for j in range(blocks):
            contract[j * shard : (j + 1) * shard, :] = sums[j]
        lanes = 128
        per = lanes // shard
        for q in range(width // lanes):
            part = [sums[blocks + j, :, q * lanes : (q + 1) * lanes] for j in range(blocks)]
            for t in range(per):
                found = jnp.concatenate([p[:, t * shard : (t + 1) * shard] for p in part], axis=1)
                at = (q * per + t) * blocks * shard
                up[:, at : at + blocks * shard] = found
        for i, ref in enumerate((output, values, query, keys)):
            ref[...] = sums[2 * blocks + i]
        own = pltpu.roll(small_sums[...], width - me[0] * shard, 1)
        for i in range(8):
            small[i][...] = own[i, :shard]
        small[8][...] = jnp.concatenate([own[8 + j : 9 + j, :shard] for j in range(blocks)], axis=1)[0]


def finish(slot_row, live_count, table, full, sums, small_sums):
    f32 = jnp.float32
    members, tokens, width = table.shape
    slots, rows = slot_row.shape[0], full.shape[0]
    assert slots == 2 * rows
    count, shard, _ = sums.shape
    blocks = (count - 4) // 2
    me = lax.axis_index(("dp", "fsdp")).astype(jnp.int32).reshape(1)
    block, pair = (1, tokens, width), (2, tokens, width)

    def fixed(shape):
        return pl.BlockSpec(shape, lambda s, *_: (0,) * len(shape))

    fixed_outs = [(shard, width)] * 4 + [(shard, blocks * width), (blocks * shard, width)]
    fixed_outs += [(shard,)] * 8 + [(blocks * shard,)]
    row = pl.BlockSpec(block, lambda s, *_: (s, 0, 0))

    def chosen(i):
        return pl.BlockSpec(block, lambda s, slot_row, *_: (jnp.clip(slot_row[2 * s + i], 0, members - 1), 0, 0))

    out = jax.ShapeDtypeStruct
    return pl.pallas_call(
        finish_kernel,
        out_shape=[
            out((slots, tokens, width), table.dtype),
            out(full.shape, f32),
            *(out(shape, f32) for shape in fixed_outs),
        ],
        grid_spec=pltpu.PrefetchScalarGridSpec(
            num_scalar_prefetch=3,
            grid=(rows,),
            in_specs=[
                chosen(0),
                chosen(1),
                row,
                fixed(sums.shape),
                fixed(small_sums.shape),
            ],
            out_specs=[
                pl.BlockSpec(pair, lambda s, *_: (s, 0, 0)),
                row,
                *(fixed(shape) for shape in fixed_outs),
            ],
        ),
        compiler_params=pltpu.CompilerParams(vmem_limit_bytes=63 * 2**20),
    )(slot_row, live_count, me, table, table, full, sums, small_sums)


def on_device_kernels(
    rows_in,
    slot_row,
    live_count,
    slot_activation_gradient,
    query_weight,
    key_weight,
    value_weight,
    output_weight,
    query_bias,
    value_bias,
    output_bias,
    attn_gain,
    attn_shift,
    expand_weight,
    up_bias,
    down_weight,
    down_bias,
    ffn_gain,
    ffn_shift,
):
    row_count, token_count, width = rows_in.shape
    nx = 2
    nz = lax.axis_size("fsdp") // nx
    small = [query_bias, value_bias, output_bias, attn_gain, attn_shift, down_bias, ffn_gain, ffn_shift, up_bias]
    x = rows_in.reshape(-1, width)
    g, probs, saved, act, slope, unit, final, own_up, across_up, small_full, inverse1, inverse2 = forward(
        x,
        [query_weight, key_weight, value_weight, output_weight],
        expand_weight,
        down_weight,
        small,
        slot_row,
        slot_activation_gradient,
        nz,
        nx,
        token_count,
    )
    sums, small_sums, input_full, table = backward(
        x,
        own_up,
        across_up,
        final,
        unit,
        inverse1,
        inverse2,
        small_full,
        act,
        slope,
        saved,
        g,
        probs,
        nz,
        nx,
        token_count,
    )
    slot_acts, input_grad, query, keys, values, output, up, contract, *small_grads = finish(
        slot_row,
        live_count,
        table.reshape(-1, token_count, width),
        input_full.reshape(rows_in.shape),
        sums,
        small_sums,
    )
    return (
        slot_acts,
        input_grad,
        query,
        keys,
        values,
        output,
        *small_grads[:5],
        up,
        small_grads[8],
        contract,
        *small_grads[5:8],
    )


def norm_forward(hidden, gain, shift):
    center = hidden - jnp.mean(hidden, axis=-1, keepdims=True)
    inverse = lax.rsqrt(jnp.mean(center * center, axis=-1, keepdims=True) + EPSILON)
    normed = center * inverse
    return (normed * gain + shift, normed, inverse)


def norm_backward(incoming, gain, normed, inverse):
    scaled = incoming * gain
    inner = (
        scaled
        - jnp.mean(scaled, axis=-1, keepdims=True)
        - normed * jnp.mean(scaled * normed, axis=-1, keepdims=True)
    )
    return (
        inner * inverse,
        jnp.sum(incoming * normed, axis=(0, 1)),
        jnp.sum(incoming, axis=(0, 1)),
    )


def apply_weight(acts, weight):
    return jnp.einsum("rsd,de->rse", acts, weight, preferred_element_type=jnp.float32)


def apply_back(grads, weight):
    return jnp.einsum("rse,de->rsd", grads, weight, preferred_element_type=jnp.float32)


def weight_term(acts, grads):
    return jnp.einsum("rsd,rse->de", acts, grads, preferred_element_type=jnp.float32)


def bias_term(grads):
    return jnp.sum(grads, axis=(0, 1), dtype=jnp.float32)


def on_device_plain(
    rows_in,
    slot_row,
    live_count,
    slot_activation_gradient,
    query_weight,
    key_weight,
    value_weight,
    output_weight,
    query_bias,
    value_bias,
    output_bias,
    attn_gain,
    attn_shift,
    expand_weight,
    up_bias,
    down_weight,
    down_bias,
    ffn_gain,
    ffn_shift,
):
    row_count, token_count, feature_count = rows_in.shape
    head_size = feature_count // HEADS
    score_scale = head_size ** (-0.5)
    split_shape = (row_count, token_count, HEADS, head_size)
    wanted = lax.broadcasted_iota(
        jnp.int32, (row_count * lax.axis_size("dp"), slot_row.shape[0]), 0
    )
    one_hot_matrix = (wanted == slot_row[None, :]).astype(jnp.bfloat16)
    upstream = lax.psum_scatter(
        jnp.einsum(
            "az,zfy->afy",
            one_hot_matrix,
            slot_activation_gradient,
            preferred_element_type=jnp.float32,
        ).astype(jnp.bfloat16),
        "dp",
        scatter_dimension=0,
        tiled=True,
    ).astype(jnp.float32)
    smalls = (query_bias, value_bias, output_bias, attn_gain, attn_shift, down_bias, ffn_gain, ffn_shift)
    small_rows = query_bias.shape[0]
    packed = jnp.concatenate([v.reshape(-1, small_rows) for v in (*smalls, up_bias)], axis=0)
    packed_full = lax.all_gather(packed, ("dp", "fsdp"), axis=0)
    (
        qbias_full,
        vbias_full,
        obias_full,
        gain1_full,
        shift1_full,
        downbias_full,
        gain2_full,
        shift2_full,
    ) = (packed_full[:, i].reshape(-1) for i in range(8))
    upbias_full = packed_full[:, 8:].reshape(-1)
    query_full, key_full, value_full, output_full, up_full, down_full = (
        lax.all_gather(weight, ("dp", "fsdp"), axis=0, tiled=True)
        for weight in (query_weight, key_weight, value_weight, output_weight, expand_weight, down_weight)
    )
    inputs = rows_in.astype(jnp.float32)
    query = (apply_weight(rows_in, query_full) + qbias_full.astype(jnp.float32)).astype(
        jnp.bfloat16
    )
    keys = apply_weight(rows_in, key_full).astype(jnp.bfloat16)
    values = (apply_weight(rows_in, value_full) + vbias_full.astype(jnp.float32)).astype(
        jnp.bfloat16
    )
    query_heads = query.reshape(split_shape)
    key_heads = keys.reshape(split_shape)
    value_heads = values.reshape(split_shape)
    scores = (
        jnp.einsum("rqhd,rkhd->rhqk", query_heads, key_heads, preferred_element_type=jnp.float32)
        * score_scale
    )
    row_top = jnp.max(scores, axis=-1, keepdims=True)
    expo = jnp.exp(scores - row_top)
    row_sum = jnp.sum(expo, axis=-1, keepdims=True)
    logsum = row_top + jnp.log(row_sum)
    probs_low = (expo / row_sum).astype(jnp.bfloat16)
    mixed = jnp.einsum(
        "rhqk,rkhd->rqhd", probs_low, value_heads, preferred_element_type=jnp.float32
    )
    mixed = mixed.reshape(row_count, token_count, feature_count).astype(jnp.bfloat16)
    gain1 = gain1_full.astype(jnp.float32)
    resid1 = inputs + apply_weight(mixed, output_full) + obias_full.astype(jnp.float32)
    normed1_out, normed1, inverse1 = norm_forward(resid1, gain1, shift1_full.astype(jnp.float32))
    normed1_low = normed1_out.astype(jnp.bfloat16)
    pre_act = apply_weight(normed1_low, up_full) + upbias_full.astype(jnp.float32)
    act_low = jax.nn.gelu(pre_act, approximate=False).astype(jnp.bfloat16)
    gain2 = gain2_full.astype(jnp.float32)
    resid2 = normed1_out + apply_weight(act_low, down_full) + downbias_full.astype(jnp.float32)
    final, second_normed, inverse2 = norm_forward(resid2, gain2, shift2_full.astype(jnp.float32))
    final_low = final.astype(jnp.bfloat16)
    shard_rows = lax.all_gather(final_low, "dp", axis=0, tiled=True)
    span_rows = shard_rows.shape[0]
    inside = (slot_row >= 0) & (slot_row < span_rows)
    picked = jnp.take(shard_rows, jnp.clip(slot_row, 0, span_rows - 1), axis=0)
    slot_acts = jnp.where(
        inside[:, None, None], picked, jnp.zeros(slot_activation_gradient.shape, jnp.bfloat16)
    )
    gain1 = gain1_full.astype(jnp.float32)
    gain2 = gain2_full.astype(jnp.float32)
    grad2, gain2_grad, shift2_grad = norm_backward(upstream, gain2, second_normed, inverse2)
    ffn_low = grad2.astype(jnp.bfloat16)
    down_grad = weight_term(act_low, ffn_low)
    down_bias_grad = bias_term(ffn_low)
    act_grad = apply_back(ffn_low, down_full)
    gelu_value, gelu_back = jax.vjp(partial(jax.nn.gelu, approximate=False), pre_act)
    pre_grad = gelu_back(act_grad)[0].astype(jnp.bfloat16)
    up_grad = weight_term(normed1_low, pre_grad)
    up_bias_grad = bias_term(pre_grad)
    normed1_grad = grad2 + apply_back(pre_grad, up_full)
    grad1, gain1_grad, shift1_grad = norm_backward(normed1_grad, gain1, normed1, inverse1)
    attn_low = grad1.astype(jnp.bfloat16)
    output_grad = weight_term(mixed, attn_low)
    output_bias_grad = bias_term(attn_low)
    mixed_grad = apply_back(attn_low, output_full).astype(jnp.bfloat16).reshape(split_shape)
    scores_again = (
        jnp.einsum("rqhd,rkhd->rhqk", query_heads, key_heads, preferred_element_type=jnp.float32)
        * score_scale
    )
    probs = jnp.exp(scores_again - logsum)
    probs_again = probs.astype(jnp.bfloat16)
    value_grad = jnp.einsum(
        "rhqk,rqhd->rkhd", probs_again, mixed_grad, preferred_element_type=jnp.float32
    )
    value_grad = value_grad.astype(jnp.bfloat16).reshape(row_count, token_count, feature_count)
    prob_grad = jnp.einsum(
        "rqhd,rkhd->rhqk", mixed_grad, value_heads, preferred_element_type=jnp.float32
    )
    score_grad = (probs * (prob_grad - jnp.sum(probs * prob_grad, axis=-1, keepdims=True))).astype(
        jnp.bfloat16
    )
    query_grad = (
        jnp.einsum("rhqk,rkhd->rqhd", score_grad, key_heads, preferred_element_type=jnp.float32)
        * score_scale
    )
    query_grad = query_grad.astype(jnp.bfloat16).reshape(row_count, token_count, feature_count)
    key_grad = (
        jnp.einsum("rhqk,rqhd->rkhd", score_grad, query_heads, preferred_element_type=jnp.float32)
        * score_scale
    )
    key_grad = key_grad.astype(jnp.bfloat16).reshape(row_count, token_count, feature_count)
    query_wgrad = weight_term(rows_in, query_grad)
    key_wgrad = weight_term(rows_in, key_grad)
    value_wgrad = weight_term(rows_in, value_grad)
    query_bias_grad = bias_term(query_grad)
    value_bias_grad = bias_term(value_grad)
    input_full = (
        grad1
        + apply_back(query_grad, query_full)
        + apply_back(key_grad, key_full)
        + apply_back(value_grad, value_full)
    )
    live_rows = lax.broadcasted_iota(jnp.int32, (row_count,), 0) < live_count[0]
    input_grad = jnp.where(live_rows[:, None, None], input_full, 0.0)
    devices = packed_full.shape[0]
    small_terms = jnp.concatenate(
        [
            v.reshape(devices, -1, small_rows)
            for v in (
                query_bias_grad,
                value_bias_grad,
                output_bias_grad,
                gain1_grad,
                shift1_grad,
                down_bias_grad,
                gain2_grad,
                shift2_grad,
                up_bias_grad,
            )
        ],
        axis=1,
    )
    small_sum = lax.psum_scatter(small_terms, ("dp", "fsdp"), scatter_dimension=0, tiled=True)[0]
    down_sum, up_sum, output_sum, value_sum, query_sum, key_sum = (
        lax.psum_scatter(
            term.astype(jnp.bfloat16), ("dp", "fsdp"), scatter_dimension=0, tiled=True
        ).astype(jnp.float32)
        for term in (down_grad, up_grad, output_grad, value_wgrad, query_wgrad, key_wgrad)
    )
    return (
        slot_acts,
        input_grad,
        query_sum,
        key_sum,
        value_sum,
        output_sum,
        small_sum[0],
        small_sum[1],
        small_sum[2],
        small_sum[3],
        small_sum[4],
        up_sum,
        small_sum[8:].reshape(-1),
        down_sum,
        small_sum[5],
        small_sum[6],
        small_sum[7],
    )


def solution(mesh):
    placed = (
        P(("dp", "fsdp"), None, None),
        P(("dp", "fsdp")),
        P(("dp", "fsdp")),
        P(("dp", "fsdp"), None, None),
        P(("dp", "fsdp"), None),
        P(("dp", "fsdp"), None),
        P(("dp", "fsdp"), None),
        P(("dp", "fsdp"), None),
        P(("dp", "fsdp")),
        P(("dp", "fsdp")),
        P(("dp", "fsdp")),
        P(("dp", "fsdp")),
        P(("dp", "fsdp")),
        P(("dp", "fsdp"), None),
        P(("dp", "fsdp")),
        P(("dp", "fsdp"), None),
        P(("dp", "fsdp")),
        P(("dp", "fsdp")),
        P(("dp", "fsdp")),
    )
    kernels = mesh.shape["dp"] == 4 and mesh.shape["fsdp"] == 8
    return jax.shard_map(
        on_device_kernels if kernels else on_device_plain,
        mesh=mesh,
        in_specs=placed,
        out_specs=(
            P(("dp", "fsdp"), None, None),
            P(("dp", "fsdp"), None, None),
            P(("dp", "fsdp"), None),
            P(("dp", "fsdp"), None),
            P(("dp", "fsdp"), None),
            P(("dp", "fsdp"), None),
            P(("dp", "fsdp")),
            P(("dp", "fsdp")),
            P(("dp", "fsdp")),
            P(("dp", "fsdp")),
            P(("dp", "fsdp")),
            P(("dp", "fsdp"), None),
            P(("dp", "fsdp")),
            P(("dp", "fsdp"), None),
            P(("dp", "fsdp")),
            P(("dp", "fsdp")),
            P(("dp", "fsdp")),
        ),
        check_vma=False,
    )
```

```python
import math
from functools import partial

import jax
import jax.numpy as jnp
from jax import lax
from jax.experimental import pallas as pl
from jax.experimental.pallas import tpu as pltpu
from jax.sharding import PartitionSpec as P

HEADS = 16


EPSILON = 1e-05


MESH = pl.DeviceIdType.MESH
LANES = 128


def place(nz, nx):
    dp, fs = lax.axis_index("dp"), lax.axis_index("fsdp")
    y, core = dp // 2, lax.rem(dp, 2)
    z, x = fs // nx, lax.rem(fs, nx)
    return y, core, z, x


def device(y, core, z, x, nx):
    return (y * 2 + core, z * nx + x)


class Partners:
    def __init__(self, nz, nx):
        self.nz, self.nx = nz, nx
        self.y, self.core, self.z, self.x = place(nz, nx)
        y, core, z, x = self.y, self.core, self.z, self.x
        self.sibling = device(y, 1 - core, z, x, nx)
        self.across_x = device(y, core, z, 1 - x, nx)
        self.across_y = device(1 - y, core, z, x, nx)
        self.along_z = [device(y, core, lax.rem(z + k, nz), x, nx) for k in range(1, nz)]
        self.all = [self.sibling, self.across_x, self.across_y, *self.along_z]

    def meet(self):
        barrier = pltpu.get_barrier_semaphore()
        for other in self.all:
            pl.semaphore_signal(barrier, inc=1, device_id=other, device_id_type=MESH)
        pl.semaphore_wait(barrier, len(self.all))


def remote(src, dst, send, recv, to):
    return pltpu.make_async_remote_copy(
        src_ref=src, dst_ref=dst, send_sem=send, recv_sem=recv, device_id=to, device_id_type=MESH
    )


def added(*blocks):
    total = blocks[0].astype(jnp.float32)
    for block in blocks[1:]:
        total = total + block.astype(jnp.float32)
    return total


class Scatter:
    def __init__(self, at, parts, rc, r3a, r3b, r2, rz, rcz, rcx, rcy, send, recv):
        self.at, self.parts = at, parts
        self.rc, self.r3a, self.r3b, self.r2, self.rz = rc, r3a, r3b, r2, rz
        self.rcz, self.rcx, self.rcy = rcz, rcx, rcy
        self.send, self.recv = send, recv

    def copy(self, m, i, src, dst, to):
        return remote(src, dst, self.send.at[m, i], self.recv.at[m, i], to)

    def to_sibling(self, m, theirs):
        return self.copy(m, 0, theirs, self.rc.at[m], self.at.sibling)

    def landings(self, m):
        a, b, c, _ = self.parts[m]
        a, b, c = (pl.ds(0, part.size) for part in (a, b, c))
        return (
            self.r3a.at[m, :, :, :, a],
            self.r3b.at[m, :, :, :, b],
            self.rcz.at[m, :, :, :, :, c],
            self.rcx.at[m, :, :, c],
            self.rcy.at[m, :, c],
        )

    def firsts(self, m):
        at, rc, nz = self.at, self.rc, self.at.nz
        a, b, c, _ = self.parts[m]
        r3a, r3b, rcz, _, _ = self.landings(m)
        return [
            self.copy(m, 1, rc.at[m, :, :, 1 - at.x, :, a], r3a, at.across_x),
            self.copy(m, 2, rc.at[m, 1 - at.y, :, :, :, b], r3b, at.across_y),
        ] + [
            self.copy(
                m, 2 + k, rc.at[m, :, lax.rem(at.z + k, nz), :, :, c], rcz.at[k - 1], at.along_z[k - 1]
            )
            for k in range(1, nz)
        ]

    def seconds(self, m):
        at, nz = self.at, self.at.nz
        a, b, _, _ = self.parts[m]
        r3a, r3b, rcz, rcx, _ = self.landings(m)
        return [
            self.copy(m, nz + 2, r3a.at[1 - at.y], self.r2.at[m, :, :, a], at.across_y),
            self.copy(m, nz + 3, r3b.at[:, 1 - at.x], self.r2.at[m, :, :, b], at.across_x),
            self.copy(m, nz + 4, rcz.at[0, :, 1 - at.x], rcx, at.across_x),
        ]

    def thirds(self, m):
        at, nz = self.at, self.at.nz
        ab = self.parts[m][3]
        rcx, rcy = self.landings(m)[3:]
        return [
            self.copy(
                m,
                nz + 4 + k,
                self.r2.at[m, lax.rem(at.z + k, nz), :, ab],
                self.rz.at[m, k - 1, :, ab],
                at.along_z[k - 1],
            )
            for k in range(1, nz)
        ] + [self.copy(m, 2 * nz + 4, rcx.at[1 - at.y], rcy, at.across_y)]

    def start(self, m, theirs):
        self.to_sibling(m, theirs).start()

    def step1(self, m, own):
        rc = self.rc
        self.to_sibling(m, rc.at[m]).wait_recv()

        rc[m] = added(rc[m], own).astype(rc.dtype)
        self.to_sibling(m, rc.at[m]).wait_send()
        for copy in self.firsts(m):
            copy.start()

    def step2(self, m):
        at, rc = self.at, self.rc
        a, b, c, _ = self.parts[m]
        r3a, r3b, rcz, _, _ = self.landings(m)
        for copy in self.firsts(m):
            copy.wait_recv()

        r3a[...] = added(r3a[...], rc[m, :, :, at.x, :, a]).astype(rc.dtype)
        r3b[...] = added(r3b[...], rc[m, at.y, :, :, :, b]).astype(rc.dtype)
        others = [rcz[k] for k in range(at.nz - 1)]
        rcz[0] = added(rc[m, :, at.z, :, :, c], *others).astype(rc.dtype)
        for copy in self.seconds(m):
            copy.start()

    def step3(self, m):
        at, r2 = self.at, self.r2
        a, b, _, _ = self.parts[m]
        r3a, r3b, rcz, rcx, _ = self.landings(m)
        for copy in self.seconds(m):
            copy.wait_recv()

        r2[m, :, :, a] = added(r2[m, :, :, a], r3a[at.y]).astype(r2.dtype)
        r2[m, :, :, b] = added(r2[m, :, :, b], r3b[:, at.x]).astype(r2.dtype)
        rcx[...] = added(rcx[...], rcz[0, :, at.x]).astype(r2.dtype)
        for copy in self.thirds(m):
            copy.start()

    def step4(self, m, out):
        at = self.at
        _, _, c, ab = self.parts[m]
        rcx, rcy = self.landings(m)[3:]
        for copy in self.thirds(m):
            copy.wait_recv()
        others = [self.rz[m, k, :, ab] for k in range(at.nz - 1)]
        out[m, :, ab] = added(self.r2[m, at.z, :, ab], *others)
        out[m, :, c] = added(rcx[at.y], rcy[...])

    def drain(self, m):
        for copy in self.firsts(m) + self.seconds(m) + self.thirds(m):
            copy.wait_send()


class SmallSum:
    def __init__(self, at, total, landing, send, recv):
        self.at, self.total, self.landing, self.send, self.recv = at, total, landing, send, recv

    def hop(self, i, to):
        return remote(self.total.at[i], self.landing.at[i], self.send.at[i], self.recv.at[i], to)

    def along(self, k):
        i = 2 + k
        return remote(self.total.at[3], self.landing.at[i], self.send.at[i], self.recv.at[i], self.at.along_z[k - 1])

    def start(self):
        self.hop(0, self.at.sibling).start()

    def step(self, i):
        at = self.at
        to = (at.sibling, at.across_x, at.across_y)
        self.hop(i, to[i]).wait_recv()
        self.total[i + 1] = self.total[i] + self.landing[i]
        if i < 2:
            self.hop(i + 1, to[i + 1]).start()
        else:
            for k in range(1, at.nz):
                self.along(k).start()

    def finish(self, out):
        at = self.at
        for k in range(1, at.nz):
            self.along(k).wait_recv()
        total = self.total[3]
        for k in range(1, at.nz):
            total = total + self.landing[2 + k]
        out[...] = total
        to = (at.sibling, at.across_x, at.across_y)
        for i in range(3):
            self.hop(i, to[i]).wait_send()
        for k in range(1, at.nz):
            self.along(k).wait_send()


def scatter_scratch(count, nz, nx, rows, columns, parts):
    bf16 = jnp.bfloat16
    a, b, c, ab = (max(part[i].size for part in parts) for i in range(4))
    return [
        pltpu.VMEM((count, 2, nz, nx, rows, columns), bf16),
        pltpu.VMEM((count, 2, nz, rows, a), bf16),
        pltpu.VMEM((count, nz, nx, rows, b), bf16),
        pltpu.VMEM((count, nz, rows, ab), bf16),
        pltpu.VMEM((count, nz - 1, rows, ab), bf16),
        pltpu.VMEM((count, nz - 1, 2, nx, rows, c), bf16),
        pltpu.VMEM((count, 2, rows, c), bf16),
        pltpu.VMEM((count, rows, c), bf16),
        pltpu.SemaphoreType.DMA((count, 2 * nz + 5)),
        pltpu.SemaphoreType.DMA((count, 2 * nz + 5)),
    ]


def small_scratch(nz, shape):
    return [
        pltpu.VMEM((4, *shape), jnp.float32),
        pltpu.VMEM((2 + nz, *shape), jnp.float32),
        pltpu.SemaphoreType.DMA((2 + nz,)),
        pltpu.SemaphoreType.DMA((2 + nz,)),
    ]


GATHER_SHARES = [
    (6, 1), (4, 2), (6, 1), (3, 4), (6, 1), (4, 3), (3, 4), (5, 1), (5, 1), (6, 1), (4, 2), (5, 1),
]
SCATTER_SHARES = [
    (5, 1), (4, 2), (6, 1), (4, 2), (4, 2), (4, 2), (5, 2), (6, 1), (6, 1), (5, 2), (4, 3), (3, 3),
]

FORWARD_ORDER = (
    100, 101, 102, 103, 0, 0, 104, 105, 0, 0, 0, 0, 200, 0, 201, 500, 300, 202, 301, 203, 302, 204, 205, 501,
    303, 400, 106, 0, 401, 107, 502, 304, 0, 402, 108, 305, 0, 403, 109, 503, 0, 206, 0, 0, 504, 0, 207, 0, 0,
    0, 404, 110, 0, 505, 0, 0, 208, 0, 306, 0, 405, 111, 0, 307, 0, 209, 0, 308, 210, 0, 406, 211, 0, 309, 407,
    506, 310, 0, 311, 408, 507, 0, 409, 508, 509, 410, 0, 510, 0, 411, 511, 0, 0,
)
BACKWARD_ORDER = (
    500, 0, 501, 0, 502, 0, 0, 503, 0, 100, 0, 0, 101, 0, 0, 504, 102, 0, 0, 103, 200, 0, 0, 0, 201, 104, 0, 0,
    505, 0, 0, 202, 105, 0, 203, 0, 300, 0, 301, 0, 106, 0, 204, 302, 0, 506, 0, 400, 0, 107, 205, 401, 303, 0,
    507, 0, 0, 508, 0, 206, 108, 402, 304, 0, 0, 0, 509, 0, 0, 403, 0, 207, 0, 305, 0, 306, 0, 510, 0, 404, 0,
    511, 0, 0, 0, 405, 208, 307, 0, 109, 0, 406, 0, 110, 0, 0, 111, 308, 407, 0, 209, 0, 210, 211, 309, 310,
    408, 311, 409, 410, 411,
)


def drive(order, items, run):
    todo = list(order)
    for item in items:
        while todo[0]:
            run(todo.pop(0))
        if callable(item):
            todo.pop(0)
            item()
            continue
        rounds, body = item
        between = []
        for _ in range(rounds):
            codes = []
            while todo[0]:
                codes.append(todo.pop(0))
            todo.pop(0)
            between.append(codes)

        def one(i, carry):
            for r, codes in enumerate(between):
                if codes:

                    @pl.when(i == r)
                    def _(codes=codes):
                        for code in codes:
                            run(code)

            body(i)
            return carry

        lax.fori_loop(0, rounds, one, 0)
    for code in todo:
        run(code)


def exact_gelu(pre):
    half = 0.5 + 0.5 * lax.erf(pre * (0.5**0.5))
    bell = jnp.exp(-0.5 * pre * pre) * ((0.5 / math.pi) ** 0.5)
    return pre * half, half + pre * bell


def rms_center(hidden):
    center = hidden - jnp.mean(hidden, axis=-1, keepdims=True)
    inverse = lax.rsqrt(jnp.mean(center * center, axis=-1, keepdims=True) + EPSILON)
    return center * inverse, inverse


def half_masks(width):
    left = (lax.broadcasted_iota(jnp.int32, (1, width), 1) < width // 2).astype(jnp.float32)
    return left.astype(jnp.bfloat16), (1.0 - left).astype(jnp.bfloat16)


def across(left, right):
    return lax.dot_general(left, right, (((1,), (1,)), ((), ())), preferred_element_type=jnp.float32)


def down(left, right):
    return lax.dot_general(left, right, (((0,), (0,)), ((), ())), preferred_element_type=jnp.float32)


def dot(left, right):
    return jnp.dot(left, right, preferred_element_type=jnp.float32)


def span(i, size):
    return pl.ds(pl.multiple_of(i * size, size), size)


class Gather:
    def __init__(self, at, parts, count, shards, g, send, recv):
        self.at, self.count, self.shards, self.g, self.send, self.recv = at, count, shards, g, send, recv
        self.parts = parts

    def copy(self, m, i, src, dst, to):
        return remote(src, dst, self.send.at[m, i], self.recv.at[m, i], to)

    def same(self, m, i, part, to):
        return self.copy(m, i, part, part, to)

    def stages(self, m):
        at, g, nz = self.at, self.g, self.at.nz
        a, b, c, ab = self.parts[m]
        y, core, z, x = at.y, at.core, at.z, at.x
        across_x, across_y, along_z = at.across_x, at.across_y, at.along_z
        first = [
            self.copy(m, k, self.shards.at[m, :, ab], g.at[m, y, core, z, x, :, ab], along_z[k])
            for k in range(nz - 1)
        ]
        first.append(self.copy(m, nz - 1, self.shards.at[m, :, c], g.at[m, y, core, z, x, :, c], across_y))
        second = [
            self.same(m, nz, g.at[m, y, core, :, x, :, a], across_y),
            self.same(m, nz + 1, g.at[m, y, core, :, x, :, b], across_x),
            self.same(m, nz + 2, g.at[m, :, core, z, x, :, c], across_x),
        ]
        third = [
            self.same(m, nz + 3, g.at[m, :, core, :, x, :, a], across_x),
            self.same(m, nz + 4, g.at[m, y, core, :, :, :, b], across_y),
        ]
        third += [self.same(m, nz + 5 + k, g.at[m, :, core, z, :, :, c], along_z[k]) for k in range(nz - 1)]
        return first, second, third, [self.same(m, 2 * nz + 4, g.at[m, :, core], at.sibling)]

    def step0(self, m):
        at = self.at
        for copy in self.stages(m)[0]:
            copy.start()
        self.g[m, at.y, at.core, at.z, at.x] = self.shards[m]

    def follow(self, stage, m):
        stages = self.stages(m)
        for copy in stages[stage - 1]:
            copy.wait_recv()
        for copy in stages[stage]:
            copy.start()

    def step1(self, m):
        self.follow(1, m)

    def step2(self, m):
        self.follow(2, m)

    def step3(self, m):
        self.follow(3, m)

    def arrive(self, m):
        part = self.g.at[m, :, self.at.core]
        self.same(m, 2 * self.at.nz + 4, part, self.at.sibling).wait_recv()

    def drain(self, m):
        for stage in self.stages(m):
            for copy in stage:
                copy.wait_send()


def column_parts(width, shares):
    lanes = 128
    a, b = (share * lanes for share in shares)
    return pl.ds(0, a), pl.ds(a, b), pl.ds(a + b, width - a - b), pl.ds(0, a + b)


UP_TILE = 256
NORM_ROWS = 192


def forward_kernel(
    nz, nx, parts, tokens, head_pair,
    x, attention_weights, expand, contract, small, slot_row, slots,
    g_out, probs_out, saved, act_out, slope_out, unit_out, final_out, own_out, across_out, small_full, inverse1, inverse2,
    g, shards, pool, hidden, landed, total, landing,
    send, recv, ssend, srecv, usend, urecv, across_send, across_recv, isem, gsem, vsem, asem, dsem, fsem, held_probs, ksem,
):
    f32, bf16 = jnp.float32, jnp.bfloat16
    count = g.shape[0]
    all_rows, width = x.shape
    rows = all_rows // tokens
    at = Partners(nz, nx)
    gather = Gather(at, parts, count, shards, g, send, recv)
    sums = SmallSum(at, total, landing, ssend, srecv)
    groups = slots.shape[0] // rows

    def fetch(i):
        return pltpu.make_async_copy(slots.at[i], pool.at[i // rows, pl.ds((i % rows) * tokens, tokens)], isem.at[i])

    shard = shards.shape[1]
    lane = lax.broadcasted_iota(jnp.int32, (1, width), 1)
    mine = lane // shard == lax.axis_index("dp") * (nz * nx) + lax.axis_index("fsdp")
    own = [ref[...].astype(f32).reshape(1, -1) for ref in small]
    own = own[:-1] + [own[-1][:, i : i + shard] for i in range(0, own[-1].shape[1], shard)]
    own += [jnp.zeros((1, shard), f32)] * (total.shape[1] - len(own))
    own = jnp.concatenate(own, axis=0)
    total[0] = jnp.where(mine, jnp.concatenate([own] * (width // shard), axis=1), 0.0)
    for m in range(4):
        shards[m] = attention_weights[m][...]
    for i in range(slots.shape[0]):
        fetch(i).start()
    at.meet()
    sums.start()

    high, part = 32, width // 2

    chosen = [
        [jnp.where(slot_row[s] == t, 1.0, 0.0) for s in range(slots.shape[0])] for t in range(2 * 2 * rows)
    ]

    def sum_slots(i, carry):
        cols = span(lax.rem(i, 2), part)
        base = i // 2 * high
        held = [
            pool[s // rows, pl.ds(pl.multiple_of(base + (s % rows) * tokens, high), high), cols].astype(f32)
            for s in range(slots.shape[0])
        ]
        for t in range(2 * 2 * rows):
            picked = chosen[t][0] * held[0]
            for s in range(1, slots.shape[0]):
                picked = picked + chosen[t][s] * held[s]
            spot = pl.ds(pl.multiple_of(base + (t % rows) * tokens, high), high)
            pool[groups + t // rows, spot, cols] = picked.astype(bf16)
        return carry

    def up_sibling(y):
        src = pool.at[groups + y * 2 + 1 - at.core]
        return remote(src, landed.at[y], usend.at[y], urecv.at[y], at.sibling)

    pieces = across_send.shape[0]

    def up_across(i):
        piece = pl.ds(i * (all_rows // pieces), all_rows // pieces)
        return remote(
            landed.at[1 - at.y, piece], across_out.at[piece], across_send.at[i], across_recv.at[i], at.across_y
        )

    up_own = pltpu.make_async_copy(landed.at[at.y], own_out, isem.at[slots.shape[0]])

    steps = tokens // high * 2

    def quarter(i):
        if i == 0:
            for s in range(slots.shape[0]):
                fetch(s).wait()
        lax.fori_loop(i * steps // 4, (i + 1) * steps // 4, sum_slots, 0)
        if i != 2:
            sums.step((0, 1, None, 2)[i])

    blocks = (count - 4) // 2

    def arrange():
        for j in range(blocks):
            shards[5 + 2 * j] = contract[j * shard : (j + 1) * shard, :]
        lanes = 128
        per = lanes // shard
        for q in range(width // lanes):
            natural = expand[:, q * lanes * blocks : (q + 1) * lanes * blocks].astype(f32)
            for j in range(blocks):
                starts = [t * blocks * shard + j * shard for t in range(per)]
                found = [natural[:, start : start + shard] for start in starts]
                shards[4 + 2 * j, :, q * lanes : (q + 1) * lanes] = jnp.concatenate(found, axis=1).astype(bf16)

    def exchange_cores():
        for y in range(2):
            up_sibling(y).start()

    def chip_sum(i, carry):
        y, spot = i // (all_rows // 192), span(lax.rem(i, all_rows // 192), 192)
        landed[y, spot] = added(landed[y, spot], pool[groups + y * 2 + at.core, spot]).astype(bf16)
        return carry

    def sum_chip():
        for y in range(2):
            up_sibling(y).wait_recv()
        lax.fori_loop(0, 2 * all_rows // 192, chip_sum, 0)
        up_own.start()
        for y in range(2):
            up_sibling(y).wait_send()

    def keep(m):
        return pltpu.make_async_copy(g.at[m], g_out.at[m], gsem.at[m])

    def arrive(m):
        gather.arrive(m)
        keep(m).start()

    def tile(m, cols):
        return g[m, :, :, :, :, :, cols].reshape(width, cols.size)

    def bias(i, cols):
        return small_full[pl.ds(i, 1), cols]

    every = pl.ds(0, all_rows)
    halves = [pl.ds(i * width // 2, width // 2) for i in range(2)]

    def tiles(size, body):
        def one(i, carry):
            body(span(i, size), every)
            return carry

        lax.fori_loop(0, width // size, one, 0)

    def save(i):
        return pltpu.make_async_copy(pool.at[i], saved.at[i], vsem.at[i])

    def project(m):
        row = lax.rem(m, 2) * 12 + m // 2
        arrive(m)
        pl.when(m == 0)(lambda: sums.finish(small_full))
        for cols in halves:
            pool[m, :, cols] = (dot(x[...], tile(m, cols)) + bias(row, cols)).astype(bf16)
        save(m).start()

    pairs = width // head_pair
    masks = half_masks(head_pair)
    scale = (head_pair // 2) ** (-0.5)

    def keep_probs(i):
        slot = lax.rem(i, 2)
        return pltpu.make_async_copy(held_probs.at[slot], probs_out.at[i], ksem.at[slot])

    def attend(i):
        spot, base = span(i // (pairs // 2), tokens), lax.rem(i, pairs // 2) * 2
        pl.when(i >= 2)(lambda: keep_probs(i - 2).wait())
        for p in range(2):
            cols = span(base + p, head_pair)
            query, keys, values = pool[0, spot, cols], pool[1, spot, cols], pool[2, spot, cols]
            query = query * jnp.asarray(scale, bf16)
            out = None
            for h, mask in enumerate(masks):
                scores = across(keys * mask, query)
                probs = jnp.exp(scores - jnp.max(scores, axis=0, keepdims=True))
                probs = (probs * (1.0 / jnp.sum(probs, axis=0, keepdims=True))).astype(bf16)
                held_probs[lax.rem(i, 2), 2 * p + h] = probs
                term = down(probs, values * mask)
                out = term if out is None else out + term
            pool[3, spot, cols] = out.astype(bf16)
        keep_probs(i).start()

    rounds = rows * pairs // 2

    def mix(cols, spot):
        hidden[spot, cols] = dot(pool[3, spot], tile(3, cols)) + x[spot, cols].astype(f32) + bias(2, cols)

    def join():
        save(3).start()
        for i in range(2):
            keep_probs(rounds - 2 + i).wait()
        arrive(3)
        for cols in halves:
            mix(cols, every)

    def unit(i):
        return pltpu.make_async_copy(pool.at[6], unit_out.at[i], fsem.at[i])

    def norm1(i, carry):
        spot = span(i, NORM_ROWS)
        normed, inverse = rms_center(hidden[spot])
        result = normed * small_full[3:4, :] + small_full[4:5, :]
        hidden[spot] = result
        pool[4, spot] = result.astype(bf16)
        pool[6, spot] = normed.astype(bf16)
        inverse1[spot] = inverse
        return carry

    def first_norm():
        lax.fori_loop(0, all_rows // NORM_ROWS, norm1, 0)
        save(4).start()
        unit(0).start()

    def save_act(j):
        return pltpu.make_async_copy(pool.at[5], act_out.at[j], asem)

    def save_slope(j):
        return pltpu.make_async_copy(pool.at[6], slope_out.at[j], dsem)

    def widen(j):
        pl.when(j == 0)(lambda: unit(0).wait())

        @pl.when(j > 0)
        def _():
            save_act(j - 1).wait()
            save_slope(j - 1).wait()

        def up(cols, spot):
            value, slope = exact_gelu(dot(pool[4, spot], tile(4 + 2 * j, cols)) + bias(8 + j, cols))
            pool[5, spot, cols] = value.astype(bf16)
            pool[6, spot, cols] = slope.astype(bf16)

        tiles(UP_TILE, up)
        save_act(j).start()
        save_slope(j).start()

    def narrow(j):
        for cols in halves:
            hidden[:, cols] = hidden[:, cols] + dot(pool[5], tile(5 + 2 * j, cols))

    def feed(i):
        arrive(4 + i)
        pl.when(lax.rem(i, 2) == 0)(lambda: widen(i // 2))
        pl.when(lax.rem(i, 2) == 1)(lambda: narrow(i // 2))

    def norm2(i, carry):
        spot = span(i, NORM_ROWS)
        normed, inverse = rms_center(hidden[spot] + small_full[5:6, :])
        pool[5, spot] = (normed * small_full[6:7, :] + small_full[7:8, :]).astype(bf16)
        pool[6, spot] = normed.astype(bf16)
        inverse2[spot] = inverse
        return carry

    finish = pltpu.make_async_copy(pool.at[5], final_out, fsem.at[2])

    def second_norm():
        save_act(blocks - 1).wait()
        save_slope(blocks - 1).wait()
        lax.fori_loop(0, all_rows // NORM_ROWS, norm2, 0)
        finish.start()
        unit(1).start()

    def run(code):
        kind, m = divmod(code, 100)
        if kind == 5:
            up_across(m).start()
        else:
            (gather.step0, gather.step1, gather.step2, gather.step3)[kind - 1](m)

    items = [partial(quarter, 0), arrange, *(partial(quarter, i) for i in (1, 2, 3)), exchange_cores, sum_chip]
    items += [(3, project), (rounds, attend), join, first_norm, (2 * blocks, feed), second_norm]
    drive(FORWARD_ORDER, items, run)
    for m in range(count):
        gather.drain(m)
        keep(m).wait()
    for i in range(5):
        save(i).wait()
    up_own.wait()
    for i in range(pieces):
        up_across(i).wait()
    finish.wait()
    unit(1).wait()


def forward(x, attention_weights, expand, contract, small, slot_row, slots, nz, nx, tokens):
    f32, bf16 = jnp.float32, jnp.bfloat16
    shard_rows, width = attention_weights[0].shape
    count = 4 + 2 * contract.shape[0] // shard_rows
    small_shape = (16, width)
    all_rows = x.shape[0]
    assert slots.shape[0] * tokens == 2 * all_rows
    vmem, anywhere = pl.BlockSpec(memory_space=pltpu.VMEM), pl.BlockSpec(memory_space=pl.ANY)
    acts = (all_rows, width)
    rows = all_rows // tokens
    blocks = (count - 4) // 2
    dma = pltpu.SemaphoreType.DMA
    full = (count, 2, 2, nz, nx, shard_rows, width)
    out = jax.ShapeDtypeStruct
    return pl.pallas_call(
        partial(forward_kernel, nz, nx, [column_parts(width, s) for s in GATHER_SHARES], tokens, 2 * width // HEADS),
        out_shape=[
            out(full, bf16),
            out((rows * HEADS // 4, 4, tokens, tokens), bf16),
            out((5, *acts), bf16),
            out((blocks, *acts), bf16),
            out((blocks, *acts), bf16),
            out((2, *acts), bf16),
            out(acts, bf16),
            out(acts, bf16),
            out(acts, bf16),
            out(small_shape, f32),
            out((all_rows, 1), f32),
            out((all_rows, 1), f32),
        ],
        in_specs=[vmem, [vmem] * 4, vmem, vmem, [vmem] * len(small), pl.BlockSpec(memory_space=pltpu.SMEM), anywhere],
        out_specs=[anywhere] * 9 + [vmem] * 3,
        scratch_shapes=[
            pltpu.VMEM(full, bf16),
            pltpu.VMEM((count, shard_rows, width), bf16),
            pltpu.VMEM((7, *acts), bf16),
            pltpu.VMEM(acts, f32),
            pltpu.VMEM((2, *acts), bf16),
            *small_scratch(nz, small_shape)[:2],
            dma((count, 2 * nz + 5)),
            dma((count, 2 * nz + 5)),
            dma((2 + nz,)),
            dma((2 + nz,)),
            dma((2,)),
            dma((2,)),
            dma((count,)),
            dma((count,)),
            dma((slots.shape[0] + 1,)),
            dma((count,)),
            dma((5,)),
            dma,
            dma,
            dma((3,)),
            pltpu.VMEM((2, 4, tokens, tokens), bf16),
            dma((2,)),
        ],
        compiler_params=pltpu.CompilerParams(
            collective_id=1, has_side_effects=True, vmem_limit_bytes=60 * 2**20
        ),
    )(x, attention_weights, expand, contract, small, slot_row, slots)


def quietly(call):
    call()


def backward_kernel(
    nz, nx, parts, tokens, head_pair,
    x, own_up, across_up, final, unit, inverse1, inverse2, small_full, act, slope, saved, g, probs,
    out, small_out, input_out, table,
    rc, r3a, r3b, r2, rz, rcz, rcx, rcy, send, recv, total, landing, ssend, srecv,
    term, weight, pool, hidden, wsem, psem, hsem, tsend, trecv, across_send, across_recv, tsem, held_probs, ksem,
):
    f32, bf16 = jnp.float32, jnp.bfloat16
    count = out.shape[0]
    all_rows, width = x.shape
    rows = all_rows // tokens
    at = Partners(nz, nx)
    scatter = Scatter(at, parts, rc, r3a, r3b, r2, rz, rcz, rcx, rcy, send, recv)
    sums = SmallSum(at, total, landing, ssend, srecv)

    here = pltpu.make_async_copy(final, table.at[at.y, at.core], tsem)
    to_sibling = remote(final, table.at[at.y, at.core], tsend.at[0], trecv.at[0], at.sibling)
    pieces = across_send.shape[0]

    def to_across(i):
        piece = pl.ds(i * (all_rows // pieces), all_rows // pieces)
        dst = table.at[at.y, at.core, piece]
        return remote(final.at[piece], dst, across_send.at[i], across_recv.at[i], at.across_y)

    passed = table.at[1 - at.y, at.core]
    pass_on = remote(passed, passed, tsend.at[1], trecv.at[1], at.sibling)

    def load(src, entry, i):
        return pltpu.make_async_copy(src, pool.at[entry], psem.at[i])

    def fetch(m, slot, i):
        return pltpu.make_async_copy(g.at[m], weight.at[slot], wsem.at[i])

    blocks = act.shape[0]
    up_block, down_block = (lambda j: 4 + 2 * j), (lambda j: 5 + 2 * j)
    unit2, own_load, across_load = load(unit.at[1], 1, 0), load(own_up, 2, 1), load(across_up, 3, 2)
    act_entry = [5, 2, 3, 5]
    act_load = [load(act.at[j], act_entry[j], 3 + j) for j in range(blocks)]
    slope_entry = [4, 2, 3, 4]
    slope_load = [load(slope.at[j], slope_entry[j], 7 + j) for j in range(blocks)]
    low_load, unit1, mixed_load = load(saved.at[4], 6, 11), load(unit.at[0], 5, 12), load(saved.at[3], 4, 13)
    query_load, key_load, value_load = (load(saved.at[i], (2, 3, 6)[i], 14 + i) for i in range(3))
    x_load = load(x, 4, 17)
    down_fetch = [fetch(down_block(j), 0, 2 * j) for j in range(blocks)]
    up_fetch = [fetch(up_block(j), 1, 2 * j + 1) for j in range(blocks)]
    last = 2 * blocks
    output_fetch, query_fetch, key_fetch, value_fetch = (
        fetch(m, slot, last + i) for i, (m, slot) in enumerate(((3, 0), (0, 1), (1, 0), (2, 1)))
    )
    for copy in (unit2, own_load, across_load, act_load[0], down_fetch[0], up_fetch[0], slope_load[0], low_load):
        copy.start()
    here.start()
    total[0] = jnp.zeros_like(total[0])
    at.meet()
    to_sibling.start()

    def folded(block):
        return jnp.sum(block.reshape(-1, 8, block.shape[-1]), axis=0)

    def norm_back(gain_row, shift_row, low_row, inverse, incoming, normed_entry, low_entry):
        def body(i, carry):
            spot = span(i, NORM_ROWS)
            grad, normed = incoming(spot), pool[normed_entry, spot].astype(f32)
            scaled = grad * small_full[gain_row : gain_row + 1, :]
            inner = (
                scaled
                - jnp.mean(scaled, axis=-1, keepdims=True)
                - normed * jnp.mean(scaled * normed, axis=-1, keepdims=True)
            )
            result = inner * inverse[spot]
            low = result.astype(bf16)
            hidden[spot] = result
            pool[low_entry, spot] = low
            return tuple(c + folded(b) for c, b in zip(carry, (grad * normed, grad, low.astype(f32))))

        zero = jnp.zeros((8, width), f32)
        found = lax.fori_loop(0, all_rows // NORM_ROWS, body, (zero, zero, zero))
        for row, value in zip((gain_row, shift_row, low_row), found):
            total[0, row : row + 1, :] = jnp.sum(value, axis=0, keepdims=True)

    def turned(slot):
        for y in range(2):
            yield pl.ds(y * width // 2, width // 2), weight[slot, y].reshape(width // 2, width)

    def own_half(slot):
        return term[slot, :, at.core]

    def half(i, m, left, right):
        core = lax.rem(at.core + 1 + i, 2)
        for y in range(2):
            picked = span(y * 2 + core, width // 4)
            value = down(pool[left, :, picked], pool[right]).astype(bf16)
            term[lax.rem(m, 2), y, core] = value.reshape(nz, nx, -1, width)
        pl.when(i == 0)(lambda: scatter.start(m, term.at[lax.rem(m, 2), :, 1 - at.core]))

    def run(code):
        kind, m = divmod(code, 100)
        if kind == 5:
            to_across(m).start()
        elif kind == 1:
            scatter.step1(m, own_half(m % 2))
        elif kind == 4:
            scatter.step4(m, out)
        else:
            (scatter.step2, scatter.step3)[kind - 2](m)

    def when(value, calls):
        for at_value, call in calls.items():
            pl.when(value == at_value)(partial(quietly, call))

    def load_second():
        for copy in (unit2, own_load, across_load):
            copy.wait()

    def second_norm():
        norm_back(6, 7, 5, inverse2, lambda spot: added(pool[2, spot], pool[3, spot]), 1, 0)
        act_load[1].start()
        act_load[2].start()

    def contract_term(i):
        j = i // 2
        middle = j * (3 - j) // 2
        when(i, {2 * n: act_load[n].wait for n in range(blocks)})
        half(lax.rem(i, 2), j, middle * (j + 1) + (1 - middle) * 5, 0)
        when(i, {1: act_load[3].start, 3: slope_load[1].start, 5: slope_load[2].start, 7: unit1.start})

    def widen_back(j):
        for n in range(blocks):
            when(j, {n: down_fetch[n].wait})
            when(j, {n: slope_load[n].wait})
        middle = j * (3 - j) // 2
        entry = middle * (j + 1) + (1 - middle) * 4
        for cols, part in turned(0):
            value = (across(pool[0], part) * pool[entry, :, cols].astype(f32)).astype(bf16)
            pool[1, :, cols] = value
            total[0, pl.ds(8 + j, 1), cols] = jnp.sum(value.astype(f32), axis=0, keepdims=True)
        fetches = [*down_fetch[1:], output_fetch]
        when(j, {n: fetches[n].start for n in range(blocks)})
        when(j, {0: slope_load[3].start, 1: query_load.start, 2: key_load.start, 3: mixed_load.start})

    def narrow_back(j):
        when(j, {n: up_fetch[n].wait for n in range(blocks)})
        for cols, part in turned(1):
            hidden[:, cols] = hidden[:, cols] + across(pool[1], part)
        fetches = [*up_fetch[1:], query_fetch]
        when(j, {n: fetches[n].start for n in range(blocks)})
        when(j, {blocks - 1: value_load.start})

    def feed_back(i):
        j, kind = i // 4, lax.rem(i, 4)
        when(i, {1: low_load.wait})
        pl.when(kind == 0)(lambda: widen_back(j))
        pl.when((kind == 1) | (kind == 2))(lambda: half(kind - 1, blocks + j, 6, 1))
        pl.when(kind == 3)(lambda: narrow_back(j))

    def first_norm():
        unit1.wait()
        norm_back(3, 4, 2, inverse1, lambda spot: hidden[spot], 5, 0)

    def mixed_back():
        output_fetch.wait()
        for cols, part in turned(0):
            pool[1, :, cols] = across(pool[0], part).astype(bf16)
        key_fetch.start()
        for copy in (query_load, key_load, value_load):
            copy.wait()
        fetch_probs(0).start()

    def output_term(i):
        when(i, {0: mixed_load.wait})
        half(i, jnp.int32(2 * blocks), 4, 0)
        when(i, {1: x_load.start})

    pairs = width // head_pair
    masks = half_masks(head_pair)
    scale = (head_pair // 2) ** (-0.5)

    def fetch_probs(i):
        slot = lax.rem(i, 2)
        return pltpu.make_async_copy(probs.at[i], held_probs.at[slot], ksem.at[slot])

    rounds = rows * pairs // 2

    def attend(i):
        pl.when(i + 1 < rounds)(lambda: fetch_probs(i + 1).start())
        fetch_probs(i).wait()
        spot, base = span(i // (pairs // 2), tokens), lax.rem(i, pairs // 2) * 2
        for p in range(2):
            cols = span(base + p, head_pair)
            query, keys, values, mixed_grad = (pool[e, spot, cols] for e in (2, 3, 6, 1))
            query_grad = key_grad = value_grad = None
            for h, mask in enumerate(masks):
                own_keys = keys * (mask * jnp.asarray(scale, bf16))
                low = held_probs[lax.rem(i, 2), 2 * p + h]
                prob = low.astype(f32)
                prob_grad = across(values * mask, mixed_grad)
                weighed = prob * prob_grad
                score_grad = (weighed - prob * jnp.sum(weighed, axis=0, keepdims=True)).astype(bf16)
                terms = (
                    down(score_grad, own_keys),
                    dot(score_grad, query * mask),
                    dot(low, mixed_grad * mask),
                )
                if query_grad is None:
                    query_grad, key_grad, value_grad = terms
                else:
                    query_grad, key_grad, value_grad = query_grad + terms[0], key_grad + terms[1], value_grad + terms[2]
            query_grad, value_grad = query_grad.astype(bf16), value_grad.astype(bf16)
            pool[2, spot, cols] = query_grad
            pool[3, spot, cols] = (key_grad * scale).astype(bf16)
            pool[6, spot, cols] = value_grad
            for row, value in ((0, query_grad), (1, value_grad)):
                found = jnp.sum(value.astype(f32), axis=0, keepdims=True)
                total[0, row : row + 1, cols] = total[0, row : row + 1, cols] + found

    def projection_term(i):
        n = i // 2
        later = (n + 1) // 2
        when(i, {0: x_load.wait})
        when(i, {0: sums.start})
        half(lax.rem(i, 2), 2 * blocks + 1 + n, 4, later * (n + 1) + (1 - later) * 6)
        when(i, {2 * n + 1: partial(sums.step, n) for n in range(3)})

    def pass_rows():
        for i in range(pieces):
            to_across(i).wait_recv()
        pass_on.start()

    done = pltpu.make_async_copy(hidden, input_out, hsem)

    def input_back(i):
        when(i, {0: query_fetch.wait, 1: key_fetch.wait, 2: value_fetch.wait})
        for cols, part in turned(lax.rem(i + 1, 2)):
            hidden[:, cols] = hidden[:, cols] + across(pool[2 + i + i // 2 * 2], part)
        when(i, {0: value_fetch.start, 1: pass_rows, 2: done.start})

    items = [load_second, second_norm, (2 * blocks, contract_term), (4 * blocks, feed_back), first_norm]
    items += [(2, output_term), mixed_back, (rounds, attend), (6, projection_term), (3, input_back)]
    drive(BACKWARD_ORDER, items, run)
    sums.finish(small_out)
    done.wait()

    for m in range(count):
        scatter.drain(m)
    here.wait()
    to_sibling.wait()
    for i in range(pieces):
        to_across(i).wait_send()
    pass_on.wait()


def backward(
    x, own_up, across_up, final, unit, inverse1, inverse2, small_full, act, slope, saved, g, probs, nz, nx, tokens
):
    f32, bf16 = jnp.float32, jnp.bfloat16
    count, _, _, _, _, shard_rows, width = g.shape
    acts = x.shape
    parts = [column_parts(width, s) for s in SCATTER_SHARES]
    vmem, anywhere = pl.BlockSpec(memory_space=pltpu.VMEM), pl.BlockSpec(memory_space=pl.ANY)
    dma = pltpu.SemaphoreType.DMA
    out = jax.ShapeDtypeStruct
    block = (2, 2, nz, nx, shard_rows, width)
    return pl.pallas_call(
        partial(backward_kernel, nz, nx, parts, tokens, 2 * width // HEADS),
        out_shape=[
            out((count, shard_rows, width), f32),
            out(small_full.shape, f32),
            out(acts, f32),
            out((2, 2, *acts), bf16),
        ],
        in_specs=[anywhere] * 5 + [vmem] * 3 + [anywhere] * 5,
        out_specs=[vmem, vmem, anywhere, anywhere],
        scratch_shapes=[
            *scatter_scratch(count, nz, nx, shard_rows, width, parts),
            *small_scratch(nz, small_full.shape),
            pltpu.VMEM((2, *block), bf16),
            pltpu.VMEM((2, *block), bf16),
            pltpu.VMEM((7, *acts), bf16),
            pltpu.VMEM(acts, f32),
            dma((count,)),
            dma((18,)),
            dma,
            dma((2,)),
            dma((2,)),
            dma((count,)),
            dma((count,)),
            dma,
            pltpu.VMEM((2, 4, tokens, tokens), bf16),
            dma((2,)),
        ],
        compiler_params=pltpu.CompilerParams(
            collective_id=2, has_side_effects=True, vmem_limit_bytes=63 * 2**20
        ),
    )(x, own_up, across_up, final, unit, inverse1, inverse2, small_full, act, slope, saved, g, probs)


def finish_kernel(
    slot_row, live_count, me, first, second, full, sums, small_sums,
    slot_acts, input_grad, query, keys, values, output, up, contract, *small,
):
    s = pl.program_id(0)
    slot_acts[0] = first[0]
    slot_acts[1] = second[0]
    input_grad[...] = jnp.where(s < live_count[0], full[...], 0.0)

    @pl.when(s == 0)
    def _():
        blocks = (sums.shape[0] - 4) // 2
        shard, width = query.shape
        for j in range(blocks):
            contract[j * shard : (j + 1) * shard, :] = sums[j]
        lanes = 128
        per = lanes // shard
        for q in range(width // lanes):
            part = [sums[blocks + j, :, q * lanes : (q + 1) * lanes] for j in range(blocks)]
            for t in range(per):
                found = jnp.concatenate([p[:, t * shard : (t + 1) * shard] for p in part], axis=1)
                at = (q * per + t) * blocks * shard
                up[:, at : at + blocks * shard] = found
        for i, ref in enumerate((output, values, query, keys)):
            ref[...] = sums[2 * blocks + i]
        own = pltpu.roll(small_sums[...], width - me[0] * shard, 1)
        for i in range(8):
            small[i][...] = own[i, :shard]
        small[8][...] = jnp.concatenate([own[8 + j : 9 + j, :shard] for j in range(blocks)], axis=1)[0]


def finish(slot_row, live_count, table, full, sums, small_sums):
    f32 = jnp.float32
    members, tokens, width = table.shape
    slots, rows = slot_row.shape[0], full.shape[0]
    assert slots == 2 * rows
    count, shard, _ = sums.shape
    blocks = (count - 4) // 2
    me = lax.axis_index(("dp", "fsdp")).astype(jnp.int32).reshape(1)
    block, pair = (1, tokens, width), (2, tokens, width)

    def fixed(shape):
        return pl.BlockSpec(shape, lambda s, *_: (0,) * len(shape))

    fixed_outs = [(shard, width)] * 4 + [(shard, blocks * width), (blocks * shard, width)]
    fixed_outs += [(shard,)] * 8 + [(blocks * shard,)]
    row = pl.BlockSpec(block, lambda s, *_: (s, 0, 0))

    def chosen(i):
        return pl.BlockSpec(block, lambda s, slot_row, *_: (jnp.clip(slot_row[2 * s + i], 0, members - 1), 0, 0))

    out = jax.ShapeDtypeStruct
    return pl.pallas_call(
        finish_kernel,
        out_shape=[
            out((slots, tokens, width), table.dtype),
            out(full.shape, f32),
            *(out(shape, f32) for shape in fixed_outs),
        ],
        grid_spec=pltpu.PrefetchScalarGridSpec(
            num_scalar_prefetch=3,
            grid=(rows,),
            in_specs=[
                chosen(0),
                chosen(1),
                row,
                fixed(sums.shape),
                fixed(small_sums.shape),
            ],
            out_specs=[
                pl.BlockSpec(pair, lambda s, *_: (s, 0, 0)),
                row,
                *(fixed(shape) for shape in fixed_outs),
            ],
        ),
        compiler_params=pltpu.CompilerParams(vmem_limit_bytes=63 * 2**20),
    )(slot_row, live_count, me, table, table, full, sums, small_sums)


def on_device_kernels(
    rows_in,
    slot_row,
    live_count,
    slot_activation_gradient,
    query_weight,
    key_weight,
    value_weight,
    output_weight,
    query_bias,
    value_bias,
    output_bias,
    attn_gain,
    attn_shift,
    expand_weight,
    up_bias,
    down_weight,
    down_bias,
    ffn_gain,
    ffn_shift,
):
    row_count, token_count, width = rows_in.shape
    nx = 2
    nz = lax.axis_size("fsdp") // nx
    small = [query_bias, value_bias, output_bias, attn_gain, attn_shift, down_bias, ffn_gain, ffn_shift, up_bias]
    x = rows_in.reshape(-1, width)
    g, probs, saved, act, slope, unit, final, own_up, across_up, small_full, inverse1, inverse2 = forward(
        x,
        [query_weight, key_weight, value_weight, output_weight],
        expand_weight,
        down_weight,
        small,
        slot_row,
        slot_activation_gradient,
        nz,
        nx,
        token_count,
    )
    sums, small_sums, input_full, table = backward(
        x,
        own_up,
        across_up,
        final,
        unit,
        inverse1,
        inverse2,
        small_full,
        act,
        slope,
        saved,
        g,
        probs,
        nz,
        nx,
        token_count,
    )
    slot_acts, input_grad, query, keys, values, output, up, contract, *small_grads = finish(
        slot_row,
        live_count,
        table.reshape(-1, token_count, width),
        input_full.reshape(rows_in.shape),
        sums,
        small_sums,
    )
    return (
        slot_acts,
        input_grad,
        query,
        keys,
        values,
        output,
        *small_grads[:5],
        up,
        small_grads[8],
        contract,
        *small_grads[5:8],
    )


def norm_forward(hidden, gain, shift):
    center = hidden - jnp.mean(hidden, axis=-1, keepdims=True)
    inverse = lax.rsqrt(jnp.mean(center * center, axis=-1, keepdims=True) + EPSILON)
    normed = center * inverse
    return (normed * gain + shift, normed, inverse)


def norm_backward(incoming, gain, normed, inverse):
    scaled = incoming * gain
    inner = (
        scaled
        - jnp.mean(scaled, axis=-1, keepdims=True)
        - normed * jnp.mean(scaled * normed, axis=-1, keepdims=True)
    )
    return (
        inner * inverse,
        jnp.sum(incoming * normed, axis=(0, 1)),
        jnp.sum(incoming, axis=(0, 1)),
    )


def apply_weight(acts, weight):
    return jnp.einsum("rsd,de->rse", acts, weight, preferred_element_type=jnp.float32)


def apply_back(grads, weight):
    return jnp.einsum("rse,de->rsd", grads, weight, preferred_element_type=jnp.float32)


def weight_term(acts, grads):
    return jnp.einsum("rsd,rse->de", acts, grads, preferred_element_type=jnp.float32)


def bias_term(grads):
    return jnp.sum(grads, axis=(0, 1), dtype=jnp.float32)


def on_device_plain(
    rows_in,
    slot_row,
    live_count,
    slot_activation_gradient,
    query_weight,
    key_weight,
    value_weight,
    output_weight,
    query_bias,
    value_bias,
    output_bias,
    attn_gain,
    attn_shift,
    expand_weight,
    up_bias,
    down_weight,
    down_bias,
    ffn_gain,
    ffn_shift,
):
    row_count, token_count, feature_count = rows_in.shape
    head_size = feature_count // HEADS
    score_scale = head_size ** (-0.5)
    split_shape = (row_count, token_count, HEADS, head_size)
    wanted = lax.broadcasted_iota(
        jnp.int32, (row_count * lax.axis_size("dp"), slot_row.shape[0]), 0
    )
    one_hot_matrix = (wanted == slot_row[None, :]).astype(jnp.bfloat16)
    upstream = lax.psum_scatter(
        jnp.einsum(
            "az,zfy->afy",
            one_hot_matrix,
            slot_activation_gradient,
            preferred_element_type=jnp.float32,
        ).astype(jnp.bfloat16),
        "dp",
        scatter_dimension=0,
        tiled=True,
    ).astype(jnp.float32)
    smalls = (query_bias, value_bias, output_bias, attn_gain, attn_shift, down_bias, ffn_gain, ffn_shift)
    small_rows = query_bias.shape[0]
    packed = jnp.concatenate([v.reshape(-1, small_rows) for v in (*smalls, up_bias)], axis=0)
    packed_full = lax.all_gather(packed, ("dp", "fsdp"), axis=0)
    (
        qbias_full,
        vbias_full,
        obias_full,
        gain1_full,
        shift1_full,
        downbias_full,
        gain2_full,
        shift2_full,
    ) = (packed_full[:, i].reshape(-1) for i in range(8))
    upbias_full = packed_full[:, 8:].reshape(-1)
    query_full, key_full, value_full, output_full, up_full, down_full = (
        lax.all_gather(weight, ("dp", "fsdp"), axis=0, tiled=True)
        for weight in (query_weight, key_weight, value_weight, output_weight, expand_weight, down_weight)
    )
    inputs = rows_in.astype(jnp.float32)
    query = (apply_weight(rows_in, query_full) + qbias_full.astype(jnp.float32)).astype(
        jnp.bfloat16
    )
    keys = apply_weight(rows_in, key_full).astype(jnp.bfloat16)
    values = (apply_weight(rows_in, value_full) + vbias_full.astype(jnp.float32)).astype(
        jnp.bfloat16
    )
    query_heads = query.reshape(split_shape)
    key_heads = keys.reshape(split_shape)
    value_heads = values.reshape(split_shape)
    scores = (
        jnp.einsum("rqhd,rkhd->rhqk", query_heads, key_heads, preferred_element_type=jnp.float32)
        * score_scale
    )
    row_top = jnp.max(scores, axis=-1, keepdims=True)
    expo = jnp.exp(scores - row_top)
    row_sum = jnp.sum(expo, axis=-1, keepdims=True)
    logsum = row_top + jnp.log(row_sum)
    probs_low = (expo / row_sum).astype(jnp.bfloat16)
    mixed = jnp.einsum(
        "rhqk,rkhd->rqhd", probs_low, value_heads, preferred_element_type=jnp.float32
    )
    mixed = mixed.reshape(row_count, token_count, feature_count).astype(jnp.bfloat16)
    gain1 = gain1_full.astype(jnp.float32)
    resid1 = inputs + apply_weight(mixed, output_full) + obias_full.astype(jnp.float32)
    normed1_out, normed1, inverse1 = norm_forward(resid1, gain1, shift1_full.astype(jnp.float32))
    normed1_low = normed1_out.astype(jnp.bfloat16)
    pre_act = apply_weight(normed1_low, up_full) + upbias_full.astype(jnp.float32)
    act_low = jax.nn.gelu(pre_act, approximate=False).astype(jnp.bfloat16)
    gain2 = gain2_full.astype(jnp.float32)
    resid2 = normed1_out + apply_weight(act_low, down_full) + downbias_full.astype(jnp.float32)
    final, second_normed, inverse2 = norm_forward(resid2, gain2, shift2_full.astype(jnp.float32))
    final_low = final.astype(jnp.bfloat16)
    shard_rows = lax.all_gather(final_low, "dp", axis=0, tiled=True)
    span_rows = shard_rows.shape[0]
    inside = (slot_row >= 0) & (slot_row < span_rows)
    picked = jnp.take(shard_rows, jnp.clip(slot_row, 0, span_rows - 1), axis=0)
    slot_acts = jnp.where(
        inside[:, None, None], picked, jnp.zeros(slot_activation_gradient.shape, jnp.bfloat16)
    )
    gain1 = gain1_full.astype(jnp.float32)
    gain2 = gain2_full.astype(jnp.float32)
    grad2, gain2_grad, shift2_grad = norm_backward(upstream, gain2, second_normed, inverse2)
    ffn_low = grad2.astype(jnp.bfloat16)
    down_grad = weight_term(act_low, ffn_low)
    down_bias_grad = bias_term(ffn_low)
    act_grad = apply_back(ffn_low, down_full)
    gelu_value, gelu_back = jax.vjp(partial(jax.nn.gelu, approximate=False), pre_act)
    pre_grad = gelu_back(act_grad)[0].astype(jnp.bfloat16)
    up_grad = weight_term(normed1_low, pre_grad)
    up_bias_grad = bias_term(pre_grad)
    normed1_grad = grad2 + apply_back(pre_grad, up_full)
    grad1, gain1_grad, shift1_grad = norm_backward(normed1_grad, gain1, normed1, inverse1)
    attn_low = grad1.astype(jnp.bfloat16)
    output_grad = weight_term(mixed, attn_low)
    output_bias_grad = bias_term(attn_low)
    mixed_grad = apply_back(attn_low, output_full).astype(jnp.bfloat16).reshape(split_shape)
    scores_again = (
        jnp.einsum("rqhd,rkhd->rhqk", query_heads, key_heads, preferred_element_type=jnp.float32)
        * score_scale
    )
    probs = jnp.exp(scores_again - logsum)
    probs_again = probs.astype(jnp.bfloat16)
    value_grad = jnp.einsum(
        "rhqk,rqhd->rkhd", probs_again, mixed_grad, preferred_element_type=jnp.float32
    )
    value_grad = value_grad.astype(jnp.bfloat16).reshape(row_count, token_count, feature_count)
    prob_grad = jnp.einsum(
        "rqhd,rkhd->rhqk", mixed_grad, value_heads, preferred_element_type=jnp.float32
    )
    score_grad = (probs * (prob_grad - jnp.sum(probs * prob_grad, axis=-1, keepdims=True))).astype(
        jnp.bfloat16
    )
    query_grad = (
        jnp.einsum("rhqk,rkhd->rqhd", score_grad, key_heads, preferred_element_type=jnp.float32)
        * score_scale
    )
    query_grad = query_grad.astype(jnp.bfloat16).reshape(row_count, token_count, feature_count)
    key_grad = (
        jnp.einsum("rhqk,rqhd->rkhd", score_grad, query_heads, preferred_element_type=jnp.float32)
        * score_scale
    )
    key_grad = key_grad.astype(jnp.bfloat16).reshape(row_count, token_count, feature_count)
    query_wgrad = weight_term(rows_in, query_grad)
    key_wgrad = weight_term(rows_in, key_grad)
    value_wgrad = weight_term(rows_in, value_grad)
    query_bias_grad = bias_term(query_grad)
    value_bias_grad = bias_term(value_grad)
    input_full = (
        grad1
        + apply_back(query_grad, query_full)
        + apply_back(key_grad, key_full)
        + apply_back(value_grad, value_full)
    )
    live_rows = lax.broadcasted_iota(jnp.int32, (row_count,), 0) < live_count[0]
    input_grad = jnp.where(live_rows[:, None, None], input_full, 0.0)
    devices = packed_full.shape[0]
    small_terms = jnp.concatenate(
        [
            v.reshape(devices, -1, small_rows)
            for v in (
                query_bias_grad,
                value_bias_grad,
                output_bias_grad,
                gain1_grad,
                shift1_grad,
                down_bias_grad,
                gain2_grad,
                shift2_grad,
                up_bias_grad,
            )
        ],
        axis=1,
    )
    small_sum = lax.psum_scatter(small_terms, ("dp", "fsdp"), scatter_dimension=0, tiled=True)[0]
    down_sum, up_sum, output_sum, value_sum, query_sum, key_sum = (
        lax.psum_scatter(
            term.astype(jnp.bfloat16), ("dp", "fsdp"), scatter_dimension=0, tiled=True
        ).astype(jnp.float32)
        for term in (down_grad, up_grad, output_grad, value_wgrad, query_wgrad, key_wgrad)
    )
    return (
        slot_acts,
        input_grad,
        query_sum,
        key_sum,
        value_sum,
        output_sum,
        small_sum[0],
        small_sum[1],
        small_sum[2],
        small_sum[3],
        small_sum[4],
        up_sum,
        small_sum[8:].reshape(-1),
        down_sum,
        small_sum[5],
        small_sum[6],
        small_sum[7],
    )


def solution(mesh):
    placed = (
        P(("dp", "fsdp"), None, None),
        P(("dp", "fsdp")),
        P(("dp", "fsdp")),
        P(("dp", "fsdp"), None, None),
        P(("dp", "fsdp"), None),
        P(("dp", "fsdp"), None),
        P(("dp", "fsdp"), None),
        P(("dp", "fsdp"), None),
        P(("dp", "fsdp")),
        P(("dp", "fsdp")),
        P(("dp", "fsdp")),
        P(("dp", "fsdp")),
        P(("dp", "fsdp")),
        P(("dp", "fsdp"), None),
        P(("dp", "fsdp")),
        P(("dp", "fsdp"), None),
        P(("dp", "fsdp")),
        P(("dp", "fsdp")),
        P(("dp", "fsdp")),
    )
    kernels = mesh.shape["dp"] == 4 and mesh.shape["fsdp"] == 8
    return jax.shard_map(
        on_device_kernels if kernels else on_device_plain,
        mesh=mesh,
        in_specs=placed,
        out_specs=(
            P(("dp", "fsdp"), None, None),
            P(("dp", "fsdp"), None, None),
            P(("dp", "fsdp"), None),
            P(("dp", "fsdp"), None),
            P(("dp", "fsdp"), None),
            P(("dp", "fsdp"), None),
            P(("dp", "fsdp")),
            P(("dp", "fsdp")),
            P(("dp", "fsdp")),
            P(("dp", "fsdp")),
            P(("dp", "fsdp")),
            P(("dp", "fsdp"), None),
            P(("dp", "fsdp")),
            P(("dp", "fsdp"), None),
            P(("dp", "fsdp")),
            P(("dp", "fsdp")),
            P(("dp", "fsdp")),
        ),
        check_vma=False,
    )
```
